32 devices in a mesh: seq: 4 (over x, core), group: 8 (over z, y).
Axes of the slice: x: 2, y: 2, z: 4, core: 2. Of those that a mesh axis runs over, the one named last changes fastest.
Arguments:
- token_ids: int32 [4, 1024], P(None, 'group'), may hold values from 0 to 50256
- target_ids: int32 [4, 1024], P(None, 'group'), may hold values from 0 to 50256
- doc_lengths: int32 [4, 8], replicated, may hold values from 1 to 1017, as said below
- expert_ids: int32 [4, 1024, 1], P('seq', 'group'), may hold values from 0 to 15; in each aligned block of 128 rows (0 to 127, 128 to 255, ..., all dimensions but the last counted through in order) at most 16 rows name the same one
- vocab_table: float32 [50304, 768], P(('seq', 'group'))
- vocab_table_mom: float32 [50304, 768], P(('seq', 'group')), may hold values from -5.340576e-05 to 5.340576e-05
- vocab_table_ema: float32 [50304, 768], P(('seq', 'group')), may hold values from -0.4375 to 0.4375
- mixer_in: float32 [768, 3072], P('group'), may hold values from -0.21875 to 0.21875
- mixer_in_mom: float32 [768, 3072], P('group'), may hold values from -5.340576e-05 to 5.340576e-05
- mixer_in_ema: float32 [768, 3072], P('group'), may hold values from -0.21875 to 0.21875
- mixer_x: float32 [1536, 128], P('group'), may hold values from -0.15625 to 0.15625
- mixer_x_mom: float32 [1536, 128], P('group'), may hold values from -5.340576e-05 to 5.340576e-05
- mixer_x_ema: float32 [1536, 128], P('group'), may hold values from -0.15625 to 0.15625
- mixer_out: float32 [1536, 768], P('group'), may hold values from -0.15625 to 0.15625
- mixer_out_mom: float32 [1536, 768], P('group'), may hold values from -5.340576e-05 to 5.340576e-05
- mixer_out_ema: float32 [1536, 768], P('group'), may hold values from -0.15625 to 0.15625
- channel: float32 [23, 1536], P(None, 'group')
- channel_mom: float32 [23, 1536], P(None, 'group'), may hold values from -5.340576e-05 to 5.340576e-05
- channel_ema: float32 [23, 1536], P(None, 'group'), may hold values from -6 to 6
- norm_gains: float32 [3, 768], P(None, 'group'), may hold values from 0.5 to 1.5
- norm_gains_mom: float32 [3, 768], P(None, 'group'), may hold values from -5.340576e-05 to 5.340576e-05
- norm_gains_ema: float32 [3, 768], P(None, 'group'), may hold values from 0.5 to 1.5
- router: float32 [768, 16], P('group'), may hold values from -0.109375 to 0.109375
- router_mom: float32 [768, 16], P('group'), may hold values from -5.340576e-05 to 5.340576e-05
- router_ema: float32 [768, 16], P('group'), may hold values from -0.109375 to 0.109375
- experts: float32 [2, 16, 3072, 768], P(None, 'seq', 'group'), may hold values from -0.21875 to 0.21875
- experts_mom: float32 [2, 16, 3072, 768], P(None, 'seq', 'group'), may hold values from -5.340576e-05 to 5.340576e-05
- experts_ema: float32 [2, 16, 3072, 768], P(None, 'seq', 'group'), may hold values from -0.21875 to 0.21875
Outputs:
- loss_sum: float32 [], replicated
- grad_norm: float32 [], replicated
- moe_branch: float32 [4, 1024, 768], P('seq', 'group')
- vocab_table_new: float32 [50304, 768], P(('seq', 'group'))
- vocab_table_mom_new: float32 [50304, 768], P(('seq', 'group'))
- vocab_table_ema_new: float32 [50304, 768], P(('seq', 'group'))
- mixer_in_new: float32 [768, 3072], P('group')
- mixer_in_mom_new: float32 [768, 3072], P('group')
- mixer_in_ema_new: float32 [768, 3072], P('group')
- mixer_x_new: float32 [1536, 128], P('group')
- mixer_x_mom_new: float32 [1536, 128], P('group')
- mixer_x_ema_new: float32 [1536, 128], P('group')
- mixer_out_new: float32 [1536, 768], P('group')
- mixer_out_mom_new: float32 [1536, 768], P('group')
- mixer_out_ema_new: float32 [1536, 768], P('group')
- channel_new: float32 [23, 1536], P(None, 'group')
- channel_mom_new: float32 [23, 1536], P(None, 'group')
- channel_ema_new: float32 [23, 1536], P(None, 'group')
- norm_gains_new: float32 [3, 768], P(None, 'group')
- norm_gains_mom_new: float32 [3, 768], P(None, 'group')
- norm_gains_ema_new: float32 [3, 768], P(None, 'group')
- router_new: float32 [768, 16], P('group')
- router_mom_new: float32 [768, 16], P('group')
- router_ema_new: float32 [768, 16], P('group')
- experts_new: float32 [2, 16, 3072, 768], P(None, 'seq', 'group')
- experts_mom_new: float32 [2, 16, 3072, 768], P(None, 'seq', 'group')
- experts_ema_new: float32 [2, 16, 3072, 768], P(None, 'seq', 'group')
The draws below stay inside these ranges and needn't reach their ends.
Inputs may be any that keep to these rules, and one draw needn't show every extreme that they name: `doc_lengths`: each row sums to 1024; the second document of every sequence starts within its first 128 positions and ends within its last 128. `expert_ids`: among the 128 rows of one device no expert is named more than 16 times, and in every draw some device names some expert exactly 16 times.
All inputs are finite; a program needn't handle non-finite values.
Results may differ from the reference program's by a relative error of at most 0.0095.
The reference program's roundings to bfloat16 on the way count: a program that leaves them out, or rounds other values in their place, can miss the bound.
Values may be sent and summed in bfloat16 or wider, within the bound.
A program may use at most 448 MiB of HBM per device.

```python
import math
import jax
import jax.numpy as jnp
import numpy as np
from jax import lax

D = 768
DI = 1536
STATE = 16
RANK = 48
CONV = 4
FF = 3072
VOCAB = 50304
VOCAB_REAL = 50257
TOK_DEV = 128
DOCS = 8
SEQS = 4
LEN = 1024
EXPERTS = 16
CAP = 16
N_SEQ = 4
N_GROUP = 8


def draw_doc_lengths(key, part):
    key = jax.random.fold_in(key, 5)
    first_key, second_key, third_key = jax.random.split(key, 3)
    leading = jax.random.randint(first_key, (SEQS, 1), 1, TOK_DEV // 2 + 1)
    trailing = jax.random.randint(second_key, (SEQS, DOCS - 2), 1, TOK_DEV // 8 + 1)
    picked = jax.random.randint(third_key, (), 0, SEQS)
    longest = (jnp.arange(SEQS, dtype=jnp.int32) == picked)[:, None]
    leading = jnp.where(longest, 1, leading)
    trailing = jnp.where(longest, 1, trailing)
    middle = LEN - jnp.sum(leading, axis=1, keepdims=True) - jnp.sum(trailing, axis=1, keepdims=True)
    return jnp.concatenate([leading, middle, trailing], axis=1).astype(jnp.int32)


def draw_vocab_table(key, part):
    key = jax.random.fold_in(key, 7)
    position = jnp.arange(VOCAB, dtype=jnp.float32)[:, None] / VOCAB
    base = jax.random.truncated_normal(key, -4.0, 4.0, (VOCAB, D))
    spread = 1.0 + 2.0 * position
    return (base * spread / D ** 0.5).astype(jnp.float32)


def draw_channel(key, part):
    key = jax.random.fold_in(key, 11)
    keys = jax.random.split(key, 5)
    conv_taps = jax.random.normal(keys[0], (CONV, DI)) * 0.5
    conv_bias = jax.random.normal(keys[1], (1, DI)) * 0.1
    skip_row = jax.random.uniform(keys[3], (1, DI), minval=0.5, maxval=1.5)
    step_bias = jax.random.uniform(keys[2], (1, DI), minval=-6.0, maxval=-2.0)
    rate_logs = jax.random.uniform(keys[4], (STATE, DI), minval=-6.0, maxval=1.0)
    return jnp.concatenate([conv_taps, conv_bias, step_bias, skip_row, rate_logs]).astype(jnp.float32)


def plant(values, own_key, smallest, high):
    longest = values.shape.index(max(values.shape))
    spots = []
    for shift in (0, 1):
        where = [jax.random.randint(jax.random.fold_in(own_key, axis), (), 0, length) for axis, length in enumerate(values.shape)]
        where[longest] = (where[longest] + shift) % values.shape[longest]
        spots.append(tuple(where))
    return values.at[spots[0]].set(smallest).at[spots[1]].set(high)


def block_levels(own_key, extent, shards, low, high):
    factor_of, own = 1.0, jax.random.fold_in(own_key, 6)
    for dim, blocks in shards:
        steps = jnp.exp(jax.random.uniform(jax.random.fold_in(own, dim), (blocks,), jnp.float32, low / len(shards), high / len(shards)))
        factor_of = factor_of * jnp.repeat(steps, extent[dim] // blocks).reshape([-1 if axis == dim else 1 for axis in range(len(extent))])
    return factor_of


def rank_bounds(amount, slope):
    weights = [(1 << 20) // math.isqrt(rank ** slope) + 1 for rank in range(1, amount + 1)]
    deviation = 1 + sum(weights) // (1 << 30)
    return np.cumsum(np.array([max(1, weight // deviation) for weight in weights]))


def ranked_ids(own_key, dims, amount, lean):
    grid = rank_bounds(amount, lean)
    lot = jax.random.randint(jax.random.fold_in(own_key, 1), dims, 0, int(grid[amount - 1]))
    grade = jnp.searchsorted(jnp.asarray(grid, jnp.int32), lot, side="right")
    return jax.random.permutation(jax.random.fold_in(own_key, 2), amount)[grade].astype(jnp.int32)


def deal_out(stream_key, own, number, rows, count, top, limit, slope):
    order = jax.random.permutation(stream_key, count)
    packed, common = load_shares(count, rows * top, limit, slope, True), load_shares(count, rows * top, limit, slope, False)
    places = jnp.arange(count)

    def named(lengths, offset_by):
        used = int((lengths > 0).sum())
        fixed = max(1, used // 4)
        passed = fixed + (places - fixed + offset_by * (used - fixed)) % max(1, count - fixed)
        return jnp.zeros((count,), jnp.int32).at[order[jnp.where(places < fixed, places, passed)]].set(jnp.asarray(lengths, jnp.int32))

    lengths = jnp.where(number % 4 == 0, named(packed, number // 4), named(common, number - number // 4 - 1))
    mixed = jax.random.permutation(jax.random.fold_in(own, 3), count)
    source_of, sink = mixed[0:count // 2 * 2:2], mixed[1:count // 2 * 2:2]
    margin = jnp.minimum(lengths[source_of] - 1, limit - lengths[sink]) // 2
    margin = jnp.where((source_of == order[0]) | (sink == order[0]) | (lengths[sink] == 0), 0, jnp.maximum(margin, 0))
    passed = jax.random.randint(jax.random.fold_in(own, 4), (count // 2,), 0, 1 << 20) % (margin + 1)
    lengths = lengths.at[source_of].add(-passed).at[sink].add(passed)
    labels = jnp.searchsorted(jnp.cumsum(lengths), jnp.arange(rows * top), side="right").astype(jnp.int32)
    grid = labels.reshape(top, rows).T
    grid = grid[jax.random.permutation(jax.random.fold_in(own, 1), rows)]
    offset_by = jax.random.randint(jax.random.fold_in(own, 2), (rows, 1), 0, top)
    return jnp.take_along_axis(grid, (jnp.arange(top)[None, :] + offset_by) % top, axis=1)


def load_shares(amount, total, reach, slope, full):
    weights = [(1 << 20) // math.isqrt(rank ** slope) + 1 for rank in range(1, amount + 1)]
    largest = reach if full else min(reach, max(-(-total // amount), total * weights[0] // sum(weights)))
    least = 1 if total - largest >= amount - 1 else 0
    given, rest = [largest] + [least] * (amount - 1), total - largest - least * (amount - 1)
    while rest > 0:
        free = [i for i in range(1, amount) if given[i] < largest] or [i for i in range(1, amount) if given[i] < reach]
        whole, remaining = sum([weights[i] for i in free]), rest
        for i in free:
            more = min(reach - given[i], max(1, remaining * weights[i] // whole), rest)
            given[i] = given[i] + more
            rest = rest - more
    return np.array(given)


def gaussian(key, shape, deviation, most, cuts=(), held_as=jnp.bfloat16):
    entries = deviation * jax.random.normal(key, shape, jnp.float32)
    if cuts:
        entries = entries * block_levels(key, shape, cuts, -0.22, 0.18)
    return jnp.clip(entries, -most, most).astype(held_as)


def setup_inputs(seed: int = 0) -> dict:
    arg_keys = jax.random.split(jax.random.key(seed), 29)
    token_ids = plant(ranked_ids(arg_keys[0], (SEQS, LEN), VOCAB_REAL, 2), jax.random.fold_in(arg_keys[0], 3), 0, VOCAB_REAL - 1).astype(jnp.int32)
    target_ids = plant(ranked_ids(arg_keys[1], (SEQS, LEN), VOCAB_REAL, 2), jax.random.fold_in(arg_keys[1], 3), 0, VOCAB_REAL - 1).astype(jnp.int32)
    doc_lengths = draw_doc_lengths(jax.random.fold_in(arg_keys[28], 71), 0)
    expert_ids_keys = jax.random.split(jax.random.fold_in(arg_keys[3], 1), SEQS * LEN // TOK_DEV)
    expert_ids_turns = jax.random.permutation(jax.random.fold_in(arg_keys[3], 3), SEQS * LEN // TOK_DEV)
    expert_ids = jax.vmap(lambda own, number: deal_out(jax.random.fold_in(arg_keys[3], 2), own, number, TOK_DEV, EXPERTS, 1, CAP, 2))(expert_ids_keys, expert_ids_turns).reshape((SEQS, LEN, 1))
    vocab_table = draw_vocab_table(jax.random.fold_in(arg_keys[28], 71), 0)
    vocab_table_mom = gaussian(arg_keys[5], (VOCAB, D), (0.1 / (VOCAB * D + 2 * EXPERTS * D * FF) ** 0.5), 5.340576171875e-05, ((0, 32),), jnp.float32)
    vocab_table_ema = gaussian(arg_keys[6], (VOCAB, D), (2.0 / D ** 0.5), 0.4375, ((0, 32),), jnp.float32)
    mixer_in = gaussian(arg_keys[7], (D, 2 * DI), D ** -0.5, 0.21875, ((0, 8),), jnp.float32)
    mixer_in_mom = gaussian(arg_keys[8], (D, 2 * DI), (0.1 / (VOCAB * D + 2 * EXPERTS * D * FF) ** 0.5), 5.340576171875e-05, ((0, 8),), jnp.float32)
    mixer_in_ema = gaussian(arg_keys[9], (D, 2 * DI), D ** -0.5, 0.21875, ((0, 8),), jnp.float32)
    mixer_x = gaussian(arg_keys[10], (DI, 2 * RANK + 2 * STATE), DI ** -0.5, 0.15625, ((0, 8),), jnp.float32)
    mixer_x_mom = gaussian(arg_keys[11], (DI, 2 * RANK + 2 * STATE), (0.1 / (VOCAB * D + 2 * EXPERTS * D * FF) ** 0.5), 5.340576171875e-05, ((0, 8),), jnp.float32)
    mixer_x_ema = gaussian(arg_keys[12], (DI, 2 * RANK + 2 * STATE), DI ** -0.5, 0.15625, ((0, 8),), jnp.float32)
    mixer_out = gaussian(arg_keys[13], (DI, D), DI ** -0.5, 0.15625, ((0, 8),), jnp.float32)
    mixer_out_mom = gaussian(arg_keys[14], (DI, D), (0.1 / (VOCAB * D + 2 * EXPERTS * D * FF) ** 0.5), 5.340576171875e-05, ((0, 8),), jnp.float32)
    mixer_out_ema = gaussian(arg_keys[15], (DI, D), DI ** -0.5, 0.15625, ((0, 8),), jnp.float32)
    channel = draw_channel(jax.random.fold_in(arg_keys[28], 71), 0)
    channel_mom = gaussian(arg_keys[17], (CONV + 3 + STATE, DI), (0.1 / (VOCAB * D + 2 * EXPERTS * D * FF) ** 0.5), 5.340576171875e-05, ((1, 8),), jnp.float32)
    channel_ema = gaussian(arg_keys[18], (CONV + 3 + STATE, DI), 1.0, 6.0, ((1, 8),), jnp.float32)
    norm_gains = jnp.clip(1.0 + 0.1 * jax.random.normal(arg_keys[19], (3, D), jnp.float32), 0.5, 1.5)
    norm_gains_mom = gaussian(arg_keys[20], (3, D), (0.1 / (VOCAB * D + 2 * EXPERTS * D * FF) ** 0.5), 5.340576171875e-05, ((1, 8),), jnp.float32)
    norm_gains_ema = jnp.clip(1.0 + 0.1 * jax.random.normal(arg_keys[21], (3, D), jnp.float32), 0.5, 1.5)
    router = gaussian(arg_keys[22], (D, EXPERTS), (0.5 / D ** 0.5), 0.109375, ((0, 8),), jnp.float32)
    router_mom = gaussian(arg_keys[23], (D, EXPERTS), (0.1 / (VOCAB * D + 2 * EXPERTS * D * FF) ** 0.5), 5.340576171875e-05, ((0, 8),), jnp.float32)
    router_ema = gaussian(arg_keys[24], (D, EXPERTS), (0.5 / D ** 0.5), 0.109375, ((0, 8),), jnp.float32)
    experts = gaussian(arg_keys[25], (2, EXPERTS, FF, D), D ** -0.5, 0.21875, ((1, 4), (2, 8)), jnp.float32)
    experts_mom = gaussian(arg_keys[26], (2, EXPERTS, FF, D), (0.1 / (VOCAB * D + 2 * EXPERTS * D * FF) ** 0.5), 5.340576171875e-05, ((1, 4), (2, 8)), jnp.float32)
    experts_ema = gaussian(arg_keys[27], (2, EXPERTS, FF, D), D ** -0.5, 0.21875, ((1, 4), (2, 8)), jnp.float32)
    return {"token_ids": token_ids, "target_ids": target_ids, "doc_lengths": doc_lengths, "expert_ids": expert_ids, "vocab_table": vocab_table, "vocab_table_mom": vocab_table_mom, "vocab_table_ema": vocab_table_ema, "mixer_in": mixer_in, "mixer_in_mom": mixer_in_mom, "mixer_in_ema": mixer_in_ema, "mixer_x": mixer_x, "mixer_x_mom": mixer_x_mom, "mixer_x_ema": mixer_x_ema, "mixer_out": mixer_out, "mixer_out_mom": mixer_out_mom, "mixer_out_ema": mixer_out_ema, "channel": channel, "channel_mom": channel_mom, "channel_ema": channel_ema, "norm_gains": norm_gains, "norm_gains_mom": norm_gains_mom, "norm_gains_ema": norm_gains_ema, "router": router, "router_mom": router_mom, "router_ema": router_ema, "experts": experts, "experts_mom": experts_mom, "experts_ema": experts_ema}


EPS = 1e-05
CLIP = 0.1
MOMENTUM = 0.9
LRATE = 1000.0
CHANNEL_LRATE = 10000.0
EMA_KEEP = 0.8
HIGHEST = lax.Precision.HIGHEST
HEAD_BLOCK = 512

@jax.custom_vjp
def low(v):
    return lax.optimization_barrier(v.astype(jnp.bfloat16)).astype(jnp.float32)

@jax.custom_vjp
def low_back(v):
    return v

def low_keep(v):
    return (low(v), None)

def low_pass(kept, grad):
    return (grad,)

def back_keep(v):
    return (v, None)

def back_low(kept, grad):
    return (low(grad),)
low.defvjp(low_keep, low_pass)
low_back.defvjp(back_keep, back_low)

def product(left, right):
    return jnp.dot(left, right, precision=HIGHEST, preferred_element_type=jnp.float32)

def product_nt(left, right):
    return lax.dot_general(left, right, (((1,), (1,)), ((), ())), precision=HIGHEST, preferred_element_type=jnp.float32)

def rms_scaled(values, gain_row):
    return values * lax.rsqrt(lax.optimization_barrier(jnp.mean(values * values, axis=-1, keepdims=True)) + EPS) * gain_row

def doc_layout(doc_lengths):
    doc_ends = jnp.cumsum(doc_lengths, axis=1)
    doc_begins = doc_ends - doc_lengths
    where_at = jnp.arange(LEN, dtype=jnp.int32)
    segment = lax.optimization_barrier(jnp.sum((where_at[None, :, None] >= doc_ends[:, None, :]).astype(jnp.int32), axis=2))
    onehot_doc = (segment[:, :, None] == jnp.arange(DOCS, dtype=jnp.int32)[None, None, :]).astype(jnp.float32)
    weight = lax.optimization_barrier(jnp.sum(onehot_doc / doc_lengths[:, None, :].astype(jnp.float32), axis=2))
    starting = lax.optimization_barrier(jnp.sum((where_at[None, :, None] == doc_begins[:, None, :]).astype(jnp.float32), axis=2))
    return (segment, weight, 1.0 - starting)

def mixer_layer(embedded, segment, keeping, weight_in, weight_x, weight_out, channel, gain_row):
    normed = low(rms_scaled(embedded, gain_row))
    projected_in = low_back(product(normed, weight_in))
    conv_input = low(projected_in[:, :DI])
    gate_z = projected_in[:, DI:]
    padded = jnp.concatenate([jnp.zeros((CONV - 1, DI), jnp.float32), conv_input])
    padded_seg = jnp.concatenate([jnp.full((CONV - 1,), -1, jnp.int32), segment])
    conv_out = channel[CONV]
    for conv_tap in range(CONV):
        same_doc = (padded_seg[conv_tap:conv_tap + LEN] == segment).astype(jnp.float32)
        conv_out = conv_out + channel[conv_tap] * padded[conv_tap:conv_tap + LEN] * same_doc[:, None]
    activated = jax.nn.silu(conv_out)
    projected = low_back(product(low(activated), weight_x[:, :RANK + 2 * STATE]))
    dt_pre = low_back(product_nt(low(projected[:, :RANK]), weight_x[:, RANK + 2 * STATE:]))
    step_size = jax.nn.softplus(dt_pre + channel[CONV + 1])
    decay_rates = -jnp.exp(channel[CONV + 3:].T)

    def advance(carry_state, inputs):
        step_row, b_row, c_row, input_row, keep_row = inputs
        carry_state = jnp.exp(step_row[:, None] * decay_rates) * keep_row * carry_state + (step_row * input_row)[:, None] * b_row[None, :]
        return (carry_state, lax.optimization_barrier(jnp.sum(carry_state * c_row[None, :], axis=1)))
    unused, scanned = lax.scan(advance, jnp.zeros((DI, STATE), jnp.float32), (step_size, projected[:, RANK:RANK + STATE], projected[:, RANK + STATE:], activated, keeping))
    outputs = (scanned + channel[CONV + 2] * activated) * jax.nn.silu(gate_z)
    return embedded + low_back(product(low(outputs), weight_out))

def experts_layer(hidden, gain_row, router, experts, expert_ids):
    normed = low(rms_scaled(hidden, gain_row))
    probability = jax.nn.softmax(product(normed, router), axis=-1)
    chosen = (expert_ids[:, None] == jnp.arange(EXPERTS, dtype=jnp.int32)[None, :]).astype(jnp.float32)
    gate_value = lax.optimization_barrier(jnp.sum(probability * chosen, axis=1))
    slot_index = lax.optimization_barrier(jnp.sum((jnp.cumsum(chosen, axis=0) - 1.0) * chosen, axis=1)).astype(jnp.int32)
    sent_rows = low_back(normed)
    slot_rows = jnp.zeros((EXPERTS, CAP * N_SEQ * N_GROUP, D), jnp.float32).at[expert_ids, slot_index].set(sent_rows)
    before = low_back(jnp.einsum('ecd,efd->ecf', slot_rows, experts[0], precision=HIGHEST))
    inner_act = low(jax.nn.gelu(before))
    result = jnp.einsum('ecf,efd->ecd', inner_act, experts[1], precision=HIGHEST)
    returned = low_back(low(result[expert_ids, slot_index]))
    branch = gate_value[:, None] * returned
    return (hidden + branch, branch)

def head_loss(normed, table, target_ids, weight):
    columns = jnp.arange(VOCAB, dtype=jnp.int32)

    def block_loss(inputs):
        block_rows, block_targets, block_weight = inputs
        logits = low_back(product_nt(block_rows, table))
        logits = jnp.where(columns[None, :] < VOCAB_REAL, logits, -1e+30)
        largest = lax.optimization_barrier(jnp.max(logits, axis=1, keepdims=True))
        log_total = largest[:, 0] + jnp.log(lax.optimization_barrier(jnp.sum(jnp.exp(logits - largest), axis=1)))
        picked = lax.optimization_barrier(jnp.sum(jnp.where(columns[None, :] == block_targets[:, None], logits, 0.0), axis=1))
        return jnp.sum(block_weight * (log_total - picked))
    block_count = normed.shape[0] // HEAD_BLOCK
    pieces = lax.map(jax.checkpoint(block_loss), (normed.reshape(block_count, HEAD_BLOCK, D), target_ids.reshape(block_count, HEAD_BLOCK), weight.reshape(block_count, HEAD_BLOCK)))
    return jnp.sum(pieces)

def forward(weights, token_ids, target_ids, doc_lengths, expert_ids):
    table, weight_in, weight_x, weight_out, channel, gains, router, experts = [low(member) for member in weights]
    segment, weight, keeping = doc_layout(doc_lengths)
    embedded = low_back(table[token_ids])

    def one_sequence(inputs):
        return mixer_layer(inputs[0], inputs[1], inputs[2], weight_in, weight_x, weight_out, channel, gains[0])
    mixed_out = lax.map(jax.checkpoint(one_sequence), (embedded, segment, keeping))
    hidden, branch = experts_layer(mixed_out.reshape(SEQS * LEN, D), gains[1], router, experts, expert_ids.reshape(SEQS * LEN))
    normed = low(rms_scaled(hidden, gains[2]))
    loss = head_loss(normed, table, target_ids.reshape(SEQS * LEN), weight.reshape(SEQS * LEN))
    return (loss, branch.reshape(SEQS, LEN, D))

def renewed(master, moment, average, gradient, clip_factor, rate):
    scaled = clip_factor * gradient
    moment_new = MOMENTUM * moment + scaled
    master_new = master - rate * (scaled + MOMENTUM * moment_new)
    return (master_new, moment_new, EMA_KEEP * average + (1.0 - EMA_KEEP) * master_new)

def reference(token_ids, target_ids, doc_lengths, expert_ids, vocab_table, vocab_table_mom, vocab_table_ema, mixer_in, mixer_in_mom, mixer_in_ema, mixer_x, mixer_x_mom, mixer_x_ema, mixer_out, mixer_out_mom, mixer_out_ema, channel, channel_mom, channel_ema, norm_gains, norm_gains_mom, norm_gains_ema, router, router_mom, router_ema, experts, experts_mom, experts_ema):
    masters = (vocab_table, mixer_in, mixer_x, mixer_out, channel, norm_gains, router, experts)
    moments = (vocab_table_mom, mixer_in_mom, mixer_x_mom, mixer_out_mom, channel_mom, norm_gains_mom, router_mom, experts_mom)
    averages = (vocab_table_ema, mixer_in_ema, mixer_x_ema, mixer_out_ema, channel_ema, norm_gains_ema, router_ema, experts_ema)
    loss_sum, pullback, moe_branch = jax.vjp(lambda *member: forward(member, token_ids, target_ids, doc_lengths, expert_ids), *masters, has_aux=True)
    gradients = pullback(jnp.ones_like(loss_sum))
    grad_norm = jnp.sqrt(sum((jnp.sum(entry * entry) for entry in gradients)))
    clip_factor = jnp.minimum(1.0, CLIP / (grad_norm + 1e-06))
    triples = [renewed(masters[index], moments[index], averages[index], gradients[index], clip_factor, CHANNEL_LRATE if index == 4 else LRATE) for index in range(8)]
    return (loss_sum, grad_norm, moe_branch, triples[0][0], triples[0][1], triples[0][2], triples[1][0], triples[1][1], triples[1][2], triples[2][0], triples[2][1], triples[2][2], triples[3][0], triples[3][1], triples[3][2], triples[4][0], triples[4][1], triples[4][2], triples[5][0], triples[5][1], triples[5][2], triples[6][0], triples[6][1], triples[6][2], triples[7][0], triples[7][1], triples[7][2])
```

```python
import functools

import jax
import jax.numpy as jnp
from jax import lax
from jax.experimental import pallas as pl
from jax.experimental.pallas import tpu as pltpu
from jax.sharding import PartitionSpec as P

D = 768
DI = 1536
STATE = 16
RANK = 48
CONV = 4
VOCAB_REAL = 50257


EPS = 1e-05
CLIP = 0.1
MOMENTUM = 0.9
LRATE = 1000.0
CHANNEL_LRATE = 10000.0
EMA_KEEP = 0.8
HIGHEST = lax.Precision.HIGHEST
MESH = pl.DeviceIdType.MESH
VMEM_LIMIT = 56 << 20
LANES = 128


def axis_sizes():
    seq, group = (lax.axis_size("seq"), lax.axis_size("group"))
    core = 2 if seq % 2 == 0 else 1
    y = 1
    while 4 * y * y <= group and group % (2 * y) == 0:
        y *= 2
    return {"x": seq // core, "core": core, "z": group // y, "y": y}


def my_place(sizes):
    seq, group = (lax.axis_index("seq"), lax.axis_index("group"))
    return {
        "x": seq // sizes["core"],
        "core": seq % sizes["core"],
        "z": group // sizes["y"],
        "y": group % sizes["y"],
    }


def device_of(place, sizes):
    return (place["x"] * sizes["core"] + place["core"], place["z"] * sizes["y"] + place["y"])


def moved(place, axis, by, sizes):
    return {**place, axis: lax.rem(place[axis] + by + sizes[axis], sizes[axis])}


def block_of(place, sizes):
    seq, group = device_of(place, sizes)
    return seq * (sizes["z"] * sizes["y"]) + group


def meet(peers):
    barrier = pltpu.get_barrier_semaphore()
    for peer in peers:
        pl.semaphore_signal(barrier, inc=1, device_id=peer, device_id_type=MESH)
    pl.semaphore_wait(barrier, len(peers))


def line_peers(place, sizes):
    return [
        device_of(moved(place, axis, by, sizes), sizes)
        for axis in ("x", "core", "z", "y")
        for by in range(1, sizes[axis])
    ]


GATHER_ORDERS = (
    ("z", "y", "x", "core"),
    ("z", "x", "y", "core"),
    ("x", "z", "y", "core"),
    ("y", "z", "x", "core"),
)


def gather_kernel(sizes, pieces, own_ref, all_ref, local_sem, send_sem, recv_sem):
    place = my_place(sizes)
    meet(line_peers(place, sizes))
    keep_own = pltpu.make_async_copy(own_ref, all_ref.at[block_of(place, sizes)], local_sem)
    keep_own.start()
    held = [[(place, None)] for _ in pieces]
    sends = []
    for phase in range(4):
        fresh = [[] for _ in pieces]
        for turn in range(max(len(blocks) for blocks in held)):
            for which, (order, first, rows) in enumerate(pieces):
                if turn >= len(held[which]):
                    continue
                axis = order[phase]
                where, arrival = held[which][turn]
                if arrival is not None:
                    copy, seen = arrival
                    if not seen:
                        copy.wait_recv()
                        held[which][turn] = (where, (copy, True))
                span = pl.ds(first, rows)
                for by in range(1, sizes[axis]):
                    block = block_of(where, sizes)
                    source = own_ref.at[span] if arrival is None else all_ref.at[block, span]
                    number = len(sends)
                    copy = pltpu.make_async_remote_copy(
                        src_ref=source,
                        dst_ref=all_ref.at[block, span],
                        send_sem=send_sem.at[number],
                        recv_sem=recv_sem.at[number],
                        device_id=device_of(moved(place, axis, by, sizes), sizes),
                        device_id_type=MESH,
                    )
                    copy.start()
                    sends.append(copy)
                    fresh[which].append((moved(where, axis, -by, sizes), (copy, False)))
        held = [old + new for old, new in zip(held, fresh)]
    for blocks in held:
        for _, arrival in blocks:
            if arrival is not None and not arrival[1]:
                arrival[0].wait_recv()
    for copy in sends:
        copy.wait_send()
    keep_own.wait()


def split_rows(rows, orders):
    unit = 32 if rows % 32 == 0 else 16
    count = rows // unit
    pieces, first = ([], 0)
    for which in range(min(count, 4)):
        size = (count * (which + 1) // min(count, 4)) * unit - first
        pieces.append((orders[which % len(orders)], first, size))
        first += size
    return pieces


def gather_all(rows, collective_id):
    sizes = axis_sizes()
    devices = sizes["x"] * sizes["core"] * sizes["z"] * sizes["y"]
    pieces = split_rows(rows.shape[0], GATHER_ORDERS)
    copies = (devices - 1) * len(pieces)
    return pl.pallas_call(
        functools.partial(gather_kernel, sizes, pieces),
        out_shape=jax.ShapeDtypeStruct((devices,) + rows.shape, rows.dtype),
        in_specs=[pl.BlockSpec(memory_space=pltpu.VMEM)],
        out_specs=pl.BlockSpec(memory_space=pl.ANY),
        scratch_shapes=[
            pltpu.SemaphoreType.DMA,
            pltpu.SemaphoreType.DMA((copies,)),
            pltpu.SemaphoreType.DMA((copies,)),
        ],
        compiler_params=pltpu.CompilerParams(
            collective_id=collective_id, has_side_effects=True, vmem_limit_bytes=VMEM_LIMIT
        ),
        name="gather_all",
    )(rows)


SCATTER_ORDERS = (
    ("core", "x", "y", "z"),
    ("core", "y", "x", "z"),
    ("core", "y", "z", "x"),
    ("core", "x", "z", "y"),
)
NATURAL = ("x", "core", "z", "y")


def unravel(number, extents):
    places = []
    for extent in reversed(extents):
        places.append(lax.rem(number, extent))
        number = lax.div(number, extent)
    return tuple(reversed(places))


def scatter_kernel(sizes, pieces, full_ref, own_ref, *scratch):
    place = my_place(sizes)
    per_piece = len(scratch) // len(pieces)
    meet(line_peers(place, sizes))
    started = []
    flights = [None] * len(pieces)
    kept = []
    for which, (order, first, rows) in enumerate(pieces):
        index = tuple(place[a] if a == order[0] else slice(None) for a in NATURAL)
        copy = pltpu.make_async_copy(
            full_ref.at[index + (pl.ds(first, rows),)],
            scratch[which * per_piece + 4],
            scratch[which * per_piece + per_piece - 1],
        )
        copy.start()
        kept.append(copy)

    def launch(which, phase):
        order, first, rows = pieces[which]
        axis = order[phase]
        refs = scratch[which * per_piece : (which + 1) * per_piece]
        landing, send_sem, recv_sem = (refs[phase], refs[7 + 2 * phase], refs[8 + 2 * phase])
        left = [a for a in NATURAL if a not in order[:phase]]
        copies = []
        for by in range(1, sizes[axis]):
            to = moved(place, axis, by, sizes)
            index = tuple(to[axis] if a == axis else slice(None) for a in left)
            if phase == 0:
                source = full_ref.at[index + (pl.ds(first, rows),)]
            else:
                source = refs[3 + phase].at[index]
            copy = pltpu.make_async_remote_copy(
                src_ref=source,
                dst_ref=landing.at[by - 1],
                send_sem=send_sem.at[by - 1],
                recv_sem=recv_sem.at[by - 1],
                device_id=device_of(to, sizes),
                device_id_type=MESH,
            )
            copy.start()
            copies.append(copy)
            started.append(copy)
        flights[which] = copies

    def absorb(which, phase):
        order, first, rows = pieces[which]
        axis = order[phase]
        refs = scratch[which * per_piece : (which + 1) * per_piece]
        landing = refs[phase]
        before = [a for a in NATURAL if a not in order[:phase]]
        after = [a for a in before if a != axis]
        if phase == 0:
            kept[which].wait()
        for copy in flights[which]:
            copy.wait_recv()
        extents = tuple(sizes[a] for a in after)
        number = 1
        for extent in extents:
            number *= extent

        def add(step, carry):
            spot = dict(zip(after, unravel(step, extents)))
            mine = tuple(place[axis] if a == axis else spot[a] for a in before)
            there = tuple(spot[a] for a in after)
            kept_part = refs[4][there] if phase == 0 else refs[3 + phase][mine]
            total = kept_part.astype(jnp.float32)
            for by in range(1, sizes[axis]):
                total = total + landing[(by - 1,) + there].astype(jnp.float32)
            if phase == 3:
                own_ref[pl.ds(first, rows)] = total
            else:
                refs[4 + phase][there] = total.astype(jnp.bfloat16)
            return carry

        if number == 1:
            add(0, 0)
        else:
            lax.fori_loop(0, number, add, 0)

    for which in range(len(pieces)):
        launch(which, 0)
    for phase in range(4):
        for which in range(len(pieces)):
            absorb(which, phase)
            if phase < 3:
                launch(which, phase + 1)
    for copy in started:
        copy.wait_send()


def scatter_all(blocks, collective_id):
    sizes = axis_sizes()
    rows, width = blocks.shape[-2:]
    pieces = split_rows(rows, SCATTER_ORDERS)
    scratch = []
    for order, _, height in pieces:
        landings, sums, semaphores = ([], [], [])
        for phase in range(4):
            left = tuple(sizes[a] for a in NATURAL if a not in order[: phase + 1])
            others = max(1, sizes[order[phase]] - 1)
            landings.append(pltpu.VMEM((others,) + left + (height, width), jnp.bfloat16))
            if phase < 3:
                sums.append(pltpu.VMEM(left + (height, width), jnp.bfloat16))
            semaphores.append(pltpu.SemaphoreType.DMA((others,)))
            semaphores.append(pltpu.SemaphoreType.DMA((others,)))
        scratch += landings + sums + semaphores + [pltpu.SemaphoreType.DMA]
    shaped = blocks.reshape(tuple(sizes[a] for a in NATURAL) + (rows, width))
    return pl.pallas_call(
        functools.partial(scatter_kernel, sizes, pieces),
        out_shape=jax.ShapeDtypeStruct((rows, width), jnp.float32),
        in_specs=[pl.BlockSpec(memory_space=pl.ANY)],
        out_specs=pl.BlockSpec(memory_space=pltpu.VMEM),
        scratch_shapes=scratch,
        compiler_params=pltpu.CompilerParams(
            collective_id=collective_id, has_side_effects=True, vmem_limit_bytes=VMEM_LIMIT
        ),
        name="scatter_all",
    )(shaped)


def everyone(devices, groups, me, act):
    def step(by, carry):
        peer = lax.rem(me + by, devices)
        act(by, peer, (lax.div(peer, groups), lax.rem(peer, groups)))
        return carry

    lax.fori_loop(1, devices, step, 0)


def greet_everyone(devices, groups, me):
    barrier = pltpu.get_barrier_semaphore()

    def greet(by, peer, address):
        pl.semaphore_signal(barrier, inc=1, device_id=address, device_id_type=MESH)

    everyone(devices, groups, me, greet)
    pl.semaphore_wait(barrier, devices - 1)


def flat_place():
    groups = lax.axis_size("group")
    return (
        lax.axis_size("seq") * groups,
        groups,
        lax.axis_index("seq") * groups + lax.axis_index("group"),
    )


def share_kernel(own_ref, all_ref, send_sem, recv_sem):
    devices, groups, me = flat_place()
    greet_everyone(devices, groups, me)

    def copy_to(by, address):
        return pltpu.make_async_remote_copy(
            src_ref=own_ref,
            dst_ref=all_ref.at[me],
            send_sem=send_sem.at[by],
            recv_sem=recv_sem.at[by],
            device_id=address,
            device_id_type=MESH,
        )

    everyone(devices, groups, me, lambda by, peer, address: copy_to(by, address).start())
    all_ref[me] = own_ref[...]
    everyone(devices, groups, me, lambda by, peer, address: copy_to(by, address).wait())


def share_small(values, collective_id):
    devices = lax.axis_size("seq") * lax.axis_size("group")
    return pl.pallas_call(
        share_kernel,
        out_shape=jax.ShapeDtypeStruct((devices,) + values.shape, values.dtype),
        in_specs=[pl.BlockSpec(memory_space=pltpu.VMEM)],
        out_specs=pl.BlockSpec(memory_space=pltpu.VMEM),
        scratch_shapes=[
            pltpu.SemaphoreType.DMA((devices,)),
            pltpu.SemaphoreType.DMA((devices,)),
        ],
        compiler_params=pltpu.CompilerParams(collective_id=collective_id, has_side_effects=True),
        name="share_small",
    )(values)


def stats_kernel(parts_ref, all_ref, own_ref, got_ref, mine_ref, send_sem, recv_sem):
    devices, groups, me = flat_place()
    greet_everyone(devices, groups, me)

    def part_to(by, peer, address):
        return pltpu.make_async_remote_copy(
            src_ref=parts_ref.at[peer],
            dst_ref=got_ref.at[me],
            send_sem=send_sem.at[0, by],
            recv_sem=recv_sem.at[0, by],
            device_id=address,
            device_id_type=MESH,
        )

    def total_to(by, address):
        return pltpu.make_async_remote_copy(
            src_ref=mine_ref,
            dst_ref=all_ref.at[me],
            send_sem=send_sem.at[1, by],
            recv_sem=recv_sem.at[1, by],
            device_id=address,
            device_id_type=MESH,
        )

    everyone(devices, groups, me, lambda by, peer, address: part_to(by, peer, address).start())
    got_ref[me] = parts_ref[me]
    everyone(devices, groups, me, lambda by, peer, address: part_to(by, peer, address).wait())
    tops = got_ref[:, 0, :]
    top = jnp.max(tops, axis=0, keepdims=True)
    mass = jnp.sum(got_ref[:, 1, :] * jnp.exp(tops - top), axis=0, keepdims=True)
    hit = jnp.sum(got_ref[:, 2, :], axis=0, keepdims=True)
    level = top + jnp.log(mass)
    mine_ref[...] = jnp.broadcast_to(level, mine_ref.shape)
    everyone(devices, groups, me, lambda by, peer, address: total_to(by, address).start())
    all_ref[me] = mine_ref[...]
    own_ref[...] = jnp.broadcast_to(level - hit, own_ref.shape)
    everyone(devices, groups, me, lambda by, peer, address: total_to(by, address).wait())


def combine_stats(parts, collective_id):
    devices = parts.shape[0]
    shape = parts.shape[1:]
    return pl.pallas_call(
        stats_kernel,
        out_shape=(
            jax.ShapeDtypeStruct(parts.shape, jnp.float32),
            jax.ShapeDtypeStruct(shape, jnp.float32),
        ),
        in_specs=[pl.BlockSpec(memory_space=pltpu.VMEM)],
        out_specs=(pl.BlockSpec(memory_space=pltpu.VMEM),) * 2,
        scratch_shapes=[
            pltpu.VMEM(parts.shape, jnp.float32),
            pltpu.VMEM(shape, jnp.float32),
            pltpu.SemaphoreType.DMA((2, devices)),
            pltpu.SemaphoreType.DMA((2, devices)),
        ],
        compiler_params=pltpu.CompilerParams(collective_id=collective_id, has_side_effects=True),
        name="combine_stats",
    )(parts)


def chain_exchange(rates, total_step, flag, end_state, backwards, out_buf, in_buf, sems):
    devices, me = (lax.axis_size("group"), lax.axis_index("group"))
    seq = lax.axis_index("seq")
    send_sem, recv_sem = sems
    width = rates.shape[1]

    def join(first, second):
        return (
            jnp.exp(second[0] * rates) * second[1] * first[2] + second[2],
            first[0] + second[0],
            first[1] * second[1],
        )

    window = (total_step, flag, end_state)
    before = None
    distance, lap = (1, 0)
    copies = []
    while distance < devices:
        to = lax.rem(me + (devices - distance if backwards else distance), devices)
        out_buf[lap, 0:STATE] = window[2]
        out_buf[lap, STATE : STATE + 8] = jnp.concatenate(
            [
                jnp.broadcast_to(window[0], (4, width)),
                jnp.broadcast_to(window[1], (4, width)),
            ],
            axis=0,
        )
        copy = pltpu.make_async_remote_copy(
            src_ref=out_buf.at[lap],
            dst_ref=in_buf.at[lap],
            send_sem=send_sem.at[lap],
            recv_sem=recv_sem.at[lap],
            device_id=(seq, to),
            device_id_type=MESH,
        )
        copy.start()
        copies.append(copy)
        copy.wait_recv()
        reached = (me + distance < devices) if backwards else (me >= distance)
        real = jnp.where(reached, 1.0, 0.0)
        tail = in_buf[lap, STATE : STATE + 8]
        got = (
            tail[0:1] * real,
            tail[4:5] * real + (1.0 - real),
            in_buf[lap, 0:STATE] * real,
        )
        if before is None:
            before = got
        else:
            merged = join(got, before)
            before = (merged[1], merged[2], merged[0])
        merged = join(got, window)
        window = (merged[1], merged[2], merged[0])
        distance *= 2
        lap += 1
    for copy in copies:
        copy.wait_send()
    if before is None:
        return jnp.zeros_like(end_state)
    return before[2]


def chain_peers():
    devices, me = (lax.axis_size("group"), lax.axis_index("group"))
    seq = lax.axis_index("seq")
    distances = []
    distance = 1
    while distance < devices:
        distances += [distance, devices - distance]
        distance *= 2
    return [(seq, lax.rem(me + by, devices)) for by in sorted(set(distances))]


def chain_laps():
    laps, distance = (0, 1)
    while distance < lax.axis_size("group"):
        laps, distance = (laps + 1, distance * 2)
    return max(1, laps)


def spans(width):
    size = 512 if width % 512 == 0 else width
    return [slice(first, first + size) for first in range(0, width, size)]


def wide(value, copies):
    return jnp.concatenate([value] * copies, axis=1)


def folded(value):
    total = value[:, :LANES]
    for first in range(LANES, value.shape[1], LANES):
        total = total + value[:, first : first + LANES]
    return total


def scan_forward_kernel(
    step_ref, act_ref, b_ref, c_ref, keep_ref, rate_ref, y_ref, in_ref, out_buf, in_buf, ss, rs
):
    meet(chain_peers())
    tokens, width = step_ref.shape
    ends = []
    for span in spans(width):
        copies = (span.stop - span.start) // LANES
        rates = rate_ref[:, span]

        def advance(block, state, span=span, copies=copies, rates=rates):
            rows = pl.ds(pl.multiple_of(block * 8, 8), 8)
            steps = step_ref[rows, span]
            drives = steps * act_ref[rows, span]
            keeps = wide(keep_ref[rows, :], copies)
            for r in range(8):
                decay = jnp.exp(steps[r : r + 1] * rates) * keeps[r : r + 1]
                state = decay * state + drives[r : r + 1] * wide(b_ref[block * 8 + r], copies)
            return state

        ends.append(
            lax.fori_loop(
                0, tokens // 8, advance, jnp.zeros((STATE, span.stop - span.start), jnp.float32)
            )
        )
    total_step = jnp.sum(step_ref[...], axis=0, keepdims=True)
    flag = wide(jnp.min(keep_ref[...], axis=0, keepdims=True), width // LANES)
    incoming = chain_exchange(
        rate_ref[...],
        total_step,
        flag,
        jnp.concatenate(ends, axis=1),
        False,
        out_buf,
        in_buf,
        (ss, rs),
    )
    in_ref[...] = incoming
    for span in spans(width):
        copies = (span.stop - span.start) // LANES
        rates = rate_ref[:, span]

        def produce(block, state, span=span, copies=copies, rates=rates):
            rows = pl.ds(pl.multiple_of(block * 8, 8), 8)
            steps = step_ref[rows, span]
            drives = steps * act_ref[rows, span]
            keeps = wide(keep_ref[rows, :], copies)
            results = []
            for r in range(8):
                decay = jnp.exp(steps[r : r + 1] * rates) * keeps[r : r + 1]
                state = decay * state + drives[r : r + 1] * wide(b_ref[block * 8 + r], copies)
                results.append(
                    jnp.sum(state * wide(c_ref[block * 8 + r], copies), axis=0, keepdims=True)
                )
            y_ref[rows, span] = jnp.concatenate(results, axis=0)
            return state

        lax.fori_loop(0, tokens // 8, produce, in_ref[:, span])


def scan_scratch(width):
    laps = chain_laps()
    return [
        pltpu.VMEM((laps, STATE + 8, width), jnp.float32),
        pltpu.VMEM((laps, STATE + 8, width), jnp.float32),
        pltpu.SemaphoreType.DMA((laps,)),
        pltpu.SemaphoreType.DMA((laps,)),
    ]


def scan_forward(step, act, b_wide, c_wide, keep_wide, rates, collective_id):
    tokens, width = step.shape
    return pl.pallas_call(
        scan_forward_kernel,
        out_shape=(
            jax.ShapeDtypeStruct((tokens, width), jnp.float32),
            jax.ShapeDtypeStruct((STATE, width), jnp.float32),
        ),
        in_specs=[pl.BlockSpec(memory_space=pltpu.VMEM)] * 6,
        out_specs=(pl.BlockSpec(memory_space=pltpu.VMEM),) * 2,
        scratch_shapes=scan_scratch(width),
        compiler_params=pltpu.CompilerParams(
            collective_id=collective_id, has_side_effects=True, vmem_limit_bytes=VMEM_LIMIT
        ),
        name="scan_forward",
    )(step, act, b_wide, c_wide, keep_wide, rates)


def scan_backward_kernel(
    step_ref,
    act_ref,
    b_ref,
    c_ref,
    keep_ref,
    rate_ref,
    in_ref,
    grad_ref,
    along_ref,
    decayed_ref,
    gb_ref,
    gc_ref,
    grate_ref,
    prev_ref,
    carry_ref,
    out_buf,
    in_buf,
    ss,
    rs,
):
    meet(chain_peers())
    tokens, width = step_ref.shape
    blocks = tokens // 8
    ends = []
    for number, span in enumerate(spans(width)):
        size = span.stop - span.start
        copies = size // LANES
        rates = rate_ref[:, span]

        def replay(block, state, number=number, span=span, copies=copies, rates=rates):
            rows = pl.ds(pl.multiple_of(block * 8, 8), 8)
            steps = step_ref[rows, span]
            drives = steps * act_ref[rows, span]
            keeps = wide(keep_ref[rows, :], copies)
            grads = grad_ref[rows, span]
            for r in range(8):
                at = block * 8 + r
                prev_ref[at, :, span] = state
                decay = jnp.exp(steps[r : r + 1] * rates) * keeps[r : r + 1]
                state = decay * state + drives[r : r + 1] * wide(b_ref[at], copies)
                share = folded(grads[r : r + 1] * state)
                gc_ref[at] = share if number == 0 else gc_ref[at] + share
            return state

        lax.fori_loop(0, blocks, replay, in_ref[:, span])

        def pull(lap, carry, span=span, copies=copies, rates=rates):
            block = blocks - 1 - lap
            rows = pl.ds(pl.multiple_of(block * 8, 8), 8)
            steps = step_ref[rows, span]
            keeps = wide(keep_ref[rows, :], copies)
            grads = grad_ref[rows, span]
            for r in range(7, -1, -1):
                decay = jnp.exp(steps[r : r + 1] * rates) * keeps[r : r + 1]
                adjoint = grads[r : r + 1] * wide(c_ref[block * 8 + r], copies) + carry
                carry = decay * adjoint
            return carry

        ends.append(lax.fori_loop(0, blocks, pull, jnp.zeros((STATE, size), jnp.float32)))
    total_step = jnp.sum(step_ref[...], axis=0, keepdims=True)
    flag = wide(jnp.min(keep_ref[...], axis=0, keepdims=True), width // LANES)
    carry_ref[...] = chain_exchange(
        rate_ref[...],
        total_step,
        flag,
        jnp.concatenate(ends, axis=1),
        True,
        out_buf,
        in_buf,
        (ss, rs),
    )
    for number, span in enumerate(spans(width)):
        size = span.stop - span.start
        copies = size // LANES
        rates = rate_ref[:, span]

        def settle(lap, carries, number=number, span=span, copies=copies, rates=rates):
            carry, rate_total = carries
            block = blocks - 1 - lap
            rows = pl.ds(pl.multiple_of(block * 8, 8), 8)
            steps = step_ref[rows, span]
            drives = steps * act_ref[rows, span]
            keeps = wide(keep_ref[rows, :], copies)
            grads = grad_ref[rows, span]
            alongs, decays = ([None] * 8, [None] * 8)
            for r in range(7, -1, -1):
                at = block * 8 + r
                decay = jnp.exp(steps[r : r + 1] * rates) * keeps[r : r + 1]
                adjoint = grads[r : r + 1] * wide(c_ref[at], copies) + carry
                carry = decay * adjoint
                grad_exp = carry * prev_ref[at, :, span]
                rate_total = rate_total + grad_exp * steps[r : r + 1]
                alongs[r] = jnp.sum(adjoint * wide(b_ref[at], copies), axis=0, keepdims=True)
                decays[r] = jnp.sum(grad_exp * rates, axis=0, keepdims=True)
                share = folded(adjoint * drives[r : r + 1])
                gb_ref[at] = share if number == 0 else gb_ref[at] + share
            along_ref[rows, span] = jnp.concatenate(alongs, axis=0)
            decayed_ref[rows, span] = jnp.concatenate(decays, axis=0)
            return (carry, rate_total)

        _, rate_total = lax.fori_loop(
            0, blocks, settle, (carry_ref[:, span], jnp.zeros((STATE, size), jnp.float32))
        )
        grate_ref[:, span] = rate_total * rates


def scan_backward(step, act, b_wide, c_wide, keep_wide, rates, incoming, grad, collective_id):
    tokens, width = step.shape
    full = jax.ShapeDtypeStruct((tokens, width), jnp.float32)
    return pl.pallas_call(
        scan_backward_kernel,
        out_shape=(
            full,
            full,
            jax.ShapeDtypeStruct(b_wide.shape, jnp.float32),
            jax.ShapeDtypeStruct(c_wide.shape, jnp.float32),
            jax.ShapeDtypeStruct((STATE, width), jnp.float32),
        ),
        in_specs=[pl.BlockSpec(memory_space=pltpu.VMEM)] * 8,
        out_specs=(pl.BlockSpec(memory_space=pltpu.VMEM),) * 5,
        scratch_shapes=[
            pltpu.VMEM((tokens, STATE, width), jnp.float32),
            pltpu.VMEM((STATE, width), jnp.float32),
        ]
        + scan_scratch(width),
        compiler_params=pltpu.CompilerParams(
            collective_id=collective_id, has_side_effects=True, vmem_limit_bytes=VMEM_LIMIT
        ),
        name="scan_backward",
    )(step, act, b_wide, c_wide, keep_wide, rates, incoming, grad)


def from_behind(value, axis, by):
    devices = lax.axis_size(axis)
    pairs = [(i, i + by) for i in range(devices) if 0 <= i + by < devices]
    return lax.ppermute(value, axis, pairs)


def matmul(left, right):
    return jnp.dot(left, right, preferred_element_type=jnp.float32)


def matmul_nt(left, right):
    return lax.dot_general(
        left, right, (((1,), (1,)), ((), ())), preferred_element_type=jnp.float32
    )


def matmul_tn(left, right):
    return lax.dot_general(
        left, right, (((0,), (0,)), ((), ())), preferred_element_type=jnp.float32
    )


def silu_slope(preact):
    logistic = jax.nn.sigmoid(preact)
    return logistic * (1.0 + preact * (1.0 - logistic))


def inverse_rms(values):
    return lax.rsqrt(jnp.mean(values * values, axis=-1, keepdims=True) + EPS)


def norm_back(values, inv_scale, gain_row, grad_in):
    scaled = grad_in * gain_row
    grad_gain = jnp.sum(grad_in * values * inv_scale, axis=0)
    grad_values = inv_scale * scaled - values * inv_scale**3 * jnp.mean(
        scaled * values, axis=-1, keepdims=True
    )
    return (grad_values, grad_gain)


def neighbour_rows(edge_rows, offset):
    return from_behind(edge_rows, "group", offset)


def doc_layout(doc_lengths, first_pos, span_len):
    doc_ends = jnp.cumsum(doc_lengths, axis=1)
    doc_begins = doc_ends - doc_lengths
    where_at = first_pos + jnp.arange(span_len, dtype=jnp.int32)
    segment = jnp.sum((where_at[None, :, None] >= doc_ends[:, None, :]).astype(jnp.int32), axis=2)
    onehot_doc = (
        segment[:, :, None] == jnp.arange(doc_lengths.shape[1], dtype=jnp.int32)[None, None, :]
    ).astype(jnp.float32)
    weight = jnp.sum(onehot_doc / doc_lengths[:, None, :].astype(jnp.float32), axis=2)
    starting = jnp.sum(
        (where_at[None, :, None] == doc_begins[:, None, :]).astype(jnp.float32), axis=2
    )
    return (segment, weight, 1.0 - starting)


def lane_copies(columns):
    return jnp.broadcast_to(columns[..., None], columns.shape + (LANES,))


def mixer_forward(embedded, segment, keeping, weight_in, weight_x, weight_out, channel, gain_row):
    tokens = embedded.shape[0]
    scale_in = inverse_rms(embedded)
    normed = (embedded * scale_in * gain_row).astype(jnp.bfloat16)
    projected_in = matmul(normed, weight_in)
    conv_input = projected_in[:, :DI].astype(jnp.bfloat16)
    gate_z = projected_in[:, DI:]
    rim_rows = neighbour_rows(conv_input[tokens - CONV + 1 :].astype(jnp.float32), 1)
    padded = jnp.concatenate([rim_rows, conv_input.astype(jnp.float32)])
    same_doc = [
        (segment[conv_tap : conv_tap + tokens] == segment[CONV - 1 :]).astype(jnp.float32)[:, None]
        for conv_tap in range(CONV)
    ]
    conv_out = channel[CONV] + jnp.zeros_like(padded[CONV - 1 :])
    for conv_tap in range(CONV):
        conv_out = (
            conv_out + channel[conv_tap] * padded[conv_tap : conv_tap + tokens] * same_doc[conv_tap]
        )
    activated = jax.nn.silu(conv_out)
    act_low = activated.astype(jnp.bfloat16)
    projected = matmul(act_low, weight_x[:, : RANK + 2 * STATE])
    dt_input = projected[:, :RANK].astype(jnp.bfloat16)
    dt_pre = matmul_nt(dt_input, weight_x[:, RANK + 2 * STATE :])
    step_size = jax.nn.softplus(dt_pre + channel[CONV + 1])
    decay_rates = -jnp.exp(channel[CONV + 3 :])
    b_wide = lane_copies(projected[:, RANK : RANK + STATE])
    c_wide = lane_copies(projected[:, RANK + STATE :])
    keep_wide = lane_copies(keeping)
    reached, incoming = scan_forward(
        step_size, activated, b_wide, c_wide, keep_wide, decay_rates, 4
    )
    scanned = reached + channel[CONV + 2] * activated
    gate_act = jax.nn.silu(gate_z)
    gated = (scanned * gate_act).astype(jnp.bfloat16)
    mixed_out = embedded + matmul(gated, weight_out)
    kept_values = (
        scale_in,
        normed,
        gate_z,
        padded,
        same_doc,
        conv_out,
        activated,
        act_low,
        b_wide,
        c_wide,
        keep_wide,
        dt_input,
        dt_pre,
        step_size,
        decay_rates,
        incoming,
        scanned,
        gate_act,
        gated,
    )
    return (mixed_out, kept_values)


def mixer_backward(
    grad_out, embedded, kept_values, weight_in, weight_x, weight_out, channel, gain_row
):
    (
        scale_in,
        normed,
        gate_z,
        padded,
        same_doc,
        conv_out,
        activated,
        act_low,
        b_wide,
        c_wide,
        keep_wide,
        dt_input,
        dt_pre,
        step_size,
        decay_rates,
        incoming,
        scanned,
        gate_act,
        gated,
    ) = kept_values
    tokens = embedded.shape[0]
    grad_low = grad_out.astype(jnp.bfloat16)
    grad_wout = matmul_tn(gated, grad_low)
    grad_gated = matmul_nt(grad_low, weight_out)
    grad_scan = grad_gated * gate_act
    grad_z = grad_gated * scanned * silu_slope(gate_z)
    grad_skip = jnp.sum(grad_scan * activated, axis=0)
    along_b, decayed, wide_gb, wide_gc, grad_rates_log = scan_backward(
        step_size, activated, b_wide, c_wide, keep_wide, decay_rates, incoming, grad_scan, 5
    )
    grad_b = jnp.sum(wide_gb, axis=2)
    grad_c = jnp.sum(wide_gc, axis=2)
    grad_act = grad_scan * channel[CONV + 2] + along_b * step_size
    grad_step = decayed + along_b * activated
    grad_dtpre = grad_step * jax.nn.sigmoid(dt_pre + channel[CONV + 1])
    grad_dtbias = jnp.sum(grad_dtpre, axis=0)
    grad_dtlow = grad_dtpre.astype(jnp.bfloat16)
    grad_wdt = matmul_tn(grad_dtlow, dt_input)
    grad_dtin = matmul(grad_dtlow, weight_x[:, RANK + 2 * STATE :])
    grad_proj = jnp.concatenate([grad_dtin, grad_b, grad_c], axis=1).astype(jnp.bfloat16)
    grad_wx = jnp.concatenate([matmul_tn(act_low, grad_proj), grad_wdt], axis=1)
    grad_act = grad_act + matmul_nt(grad_proj, weight_x[:, : RANK + 2 * STATE])
    grad_conv = grad_act * silu_slope(conv_out)
    grad_taps = [
        jnp.sum(grad_conv * padded[conv_tap : conv_tap + tokens] * same_doc[conv_tap], axis=0)
        for conv_tap in range(CONV)
    ]
    grad_padded = sum(
        (
            jnp.pad(
                channel[conv_tap] * grad_conv * same_doc[conv_tap],
                ((conv_tap, CONV - 1 - conv_tap), (0, 0)),
            )
            for conv_tap in range(CONV)
        )
    )
    from_next = neighbour_rows(grad_padded[: CONV - 1], -1)
    grad_input = grad_padded[CONV - 1 :] + jnp.pad(from_next, ((tokens - CONV + 1, 0), (0, 0)))
    grad_both = jnp.concatenate([grad_input, grad_z], axis=1).astype(jnp.bfloat16)
    grad_win = matmul_tn(normed, grad_both)
    grad_normed = matmul_nt(grad_both, weight_in)
    grad_embed, grad_gain = norm_back(embedded, scale_in, gain_row, grad_normed)
    grad_channel = jnp.concatenate(
        [
            jnp.stack(grad_taps),
            jnp.sum(grad_conv, axis=0)[None],
            grad_dtbias[None],
            grad_skip[None],
            grad_rates_log,
        ]
    )
    return (grad_out + grad_embed, grad_win, grad_wx, grad_wout, grad_channel, grad_gain)


def choice_of(route_flat, experts_total):
    return (route_flat[:, None] == jnp.arange(experts_total, dtype=jnp.int32)[None, :]).astype(
        jnp.float32
    )


def dispatch_table(routes, first_expert, experts_here, capacity):
    tokens = routes.shape[1]
    chosen = (
        routes[:, :, None] == first_expert + jnp.arange(experts_here, dtype=jnp.int32)
    ).astype(jnp.float32)
    earlier = jnp.cumsum(chosen, axis=1) - chosen
    rank = jnp.sum(earlier * chosen, axis=2).astype(jnp.int32)
    local = routes - first_expert
    slot = jnp.where((local >= 0) & (local < experts_here), local * capacity + rank, -1)
    return (
        slot[:, None, :] == jnp.arange(experts_here * capacity, dtype=jnp.int32)[None, :, None]
    ).astype(jnp.bfloat16)


def to_slots(select, rows, experts_here, capacity):
    slots = jnp.einsum("bst,btd->bsd", select, rows, preferred_element_type=jnp.float32)
    slots = slots.astype(jnp.bfloat16).reshape(-1, experts_here, capacity, D)
    return jnp.swapaxes(slots, 0, 1).reshape(experts_here, -1, D)


def to_rows(select, slots, capacity):
    experts_here = slots.shape[0]
    slots = slots.astype(jnp.bfloat16).reshape(experts_here, -1, capacity, D)
    slots = jnp.swapaxes(slots, 0, 1).reshape(-1, experts_here * capacity, D)
    return jnp.einsum("bst,bsd->btd", select, slots, preferred_element_type=jnp.float32).astype(
        jnp.bfloat16
    )


def packed_rows(arrays, devices_seq):
    flat = jnp.concatenate([part.reshape(-1) for part in arrays])
    unit = devices_seq * 16 * D
    size = -(-flat.shape[0] // unit) * unit
    return jnp.pad(flat, (0, size - flat.shape[0])).reshape(-1, D)


def unpacked(flat, shapes):
    parts, first = ([], 0)
    for shape in shapes:
        size = 1
        for extent in shape:
            size *= extent
        parts.append(flat[..., first : first + size].reshape(flat.shape[:-1] + shape))
        first += size
    return parts


def whole_of(shards, axis):
    moved_axis = jnp.moveaxis(shards, 0, axis)
    shape = moved_axis.shape
    return moved_axis.reshape(shape[:axis] + (shape[axis] * shape[axis + 1],) + shape[axis + 2 :])


def shards_of(whole, axis, count):
    shape = whole.shape
    split = whole.reshape(shape[:axis] + (count, shape[axis] // count) + shape[axis + 1 :])
    return jnp.moveaxis(split, axis, 0)


def renewed(master, moment, average, gradient, clip_factor, rate):
    scaled = clip_factor * gradient
    moment_new = MOMENTUM * moment + scaled
    master_new = master - rate * (scaled + MOMENTUM * moment_new)
    return (master_new, moment_new, EMA_KEEP * average + (1.0 - EMA_KEEP) * master_new)


def per_device(
    token_ids,
    target_ids,
    doc_lengths,
    expert_ids,
    vocab_table,
    vocab_table_mom,
    vocab_table_ema,
    mixer_in,
    mixer_in_mom,
    mixer_in_ema,
    mixer_x,
    mixer_x_mom,
    mixer_x_ema,
    mixer_out,
    mixer_out_mom,
    mixer_out_ema,
    channel,
    channel_mom,
    channel_ema,
    norm_gains,
    norm_gains_mom,
    norm_gains_ema,
    router,
    router_mom,
    router_ema,
    experts,
    experts_mom,
    experts_ema,
):
    seq_count = lax.axis_size("seq")
    group_count = lax.axis_size("group")
    seq_index = lax.axis_index("seq")
    group_index = lax.axis_index("group")
    devices = seq_count * group_count
    tokens = token_ids.shape[1]
    sequences = token_ids.shape[0]
    experts_total = router.shape[1]
    local_experts = experts.shape[1]
    capacity = max(2, 2 * tokens // experts_total)
    own_vocab = vocab_table.shape[0]
    routes = expert_ids.reshape(1, tokens)
    numbers = jnp.concatenate([token_ids, target_ids, routes])
    numbers = jnp.pad(numbers, ((0, -numbers.shape[0] % 8), (0, 0)))
    numbers_all = share_small(numbers, 1)
    from_groups = jnp.swapaxes(numbers_all[:group_count, : 2 * sequences], 0, 1)
    tokens_all = from_groups[:sequences].reshape(-1)
    targets_all = from_groups[sequences:].reshape(-1)
    routes_all = numbers_all[:, 2 * sequences]

    mixer_parts = (mixer_in, mixer_x, mixer_out, channel, norm_gains, router)
    part_axes = (0, 0, 0, 1, 1, 0)
    part_shapes = [part.shape for part in mixer_parts]
    pack = packed_rows([part.astype(jnp.bfloat16) for part in mixer_parts], seq_count)
    pack_rows = pack.shape[0] // seq_count
    own_pack = lax.dynamic_slice_in_dim(pack, seq_index * pack_rows, pack_rows, 0)
    packs = gather_all(own_pack, 2).reshape(seq_count, group_count, pack_rows * D)
    shards = unpacked(jnp.swapaxes(packs, 0, 1).reshape(group_count, -1), part_shapes)
    weight_in, weight_x, weight_out, channel_low, gains_low, router_low = [
        whole_of(shard, axis) for shard, axis in zip(shards, part_axes)
    ]
    table_low = vocab_table.astype(jnp.bfloat16)
    experts_low = experts.astype(jnp.bfloat16)
    up_weight, down_weight = (experts_low[0], experts_low[1])
    channel_vals = channel_low.astype(jnp.float32)
    gain_vals = gains_low.astype(jnp.float32)

    vocab_start = (seq_index * group_count + group_index) * own_vocab
    column_ids = jnp.arange(own_vocab, dtype=jnp.int32)
    held_token = ((tokens_all - vocab_start)[:, None] == column_ids[None, :]).astype(jnp.bfloat16)
    looked_up = matmul(held_token, table_low).astype(jnp.bfloat16)
    embedded = scatter_all(looked_up.reshape(devices, tokens, D), 3)

    segment_all, weight_all, keep_all = doc_layout(
        doc_lengths, group_index * tokens - CONV + 1, tokens + CONV - 1
    )
    own_segment = lax.dynamic_index_in_dim(segment_all, seq_index, 0, keepdims=False)
    keeping = lax.dynamic_index_in_dim(keep_all, seq_index, 0, keepdims=False)[CONV - 1 :]
    own_weight = lax.dynamic_index_in_dim(weight_all, seq_index, 0, keepdims=False)[CONV - 1 :]
    _, every_weight, _ = doc_layout(doc_lengths, 0, tokens * group_count)
    row_weight = every_weight.reshape(-1)
    mixed_out, kept_values = mixer_forward(
        embedded, own_segment, keeping, weight_in, weight_x, weight_out, channel_vals, gain_vals[0]
    )
    scale_mid = inverse_rms(mixed_out)
    moe_in = (mixed_out * scale_mid * gain_vals[1]).astype(jnp.bfloat16)
    chosen = choice_of(expert_ids.reshape(-1), experts_total)
    select = dispatch_table(routes_all, seq_index * local_experts, local_experts, capacity)
    probability = jax.nn.softmax(matmul(moe_in, router_low), axis=-1)
    gate_value = jnp.sum(probability * chosen, axis=1)
    arrived = to_slots(select, gather_all(moe_in, 6), local_experts, capacity)
    before = jnp.einsum("erd,efd->erf", arrived, up_weight, preferred_element_type=jnp.float32)
    inner_act = jax.nn.gelu(before).astype(jnp.bfloat16)
    partial_out = jnp.einsum(
        "erf,efd->erd", inner_act, down_weight, preferred_element_type=jnp.float32
    )
    returned = scatter_all(to_rows(select, partial_out, capacity), 3)
    expert_value = returned.astype(jnp.bfloat16).astype(jnp.float32)
    branch = gate_value[:, None] * expert_value
    hidden = mixed_out + branch
    scale_out = inverse_rms(hidden)
    final_low = (hidden * scale_out * gain_vals[2]).astype(jnp.bfloat16)
    all_final = gather_all(final_low, 6).reshape(devices * tokens, D)
    valid_cols = vocab_start + column_ids < VOCAB_REAL
    hit_target = (targets_all - vocab_start)[:, None] == column_ids[None, :]
    logits = jnp.where(valid_cols[None, :], matmul_nt(all_final, table_low), -1e30)
    largest = jnp.max(logits, axis=1)
    exp_total = jnp.sum(jnp.exp(logits - largest[:, None]), axis=1)
    picked = jnp.sum(jnp.where(hit_target, logits, 0.0), axis=1)
    parts = jnp.stack([largest, exp_total, picked]).reshape(3, devices, tokens)
    parts = jnp.pad(jnp.swapaxes(parts, 0, 1), ((0, 0), (0, 5), (0, 0)))
    levels, entropy = combine_stats(parts, 7)
    log_total = levels[:, 0].reshape(-1)
    loss_part = jnp.sum(own_weight * entropy[0])
    grad_logits = (
        row_weight[:, None]
        * (jnp.exp(logits - log_total[:, None]) - hit_target.astype(jnp.float32))
    ).astype(jnp.bfloat16)
    table_grad = matmul_tn(grad_logits, all_final)
    grad_rows = matmul(grad_logits, table_low).astype(jnp.bfloat16)
    grad_final = scatter_all(grad_rows.reshape(devices, tokens, D), 3)
    grad_hidden, grad_gain_out = norm_back(hidden, scale_out, gain_vals[2], grad_final)
    grad_gate = jnp.sum(grad_hidden * expert_value, axis=1)
    grad_expert = (gate_value[:, None] * grad_hidden).astype(jnp.bfloat16)
    grad_arrived = to_slots(select, gather_all(grad_expert, 6), local_experts, capacity)
    grad_inner = jnp.einsum(
        "erd,efd->erf", grad_arrived, down_weight, preferred_element_type=jnp.float32
    )
    grad_before = jax.vjp(jax.nn.gelu, before)[1](grad_inner)[0].astype(jnp.bfloat16)
    grad_down = jnp.einsum(
        "erf,erd->efd", inner_act, grad_arrived, preferred_element_type=jnp.float32
    )
    grad_up = jnp.einsum("erf,erd->efd", grad_before, arrived, preferred_element_type=jnp.float32)
    grad_part = jnp.einsum(
        "erf,efd->erd", grad_before, up_weight, preferred_element_type=jnp.float32
    )
    grad_moe_in = scatter_all(to_rows(select, grad_part, capacity), 3)
    grad_moe_in = grad_moe_in.astype(jnp.bfloat16).astype(jnp.float32)
    grad_router_logits = (grad_gate * gate_value)[:, None] * (chosen - probability)
    grad_moe_in = grad_moe_in + jnp.dot(
        grad_router_logits, router_low.astype(jnp.float32).T, precision=HIGHEST
    )
    grad_router = jnp.dot(moe_in.astype(jnp.float32).T, grad_router_logits, precision=HIGHEST)
    grad_mid, grad_gain_mid = norm_back(mixed_out, scale_mid, gain_vals[1], grad_moe_in)
    grad_mixed = grad_hidden + grad_mid
    grad_embedded, grad_win, grad_wx, grad_wout, grad_channel, grad_gain_in = mixer_backward(
        grad_mixed,
        embedded,
        kept_values,
        weight_in,
        weight_x,
        weight_out,
        channel_vals,
        gain_vals[0],
    )
    all_grad_embed = gather_all(grad_embedded.astype(jnp.bfloat16), 6).reshape(-1, D)
    table_grad = table_grad + matmul_tn(held_token, all_grad_embed)
    grad_gains = jnp.stack([grad_gain_in, grad_gain_mid, grad_gain_out])
    mixer_wholes = (grad_win, grad_wx, grad_wout, grad_channel, grad_gains, grad_router)
    wholes_low = [
        shards_of(whole.astype(jnp.bfloat16), axis, group_count).reshape(group_count, -1)
        for whole, axis in zip(mixer_wholes, part_axes)
    ]
    flat = jnp.concatenate(wholes_low, axis=1)
    flat = jnp.pad(flat, ((0, 0), (0, seq_count * pack_rows * D - flat.shape[1])))
    flat = jnp.swapaxes(flat.reshape(group_count, seq_count, pack_rows, D), 0, 1)
    own_quarter = scatter_all(flat.reshape(devices, pack_rows, D), 8)
    quarters = lax.all_gather(own_quarter, "seq", axis=0, tiled=True).reshape(-1)
    mixer_grads = unpacked(quarters, part_shapes)
    grad_experts = jnp.stack([grad_up, grad_down])
    local_square = (
        jnp.sum(table_grad * table_grad)
        + jnp.sum(grad_experts * grad_experts)
        + jnp.sum(own_quarter * own_quarter)
    )
    two = jnp.concatenate(
        [jnp.full((4, LANES), local_square), jnp.full((4, LANES), loss_part)], axis=0
    )
    sums = jnp.sum(share_small(two, 9), axis=0)
    total_square, loss_sum = (sums[0, 0], sums[4, 0])
    grad_norm = jnp.sqrt(total_square)
    clip_factor = jnp.minimum(1.0, CLIP / (grad_norm + 1e-06))
    table_new = renewed(
        vocab_table, vocab_table_mom, vocab_table_ema, table_grad, clip_factor, LRATE
    )
    in_new = renewed(mixer_in, mixer_in_mom, mixer_in_ema, mixer_grads[0], clip_factor, LRATE)
    x_new = renewed(mixer_x, mixer_x_mom, mixer_x_ema, mixer_grads[1], clip_factor, LRATE)
    out_new = renewed(mixer_out, mixer_out_mom, mixer_out_ema, mixer_grads[2], clip_factor, LRATE)
    channel_new = renewed(
        channel, channel_mom, channel_ema, mixer_grads[3], clip_factor, CHANNEL_LRATE
    )
    gains_new = renewed(
        norm_gains, norm_gains_mom, norm_gains_ema, mixer_grads[4], clip_factor, LRATE
    )
    router_new = renewed(router, router_mom, router_ema, mixer_grads[5], clip_factor, LRATE)
    experts_new = renewed(experts, experts_mom, experts_ema, grad_experts, clip_factor, LRATE)
    return (
        loss_sum,
        grad_norm,
        branch.reshape(1, tokens, D),
        table_new[0],
        table_new[1],
        table_new[2],
        in_new[0],
        in_new[1],
        in_new[2],
        x_new[0],
        x_new[1],
        x_new[2],
        out_new[0],
        out_new[1],
        out_new[2],
        channel_new[0],
        channel_new[1],
        channel_new[2],
        gains_new[0],
        gains_new[1],
        gains_new[2],
        router_new[0],
        router_new[1],
        router_new[2],
        experts_new[0],
        experts_new[1],
        experts_new[2],
    )


def solution(mesh):
    placed = (
        P(None, "group"),
        P(None, "group"),
        P(),
        P("seq", "group", None),
        P(("seq", "group"), None),
        P(("seq", "group"), None),
        P(("seq", "group"), None),
        P("group", None),
        P("group", None),
        P("group", None),
        P("group", None),
        P("group", None),
        P("group", None),
        P("group", None),
        P("group", None),
        P("group", None),
        P(None, "group"),
        P(None, "group"),
        P(None, "group"),
        P(None, "group"),
        P(None, "group"),
        P(None, "group"),
        P("group", None),
        P("group", None),
        P("group", None),
        P(None, "seq", "group", None),
        P(None, "seq", "group", None),
        P(None, "seq", "group", None),
    )
    return jax.shard_map(
        per_device,
        mesh=mesh,
        in_specs=placed,
        out_specs=(
            P(),
            P(),
            P("seq", "group", None),
            P(("seq", "group"), None),
            P(("seq", "group"), None),
            P(("seq", "group"), None),
            P("group", None),
            P("group", None),
            P("group", None),
            P("group", None),
            P("group", None),
            P("group", None),
            P("group", None),
            P("group", None),
            P("group", None),
            P(None, "group"),
            P(None, "group"),
            P(None, "group"),
            P(None, "group"),
            P(None, "group"),
            P(None, "group"),
            P("group", None),
            P("group", None),
            P("group", None),
            P(None, "seq", "group", None),
            P(None, "seq", "group", None),
            P(None, "seq", "group", None),
        ),
        check_vma=False,
    )
```

```python
import functools

import jax
import jax.numpy as jnp
from jax import lax
from jax.experimental import pallas as pl
from jax.experimental.pallas import tpu as pltpu
from jax.sharding import PartitionSpec as P

D = 768
DI = 1536
STATE = 16
RANK = 48
CONV = 4
VOCAB_REAL = 50257


EPS = 1e-05
CLIP = 0.1
MOMENTUM = 0.9
LRATE = 1000.0
CHANNEL_LRATE = 10000.0
EMA_KEEP = 0.8
HIGHEST = lax.Precision.HIGHEST
MESH = pl.DeviceIdType.MESH
VMEM_LIMIT = 56 << 20
LANES = 128


def axis_sizes():
    seq, group = (lax.axis_size("seq"), lax.axis_size("group"))
    core = 2 if seq % 2 == 0 else 1
    y = 1
    while 4 * y * y <= group and group % (2 * y) == 0:
        y *= 2
    return {"x": seq // core, "core": core, "z": group // y, "y": y}


def my_place(sizes):
    seq, group = (lax.axis_index("seq"), lax.axis_index("group"))
    return {
        "x": seq // sizes["core"],
        "core": seq % sizes["core"],
        "z": group // sizes["y"],
        "y": group % sizes["y"],
    }


def device_of(place, sizes):
    return (place["x"] * sizes["core"] + place["core"], place["z"] * sizes["y"] + place["y"])


def moved(place, axis, by, sizes):
    return {**place, axis: lax.rem(place[axis] + by + sizes[axis], sizes[axis])}


def block_of(place, sizes):
    seq, group = device_of(place, sizes)
    return seq * (sizes["z"] * sizes["y"]) + group


def meet(peers):
    barrier = pltpu.get_barrier_semaphore()
    for peer in peers:
        pl.semaphore_signal(barrier, inc=1, device_id=peer, device_id_type=MESH)
    pl.semaphore_wait(barrier, len(peers))


def line_peers(place, sizes):
    return [
        device_of(moved(place, axis, by, sizes), sizes)
        for axis in ("x", "core", "z", "y")
        for by in range(1, sizes[axis])
    ]


GATHER_ORDERS = (
    ("z", "y", "x", "core"),
    ("z", "x", "y", "core"),
    ("x", "z", "y", "core"),
    ("y", "z", "x", "core"),
)


def gather_kernel(sizes, pieces, own_ref, all_ref, local_sem, send_sem, recv_sem):
    place = my_place(sizes)
    meet(line_peers(place, sizes))
    keep_own = pltpu.make_async_copy(own_ref, all_ref.at[block_of(place, sizes)], local_sem)
    keep_own.start()
    held = [[(place, None)] for _ in pieces]
    sends = []
    for phase in range(4):
        fresh = [[] for _ in pieces]
        for turn in range(max(len(blocks) for blocks in held)):
            for which, (order, first, rows) in enumerate(pieces):
                if turn >= len(held[which]):
                    continue
                axis = order[phase]
                where, arrival = held[which][turn]
                if arrival is not None:
                    copy, seen = arrival
                    if not seen:
                        copy.wait_recv()
                        held[which][turn] = (where, (copy, True))
                span = pl.ds(first, rows)
                for by in range(1, sizes[axis]):
                    block = block_of(where, sizes)
                    source = own_ref.at[span] if arrival is None else all_ref.at[block, span]
                    number = len(sends)
                    copy = pltpu.make_async_remote_copy(
                        src_ref=source,
                        dst_ref=all_ref.at[block, span],
                        send_sem=send_sem.at[number],
                        recv_sem=recv_sem.at[number],
                        device_id=device_of(moved(place, axis, by, sizes), sizes),
                        device_id_type=MESH,
                    )
                    copy.start()
                    sends.append(copy)
                    fresh[which].append((moved(where, axis, -by, sizes), (copy, False)))
        held = [old + new for old, new in zip(held, fresh)]
    for blocks in held:
        for _, arrival in blocks:
            if arrival is not None and not arrival[1]:
                arrival[0].wait_recv()
    for copy in sends:
        copy.wait_send()
    keep_own.wait()


def split_rows(rows, orders):
    unit = 32 if rows % 32 == 0 else 16
    count = rows // unit
    pieces, first = ([], 0)
    for which in range(min(count, 4)):
        size = (count * (which + 1) // min(count, 4)) * unit - first
        pieces.append((orders[which % len(orders)], first, size))
        first += size
    return pieces


def gather_all(rows, collective_id):
    sizes = axis_sizes()
    devices = sizes["x"] * sizes["core"] * sizes["z"] * sizes["y"]
    pieces = split_rows(rows.shape[0], GATHER_ORDERS)
    copies = (devices - 1) * len(pieces)
    return pl.pallas_call(
        functools.partial(gather_kernel, sizes, pieces),
        out_shape=jax.ShapeDtypeStruct((devices,) + rows.shape, rows.dtype),
        in_specs=[pl.BlockSpec(memory_space=pltpu.VMEM)],
        out_specs=pl.BlockSpec(memory_space=pl.ANY),
        scratch_shapes=[
            pltpu.SemaphoreType.DMA,
            pltpu.SemaphoreType.DMA((copies,)),
            pltpu.SemaphoreType.DMA((copies,)),
        ],
        compiler_params=pltpu.CompilerParams(
            collective_id=collective_id, has_side_effects=True, vmem_limit_bytes=VMEM_LIMIT
        ),
        name="gather_all",
    )(rows)


SCATTER_ORDERS = (("core", "x", "y", "z"), ("core", "y", "x", "z"))
GATHER_PAIR = (("z", "y", "x", "core"), ("z", "x", "y", "core"))
NATURAL = ("x", "core", "z", "y")
PIECE = 16
SPAN = 2 * PIECE


def unravel(number, extents):
    places = []
    for extent in reversed(extents):
        places.append(lax.rem(number, extent))
        number = lax.div(number, extent)
    return tuple(reversed(places))


def piece_rows(pair, kind):
    first = pair * SPAN + kind * PIECE
    if not isinstance(first, int):
        first = pl.multiple_of(first, PIECE)
    return pl.ds(first, PIECE)


def scatter_scratch(sizes, pairs, width, keep):
    scratch = []
    for order in SCATTER_ORDERS:
        landings, sums, semaphores = ([], [], [])
        for phase in range(4):
            left = tuple(sizes[a] for a in NATURAL if a not in order[: phase + 1])
            others = max(1, sizes[order[phase]] - 1)
            landings.append(pltpu.VMEM((pairs, others) + left + (PIECE, width), jnp.bfloat16))
            if phase < 3:
                sums.append(pltpu.VMEM((pairs,) + left + (PIECE, width), jnp.bfloat16))
            semaphores.append(pltpu.SemaphoreType.DMA((pairs, others)))
            semaphores.append(pltpu.SemaphoreType.DMA((pairs, others)))
        scratch += landings + sums + semaphores
        scratch += [pltpu.SemaphoreType.DMA((pairs,))] if keep else []
    return scratch


class Scatter:
    def __init__(self, sizes, pairs, full_ref, own_ref, scratch, keep):
        self.sizes, self.pairs, self.keep = (sizes, pairs, keep)
        self.full_ref, self.own_ref = (full_ref, own_ref)
        self.place = my_place(sizes)
        size = len(scratch) // 2
        self.refs = (scratch[:size], scratch[size:])

    def kept(self, kind, pair):
        order = SCATTER_ORDERS[kind]
        index = tuple(self.place[a] if a == order[0] else slice(None) for a in NATURAL)
        return pltpu.make_async_copy(
            self.full_ref.at[index + (piece_rows(pair, kind),)],
            self.refs[kind][4].at[pair],
            self.refs[kind][15].at[pair],
        )

    def copies(self, kind, pair, phase):
        order, refs, sizes = (SCATTER_ORDERS[kind], self.refs[kind], self.sizes)
        axis = order[phase]
        left = [a for a in NATURAL if a not in order[:phase]]
        made = []
        for by in range(1, sizes[axis]):
            to = moved(self.place, axis, by, sizes)
            index = tuple(to[axis] if a == axis else slice(None) for a in left)
            if phase == 0:
                source = self.full_ref.at[index + (piece_rows(pair, kind),)]
            else:
                source = refs[3 + phase].at[(pair,) + index]
            made.append(
                pltpu.make_async_remote_copy(
                    src_ref=source,
                    dst_ref=refs[phase].at[pair, by - 1],
                    send_sem=refs[7 + 2 * phase].at[pair, by - 1],
                    recv_sem=refs[8 + 2 * phase].at[pair, by - 1],
                    device_id=device_of(to, sizes),
                    device_id_type=MESH,
                )
            )
        return made

    def launch(self, pair, phase):
        for kind in range(2):
            for copy in self.copies(kind, pair, phase):
                copy.start()

    def absorb(self, kind, pair, phase):
        order, refs, sizes, place = (
            SCATTER_ORDERS[kind],
            self.refs[kind],
            self.sizes,
            self.place,
        )
        axis = order[phase]
        before = [a for a in NATURAL if a not in order[:phase]]
        after = [a for a in before if a != axis]
        if phase == 0 and self.keep:
            self.kept(kind, pair).wait()
        for copy in self.copies(kind, pair, phase):
            copy.wait_recv()
        extents = tuple(sizes[a] for a in after)
        number = 1
        for extent in extents:
            number *= extent

        def add(step, carry):
            spot = dict(zip(after, unravel(step, extents)))
            mine = tuple(place[axis] if a == axis else spot[a] for a in before)
            there = tuple(spot[a] for a in after)
            if phase > 0:
                kept_part = refs[3 + phase][(pair,) + mine]
            elif self.keep:
                kept_part = refs[4][(pair,) + there]
            else:
                kept_part = self.full_ref[mine + (piece_rows(pair, kind),)]
            total = kept_part.astype(jnp.float32)
            for by in range(1, sizes[axis]):
                total = total + refs[phase][(pair, by - 1) + there].astype(jnp.float32)
            if phase == 3:
                self.own_ref[piece_rows(pair, kind)] = total
            else:
                refs[4 + phase][(pair,) + there] = total.astype(jnp.bfloat16)
            return carry

        if number == 1:
            add(0, 0)
        else:
            lax.fori_loop(0, number, add, 0)

    def advance(self, pair, phase):
        for kind in range(2):
            self.absorb(kind, pair, phase)
            if phase < 3:
                for copy in self.copies(kind, pair, phase + 1):
                    copy.start()

    def finish(self):
        def one(pair, carry):
            for kind in range(2):
                for phase in range(4):
                    for copy in self.copies(kind, pair, phase):
                        copy.wait_send()
            return carry

        lax.fori_loop(0, self.pairs, one, 0)


def wave(pairs, phases, act):
    def step(turn, carry):
        for phase in range(phases - 1, -1, -1):
            pair = turn - phase

            @pl.when((pair >= 0) & (pair < pairs))
            def _(pair=pair, phase=phase):
                act(pair, phase)

        return carry

    lax.fori_loop(0, pairs + phases - 1, step, 0)


def scatter_kernel(sizes, pairs, full_ref, own_ref, *scratch):
    meet(line_peers(my_place(sizes), sizes))
    scatter = Scatter(sizes, pairs, full_ref, own_ref, scratch, True)
    for pair in range(pairs):
        scatter.launch(pair, 0)
        for kind in range(2):
            scatter.kept(kind, pair).start()
    wave(pairs, 4, scatter.advance)
    scatter.finish()


def scatter_all(blocks, collective_id):
    sizes = axis_sizes()
    rows, width = blocks.shape[-2:]
    pairs = rows // SPAN
    shaped = blocks.reshape(tuple(sizes[a] for a in NATURAL) + (rows, width))
    return pl.pallas_call(
        functools.partial(scatter_kernel, sizes, pairs),
        out_shape=jax.ShapeDtypeStruct((rows, width), jnp.float32),
        in_specs=[pl.BlockSpec(memory_space=pl.ANY)],
        out_specs=pl.BlockSpec(memory_space=pltpu.VMEM),
        scratch_shapes=scatter_scratch(sizes, pairs, width, True),
        compiler_params=pltpu.CompilerParams(
            collective_id=collective_id, has_side_effects=True, vmem_limit_bytes=VMEM_LIMIT
        ),
        name="scatter_all",
    )(shaped)


class Gather:
    def __init__(self, sizes, pairs, own_ref, all_ref, semaphores):
        self.sizes, self.pairs = (sizes, pairs)
        self.own_ref, self.all_ref = (own_ref, all_ref)
        self.semaphores = semaphores
        self.place = my_place(sizes)

    def copies(self, kind, pair, phase):
        order = GATHER_PAIR[kind]
        axis, span = (order[phase], piece_rows(pair, kind))
        block = tuple(slice(None) if a in order[:phase] else self.place[a] for a in NATURAL)
        there = self.all_ref.at[block + (span,)]
        send_sem, recv_sem = (self.semaphores[2 * phase], self.semaphores[2 * phase + 1])
        return [
            pltpu.make_async_remote_copy(
                src_ref=self.own_ref.at[span] if phase == 0 else there,
                dst_ref=there,
                send_sem=send_sem.at[kind, pair, by - 1],
                recv_sem=recv_sem.at[kind, pair, by - 1],
                device_id=device_of(moved(self.place, axis, by, self.sizes), self.sizes),
                device_id_type=MESH,
            )
            for by in range(1, self.sizes[axis])
        ]

    def advance(self, pair, phase):
        for kind in range(2):
            if phase > 0:
                for copy in self.copies(kind, pair, phase - 1):
                    copy.wait_recv()
            if phase < 4:
                for copy in self.copies(kind, pair, phase):
                    copy.start()

    def finish(self):
        def one(pair, carry):
            for kind in range(2):
                for phase in range(4):
                    for copy in self.copies(kind, pair, phase):
                        copy.wait_send()
            return carry

        lax.fori_loop(0, self.pairs, one, 0)


def gather_semaphores(sizes, pairs):
    longest = max(sizes.values())
    return [pltpu.SemaphoreType.DMA((2, pairs, longest)) for _ in range(8)]


def seq_place(seq, sizes):
    return (lax.div(seq, sizes["core"]), lax.rem(seq, sizes["core"]))


def merge_stats(first, second):
    high = jnp.maximum(first[0], second[0])
    mass = first[1] * jnp.exp(first[0] - high) + second[1] * jnp.exp(second[0] - high)
    return (high, mass, first[2] + second[2])


def span_rows(pair):
    return pl.ds(pl.multiple_of(pair * SPAN, SPAN), SPAN)


def masked_logits(table_ref, rows_in, first_masked, limit):
    logits = matmul_nt(table_ref[...], rows_in)
    tail = logits[first_masked:]
    numbers = first_masked + lax.broadcasted_iota(jnp.int32, tail.shape, 0)
    return jnp.concatenate([logits[:first_masked], jnp.where(numbers < limit, tail, -1e30)], axis=0)


def vocab_limit(own_vocab):
    devices, _, me = flat_place()
    least = max(0, VOCAB_REAL - (devices - 1) * own_vocab)
    limit = jnp.minimum(own_vocab, VOCAB_REAL - me * own_vocab)
    return (min(least, own_vocab) // 16 * 16, limit)


def head_forward_kernel(
    sizes,
    pairs,
    own_vocab,
    own_ref,
    table_ref,
    target_ref,
    all_ref,
    stats_ref,
    mine_ref,
    landing_ref,
    local_sem,
    stat_send,
    stat_recv,
    *semaphores,
):
    place = my_place(sizes)
    meet(line_peers(place, sizes))
    gather = Gather(sizes, pairs, own_ref, all_ref, semaphores)
    keep_own = pltpu.make_async_copy(
        own_ref, all_ref.at[tuple(place[a] for a in NATURAL)], local_sem
    )
    keep_own.start()
    groups = sizes["z"] * sizes["y"]
    seqs = sizes["x"] * sizes["core"]
    first_masked, limit = vocab_limit(own_vocab)

    def seq_stats(pair, seq):
        x, core = seq_place(seq, sizes)
        rows_in = all_ref[x, core, :, :, span_rows(pair), :].reshape(groups * SPAN, D)
        logits = masked_logits(table_ref, rows_in, first_masked, limit)
        spot = pl.ds(pair * seqs + seq, 1)
        numbers = lax.broadcasted_iota(jnp.int32, logits.shape, 0)
        top = jnp.max(logits, axis=0, keepdims=True)
        mine_ref[0, 0, spot] = top
        mine_ref[0, 1, spot] = jnp.sum(jnp.exp(logits - top), axis=0, keepdims=True)
        mine_ref[0, 2, spot] = jnp.sum(
            jnp.where(numbers == target_ref[spot], logits, 0.0), axis=0, keepdims=True
        )

    def turn_step(turn, carry):
        for phase in range(4, -1, -1):
            pair = turn - phase

            @pl.when((pair >= 0) & (pair < pairs))
            def _(pair=pair, phase=phase):
                gather.advance(pair, phase)

        @pl.when(turn == 0)
        def _():
            keep_own.wait()

        @pl.when(turn >= 4)
        def _():
            def one(seq, carry):
                seq_stats(turn - 4, seq)
                return carry

            lax.fori_loop(0, seqs, one, 0)

        return carry

    lax.fori_loop(0, pairs + 4, turn_step, 0)
    started = []
    stats = tuple(mine_ref[0, k] for k in range(3))
    for phase, axis in enumerate(("core", "x", "y", "z")):
        arrivals = []
        for by in range(1, sizes[axis]):
            slot = len(started)
            copy = pltpu.make_async_remote_copy(
                src_ref=mine_ref.at[phase],
                dst_ref=landing_ref.at[slot],
                send_sem=stat_send.at[slot],
                recv_sem=stat_recv.at[slot],
                device_id=device_of(moved(place, axis, by, sizes), sizes),
                device_id_type=MESH,
            )
            copy.start()
            arrivals.append((copy, slot))
            started.append(copy)
        for copy, slot in arrivals:
            copy.wait_recv()
            stats = merge_stats(stats, tuple(landing_ref[slot, k] for k in range(3)))
        if phase < 3:
            for k in range(3):
                mine_ref[phase + 1, k] = stats[k]
    stats_ref[0] = stats[0] + jnp.log(stats[1])
    stats_ref[1] = stats[2]
    gather.finish()
    for copy in started:
        copy.wait_send()


def head_forward(rows, table, own_vocab, targets, collective_id):
    sizes = axis_sizes()
    pairs = rows.shape[0] // SPAN
    hops = sum(extent - 1 for extent in sizes.values())
    natural = tuple(sizes[a] for a in NATURAL)
    packed = (3,) + targets.shape
    vmem = pl.BlockSpec(memory_space=pltpu.VMEM)
    return pl.pallas_call(
        functools.partial(head_forward_kernel, sizes, pairs, own_vocab),
        out_shape=(
            jax.ShapeDtypeStruct(natural + rows.shape, rows.dtype),
            jax.ShapeDtypeStruct((2,) + targets.shape, jnp.float32),
        ),
        in_specs=[vmem] * 3,
        out_specs=(vmem,) * 2,
        scratch_shapes=[
            pltpu.VMEM((4,) + packed, jnp.float32),
            pltpu.VMEM((hops,) + packed, jnp.float32),
            pltpu.SemaphoreType.DMA,
            pltpu.SemaphoreType.DMA((hops,)),
            pltpu.SemaphoreType.DMA((hops,)),
        ]
        + gather_semaphores(sizes, pairs),
        compiler_params=pltpu.CompilerParams(
            collective_id=collective_id, has_side_effects=True, vmem_limit_bytes=VMEM_LIMIT
        ),
        name="head_forward",
    )(rows, table, targets)


def head_backward_kernel(
    sizes,
    pairs,
    own_vocab,
    all_ref,
    table_ref,
    turned_ref,
    target_ref,
    level_ref,
    weight_ref,
    own_ref,
    tgrad_ref,
    full_ref,
    grad_ref,
    *scratch,
):
    meet(line_peers(my_place(sizes), sizes))
    scatter = Scatter(sizes, pairs, full_ref, own_ref, scratch, False)
    groups = sizes["z"] * sizes["y"]
    seqs = sizes["x"] * sizes["core"]
    first_masked, limit = vocab_limit(own_vocab)
    height = table_ref.shape[0]
    block = groups * SPAN

    def seq_grads(pair, seq):
        x, core = divmod(seq, sizes["core"])
        rows_in = all_ref[x, core, :, :, span_rows(pair), :].reshape(block, D)
        logits = masked_logits(table_ref, rows_in, first_masked, limit)
        spot = pl.ds(pair * seqs + seq, 1)
        numbers = lax.broadcasted_iota(jnp.int32, logits.shape, 0)
        share = jnp.exp(logits - level_ref[spot])
        share = jnp.where(numbers == target_ref[spot], share - 1.0, share)
        grad_ref[pair, 0:height, seq * block : (seq + 1) * block] = (
            weight_ref[spot] * share
        ).astype(jnp.bfloat16)

    def row_product(pair):
        turned = matmul(turned_ref[...], grad_ref[pair])
        full_ref[:, :, :, :, span_rows(pair), :] = turned.T.astype(jnp.bfloat16).reshape(
            tuple(sizes[a] for a in NATURAL) + (SPAN, D)
        )

    def table_product(pair):
        rows_in = all_ref[:, :, :, :, span_rows(pair), :].reshape(seqs * block, D)
        return matmul(grad_ref[pair, 0:height], rows_in)

    if grad_ref.shape[1] > height:
        grad_ref[:, height:] = jnp.zeros_like(grad_ref[:, height:])

    def turn_step(turn, carry):
        def older(by, phase):
            pair = turn - by

            @pl.when((pair >= 0) & (pair < pairs))
            def _():
                scatter.advance(pair, phase)

        def compute(act):
            @pl.when(turn < pairs)
            def _():
                act()

        for part in range(4):
            for seq in range(part * seqs // 4, (part + 1) * seqs // 4):
                compute(lambda seq=seq: seq_grads(turn, seq))
            if part == 0:
                older(1, 0)
            elif part == 1:
                older(2, 3)
            elif part == 2:
                older(1, 1)
        compute(lambda: row_product(turn))
        older(1, 2)
        compute(lambda: scatter.launch(turn, 0))
        return carry

    lax.fori_loop(0, pairs, turn_step, 0)
    tgrad_ref[...] = table_product(0)
    scatter.advance(pairs - 1, 0)
    if pairs > 1:
        scatter.advance(pairs - 2, 3)

    def late(pair, carry):
        tgrad_ref[...] += table_product(pair)

        @pl.when(pair < 3)
        def _():
            for phase in (1, 2):

                @pl.when(pair == phase)
                def _(phase=phase):
                    scatter.advance(pairs - 1, phase)

        return carry

    lax.fori_loop(1, pairs, late, 0)
    for phase in range(max(1, pairs), 4):
        if phase < 3:
            scatter.advance(pairs - 1, phase)
    scatter.advance(pairs - 1, 3)
    scatter.finish()


def head_backward(all_rows, table, turned, own_vocab, targets, levels, weights, collective_id):
    sizes = axis_sizes()
    tokens = all_rows.shape[-2]
    pairs = tokens // SPAN
    vmem = pl.BlockSpec(memory_space=pltpu.VMEM)
    block = targets.shape[1]
    seqs = sizes["x"] * sizes["core"]
    return pl.pallas_call(
        functools.partial(head_backward_kernel, sizes, pairs, own_vocab),
        out_shape=(
            jax.ShapeDtypeStruct((tokens, D), jnp.float32),
            jax.ShapeDtypeStruct(table.shape, jnp.float32),
        ),
        in_specs=[vmem] * 6,
        out_specs=(vmem,) * 2,
        scratch_shapes=[
            pltpu.VMEM(all_rows.shape, jnp.bfloat16),
            pltpu.VMEM((pairs, turned.shape[1], seqs * block), jnp.bfloat16),
        ]
        + scatter_scratch(sizes, pairs, D, False),
        compiler_params=pltpu.CompilerParams(
            collective_id=collective_id, has_side_effects=True, vmem_limit_bytes=VMEM_LIMIT
        ),
        name="head_backward",
    )(all_rows, table, turned, targets, levels, weights)


def everyone(devices, groups, me, act):
    def step(by, carry):
        peer = lax.rem(me + by, devices)
        act(by, peer, (lax.div(peer, groups), lax.rem(peer, groups)))
        return carry

    lax.fori_loop(1, devices, step, 0)


def greet_everyone(devices, groups, me):
    barrier = pltpu.get_barrier_semaphore()

    def greet(by, peer, address):
        pl.semaphore_signal(barrier, inc=1, device_id=address, device_id_type=MESH)

    everyone(devices, groups, me, greet)
    pl.semaphore_wait(barrier, devices - 1)


def flat_place():
    groups = lax.axis_size("group")
    return (
        lax.axis_size("seq") * groups,
        groups,
        lax.axis_index("seq") * groups + lax.axis_index("group"),
    )


def share_kernel(own_ref, all_ref, send_sem, recv_sem):
    devices, groups, me = flat_place()
    greet_everyone(devices, groups, me)

    def copy_to(by, address):
        return pltpu.make_async_remote_copy(
            src_ref=own_ref,
            dst_ref=all_ref.at[me],
            send_sem=send_sem.at[by],
            recv_sem=recv_sem.at[by],
            device_id=address,
            device_id_type=MESH,
        )

    everyone(devices, groups, me, lambda by, peer, address: copy_to(by, address).start())
    all_ref[me] = own_ref[...]
    everyone(devices, groups, me, lambda by, peer, address: copy_to(by, address).wait())


def share_small(values, collective_id):
    devices = lax.axis_size("seq") * lax.axis_size("group")
    return pl.pallas_call(
        share_kernel,
        out_shape=jax.ShapeDtypeStruct((devices,) + values.shape, values.dtype),
        in_specs=[pl.BlockSpec(memory_space=pltpu.VMEM)],
        out_specs=pl.BlockSpec(memory_space=pltpu.VMEM),
        scratch_shapes=[
            pltpu.SemaphoreType.DMA((devices,)),
            pltpu.SemaphoreType.DMA((devices,)),
        ],
        compiler_params=pltpu.CompilerParams(collective_id=collective_id, has_side_effects=True),
        name="share_small",
    )(values)


def stats_kernel(parts_ref, all_ref, own_ref, got_ref, mine_ref, send_sem, recv_sem):
    devices, groups, me = flat_place()
    greet_everyone(devices, groups, me)

    def part_to(by, peer, address):
        return pltpu.make_async_remote_copy(
            src_ref=parts_ref.at[peer],
            dst_ref=got_ref.at[me],
            send_sem=send_sem.at[0, by],
            recv_sem=recv_sem.at[0, by],
            device_id=address,
            device_id_type=MESH,
        )

    def total_to(by, address):
        return pltpu.make_async_remote_copy(
            src_ref=mine_ref,
            dst_ref=all_ref.at[me],
            send_sem=send_sem.at[1, by],
            recv_sem=recv_sem.at[1, by],
            device_id=address,
            device_id_type=MESH,
        )

    everyone(devices, groups, me, lambda by, peer, address: part_to(by, peer, address).start())
    got_ref[me] = parts_ref[me]
    everyone(devices, groups, me, lambda by, peer, address: part_to(by, peer, address).wait())
    tops = got_ref[:, 0, :]
    top = jnp.max(tops, axis=0, keepdims=True)
    mass = jnp.sum(got_ref[:, 1, :] * jnp.exp(tops - top), axis=0, keepdims=True)
    hit = jnp.sum(got_ref[:, 2, :], axis=0, keepdims=True)
    level = top + jnp.log(mass)
    mine_ref[...] = jnp.broadcast_to(level, mine_ref.shape)
    everyone(devices, groups, me, lambda by, peer, address: total_to(by, address).start())
    all_ref[me] = mine_ref[...]
    own_ref[...] = jnp.broadcast_to(level - hit, own_ref.shape)
    everyone(devices, groups, me, lambda by, peer, address: total_to(by, address).wait())


def combine_stats(parts, collective_id):
    devices = parts.shape[0]
    shape = parts.shape[1:]
    return pl.pallas_call(
        stats_kernel,
        out_shape=(
            jax.ShapeDtypeStruct(parts.shape, jnp.float32),
            jax.ShapeDtypeStruct(shape, jnp.float32),
        ),
        in_specs=[pl.BlockSpec(memory_space=pltpu.VMEM)],
        out_specs=(pl.BlockSpec(memory_space=pltpu.VMEM),) * 2,
        scratch_shapes=[
            pltpu.VMEM(parts.shape, jnp.float32),
            pltpu.VMEM(shape, jnp.float32),
            pltpu.SemaphoreType.DMA((2, devices)),
            pltpu.SemaphoreType.DMA((2, devices)),
        ],
        compiler_params=pltpu.CompilerParams(collective_id=collective_id, has_side_effects=True),
        name="combine_stats",
    )(parts)


def chain_exchange(rates, total_step, flag, end_state, backwards, out_buf, in_buf, sems):
    devices, me = (lax.axis_size("group"), lax.axis_index("group"))
    seq = lax.axis_index("seq")
    send_sem, recv_sem = sems
    width = rates.shape[1]

    def join(first, second):
        return (
            jnp.exp(second[0] * rates) * second[1] * first[2] + second[2],
            first[0] + second[0],
            first[1] * second[1],
        )

    window = (total_step, flag, end_state)
    before = None
    distance, lap = (1, 0)
    copies = []
    while distance < devices:
        to = lax.rem(me + (devices - distance if backwards else distance), devices)
        out_buf[lap, 0:STATE] = window[2]
        out_buf[lap, STATE : STATE + 8] = jnp.concatenate(
            [
                jnp.broadcast_to(window[0], (4, width)),
                jnp.broadcast_to(window[1], (4, width)),
            ],
            axis=0,
        )
        copy = pltpu.make_async_remote_copy(
            src_ref=out_buf.at[lap],
            dst_ref=in_buf.at[lap],
            send_sem=send_sem.at[lap],
            recv_sem=recv_sem.at[lap],
            device_id=(seq, to),
            device_id_type=MESH,
        )
        copy.start()
        copies.append(copy)
        copy.wait_recv()
        reached = (me + distance < devices) if backwards else (me >= distance)
        real = jnp.where(reached, 1.0, 0.0)
        tail = in_buf[lap, STATE : STATE + 8]
        got = (
            tail[0:1] * real,
            tail[4:5] * real + (1.0 - real),
            in_buf[lap, 0:STATE] * real,
        )
        if before is None:
            before = got
        else:
            merged = join(got, before)
            before = (merged[1], merged[2], merged[0])
        merged = join(got, window)
        window = (merged[1], merged[2], merged[0])
        distance *= 2
        lap += 1
    for copy in copies:
        copy.wait_send()
    if before is None:
        return jnp.zeros_like(end_state)
    return before[2]


def chain_peers():
    devices, me = (lax.axis_size("group"), lax.axis_index("group"))
    seq = lax.axis_index("seq")
    distances = []
    distance = 1
    while distance < devices:
        distances += [distance, devices - distance]
        distance *= 2
    return [(seq, lax.rem(me + by, devices)) for by in sorted(set(distances))]


def chain_laps():
    laps, distance = (0, 1)
    while distance < lax.axis_size("group"):
        laps, distance = (laps + 1, distance * 2)
    return max(1, laps)


def spans(width):
    size = 512 if width % 512 == 0 else width
    return [slice(first, first + size) for first in range(0, width, size)]


def wide(value, copies):
    return jnp.concatenate([value] * copies, axis=1)


def folded(value):
    total = value[:, :LANES]
    for first in range(LANES, value.shape[1], LANES):
        total = total + value[:, first : first + LANES]
    return total


def scan_forward_kernel(
    step_ref, act_ref, b_ref, c_ref, keep_ref, rate_ref, y_ref, in_ref, out_buf, in_buf, ss, rs
):
    meet(chain_peers())
    tokens, width = step_ref.shape
    ends = []
    for span in spans(width):
        copies = (span.stop - span.start) // LANES
        rates = rate_ref[:, span]

        def advance(block, state, span=span, copies=copies, rates=rates):
            rows = pl.ds(pl.multiple_of(block * 8, 8), 8)
            steps = step_ref[rows, span]
            drives = steps * act_ref[rows, span]
            keeps = wide(keep_ref[rows, :], copies)
            for r in range(8):
                decay = jnp.exp(steps[r : r + 1] * rates) * keeps[r : r + 1]
                state = decay * state + drives[r : r + 1] * wide(b_ref[block * 8 + r], copies)
            return state

        ends.append(
            lax.fori_loop(
                0, tokens // 8, advance, jnp.zeros((STATE, span.stop - span.start), jnp.float32)
            )
        )
    total_step = jnp.sum(step_ref[...], axis=0, keepdims=True)
    flag = wide(jnp.min(keep_ref[...], axis=0, keepdims=True), width // LANES)
    incoming = chain_exchange(
        rate_ref[...],
        total_step,
        flag,
        jnp.concatenate(ends, axis=1),
        False,
        out_buf,
        in_buf,
        (ss, rs),
    )
    in_ref[...] = incoming
    for span in spans(width):
        copies = (span.stop - span.start) // LANES
        rates = rate_ref[:, span]

        def produce(block, state, span=span, copies=copies, rates=rates):
            rows = pl.ds(pl.multiple_of(block * 8, 8), 8)
            steps = step_ref[rows, span]
            drives = steps * act_ref[rows, span]
            keeps = wide(keep_ref[rows, :], copies)
            results = []
            for r in range(8):
                decay = jnp.exp(steps[r : r + 1] * rates) * keeps[r : r + 1]
                state = decay * state + drives[r : r + 1] * wide(b_ref[block * 8 + r], copies)
                results.append(
                    jnp.sum(state * wide(c_ref[block * 8 + r], copies), axis=0, keepdims=True)
                )
            y_ref[rows, span] = jnp.concatenate(results, axis=0)
            return state

        lax.fori_loop(0, tokens // 8, produce, in_ref[:, span])


def scan_scratch(width):
    laps = chain_laps()
    return [
        pltpu.VMEM((laps, STATE + 8, width), jnp.float32),
        pltpu.VMEM((laps, STATE + 8, width), jnp.float32),
        pltpu.SemaphoreType.DMA((laps,)),
        pltpu.SemaphoreType.DMA((laps,)),
    ]


def scan_forward(step, act, b_wide, c_wide, keep_wide, rates, collective_id):
    tokens, width = step.shape
    return pl.pallas_call(
        scan_forward_kernel,
        out_shape=(
            jax.ShapeDtypeStruct((tokens, width), jnp.float32),
            jax.ShapeDtypeStruct((STATE, width), jnp.float32),
        ),
        in_specs=[pl.BlockSpec(memory_space=pltpu.VMEM)] * 6,
        out_specs=(pl.BlockSpec(memory_space=pltpu.VMEM),) * 2,
        scratch_shapes=scan_scratch(width),
        compiler_params=pltpu.CompilerParams(
            collective_id=collective_id, has_side_effects=True, vmem_limit_bytes=VMEM_LIMIT
        ),
        name="scan_forward",
    )(step, act, b_wide, c_wide, keep_wide, rates)


def scan_backward_kernel(
    step_ref,
    act_ref,
    b_ref,
    c_ref,
    keep_ref,
    rate_ref,
    in_ref,
    grad_ref,
    along_ref,
    decayed_ref,
    gb_ref,
    gc_ref,
    grate_ref,
    prev_ref,
    carry_ref,
    out_buf,
    in_buf,
    ss,
    rs,
):
    meet(chain_peers())
    tokens, width = step_ref.shape
    blocks = tokens // 8
    ends = []
    for number, span in enumerate(spans(width)):
        size = span.stop - span.start
        copies = size // LANES
        rates = rate_ref[:, span]

        def replay(block, state, number=number, span=span, copies=copies, rates=rates):
            rows = pl.ds(pl.multiple_of(block * 8, 8), 8)
            steps = step_ref[rows, span]
            drives = steps * act_ref[rows, span]
            keeps = wide(keep_ref[rows, :], copies)
            grads = grad_ref[rows, span]
            for r in range(8):
                at = block * 8 + r
                prev_ref[at, :, span] = state
                decay = jnp.exp(steps[r : r + 1] * rates) * keeps[r : r + 1]
                state = decay * state + drives[r : r + 1] * wide(b_ref[at], copies)
                share = folded(grads[r : r + 1] * state)
                gc_ref[at] = share if number == 0 else gc_ref[at] + share
            return state

        lax.fori_loop(0, blocks, replay, in_ref[:, span])

        def pull(lap, carry, span=span, copies=copies, rates=rates):
            block = blocks - 1 - lap
            rows = pl.ds(pl.multiple_of(block * 8, 8), 8)
            steps = step_ref[rows, span]
            keeps = wide(keep_ref[rows, :], copies)
            grads = grad_ref[rows, span]
            for r in range(7, -1, -1):
                decay = jnp.exp(steps[r : r + 1] * rates) * keeps[r : r + 1]
                adjoint = grads[r : r + 1] * wide(c_ref[block * 8 + r], copies) + carry
                carry = decay * adjoint
            return carry

        ends.append(lax.fori_loop(0, blocks, pull, jnp.zeros((STATE, size), jnp.float32)))
    total_step = jnp.sum(step_ref[...], axis=0, keepdims=True)
    flag = wide(jnp.min(keep_ref[...], axis=0, keepdims=True), width // LANES)
    carry_ref[...] = chain_exchange(
        rate_ref[...],
        total_step,
        flag,
        jnp.concatenate(ends, axis=1),
        True,
        out_buf,
        in_buf,
        (ss, rs),
    )
    for number, span in enumerate(spans(width)):
        size = span.stop - span.start
        copies = size // LANES
        rates = rate_ref[:, span]

        def settle(lap, carries, number=number, span=span, copies=copies, rates=rates):
            carry, rate_total = carries
            block = blocks - 1 - lap
            rows = pl.ds(pl.multiple_of(block * 8, 8), 8)
            steps = step_ref[rows, span]
            drives = steps * act_ref[rows, span]
            keeps = wide(keep_ref[rows, :], copies)
            grads = grad_ref[rows, span]
            alongs, decays = ([None] * 8, [None] * 8)
            for r in range(7, -1, -1):
                at = block * 8 + r
                decay = jnp.exp(steps[r : r + 1] * rates) * keeps[r : r + 1]
                adjoint = grads[r : r + 1] * wide(c_ref[at], copies) + carry
                carry = decay * adjoint
                grad_exp = carry * prev_ref[at, :, span]
                rate_total = rate_total + grad_exp * steps[r : r + 1]
                alongs[r] = jnp.sum(adjoint * wide(b_ref[at], copies), axis=0, keepdims=True)
                decays[r] = jnp.sum(grad_exp * rates, axis=0, keepdims=True)
                share = folded(adjoint * drives[r : r + 1])
                gb_ref[at] = share if number == 0 else gb_ref[at] + share
            along_ref[rows, span] = jnp.concatenate(alongs, axis=0)
            decayed_ref[rows, span] = jnp.concatenate(decays, axis=0)
            return (carry, rate_total)

        _, rate_total = lax.fori_loop(
            0, blocks, settle, (carry_ref[:, span], jnp.zeros((STATE, size), jnp.float32))
        )
        grate_ref[:, span] = rate_total * rates


def scan_backward(step, act, b_wide, c_wide, keep_wide, rates, incoming, grad, collective_id):
    tokens, width = step.shape
    full = jax.ShapeDtypeStruct((tokens, width), jnp.float32)
    return pl.pallas_call(
        scan_backward_kernel,
        out_shape=(
            full,
            full,
            jax.ShapeDtypeStruct(b_wide.shape, jnp.float32),
            jax.ShapeDtypeStruct(c_wide.shape, jnp.float32),
            jax.ShapeDtypeStruct((STATE, width), jnp.float32),
        ),
        in_specs=[pl.BlockSpec(memory_space=pltpu.VMEM)] * 8,
        out_specs=(pl.BlockSpec(memory_space=pltpu.VMEM),) * 5,
        scratch_shapes=[
            pltpu.VMEM((tokens, STATE, width), jnp.float32),
            pltpu.VMEM((STATE, width), jnp.float32),
        ]
        + scan_scratch(width),
        compiler_params=pltpu.CompilerParams(
            collective_id=collective_id, has_side_effects=True, vmem_limit_bytes=VMEM_LIMIT
        ),
        name="scan_backward",
    )(step, act, b_wide, c_wide, keep_wide, rates, incoming, grad)


def everyone_peer_greeting():
    devices, groups, me = flat_place()
    greet_everyone(devices, groups, me)
    return (devices, groups, me)


def one_hot_turned(ids, height):
    numbers = lax.broadcasted_iota(jnp.int32, (height, ids.shape[1]), 0)
    return (numbers == ids).astype(jnp.float32).astype(jnp.bfloat16)


def start_kernel(
    sizes,
    pairs,
    pack_pairs,
    own_vocab,
    number_ref,
    pack_ref,
    turned_ref,
    numbers_ref,
    packs_ref,
    own_ref,
    full_ref,
    pack_sem,
    send_sem,
    recv_sem,
    *scratch,
):
    devices, groups, me = everyone_peer_greeting()
    place = my_place(sizes)
    seqs = sizes["x"] * sizes["core"]
    gather = Gather(sizes, pack_pairs, pack_ref, packs_ref, scratch[:8])
    scatter = Scatter(sizes, pairs, full_ref, own_ref, scratch[8:], False)
    own_pack = pltpu.make_async_copy(
        pack_ref, packs_ref.at[tuple(place[a] for a in NATURAL)], pack_sem
    )
    own_pack.start()

    def number_copy(by, address):
        return pltpu.make_async_remote_copy(
            src_ref=number_ref,
            dst_ref=numbers_ref.at[me],
            send_sem=send_sem.at[by],
            recv_sem=recv_sem.at[by],
            device_id=address,
            device_id_type=MESH,
        )

    def weights(turn):
        for phase in range(4, -1, -1):
            if 0 <= turn - phase < pack_pairs:
                gather.advance(turn - phase, phase)

    everyone(devices, groups, me, lambda by, peer, address: number_copy(by, address).start())
    weights(0)
    numbers_ref[me] = number_ref[...]
    own_pack.wait()
    everyone(devices, groups, me, lambda by, peer, address: number_copy(by, address).wait())
    weights(1)

    def look_up(step, carry):
        seq, group = (lax.div(step, groups // 2), lax.rem(step, groups // 2) * 2)
        x, core = seq_place(seq, sizes)
        ids = jnp.concatenate(
            [numbers_ref[group, pl.ds(seq, 1)], numbers_ref[group + 1, pl.ds(seq, 1)]], axis=1
        )
        found = one_hot_turned(ids - me * own_vocab, turned_ref.shape[1])
        rows = matmul(turned_ref[...], found).T.astype(jnp.bfloat16)
        tokens = number_ref.shape[1]
        for half in range(2):
            z, y = (lax.div(group + half, sizes["y"]), lax.rem(group + half, sizes["y"]))
            full_ref[x, core, z, y] = rows[half * tokens : (half + 1) * tokens]
        return carry

    chunks = seqs * groups // 2
    for part in range(4):
        lax.fori_loop(part * chunks // 4, (part + 1) * chunks // 4, look_up, 0)
        weights(2 + part)
    for pair in range(pairs):
        scatter.launch(pair, 0)
    for turn in range(max(pairs + 3, pack_pairs - 2)):
        weights(6 + turn)
        for phase in range(3, -1, -1):
            if 0 <= turn - phase < pairs:
                scatter.advance(turn - phase, phase)
    gather.finish()
    scatter.finish()


def start_all(numbers, pack, turned, own_vocab, collective_id):
    sizes = axis_sizes()
    natural = tuple(sizes[a] for a in NATURAL)
    devices = lax.axis_size("seq") * lax.axis_size("group")
    tokens = numbers.shape[1]
    pairs, pack_pairs = (tokens // SPAN, pack.shape[0] // SPAN)
    vmem = pl.BlockSpec(memory_space=pltpu.VMEM)
    return pl.pallas_call(
        functools.partial(start_kernel, sizes, pairs, pack_pairs, own_vocab),
        out_shape=(
            jax.ShapeDtypeStruct((devices,) + numbers.shape, numbers.dtype),
            jax.ShapeDtypeStruct(natural + pack.shape, pack.dtype),
            jax.ShapeDtypeStruct((tokens, D), jnp.float32),
        ),
        in_specs=[vmem] * 3,
        out_specs=(vmem, pl.BlockSpec(memory_space=pl.ANY), vmem),
        scratch_shapes=[
            pltpu.VMEM(natural + (tokens, D), jnp.bfloat16),
            pltpu.SemaphoreType.DMA,
            pltpu.SemaphoreType.DMA((devices,)),
            pltpu.SemaphoreType.DMA((devices,)),
        ]
        + gather_semaphores(sizes, pack_pairs)
        + scatter_scratch(sizes, pairs, D, False),
        compiler_params=pltpu.CompilerParams(
            collective_id=collective_id, has_side_effects=True, vmem_limit_bytes=VMEM_LIMIT
        ),
        name="start_all",
    )(numbers, pack, turned)


def finish_kernel(
    sizes,
    pairs,
    pack_pairs,
    own_ref,
    pack_ref,
    token_ref,
    head_ref,
    scalar_ref,
    tgrad_ref,
    quarters_ref,
    sums_ref,
    all_ref,
    found_ref,
    mine_ref,
    ring_ref,
    own_sem,
    quarter_send,
    quarter_recv,
    ring_send,
    ring_recv,
    *scratch,
):
    place = my_place(sizes)
    meet(line_peers(place, sizes))
    seqs = sizes["x"] * sizes["core"]
    groups = sizes["z"] * sizes["y"]
    block = groups * SPAN
    height = head_ref.shape[0]
    gather = Gather(sizes, pairs, own_ref, all_ref, scratch[:8])
    scatter = Scatter(sizes, pack_pairs, pack_ref, mine_ref, scratch[8:], True)
    keep_own = pltpu.make_async_copy(
        own_ref, all_ref.at[tuple(place[a] for a in NATURAL)], own_sem
    )
    keep_own.start()

    def spread_table(pair):
        for seq in range(seqs):
            ids = token_ref[pair * seqs + seq : pair * seqs + seq + 1]
            found_ref[:, seq * block : (seq + 1) * block] = one_hot_turned(ids, height)
        rows = all_ref[:, :, :, :, pl.ds(pair * SPAN, SPAN), :].reshape(seqs * block, D)
        update = matmul(found_ref[...], rows)
        tgrad_ref[...] = (head_ref[...] if pair == 0 else tgrad_ref[...]) + update

    for pair in range(pack_pairs):
        scatter.launch(pair, 0)
        for kind in range(2):
            scatter.kept(kind, pair).start()
    for turn in range(max(pairs + 4, pack_pairs + 3)):
        if 0 <= turn - 4 < pairs:
            gather.advance(turn - 4, 4)
        for phase in range(3, -1, -1):
            if 0 <= turn - phase < pairs:
                gather.advance(turn - phase, phase)
            if 0 <= turn - phase < pack_pairs:
                scatter.advance(turn - phase, phase)
        if turn == 0:
            keep_own.wait()
        if 0 <= turn - 4 < pairs:
            spread_table(turn - 4)

    seq = place["x"] * sizes["core"] + place["core"]
    quarters_ref[seq] = mine_ref[...].astype(jnp.bfloat16)
    started = []

    def send_quarters(axis, first):
        sent = []
        for by in range(1, sizes[axis]):
            to = moved(place, axis, by, sizes)
            for x in range(sizes["x"] if axis == "core" else 1):
                held = x * sizes["core"] + place["core"] if axis == "core" else seq
                number = first + len(sent)
                copy = pltpu.make_async_remote_copy(
                    src_ref=quarters_ref.at[held],
                    dst_ref=quarters_ref.at[held],
                    send_sem=quarter_send.at[number],
                    recv_sem=quarter_recv.at[number],
                    device_id=device_of(to, sizes),
                    device_id_type=MESH,
                )
                copy.start()
                sent.append(copy)
        started.extend(sent)
        return sent

    x_sent = send_quarters("x", 0)
    square = jnp.sum(tgrad_ref[...] * tgrad_ref[...]) + jnp.sum(mine_ref[...] * mine_ref[...])
    row = lax.broadcasted_iota(jnp.int32, (8, LANES), 0)
    value = scalar_ref[...] + jnp.where(row < 4, square, 0.0)
    core_sent = []
    first = 0
    for axis in ("core", "x", "y", "z"):
        ring_ref[first + place[axis]] = value
        sent = []
        for by in range(1, sizes[axis]):
            copy = pltpu.make_async_remote_copy(
                src_ref=ring_ref.at[first + place[axis]],
                dst_ref=ring_ref.at[first + place[axis]],
                send_sem=ring_send.at[first + by],
                recv_sem=ring_recv.at[first + by],
                device_id=device_of(moved(place, axis, by, sizes), sizes),
                device_id_type=MESH,
            )
            copy.start()
            sent.append(copy)
        started.extend(sent)
        if axis == "y":
            for copy in x_sent:
                copy.wait_recv()
            core_sent = send_quarters("core", len(x_sent))
        for copy in sent:
            copy.wait_recv()
        value = ring_ref[first]
        for other in range(1, sizes[axis]):
            value = value + ring_ref[first + other]
        first += sizes[axis]
    sums_ref[...] = value
    for copy in core_sent:
        copy.wait_recv()
    for copy in started:
        copy.wait_send()
    gather.finish()
    scatter.finish()


def finish_all(rows, packs, token_rows, head_grad, scalars, collective_id):
    sizes = axis_sizes()
    natural = tuple(sizes[a] for a in NATURAL)
    tokens = rows.shape[0]
    seqs = sizes["x"] * sizes["core"]
    pack_rows, pack_width = packs.shape[-2:]
    pairs, pack_pairs = (tokens // SPAN, pack_rows // SPAN)
    slots = sum(sizes.values())
    quarter_copies = (sizes["x"] - 1) + (sizes["core"] - 1) * sizes["x"] + 1
    vmem = pl.BlockSpec(memory_space=pltpu.VMEM)
    return pl.pallas_call(
        functools.partial(finish_kernel, sizes, pairs, pack_pairs),
        out_shape=(
            jax.ShapeDtypeStruct(head_grad.shape, jnp.float32),
            jax.ShapeDtypeStruct((seqs, pack_rows, pack_width), jnp.bfloat16),
            jax.ShapeDtypeStruct((8, LANES), jnp.float32),
        ),
        in_specs=[vmem, pl.BlockSpec(memory_space=pl.ANY), vmem, vmem, vmem],
        out_specs=(vmem,) * 3,
        scratch_shapes=[
            pltpu.VMEM(natural + rows.shape, jnp.bfloat16),
            pltpu.VMEM((head_grad.shape[0], seqs * token_rows.shape[1]), jnp.bfloat16),
            pltpu.VMEM((pack_rows, pack_width), jnp.float32),
            pltpu.VMEM((slots, 8, LANES), jnp.float32),
            pltpu.SemaphoreType.DMA,
            pltpu.SemaphoreType.DMA((quarter_copies,)),
            pltpu.SemaphoreType.DMA((quarter_copies,)),
            pltpu.SemaphoreType.DMA((slots,)),
            pltpu.SemaphoreType.DMA((slots,)),
        ]
        + gather_semaphores(sizes, pairs)
        + scatter_scratch(sizes, pack_pairs, pack_width, True),
        compiler_params=pltpu.CompilerParams(
            collective_id=collective_id, has_side_effects=True, vmem_limit_bytes=VMEM_LIMIT
        ),
        name="finish_all",
    )(rows, packs.reshape(natural + (pack_rows, pack_width)), token_rows, head_grad, scalars)


def own_pack_of(parts, seq_index, seq_count):
    mixer_in, mixer_x, mixer_out, channel, gains, router = [
        part.astype(jnp.bfloat16) for part in parts
    ]
    tall, wide_rows = (mixer_in.shape[0], mixer_x.shape[0] // seq_count)
    sides = jnp.pad(
        jnp.concatenate([router, gains.T], axis=1),
        ((0, 0), (0, LANES - router.shape[1] - gains.shape[0])),
    )
    top = jnp.concatenate(
        [lax.dynamic_slice_in_dim(mixer_in, seq_index * D, D, 1), sides], axis=1
    )
    middle = jnp.concatenate(
        [
            lax.dynamic_slice_in_dim(mixer_out, seq_index * wide_rows, wide_rows, 0),
            lax.dynamic_slice_in_dim(mixer_x, seq_index * wide_rows, wide_rows, 0),
        ],
        axis=1,
    )
    bottom = channel_tiles(
        lax.dynamic_slice_in_dim(channel, seq_index * wide_rows, wide_rows, 1)
    )
    return jnp.concatenate([top, middle, bottom])


def channel_tiles(channel):
    lead = [(0, 0)] * (channel.ndim - 2)
    rows, width = channel.shape[-2:]
    first = jnp.pad(channel[..., :16, :], lead + [(0, 0), (0, LANES - width)])
    second = jnp.pad(channel[..., 16:, :], lead + [(0, 32 - rows), (0, D - width)])
    return jnp.concatenate([first, second], axis=-1)


def weights_of(packs, experts_total):
    seqs, groups = packs.shape[:2]
    tall, wide_rows = (D // groups, DI // (seqs * groups))
    top, middle = (packs[:, :, :tall], packs[:, :, tall : tall + wide_rows])
    bottom = packs[:, :, tall + wide_rows :]
    weight_in = top[..., :D].transpose(1, 2, 0, 3).reshape(D, -1)
    sides = top[0, :, :, D:].reshape(D, LANES)
    weight_out = middle[..., :D].transpose(1, 0, 2, 3).reshape(-1, D)
    weight_x = middle[..., D:].transpose(1, 0, 2, 3).reshape(-1, LANES)
    rows = CONV + 3 + STATE
    channel = jnp.concatenate(
        [
            bottom[..., :16, :wide_rows].transpose(2, 1, 0, 3).reshape(16, -1),
            bottom[..., : rows - 16, LANES : LANES + wide_rows]
            .transpose(2, 1, 0, 3)
            .reshape(rows - 16, -1),
        ]
    )
    router = sides[:, :experts_total]
    gains = sides[:, experts_total : experts_total + 3].T
    return (weight_in, weight_x, weight_out, channel, gains, router)


def grad_packs(parts, seqs, groups):
    grad_in, grad_x, grad_out, grad_channel, grad_gains, grad_router = [
        part.astype(jnp.bfloat16) for part in parts
    ]
    tall, wide_rows = (D // groups, DI // (seqs * groups))
    sides = jnp.pad(
        jnp.concatenate([grad_router, grad_gains.T], axis=1),
        ((0, 0), (0, LANES - grad_router.shape[1] - grad_gains.shape[0])),
    ).reshape(1, groups, tall, LANES)
    sides = jnp.pad(sides, ((0, seqs - 1), (0, 0), (0, 0), (0, 0)))
    top = jnp.concatenate(
        [grad_in.reshape(groups, tall, seqs, D).transpose(2, 0, 1, 3), sides], axis=3
    )
    middle = jnp.concatenate(
        [
            part.reshape(groups, seqs, wide_rows, part.shape[1]).transpose(1, 0, 2, 3)
            for part in (grad_out, grad_x)
        ],
        axis=3,
    )
    rows = grad_channel.shape[0]
    bottom = channel_tiles(
        grad_channel.reshape(rows, groups, seqs, wide_rows).transpose(2, 1, 0, 3)
    )
    return jnp.concatenate([top, middle, bottom], axis=2)


def own_grads_of(quarters, experts_total):
    seqs, _, width = quarters.shape
    tall = quarters.shape[1] - 16 - DI // (seqs * lax.axis_size("group"))
    wide_rows = quarters.shape[1] - 16 - tall
    values = quarters.astype(jnp.float32)
    top, middle = (values[:, :tall], values[:, tall : tall + wide_rows])
    bottom = values[:, tall + wide_rows :]
    grad_in = top[..., :D].transpose(1, 0, 2).reshape(tall, -1)
    sides = top[0, :, D:]
    grad_out = middle[..., :D].reshape(-1, D)
    grad_x = middle[..., D:].reshape(-1, LANES)
    rows = CONV + 3 + STATE
    grad_channel = jnp.concatenate(
        [
            bottom[:, :16, :wide_rows].transpose(1, 0, 2).reshape(16, -1),
            bottom[:, : rows - 16, LANES : LANES + wide_rows]
            .transpose(1, 0, 2)
            .reshape(rows - 16, -1),
        ]
    )
    return (
        grad_in,
        grad_x,
        grad_out,
        grad_channel,
        sides[:, experts_total : experts_total + 3].T,
        sides[:, :experts_total],
    )


def from_behind(value, axis, by):
    devices = lax.axis_size(axis)
    pairs = [(i, i + by) for i in range(devices) if 0 <= i + by < devices]
    return lax.ppermute(value, axis, pairs)


def matmul(left, right):
    return jnp.dot(left, right, preferred_element_type=jnp.float32)


def matmul_nt(left, right):
    return lax.dot_general(
        left, right, (((1,), (1,)), ((), ())), preferred_element_type=jnp.float32
    )


def matmul_tn(left, right):
    return lax.dot_general(
        left, right, (((0,), (0,)), ((), ())), preferred_element_type=jnp.float32
    )


def silu_slope(preact):
    logistic = jax.nn.sigmoid(preact)
    return logistic * (1.0 + preact * (1.0 - logistic))


def inverse_rms(values):
    return lax.rsqrt(jnp.mean(values * values, axis=-1, keepdims=True) + EPS)


def norm_back(values, inv_scale, gain_row, grad_in):
    scaled = grad_in * gain_row
    grad_gain = jnp.sum(grad_in * values * inv_scale, axis=0)
    grad_values = inv_scale * scaled - values * inv_scale**3 * jnp.mean(
        scaled * values, axis=-1, keepdims=True
    )
    return (grad_values, grad_gain)


def neighbour_rows(edge_rows, offset):
    return from_behind(edge_rows, "group", offset)


def doc_layout(doc_lengths, first_pos, span_len):
    doc_ends = jnp.cumsum(doc_lengths, axis=1)
    doc_begins = doc_ends - doc_lengths
    where_at = first_pos + jnp.arange(span_len, dtype=jnp.int32)
    segment = jnp.sum((where_at[None, :, None] >= doc_ends[:, None, :]).astype(jnp.int32), axis=2)
    onehot_doc = (
        segment[:, :, None] == jnp.arange(doc_lengths.shape[1], dtype=jnp.int32)[None, None, :]
    ).astype(jnp.float32)
    weight = jnp.sum(onehot_doc / doc_lengths[:, None, :].astype(jnp.float32), axis=2)
    starting = jnp.sum(
        (where_at[None, :, None] == doc_begins[:, None, :]).astype(jnp.float32), axis=2
    )
    return (segment, weight, 1.0 - starting)


def lane_copies(columns):
    return jnp.broadcast_to(columns[..., None], columns.shape + (LANES,))


def mixer_forward(embedded, segment, keeping, weight_in, weight_x, weight_out, channel, gain_row):
    tokens = embedded.shape[0]
    scale_in = inverse_rms(embedded)
    normed = (embedded * scale_in * gain_row).astype(jnp.bfloat16)
    projected_in = matmul(normed, weight_in)
    conv_input = projected_in[:, :DI].astype(jnp.bfloat16)
    gate_z = projected_in[:, DI:]
    rim_rows = neighbour_rows(conv_input[tokens - CONV + 1 :].astype(jnp.float32), 1)
    padded = jnp.concatenate([rim_rows, conv_input.astype(jnp.float32)])
    same_doc = [
        (segment[conv_tap : conv_tap + tokens] == segment[CONV - 1 :]).astype(jnp.float32)[:, None]
        for conv_tap in range(CONV)
    ]
    conv_out = channel[CONV] + jnp.zeros_like(padded[CONV - 1 :])
    for conv_tap in range(CONV):
        conv_out = (
            conv_out + channel[conv_tap] * padded[conv_tap : conv_tap + tokens] * same_doc[conv_tap]
        )
    activated = jax.nn.silu(conv_out)
    act_low = activated.astype(jnp.bfloat16)
    projected = matmul(act_low, weight_x[:, : RANK + 2 * STATE])
    dt_input = projected[:, :RANK].astype(jnp.bfloat16)
    dt_pre = matmul_nt(dt_input, weight_x[:, RANK + 2 * STATE :])
    step_size = jax.nn.softplus(dt_pre + channel[CONV + 1])
    decay_rates = -jnp.exp(channel[CONV + 3 :])
    b_wide = lane_copies(projected[:, RANK : RANK + STATE])
    c_wide = lane_copies(projected[:, RANK + STATE :])
    keep_wide = lane_copies(keeping)
    reached, incoming = scan_forward(
        step_size, activated, b_wide, c_wide, keep_wide, decay_rates, 4
    )
    scanned = reached + channel[CONV + 2] * activated
    gate_act = jax.nn.silu(gate_z)
    gated = (scanned * gate_act).astype(jnp.bfloat16)
    mixed_out = embedded + matmul(gated, weight_out)
    kept_values = (
        scale_in,
        normed,
        gate_z,
        padded,
        same_doc,
        conv_out,
        activated,
        act_low,
        b_wide,
        c_wide,
        keep_wide,
        dt_input,
        dt_pre,
        step_size,
        decay_rates,
        incoming,
        scanned,
        gate_act,
        gated,
    )
    return (mixed_out, kept_values)


def mixer_backward(
    grad_out, embedded, kept_values, weight_in, weight_x, weight_out, channel, gain_row
):
    (
        scale_in,
        normed,
        gate_z,
        padded,
        same_doc,
        conv_out,
        activated,
        act_low,
        b_wide,
        c_wide,
        keep_wide,
        dt_input,
        dt_pre,
        step_size,
        decay_rates,
        incoming,
        scanned,
        gate_act,
        gated,
    ) = kept_values
    tokens = embedded.shape[0]
    grad_low = grad_out.astype(jnp.bfloat16)
    grad_wout = matmul_tn(gated, grad_low)
    grad_gated = matmul_nt(grad_low, weight_out)
    grad_scan = grad_gated * gate_act
    grad_z = grad_gated * scanned * silu_slope(gate_z)
    grad_skip = jnp.sum(grad_scan * activated, axis=0)
    along_b, decayed, wide_gb, wide_gc, grad_rates_log = scan_backward(
        step_size, activated, b_wide, c_wide, keep_wide, decay_rates, incoming, grad_scan, 5
    )
    grad_b = jnp.sum(wide_gb, axis=2)
    grad_c = jnp.sum(wide_gc, axis=2)
    grad_act = grad_scan * channel[CONV + 2] + along_b * step_size
    grad_step = decayed + along_b * activated
    grad_dtpre = grad_step * jax.nn.sigmoid(dt_pre + channel[CONV + 1])
    grad_dtbias = jnp.sum(grad_dtpre, axis=0)
    grad_dtlow = grad_dtpre.astype(jnp.bfloat16)
    grad_wdt = matmul_tn(grad_dtlow, dt_input)
    grad_dtin = matmul(grad_dtlow, weight_x[:, RANK + 2 * STATE :])
    grad_proj = jnp.concatenate([grad_dtin, grad_b, grad_c], axis=1).astype(jnp.bfloat16)
    grad_wx = jnp.concatenate([matmul_tn(act_low, grad_proj), grad_wdt], axis=1)
    grad_act = grad_act + matmul_nt(grad_proj, weight_x[:, : RANK + 2 * STATE])
    grad_conv = grad_act * silu_slope(conv_out)
    grad_taps = [
        jnp.sum(grad_conv * padded[conv_tap : conv_tap + tokens] * same_doc[conv_tap], axis=0)
        for conv_tap in range(CONV)
    ]
    grad_padded = sum(
        (
            jnp.pad(
                channel[conv_tap] * grad_conv * same_doc[conv_tap],
                ((conv_tap, CONV - 1 - conv_tap), (0, 0)),
            )
            for conv_tap in range(CONV)
        )
    )
    from_next = neighbour_rows(grad_padded[: CONV - 1], -1)
    grad_input = grad_padded[CONV - 1 :] + jnp.pad(from_next, ((tokens - CONV + 1, 0), (0, 0)))
    grad_both = jnp.concatenate([grad_input, grad_z], axis=1).astype(jnp.bfloat16)
    grad_win = matmul_tn(normed, grad_both)
    grad_normed = matmul_nt(grad_both, weight_in)
    grad_embed, grad_gain = norm_back(embedded, scale_in, gain_row, grad_normed)
    grad_channel = jnp.concatenate(
        [
            jnp.stack(grad_taps),
            jnp.sum(grad_conv, axis=0)[None],
            grad_dtbias[None],
            grad_skip[None],
            grad_rates_log,
        ]
    )
    return (grad_out + grad_embed, grad_win, grad_wx, grad_wout, grad_channel, grad_gain)


def choice_of(route_flat, experts_total):
    return (route_flat[:, None] == jnp.arange(experts_total, dtype=jnp.int32)[None, :]).astype(
        jnp.float32
    )


def dispatch_table(routes, first_expert, experts_here, capacity):
    tokens = routes.shape[1]
    chosen = (
        routes[:, :, None] == first_expert + jnp.arange(experts_here, dtype=jnp.int32)
    ).astype(jnp.float32)
    earlier = jnp.cumsum(chosen, axis=1) - chosen
    rank = jnp.sum(earlier * chosen, axis=2).astype(jnp.int32)
    local = routes - first_expert
    slot = jnp.where((local >= 0) & (local < experts_here), local * capacity + rank, -1)
    return (
        slot[:, None, :] == jnp.arange(experts_here * capacity, dtype=jnp.int32)[None, :, None]
    ).astype(jnp.bfloat16)


def to_slots(select, rows, experts_here, capacity):
    slots = jnp.einsum("bst,btd->bsd", select, rows, preferred_element_type=jnp.float32)
    slots = slots.astype(jnp.bfloat16).reshape(-1, experts_here, capacity, D)
    return jnp.swapaxes(slots, 0, 1).reshape(experts_here, -1, D)


def to_rows(select, slots, capacity):
    experts_here = slots.shape[0]
    slots = slots.astype(jnp.bfloat16).reshape(experts_here, -1, capacity, D)
    slots = jnp.swapaxes(slots, 0, 1).reshape(-1, experts_here * capacity, D)
    return jnp.einsum("bst,bsd->btd", select, slots, preferred_element_type=jnp.float32).astype(
        jnp.bfloat16
    )


def packed_rows(arrays, devices_seq):
    flat = jnp.concatenate([part.reshape(-1) for part in arrays])
    unit = devices_seq * SPAN * D
    size = -(-flat.shape[0] // unit) * unit
    return jnp.pad(flat, (0, size - flat.shape[0])).reshape(-1, D)


def unpacked(flat, shapes):
    parts, first = ([], 0)
    for shape in shapes:
        size = 1
        for extent in shape:
            size *= extent
        parts.append(flat[..., first : first + size].reshape(flat.shape[:-1] + shape))
        first += size
    return parts


def whole_of(shards, axis):
    moved_axis = jnp.moveaxis(shards, 0, axis)
    shape = moved_axis.shape
    return moved_axis.reshape(shape[:axis] + (shape[axis] * shape[axis + 1],) + shape[axis + 2 :])


def shards_of(whole, axis, count):
    shape = whole.shape
    split = whole.reshape(shape[:axis] + (count, shape[axis] // count) + shape[axis + 1 :])
    return jnp.moveaxis(split, axis, 0)


def renewed(master, moment, average, gradient, clip_factor, rate):
    scaled = clip_factor * gradient
    moment_new = MOMENTUM * moment + scaled
    master_new = master - rate * (scaled + MOMENTUM * moment_new)
    return (master_new, moment_new, EMA_KEEP * average + (1.0 - EMA_KEEP) * master_new)


def per_device(
    token_ids,
    target_ids,
    doc_lengths,
    expert_ids,
    vocab_table,
    vocab_table_mom,
    vocab_table_ema,
    mixer_in,
    mixer_in_mom,
    mixer_in_ema,
    mixer_x,
    mixer_x_mom,
    mixer_x_ema,
    mixer_out,
    mixer_out_mom,
    mixer_out_ema,
    channel,
    channel_mom,
    channel_ema,
    norm_gains,
    norm_gains_mom,
    norm_gains_ema,
    router,
    router_mom,
    router_ema,
    experts,
    experts_mom,
    experts_ema,
):
    seq_count = lax.axis_size("seq")
    group_count = lax.axis_size("group")
    seq_index = lax.axis_index("seq")
    group_index = lax.axis_index("group")
    devices = seq_count * group_count
    tokens = token_ids.shape[1]
    sequences = token_ids.shape[0]
    experts_total = router.shape[1]
    local_experts = experts.shape[1]
    capacity = max(2, 2 * tokens // experts_total)
    own_vocab = vocab_table.shape[0]
    routes = expert_ids.reshape(1, tokens)
    numbers = jnp.concatenate([token_ids, target_ids, routes])
    numbers = jnp.pad(numbers, ((0, -numbers.shape[0] % 8), (0, 0)))
    mixer_parts = (mixer_in, mixer_x, mixer_out, channel, norm_gains, router)
    part_axes = (0, 0, 0, 1, 1, 0)
    part_shapes = [part.shape for part in mixer_parts]
    table_low = vocab_table.astype(jnp.bfloat16)
    experts_low = experts.astype(jnp.bfloat16)
    up_weight, down_weight = (experts_low[0], experts_low[1])
    vocab_start = (seq_index * group_count + group_index) * own_vocab
    column_ids = jnp.arange(own_vocab, dtype=jnp.int32)
    wide_rows = DI // (seq_count * group_count)
    compact = devices * tokens <= 4096 and 2 * DI == seq_count * D
    if compact:
        table_turned = jnp.pad(table_low.T, ((0, 0), (0, -own_vocab % LANES)))
        own_pack = own_pack_of(mixer_parts, seq_index, seq_count)
        numbers_all, packs, embedded = start_all(numbers, own_pack, table_turned, own_vocab, 1)
        packs = packs.reshape((seq_count, group_count) + own_pack.shape)
        weight_in, weight_x, weight_out, channel_low, gains_low, router_low = weights_of(
            packs, experts_total
        )
    else:
        numbers_all = share_small(numbers, 1)
    from_groups = jnp.swapaxes(numbers_all[:group_count, : 2 * sequences], 0, 1)
    tokens_all = from_groups[:sequences].reshape(-1)
    targets_all = from_groups[sequences:].reshape(-1)
    routes_all = numbers_all[:, 2 * sequences]
    if not compact:
        pack = packed_rows([part.astype(jnp.bfloat16) for part in mixer_parts], seq_count)
        pack_rows = pack.shape[0] // seq_count
        own_pack = lax.dynamic_slice_in_dim(pack, seq_index * pack_rows, pack_rows, 0)
        packs = gather_all(own_pack, 2).reshape(seq_count, group_count, pack_rows * D)
        shards = unpacked(jnp.swapaxes(packs, 0, 1).reshape(group_count, -1), part_shapes)
        weight_in, weight_x, weight_out, channel_low, gains_low, router_low = [
            whole_of(shard, axis) for shard, axis in zip(shards, part_axes)
        ]
        held_token = (tokens_all - vocab_start)[:, None] == column_ids[None, :]
        held_token = held_token.astype(jnp.bfloat16)
        looked_up = matmul(held_token, table_low).astype(jnp.bfloat16)
        embedded = scatter_all(looked_up.reshape(devices, tokens, D), 3)
    channel_vals = channel_low.astype(jnp.float32)
    gain_vals = gains_low.astype(jnp.float32)

    segment_all, weight_all, keep_all = doc_layout(
        doc_lengths, group_index * tokens - CONV + 1, tokens + CONV - 1
    )
    own_segment = lax.dynamic_index_in_dim(segment_all, seq_index, 0, keepdims=False)
    keeping = lax.dynamic_index_in_dim(keep_all, seq_index, 0, keepdims=False)[CONV - 1 :]
    own_weight = lax.dynamic_index_in_dim(weight_all, seq_index, 0, keepdims=False)[CONV - 1 :]
    _, every_weight, _ = doc_layout(doc_lengths, 0, tokens * group_count)
    row_weight = every_weight.reshape(-1)
    mixed_out, kept_values = mixer_forward(
        embedded, own_segment, keeping, weight_in, weight_x, weight_out, channel_vals, gain_vals[0]
    )
    scale_mid = inverse_rms(mixed_out)
    moe_in = (mixed_out * scale_mid * gain_vals[1]).astype(jnp.bfloat16)
    chosen = choice_of(expert_ids.reshape(-1), experts_total)
    select = dispatch_table(routes_all, seq_index * local_experts, local_experts, capacity)
    probability = jax.nn.softmax(matmul(moe_in, router_low), axis=-1)
    gate_value = jnp.sum(probability * chosen, axis=1)
    arrived = to_slots(select, gather_all(moe_in, 6), local_experts, capacity)
    before = jnp.einsum("erd,efd->erf", arrived, up_weight, preferred_element_type=jnp.float32)
    inner_act = jax.nn.gelu(before).astype(jnp.bfloat16)
    partial_out = jnp.einsum(
        "erf,efd->erd", inner_act, down_weight, preferred_element_type=jnp.float32
    )
    returned = scatter_all(to_rows(select, partial_out, capacity), 3)
    expert_value = returned.astype(jnp.bfloat16).astype(jnp.float32)
    branch = gate_value[:, None] * expert_value
    hidden = mixed_out + branch
    scale_out = inverse_rms(hidden)
    final_low = (hidden * scale_out * gain_vals[2]).astype(jnp.bfloat16)
    if compact:

        def spread(values):
            split = values.reshape(seq_count, group_count, tokens // SPAN, SPAN)
            return split.transpose(2, 0, 1, 3).reshape(-1, group_count * SPAN)

        table_padded = jnp.pad(table_low, ((0, -own_vocab % 16), (0, 0)))
        target_local = targets_all - vocab_start
        target_local = spread(jnp.where(target_local < own_vocab, target_local, -1))
        all_final, stats = head_forward(final_low, table_padded, own_vocab, target_local, 7)
        own_entropy = (stats[0] - stats[1]).reshape(-1, seq_count, group_count, SPAN)
        own_entropy = lax.dynamic_index_in_dim(own_entropy, seq_index, 1, keepdims=False)
        own_entropy = lax.dynamic_index_in_dim(own_entropy, group_index, 1, keepdims=False)
        loss_part = jnp.sum(own_weight * own_entropy.reshape(-1))
        grad_final, table_grad = head_backward(
            all_final,
            table_padded,
            table_turned,
            own_vocab,
            target_local,
            stats[0],
            spread(row_weight),
            10,
        )
    else:
        all_final = gather_all(final_low, 6).reshape(devices * tokens, D)
        valid_cols = vocab_start + column_ids < VOCAB_REAL
        hit_target = (targets_all - vocab_start)[:, None] == column_ids[None, :]
        logits = jnp.where(valid_cols[None, :], matmul_nt(all_final, table_low), -1e30)
        largest = jnp.max(logits, axis=1)
        exp_total = jnp.sum(jnp.exp(logits - largest[:, None]), axis=1)
        picked = jnp.sum(jnp.where(hit_target, logits, 0.0), axis=1)
        parts = jnp.stack([largest, exp_total, picked]).reshape(3, devices, tokens)
        parts = jnp.pad(jnp.swapaxes(parts, 0, 1), ((0, 0), (0, 5), (0, 0)))
        levels, entropy = combine_stats(parts, 7)
        log_total = levels[:, 0].reshape(-1)
        loss_part = jnp.sum(own_weight * entropy[0])
        grad_logits = (
            row_weight[:, None]
            * (jnp.exp(logits - log_total[:, None]) - hit_target.astype(jnp.float32))
        ).astype(jnp.bfloat16)
        table_grad = matmul_tn(grad_logits, all_final)
        grad_rows = matmul(grad_logits, table_low).astype(jnp.bfloat16)
        grad_final = scatter_all(grad_rows.reshape(devices, tokens, D), 3)
    grad_hidden, grad_gain_out = norm_back(hidden, scale_out, gain_vals[2], grad_final)
    grad_gate = jnp.sum(grad_hidden * expert_value, axis=1)
    grad_expert = (gate_value[:, None] * grad_hidden).astype(jnp.bfloat16)
    grad_arrived = to_slots(select, gather_all(grad_expert, 6), local_experts, capacity)
    grad_inner = jnp.einsum(
        "erd,efd->erf", grad_arrived, down_weight, preferred_element_type=jnp.float32
    )
    grad_before = jax.vjp(jax.nn.gelu, before)[1](grad_inner)[0].astype(jnp.bfloat16)
    grad_down = jnp.einsum(
        "erf,erd->efd", inner_act, grad_arrived, preferred_element_type=jnp.float32
    )
    grad_up = jnp.einsum("erf,erd->efd", grad_before, arrived, preferred_element_type=jnp.float32)
    grad_part = jnp.einsum(
        "erf,efd->erd", grad_before, up_weight, preferred_element_type=jnp.float32
    )
    grad_moe_in = scatter_all(to_rows(select, grad_part, capacity), 3)
    grad_moe_in = grad_moe_in.astype(jnp.bfloat16).astype(jnp.float32)
    grad_router_logits = (grad_gate * gate_value)[:, None] * (chosen - probability)
    grad_moe_in = grad_moe_in + jnp.dot(
        grad_router_logits, router_low.astype(jnp.float32).T, precision=HIGHEST
    )
    grad_router = jnp.dot(moe_in.astype(jnp.float32).T, grad_router_logits, precision=HIGHEST)
    grad_mid, grad_gain_mid = norm_back(mixed_out, scale_mid, gain_vals[1], grad_moe_in)
    grad_mixed = grad_hidden + grad_mid
    grad_embedded, grad_win, grad_wx, grad_wout, grad_channel, grad_gain_in = mixer_backward(
        grad_mixed,
        embedded,
        kept_values,
        weight_in,
        weight_x,
        weight_out,
        channel_vals,
        gain_vals[0],
    )
    grad_gains = jnp.stack([grad_gain_in, grad_gain_mid, grad_gain_out])
    mixer_wholes = (grad_win, grad_wx, grad_wout, grad_channel, grad_gains, grad_router)
    grad_experts = jnp.stack([grad_up, grad_down])
    experts_square = jnp.sum(grad_experts * grad_experts)
    if compact:
        token_local = tokens_all - vocab_start
        token_local = spread(jnp.where(token_local < own_vocab, token_local, -1))
        scalars = jnp.concatenate(
            [jnp.full((4, LANES), experts_square), jnp.full((4, LANES), loss_part)], axis=0
        )
        table_grad, quarters, sums = finish_all(
            grad_embedded.astype(jnp.bfloat16),
            grad_packs(mixer_wholes, seq_count, group_count),
            token_local,
            table_grad,
            scalars,
            9,
        )
        table_grad = table_grad[:own_vocab]
        mixer_grads = own_grads_of(quarters, experts_total)
    else:
        all_grad_embed = gather_all(grad_embedded.astype(jnp.bfloat16), 6).reshape(-1, D)
        table_grad = table_grad + matmul_tn(held_token, all_grad_embed)
        wholes_low = [
            shards_of(whole.astype(jnp.bfloat16), axis, group_count).reshape(group_count, -1)
            for whole, axis in zip(mixer_wholes, part_axes)
        ]
        flat = jnp.concatenate(wholes_low, axis=1)
        flat = jnp.pad(flat, ((0, 0), (0, seq_count * pack_rows * D - flat.shape[1])))
        flat = jnp.swapaxes(flat.reshape(group_count, seq_count, pack_rows, D), 0, 1)
        own_quarter = scatter_all(flat.reshape(devices, pack_rows, D), 8)
        quarters = lax.all_gather(own_quarter, "seq", axis=0, tiled=True).reshape(-1)
        mixer_grads = unpacked(quarters, part_shapes)
        local_square = (
            jnp.sum(table_grad * table_grad) + experts_square + jnp.sum(own_quarter * own_quarter)
        )
        two = jnp.concatenate(
            [jnp.full((4, LANES), local_square), jnp.full((4, LANES), loss_part)], axis=0
        )
        sums = jnp.sum(share_small(two, 9), axis=0)
    total_square, loss_sum = (sums[0, 0], sums[4, 0])
    grad_norm = jnp.sqrt(total_square)
    clip_factor = jnp.minimum(1.0, CLIP / (grad_norm + 1e-06))
    table_new = renewed(
        vocab_table, vocab_table_mom, vocab_table_ema, table_grad, clip_factor, LRATE
    )
    in_new = renewed(mixer_in, mixer_in_mom, mixer_in_ema, mixer_grads[0], clip_factor, LRATE)
    x_new = renewed(mixer_x, mixer_x_mom, mixer_x_ema, mixer_grads[1], clip_factor, LRATE)
    out_new = renewed(mixer_out, mixer_out_mom, mixer_out_ema, mixer_grads[2], clip_factor, LRATE)
    channel_new = renewed(
        channel, channel_mom, channel_ema, mixer_grads[3], clip_factor, CHANNEL_LRATE
    )
    gains_new = renewed(
        norm_gains, norm_gains_mom, norm_gains_ema, mixer_grads[4], clip_factor, LRATE
    )
    router_new = renewed(router, router_mom, router_ema, mixer_grads[5], clip_factor, LRATE)
    experts_new = renewed(experts, experts_mom, experts_ema, grad_experts, clip_factor, LRATE)
    return (
        loss_sum,
        grad_norm,
        branch.reshape(1, tokens, D),
        table_new[0],
        table_new[1],
        table_new[2],
        in_new[0],
        in_new[1],
        in_new[2],
        x_new[0],
        x_new[1],
        x_new[2],
        out_new[0],
        out_new[1],
        out_new[2],
        channel_new[0],
        channel_new[1],
        channel_new[2],
        gains_new[0],
        gains_new[1],
        gains_new[2],
        router_new[0],
        router_new[1],
        router_new[2],
        experts_new[0],
        experts_new[1],
        experts_new[2],
    )


def solution(mesh):
    placed = (
        P(None, "group"),
        P(None, "group"),
        P(),
        P("seq", "group", None),
        P(("seq", "group"), None),
        P(("seq", "group"), None),
        P(("seq", "group"), None),
        P("group", None),
        P("group", None),
        P("group", None),
        P("group", None),
        P("group", None),
        P("group", None),
        P("group", None),
        P("group", None),
        P("group", None),
        P(None, "group"),
        P(None, "group"),
        P(None, "group"),
        P(None, "group"),
        P(None, "group"),
        P(None, "group"),
        P("group", None),
        P("group", None),
        P("group", None),
        P(None, "seq", "group", None),
        P(None, "seq", "group", None),
        P(None, "seq", "group", None),
    )
    return jax.shard_map(
        per_device,
        mesh=mesh,
        in_specs=placed,
        out_specs=(
            P(),
            P(),
            P("seq", "group", None),
            P(("seq", "group"), None),
            P(("seq", "group"), None),
            P(("seq", "group"), None),
            P("group", None),
            P("group", None),
            P("group", None),
            P("group", None),
            P("group", None),
            P("group", None),
            P("group", None),
            P("group", None),
            P("group", None),
            P(None, "group"),
            P(None, "group"),
            P(None, "group"),
            P(None, "group"),
            P(None, "group"),
            P(None, "group"),
            P("group", None),
            P("group", None),
            P("group", None),
            P(None, "seq", "group", None),
            P(None, "seq", "group", None),
            P(None, "seq", "group", None),
        ),
        check_vma=False,
    )
```

```python
import functools

import jax
import jax.numpy as jnp
from jax import lax
from jax.experimental import pallas as pl
from jax.experimental.pallas import tpu as pltpu
from jax.sharding import PartitionSpec as P

D = 768
DI = 1536
STATE = 16
RANK = 48
CONV = 4
VOCAB_REAL = 50257


EPS = 1e-05
CLIP = 0.1
MOMENTUM = 0.9
LRATE = 1000.0
CHANNEL_LRATE = 10000.0
EMA_KEEP = 0.8
HIGHEST = lax.Precision.HIGHEST
MESH = pl.DeviceIdType.MESH
VMEM_LIMIT = 58 << 20
LANES = 128
SIDE_LANE = 32


def axis_sizes():
    seq, group = (lax.axis_size("seq"), lax.axis_size("group"))
    core = 2 if seq % 2 == 0 else 1
    y = 1
    while 4 * y * y <= group and group % (2 * y) == 0:
        y *= 2
    return {"x": seq // core, "core": core, "z": group // y, "y": y}


def my_place(sizes):
    seq, group = (lax.axis_index("seq"), lax.axis_index("group"))
    return {
        "x": seq // sizes["core"],
        "core": seq % sizes["core"],
        "z": group // sizes["y"],
        "y": group % sizes["y"],
    }


def device_of(place, sizes):
    return (place["x"] * sizes["core"] + place["core"], place["z"] * sizes["y"] + place["y"])


def moved(place, axis, by, sizes):
    return {**place, axis: lax.rem(place[axis] + by + sizes[axis], sizes[axis])}


def block_of(place, sizes):
    seq, group = device_of(place, sizes)
    return seq * (sizes["z"] * sizes["y"]) + group


def meet(peers):
    barrier = pltpu.get_barrier_semaphore()
    for peer in peers:
        pl.semaphore_signal(barrier, inc=1, device_id=peer, device_id_type=MESH)
    pl.semaphore_wait(barrier, len(peers))


def line_peers(place, sizes):
    return [
        device_of(moved(place, axis, by, sizes), sizes)
        for axis in ("x", "core", "z", "y")
        for by in range(1, sizes[axis])
    ]


GATHER_ORDERS = (
    ("z", "y", "x", "core"),
    ("z", "x", "y", "core"),
    ("x", "z", "y", "core"),
    ("y", "z", "x", "core"),
)


def gather_kernel(sizes, pieces, own_ref, all_ref, local_sem, send_sem, recv_sem):
    place = my_place(sizes)
    meet(line_peers(place, sizes))
    keep_own = pltpu.make_async_copy(own_ref, all_ref.at[block_of(place, sizes)], local_sem)
    keep_own.start()
    held = [[(place, None)] for _ in pieces]
    sends = []
    for phase in range(4):
        fresh = [[] for _ in pieces]
        for turn in range(max(len(blocks) for blocks in held)):
            for which, (order, first, rows) in enumerate(pieces):
                if turn >= len(held[which]):
                    continue
                axis = order[phase]
                where, arrival = held[which][turn]
                if arrival is not None:
                    copy, seen = arrival
                    if not seen:
                        copy.wait_recv()
                        held[which][turn] = (where, (copy, True))
                span = pl.ds(first, rows)
                for by in range(1, sizes[axis]):
                    block = block_of(where, sizes)
                    source = own_ref.at[span] if arrival is None else all_ref.at[block, span]
                    number = len(sends)
                    copy = pltpu.make_async_remote_copy(
                        src_ref=source,
                        dst_ref=all_ref.at[block, span],
                        send_sem=send_sem.at[number],
                        recv_sem=recv_sem.at[number],
                        device_id=device_of(moved(place, axis, by, sizes), sizes),
                        device_id_type=MESH,
                    )
                    copy.start()
                    sends.append(copy)
                    fresh[which].append((moved(where, axis, -by, sizes), (copy, False)))
        held = [old + new for old, new in zip(held, fresh)]
    for blocks in held:
        for _, arrival in blocks:
            if arrival is not None and not arrival[1]:
                arrival[0].wait_recv()
    for copy in sends:
        copy.wait_send()
    keep_own.wait()


def split_rows(rows, orders):
    unit = 32 if rows % 32 == 0 else 16
    count = rows // unit
    pieces, first = ([], 0)
    for which in range(min(count, 4)):
        size = (count * (which + 1) // min(count, 4)) * unit - first
        pieces.append((orders[which % len(orders)], first, size))
        first += size
    return pieces


def gather_all(rows, collective_id):
    sizes = axis_sizes()
    devices = sizes["x"] * sizes["core"] * sizes["z"] * sizes["y"]
    pieces = split_rows(rows.shape[0], GATHER_ORDERS)
    copies = (devices - 1) * len(pieces)
    return pl.pallas_call(
        functools.partial(gather_kernel, sizes, pieces),
        out_shape=jax.ShapeDtypeStruct((devices,) + rows.shape, rows.dtype),
        in_specs=[pl.BlockSpec(memory_space=pltpu.VMEM)],
        out_specs=pl.BlockSpec(memory_space=pl.ANY),
        scratch_shapes=[
            pltpu.SemaphoreType.DMA,
            pltpu.SemaphoreType.DMA((copies,)),
            pltpu.SemaphoreType.DMA((copies,)),
        ],
        compiler_params=pltpu.CompilerParams(
            collective_id=collective_id, has_side_effects=True, vmem_limit_bytes=VMEM_LIMIT
        ),
        name="gather_all",
    )(rows)


SCATTER_ORDERS = (("core", "x", "y", "z"), ("core", "y", "x", "z"))
GATHER_PAIR = (("z", "y", "x", "core"), ("z", "x", "y", "core"))
NATURAL = ("x", "core", "z", "y")
PIECE = 16
SPAN = 2 * PIECE


def unravel(number, extents):
    places = []
    for extent in reversed(extents):
        places.append(lax.rem(number, extent))
        number = lax.div(number, extent)
    return tuple(reversed(places))


def piece_rows(pair, kind):
    first = pair * SPAN + kind * PIECE
    if not isinstance(first, int):
        first = pl.multiple_of(first, PIECE)
    return pl.ds(first, PIECE)


def scatter_scratch(sizes, pairs, width, keep):
    scratch = []
    for order in SCATTER_ORDERS:
        landings, sums, semaphores = ([], [], [])
        for phase in range(4):
            left = tuple(sizes[a] for a in NATURAL if a not in order[: phase + 1])
            others = max(1, sizes[order[phase]] - 1)
            landings.append(pltpu.VMEM((pairs, others) + left + (PIECE, width), jnp.bfloat16))
            if phase < 3:
                sums.append(pltpu.VMEM((pairs,) + left + (PIECE, width), jnp.bfloat16))
            semaphores.append(pltpu.SemaphoreType.DMA((pairs, others)))
            semaphores.append(pltpu.SemaphoreType.DMA((pairs, others)))
        scratch += landings + sums + semaphores
        scratch += [pltpu.SemaphoreType.DMA((pairs,))] if keep else []
    return scratch


class Scatter:
    def __init__(self, sizes, pairs, full_ref, own_ref, scratch, keep):
        self.sizes, self.pairs, self.keep = (sizes, pairs, keep)
        self.full_ref, self.own_ref = (full_ref, own_ref)
        self.place = my_place(sizes)
        size = len(scratch) // 2
        self.refs = (scratch[:size], scratch[size:])

    def kept(self, kind, pair):
        order = SCATTER_ORDERS[kind]
        index = tuple(self.place[a] if a == order[0] else slice(None) for a in NATURAL)
        return pltpu.make_async_copy(
            self.full_ref.at[index + (piece_rows(pair, kind),)],
            self.refs[kind][4].at[pair],
            self.refs[kind][15].at[pair],
        )

    def copies(self, kind, pair, phase):
        order, refs, sizes = (SCATTER_ORDERS[kind], self.refs[kind], self.sizes)
        axis = order[phase]
        left = [a for a in NATURAL if a not in order[:phase]]
        made = []
        for by in range(1, sizes[axis]):
            to = moved(self.place, axis, by, sizes)
            index = tuple(to[axis] if a == axis else slice(None) for a in left)
            if phase == 0:
                source = self.full_ref.at[index + (piece_rows(pair, kind),)]
            else:
                source = refs[3 + phase].at[(pair,) + index]
            made.append(
                pltpu.make_async_remote_copy(
                    src_ref=source,
                    dst_ref=refs[phase].at[pair, by - 1],
                    send_sem=refs[7 + 2 * phase].at[pair, by - 1],
                    recv_sem=refs[8 + 2 * phase].at[pair, by - 1],
                    device_id=device_of(to, sizes),
                    device_id_type=MESH,
                )
            )
        return made

    def launch(self, pair, phase):
        for kind in range(2):
            for copy in self.copies(kind, pair, phase):
                copy.start()

    def absorb(self, kind, pair, phase):
        order, refs, sizes, place = (
            SCATTER_ORDERS[kind],
            self.refs[kind],
            self.sizes,
            self.place,
        )
        axis = order[phase]
        before = [a for a in NATURAL if a not in order[:phase]]
        after = [a for a in before if a != axis]
        if phase == 0 and self.keep:
            self.kept(kind, pair).wait()
        for copy in self.copies(kind, pair, phase):
            copy.wait_recv()
        extents = tuple(sizes[a] for a in after)
        number = 1
        for extent in extents:
            number *= extent

        def add(step, carry):
            spot = dict(zip(after, unravel(step, extents)))
            mine = tuple(place[axis] if a == axis else spot[a] for a in before)
            there = tuple(spot[a] for a in after)
            if phase > 0:
                kept_part = refs[3 + phase][(pair,) + mine]
            elif self.keep:
                kept_part = refs[4][(pair,) + there]
            else:
                kept_part = self.full_ref[mine + (piece_rows(pair, kind),)]
            total = kept_part.astype(jnp.float32)
            for by in range(1, sizes[axis]):
                total = total + refs[phase][(pair, by - 1) + there].astype(jnp.float32)
            if phase == 3:
                self.own_ref[piece_rows(pair, kind)] = total
            else:
                refs[4 + phase][(pair,) + there] = total.astype(jnp.bfloat16)
            return carry

        if number == 1:
            add(0, 0)
        else:
            lax.fori_loop(0, number, add, 0)

    def advance(self, pair, phase):
        for kind in range(2):
            self.absorb(kind, pair, phase)
            if phase < 3:
                for copy in self.copies(kind, pair, phase + 1):
                    copy.start()

    def finish(self):
        def one(pair, carry):
            for kind in range(2):
                for phase in range(4):
                    for copy in self.copies(kind, pair, phase):
                        copy.wait_send()
            return carry

        lax.fori_loop(0, self.pairs, one, 0)


def wave(pairs, phases, act):
    def step(turn, carry):
        for phase in range(phases - 1, -1, -1):
            pair = turn - phase

            @pl.when((pair >= 0) & (pair < pairs))
            def _(pair=pair, phase=phase):
                act(pair, phase)

        return carry

    lax.fori_loop(0, pairs + phases - 1, step, 0)


def scatter_kernel(sizes, pairs, full_ref, own_ref, *scratch):
    meet(line_peers(my_place(sizes), sizes))
    scatter = Scatter(sizes, pairs, full_ref, own_ref, scratch, True)
    for pair in range(pairs):
        scatter.launch(pair, 0)
        for kind in range(2):
            scatter.kept(kind, pair).start()
    wave(pairs, 4, scatter.advance)
    scatter.finish()


def scatter_all(blocks, collective_id):
    sizes = axis_sizes()
    rows, width = blocks.shape[-2:]
    pairs = rows // SPAN
    shaped = blocks.reshape(tuple(sizes[a] for a in NATURAL) + (rows, width))
    return pl.pallas_call(
        functools.partial(scatter_kernel, sizes, pairs),
        out_shape=jax.ShapeDtypeStruct((rows, width), jnp.float32),
        in_specs=[pl.BlockSpec(memory_space=pl.ANY)],
        out_specs=pl.BlockSpec(memory_space=pltpu.VMEM),
        scratch_shapes=scatter_scratch(sizes, pairs, width, True),
        compiler_params=pltpu.CompilerParams(
            collective_id=collective_id, has_side_effects=True, vmem_limit_bytes=VMEM_LIMIT
        ),
        name="scatter_all",
    )(shaped)


class Gather:
    def __init__(self, sizes, pairs, own_ref, all_ref, semaphores):
        self.sizes, self.pairs = (sizes, pairs)
        self.own_ref, self.all_ref = (own_ref, all_ref)
        self.semaphores = semaphores
        self.place = my_place(sizes)

    def copies(self, kind, pair, phase):
        order = GATHER_PAIR[kind]
        axis, span = (order[phase], piece_rows(pair, kind))
        block = tuple(slice(None) if a in order[:phase] else self.place[a] for a in NATURAL)
        there = self.all_ref.at[block + (span,)]
        send_sem, recv_sem = (self.semaphores[2 * phase], self.semaphores[2 * phase + 1])
        return [
            pltpu.make_async_remote_copy(
                src_ref=self.own_ref.at[span] if phase == 0 else there,
                dst_ref=there,
                send_sem=send_sem.at[kind, pair, by - 1],
                recv_sem=recv_sem.at[kind, pair, by - 1],
                device_id=device_of(moved(self.place, axis, by, self.sizes), self.sizes),
                device_id_type=MESH,
            )
            for by in range(1, self.sizes[axis])
        ]

    def advance(self, pair, phase):
        for kind in range(2):
            if phase > 0:
                for copy in self.copies(kind, pair, phase - 1):
                    copy.wait_recv()
            if phase < 4:
                for copy in self.copies(kind, pair, phase):
                    copy.start()

    def finish(self):
        def one(pair, carry):
            for kind in range(2):
                for phase in range(4):
                    for copy in self.copies(kind, pair, phase):
                        copy.wait_send()
            return carry

        lax.fori_loop(0, self.pairs, one, 0)


def gather_semaphores(sizes, pairs):
    longest = max(sizes.values())
    return [pltpu.SemaphoreType.DMA((2, pairs, longest)) for _ in range(8)]


def seq_place(seq, sizes):
    return (lax.div(seq, sizes["core"]), lax.rem(seq, sizes["core"]))


def merge_stats(first, second):
    high = jnp.maximum(first[0], second[0])
    mass = first[1] * jnp.exp(first[0] - high) + second[1] * jnp.exp(second[0] - high)
    return (high, mass, first[2] + second[2])


def span_rows(pair):
    return pl.ds(pl.multiple_of(pair * SPAN, SPAN), SPAN)


def masked_logits(table_ref, rows_in, first_masked, limit):
    logits = matmul_nt(table_ref[...], rows_in)
    tail = logits[first_masked:]
    numbers = first_masked + lax.broadcasted_iota(jnp.int32, tail.shape, 0)
    return jnp.concatenate([logits[:first_masked], jnp.where(numbers < limit, tail, -1e30)], axis=0)


def vocab_limit(own_vocab):
    devices, _, me = flat_place()
    least = max(0, VOCAB_REAL - (devices - 1) * own_vocab)
    limit = jnp.minimum(own_vocab, VOCAB_REAL - me * own_vocab)
    return (min(least, own_vocab) // 16 * 16, limit)


def head_forward_kernel(
    sizes,
    pairs,
    own_vocab,
    own_ref,
    table_ref,
    target_ref,
    all_ref,
    stats_ref,
    mine_ref,
    landing_ref,
    local_sem,
    stat_send,
    stat_recv,
    *semaphores,
):
    place = my_place(sizes)
    meet(line_peers(place, sizes))
    gather = Gather(sizes, pairs, own_ref, all_ref, semaphores)
    keep_own = pltpu.make_async_copy(
        own_ref, all_ref.at[tuple(place[a] for a in NATURAL)], local_sem
    )
    keep_own.start()
    groups = sizes["z"] * sizes["y"]
    seqs = sizes["x"] * sizes["core"]
    first_masked, limit = vocab_limit(own_vocab)

    def seq_stats(pair, seq):
        x, core = seq_place(seq, sizes)
        rows_in = all_ref[x, core, :, :, span_rows(pair), :].reshape(groups * SPAN, D)
        logits = masked_logits(table_ref, rows_in, first_masked, limit)
        spot = pl.ds(pair * seqs + seq, 1)
        numbers = lax.broadcasted_iota(jnp.int32, logits.shape, 0)
        top = jnp.max(logits, axis=0, keepdims=True)
        mine_ref[0, 0, spot] = top
        mine_ref[0, 1, spot] = jnp.sum(jnp.exp(logits - top), axis=0, keepdims=True)
        mine_ref[0, 2, spot] = jnp.sum(
            jnp.where(numbers == target_ref[spot], logits, 0.0), axis=0, keepdims=True
        )

    def turn_step(turn, carry):
        for phase in range(4, -1, -1):
            pair = turn - phase

            @pl.when((pair >= 0) & (pair < pairs))
            def _(pair=pair, phase=phase):
                gather.advance(pair, phase)

        @pl.when(turn == 0)
        def _():
            keep_own.wait()

        @pl.when(turn >= 4)
        def _():
            def one(seq, carry):
                seq_stats(turn - 4, seq)
                return carry

            lax.fori_loop(0, seqs, one, 0)

        return carry

    lax.fori_loop(0, pairs + 4, turn_step, 0)
    started = []
    stats = tuple(mine_ref[0, k] for k in range(3))
    for phase, axis in enumerate(("core", "x", "y", "z")):
        arrivals = []
        for by in range(1, sizes[axis]):
            slot = len(started)
            copy = pltpu.make_async_remote_copy(
                src_ref=mine_ref.at[phase],
                dst_ref=landing_ref.at[slot],
                send_sem=stat_send.at[slot],
                recv_sem=stat_recv.at[slot],
                device_id=device_of(moved(place, axis, by, sizes), sizes),
                device_id_type=MESH,
            )
            copy.start()
            arrivals.append((copy, slot))
            started.append(copy)
        for copy, slot in arrivals:
            copy.wait_recv()
            stats = merge_stats(stats, tuple(landing_ref[slot, k] for k in range(3)))
        if phase < 3:
            for k in range(3):
                mine_ref[phase + 1, k] = stats[k]
    stats_ref[0] = stats[0] + jnp.log(stats[1])
    stats_ref[1] = stats[2]
    gather.finish()
    for copy in started:
        copy.wait_send()


def head_forward(rows, table, own_vocab, targets, collective_id):
    sizes = axis_sizes()
    pairs = rows.shape[0] // SPAN
    hops = sum(extent - 1 for extent in sizes.values())
    natural = tuple(sizes[a] for a in NATURAL)
    packed = (3,) + targets.shape
    vmem = pl.BlockSpec(memory_space=pltpu.VMEM)
    return pl.pallas_call(
        functools.partial(head_forward_kernel, sizes, pairs, own_vocab),
        out_shape=(
            jax.ShapeDtypeStruct(natural + rows.shape, rows.dtype),
            jax.ShapeDtypeStruct((2,) + targets.shape, jnp.float32),
        ),
        in_specs=[vmem] * 3,
        out_specs=(vmem,) * 2,
        scratch_shapes=[
            pltpu.VMEM((4,) + packed, jnp.float32),
            pltpu.VMEM((hops,) + packed, jnp.float32),
            pltpu.SemaphoreType.DMA,
            pltpu.SemaphoreType.DMA((hops,)),
            pltpu.SemaphoreType.DMA((hops,)),
        ]
        + gather_semaphores(sizes, pairs),
        compiler_params=pltpu.CompilerParams(
            collective_id=collective_id, has_side_effects=True, vmem_limit_bytes=VMEM_LIMIT
        ),
        name="head_forward",
    )(rows, table, targets)


def head_backward_kernel(
    sizes,
    pairs,
    own_vocab,
    all_ref,
    table_ref,
    turned_ref,
    target_ref,
    level_ref,
    weight_ref,
    own_ref,
    tgrad_ref,
    full_ref,
    grad_ref,
    *scratch,
):
    meet(line_peers(my_place(sizes), sizes))
    scatter = Scatter(sizes, pairs, full_ref, own_ref, scratch, False)
    groups = sizes["z"] * sizes["y"]
    seqs = sizes["x"] * sizes["core"]
    first_masked, limit = vocab_limit(own_vocab)
    height = table_ref.shape[0]
    block = groups * SPAN

    def seq_grads(pair, seq):
        x, core = divmod(seq, sizes["core"])
        rows_in = all_ref[x, core, :, :, span_rows(pair), :].reshape(block, D)
        logits = masked_logits(table_ref, rows_in, first_masked, limit)
        spot = pl.ds(pair * seqs + seq, 1)
        numbers = lax.broadcasted_iota(jnp.int32, logits.shape, 0)
        share = jnp.exp(logits - level_ref[spot])
        share = jnp.where(numbers == target_ref[spot], share - 1.0, share)
        grad_ref[pair, 0:height, seq * block : (seq + 1) * block] = (
            weight_ref[spot] * share
        ).astype(jnp.bfloat16)

    def row_product(pair):
        turned = matmul(turned_ref[...], grad_ref[pair])
        full_ref[:, :, :, :, span_rows(pair), :] = turned.T.astype(jnp.bfloat16).reshape(
            tuple(sizes[a] for a in NATURAL) + (SPAN, D)
        )

    def table_product(pair):
        rows_in = all_ref[:, :, :, :, span_rows(pair), :].reshape(seqs * block, D)
        return matmul(grad_ref[pair, 0:height], rows_in)

    if grad_ref.shape[1] > height:
        grad_ref[:, height:] = jnp.zeros_like(grad_ref[:, height:])

    def turn_step(turn, carry):
        def older(by, phase):
            pair = turn - by

            @pl.when((pair >= 0) & (pair < pairs))
            def _():
                scatter.advance(pair, phase)

        def compute(act):
            @pl.when(turn < pairs)
            def _():
                act()

        for part in range(4):
            for seq in range(part * seqs // 4, (part + 1) * seqs // 4):
                compute(lambda seq=seq: seq_grads(turn, seq))
            if part == 0:
                older(1, 0)
            elif part == 1:
                older(2, 3)
            elif part == 2:
                older(1, 1)
        compute(lambda: row_product(turn))
        older(1, 2)
        compute(lambda: scatter.launch(turn, 0))
        return carry

    lax.fori_loop(0, pairs, turn_step, 0)
    tgrad_ref[...] = table_product(0)
    scatter.advance(pairs - 1, 0)
    if pairs > 1:
        scatter.advance(pairs - 2, 3)

    def late(pair, carry):
        tgrad_ref[...] += table_product(pair)

        @pl.when(pair < 3)
        def _():
            for phase in (1, 2):

                @pl.when(pair == phase)
                def _(phase=phase):
                    scatter.advance(pairs - 1, phase)

        return carry

    lax.fori_loop(1, pairs, late, 0)
    for phase in range(max(1, pairs), 4):
        if phase < 3:
            scatter.advance(pairs - 1, phase)
    scatter.advance(pairs - 1, 3)
    scatter.finish()


def head_backward(all_rows, table, turned, own_vocab, targets, levels, weights, collective_id):
    sizes = axis_sizes()
    tokens = all_rows.shape[-2]
    pairs = tokens // SPAN
    vmem = pl.BlockSpec(memory_space=pltpu.VMEM)
    block = targets.shape[1]
    seqs = sizes["x"] * sizes["core"]
    return pl.pallas_call(
        functools.partial(head_backward_kernel, sizes, pairs, own_vocab),
        out_shape=(
            jax.ShapeDtypeStruct((tokens, D), jnp.float32),
            jax.ShapeDtypeStruct(table.shape, jnp.float32),
        ),
        in_specs=[vmem] * 6,
        out_specs=(vmem,) * 2,
        scratch_shapes=[
            pltpu.VMEM(all_rows.shape, jnp.bfloat16),
            pltpu.VMEM((pairs, turned.shape[1], seqs * block), jnp.bfloat16),
        ]
        + scatter_scratch(sizes, pairs, D, False),
        compiler_params=pltpu.CompilerParams(
            collective_id=collective_id, has_side_effects=True, vmem_limit_bytes=VMEM_LIMIT
        ),
        name="head_backward",
    )(all_rows, table, turned, targets, levels, weights)


def everyone(devices, groups, me, act):
    def step(by, carry):
        peer = lax.rem(me + by, devices)
        act(by, peer, (lax.div(peer, groups), lax.rem(peer, groups)))
        return carry

    lax.fori_loop(1, devices, step, 0)


def greet_everyone(devices, groups, me):
    barrier = pltpu.get_barrier_semaphore()

    def greet(by, peer, address):
        pl.semaphore_signal(barrier, inc=1, device_id=address, device_id_type=MESH)

    everyone(devices, groups, me, greet)
    pl.semaphore_wait(barrier, devices - 1)


def flat_place():
    groups = lax.axis_size("group")
    return (
        lax.axis_size("seq") * groups,
        groups,
        lax.axis_index("seq") * groups + lax.axis_index("group"),
    )


def share_kernel(own_ref, all_ref, send_sem, recv_sem):
    devices, groups, me = flat_place()
    greet_everyone(devices, groups, me)

    def copy_to(by, address):
        return pltpu.make_async_remote_copy(
            src_ref=own_ref,
            dst_ref=all_ref.at[me],
            send_sem=send_sem.at[by],
            recv_sem=recv_sem.at[by],
            device_id=address,
            device_id_type=MESH,
        )

    everyone(devices, groups, me, lambda by, peer, address: copy_to(by, address).start())
    all_ref[me] = own_ref[...]
    everyone(devices, groups, me, lambda by, peer, address: copy_to(by, address).wait())


def share_small(values, collective_id):
    devices = lax.axis_size("seq") * lax.axis_size("group")
    return pl.pallas_call(
        share_kernel,
        out_shape=jax.ShapeDtypeStruct((devices,) + values.shape, values.dtype),
        in_specs=[pl.BlockSpec(memory_space=pltpu.VMEM)],
        out_specs=pl.BlockSpec(memory_space=pltpu.VMEM),
        scratch_shapes=[
            pltpu.SemaphoreType.DMA((devices,)),
            pltpu.SemaphoreType.DMA((devices,)),
        ],
        compiler_params=pltpu.CompilerParams(collective_id=collective_id, has_side_effects=True),
        name="share_small",
    )(values)


def stats_kernel(parts_ref, all_ref, own_ref, got_ref, mine_ref, send_sem, recv_sem):
    devices, groups, me = flat_place()
    greet_everyone(devices, groups, me)

    def part_to(by, peer, address):
        return pltpu.make_async_remote_copy(
            src_ref=parts_ref.at[peer],
            dst_ref=got_ref.at[me],
            send_sem=send_sem.at[0, by],
            recv_sem=recv_sem.at[0, by],
            device_id=address,
            device_id_type=MESH,
        )

    def total_to(by, address):
        return pltpu.make_async_remote_copy(
            src_ref=mine_ref,
            dst_ref=all_ref.at[me],
            send_sem=send_sem.at[1, by],
            recv_sem=recv_sem.at[1, by],
            device_id=address,
            device_id_type=MESH,
        )

    everyone(devices, groups, me, lambda by, peer, address: part_to(by, peer, address).start())
    got_ref[me] = parts_ref[me]
    everyone(devices, groups, me, lambda by, peer, address: part_to(by, peer, address).wait())
    tops = got_ref[:, 0, :]
    top = jnp.max(tops, axis=0, keepdims=True)
    mass = jnp.sum(got_ref[:, 1, :] * jnp.exp(tops - top), axis=0, keepdims=True)
    hit = jnp.sum(got_ref[:, 2, :], axis=0, keepdims=True)
    level = top + jnp.log(mass)
    mine_ref[...] = jnp.broadcast_to(level, mine_ref.shape)
    everyone(devices, groups, me, lambda by, peer, address: total_to(by, address).start())
    all_ref[me] = mine_ref[...]
    own_ref[...] = jnp.broadcast_to(level - hit, own_ref.shape)
    everyone(devices, groups, me, lambda by, peer, address: total_to(by, address).wait())


def combine_stats(parts, collective_id):
    devices = parts.shape[0]
    shape = parts.shape[1:]
    return pl.pallas_call(
        stats_kernel,
        out_shape=(
            jax.ShapeDtypeStruct(parts.shape, jnp.float32),
            jax.ShapeDtypeStruct(shape, jnp.float32),
        ),
        in_specs=[pl.BlockSpec(memory_space=pltpu.VMEM)],
        out_specs=(pl.BlockSpec(memory_space=pltpu.VMEM),) * 2,
        scratch_shapes=[
            pltpu.VMEM(parts.shape, jnp.float32),
            pltpu.VMEM(shape, jnp.float32),
            pltpu.SemaphoreType.DMA((2, devices)),
            pltpu.SemaphoreType.DMA((2, devices)),
        ],
        compiler_params=pltpu.CompilerParams(collective_id=collective_id, has_side_effects=True),
        name="combine_stats",
    )(parts)


def chain_exchange(rates, total_step, flag, end_state, backwards, out_buf, in_buf, sems):
    devices, me = (lax.axis_size("group"), lax.axis_index("group"))
    seq = lax.axis_index("seq")
    send_sem, recv_sem = sems
    width = rates.shape[1]

    def join(first, second):
        return (
            jnp.exp(second[0] * rates) * second[1] * first[2] + second[2],
            first[0] + second[0],
            first[1] * second[1],
        )

    window = (total_step, flag, end_state)
    before = None
    distance, lap = (1, 0)
    copies = []
    while distance < devices:
        to = lax.rem(me + (devices - distance if backwards else distance), devices)
        out_buf[lap, 0:STATE] = window[2]
        out_buf[lap, STATE : STATE + 8] = jnp.concatenate(
            [
                jnp.broadcast_to(window[0], (4, width)),
                jnp.broadcast_to(window[1], (4, width)),
            ],
            axis=0,
        )
        copy = pltpu.make_async_remote_copy(
            src_ref=out_buf.at[lap],
            dst_ref=in_buf.at[lap],
            send_sem=send_sem.at[lap],
            recv_sem=recv_sem.at[lap],
            device_id=(seq, to),
            device_id_type=MESH,
        )
        copy.start()
        copies.append(copy)
        copy.wait_recv()
        reached = (me + distance < devices) if backwards else (me >= distance)
        real = jnp.where(reached, 1.0, 0.0)
        tail = in_buf[lap, STATE : STATE + 8]
        got = (
            tail[0:1] * real,
            tail[4:5] * real + (1.0 - real),
            in_buf[lap, 0:STATE] * real,
        )
        if before is None:
            before = got
        else:
            merged = join(got, before)
            before = (merged[1], merged[2], merged[0])
        merged = join(got, window)
        window = (merged[1], merged[2], merged[0])
        distance *= 2
        lap += 1
    for copy in copies:
        copy.wait_send()
    if before is None:
        return jnp.zeros_like(end_state)
    return before[2]


def chain_peers():
    devices, me = (lax.axis_size("group"), lax.axis_index("group"))
    seq = lax.axis_index("seq")
    distances = []
    distance = 1
    while distance < devices:
        distances += [distance, devices - distance]
        distance *= 2
    return [(seq, lax.rem(me + by, devices)) for by in sorted(set(distances))]


def chain_laps():
    laps, distance = (0, 1)
    while distance < lax.axis_size("group"):
        laps, distance = (laps + 1, distance * 2)
    return max(1, laps)


def spans(width):
    size = 512 if width % 512 == 0 else width
    return [slice(first, first + size) for first in range(0, width, size)]


def wide(value, copies):
    return jnp.concatenate([value] * copies, axis=1)


def folded(value):
    total = value[:, :LANES]
    for first in range(LANES, value.shape[1], LANES):
        total = total + value[:, first : first + LANES]
    return total


def scan_forward_kernel(*refs):
    meet(chain_peers())
    scan_forward_body(*refs)


def scan_forward_body(
    step_ref, act_ref, b_ref, c_ref, keep_ref, rate_ref, y_ref, in_ref, out_buf, in_buf, ss, rs
):
    tokens, width = step_ref.shape
    ends = []
    for span in spans(width):
        copies = (span.stop - span.start) // LANES
        rates = rate_ref[:, span]

        def advance(block, state, span=span, copies=copies, rates=rates):
            rows = pl.ds(pl.multiple_of(block * 8, 8), 8)
            steps = step_ref[rows, span]
            drives = steps * act_ref[rows, span]
            keeps = wide(keep_ref[rows, :], copies)
            for r in range(8):
                decay = jnp.exp(steps[r : r + 1] * rates) * keeps[r : r + 1]
                state = decay * state + drives[r : r + 1] * wide(b_ref[block * 8 + r], copies)
            return state

        ends.append(
            lax.fori_loop(
                0, tokens // 8, advance, jnp.zeros((STATE, span.stop - span.start), jnp.float32)
            )
        )
    total_step = jnp.sum(step_ref[...], axis=0, keepdims=True)
    flag = wide(jnp.min(keep_ref[...], axis=0, keepdims=True), width // LANES)
    incoming = chain_exchange(
        rate_ref[...],
        total_step,
        flag,
        jnp.concatenate(ends, axis=1),
        False,
        out_buf,
        in_buf,
        (ss, rs),
    )
    in_ref[...] = incoming
    for span in spans(width):
        copies = (span.stop - span.start) // LANES
        rates = rate_ref[:, span]

        def produce(block, state, span=span, copies=copies, rates=rates):
            rows = pl.ds(pl.multiple_of(block * 8, 8), 8)
            steps = step_ref[rows, span]
            drives = steps * act_ref[rows, span]
            keeps = wide(keep_ref[rows, :], copies)
            results = []
            for r in range(8):
                decay = jnp.exp(steps[r : r + 1] * rates) * keeps[r : r + 1]
                state = decay * state + drives[r : r + 1] * wide(b_ref[block * 8 + r], copies)
                results.append(
                    jnp.sum(state * wide(c_ref[block * 8 + r], copies), axis=0, keepdims=True)
                )
            y_ref[rows, span] = jnp.concatenate(results, axis=0)
            return state

        lax.fori_loop(0, tokens // 8, produce, in_ref[:, span])


def scan_scratch(width):
    laps = chain_laps()
    return [
        pltpu.VMEM((laps, STATE + 8, width), jnp.float32),
        pltpu.VMEM((laps, STATE + 8, width), jnp.float32),
        pltpu.SemaphoreType.DMA((laps,)),
        pltpu.SemaphoreType.DMA((laps,)),
    ]


def scan_forward(step, act, b_wide, c_wide, keep_wide, rates, collective_id):
    tokens, width = step.shape
    return pl.pallas_call(
        scan_forward_kernel,
        out_shape=(
            jax.ShapeDtypeStruct((tokens, width), jnp.float32),
            jax.ShapeDtypeStruct((STATE, width), jnp.float32),
        ),
        in_specs=[pl.BlockSpec(memory_space=pltpu.VMEM)] * 6,
        out_specs=(pl.BlockSpec(memory_space=pltpu.VMEM),) * 2,
        scratch_shapes=scan_scratch(width),
        compiler_params=pltpu.CompilerParams(
            collective_id=collective_id, has_side_effects=True, vmem_limit_bytes=VMEM_LIMIT
        ),
        name="scan_forward",
    )(step, act, b_wide, c_wide, keep_wide, rates)


def scan_backward_kernel(*refs):
    meet(chain_peers())
    scan_backward_body(*refs)


def scan_backward_body(
    step_ref,
    act_ref,
    b_ref,
    c_ref,
    keep_ref,
    rate_ref,
    in_ref,
    grad_ref,
    along_ref,
    decayed_ref,
    gb_ref,
    gc_ref,
    grate_ref,
    prev_ref,
    carry_ref,
    out_buf,
    in_buf,
    ss,
    rs,
):
    tokens, width = step_ref.shape
    blocks = tokens // 8
    ends = []
    for number, span in enumerate(spans(width)):
        size = span.stop - span.start
        copies = size // LANES
        rates = rate_ref[:, span]

        def replay(block, state, number=number, span=span, copies=copies, rates=rates):
            rows = pl.ds(pl.multiple_of(block * 8, 8), 8)
            steps = step_ref[rows, span]
            drives = steps * act_ref[rows, span]
            keeps = wide(keep_ref[rows, :], copies)
            grads = grad_ref[rows, span]
            for r in range(8):
                at = block * 8 + r
                prev_ref[at, :, span] = state
                decay = jnp.exp(steps[r : r + 1] * rates) * keeps[r : r + 1]
                state = decay * state + drives[r : r + 1] * wide(b_ref[at], copies)
                share = folded(grads[r : r + 1] * state)
                gc_ref[at] = share if number == 0 else gc_ref[at] + share
            return state

        lax.fori_loop(0, blocks, replay, in_ref[:, span])

        def pull(lap, carry, span=span, copies=copies, rates=rates):
            block = blocks - 1 - lap
            rows = pl.ds(pl.multiple_of(block * 8, 8), 8)
            steps = step_ref[rows, span]
            keeps = wide(keep_ref[rows, :], copies)
            grads = grad_ref[rows, span]
            for r in range(7, -1, -1):
                decay = jnp.exp(steps[r : r + 1] * rates) * keeps[r : r + 1]
                adjoint = grads[r : r + 1] * wide(c_ref[block * 8 + r], copies) + carry
                carry = decay * adjoint
            return carry

        ends.append(lax.fori_loop(0, blocks, pull, jnp.zeros((STATE, size), jnp.float32)))
    total_step = jnp.sum(step_ref[...], axis=0, keepdims=True)
    flag = wide(jnp.min(keep_ref[...], axis=0, keepdims=True), width // LANES)
    carry_ref[...] = chain_exchange(
        rate_ref[...],
        total_step,
        flag,
        jnp.concatenate(ends, axis=1),
        True,
        out_buf,
        in_buf,
        (ss, rs),
    )
    for number, span in enumerate(spans(width)):
        size = span.stop - span.start
        copies = size // LANES
        rates = rate_ref[:, span]

        def settle(lap, carries, number=number, span=span, copies=copies, rates=rates):
            carry, rate_total = carries
            block = blocks - 1 - lap
            rows = pl.ds(pl.multiple_of(block * 8, 8), 8)
            steps = step_ref[rows, span]
            drives = steps * act_ref[rows, span]
            keeps = wide(keep_ref[rows, :], copies)
            grads = grad_ref[rows, span]
            alongs, decays = ([None] * 8, [None] * 8)
            for r in range(7, -1, -1):
                at = block * 8 + r
                decay = jnp.exp(steps[r : r + 1] * rates) * keeps[r : r + 1]
                adjoint = grads[r : r + 1] * wide(c_ref[at], copies) + carry
                carry = decay * adjoint
                grad_exp = carry * prev_ref[at, :, span]
                rate_total = rate_total + grad_exp * steps[r : r + 1]
                alongs[r] = jnp.sum(adjoint * wide(b_ref[at], copies), axis=0, keepdims=True)
                decays[r] = jnp.sum(grad_exp * rates, axis=0, keepdims=True)
                share = folded(adjoint * drives[r : r + 1])
                gb_ref[at] = share if number == 0 else gb_ref[at] + share
            along_ref[rows, span] = jnp.concatenate(alongs, axis=0)
            decayed_ref[rows, span] = jnp.concatenate(decays, axis=0)
            return (carry, rate_total)

        _, rate_total = lax.fori_loop(
            0, blocks, settle, (carry_ref[:, span], jnp.zeros((STATE, size), jnp.float32))
        )
        grate_ref[:, span] = rate_total * rates


def scan_backward(step, act, b_wide, c_wide, keep_wide, rates, incoming, grad, collective_id):
    tokens, width = step.shape
    full = jax.ShapeDtypeStruct((tokens, width), jnp.float32)
    return pl.pallas_call(
        scan_backward_kernel,
        out_shape=(
            full,
            full,
            jax.ShapeDtypeStruct(b_wide.shape, jnp.float32),
            jax.ShapeDtypeStruct(c_wide.shape, jnp.float32),
            jax.ShapeDtypeStruct((STATE, width), jnp.float32),
        ),
        in_specs=[pl.BlockSpec(memory_space=pltpu.VMEM)] * 8,
        out_specs=(pl.BlockSpec(memory_space=pltpu.VMEM),) * 5,
        scratch_shapes=[
            pltpu.VMEM((tokens, STATE, width), jnp.float32),
            pltpu.VMEM((STATE, width), jnp.float32),
        ]
        + scan_scratch(width),
        compiler_params=pltpu.CompilerParams(
            collective_id=collective_id, has_side_effects=True, vmem_limit_bytes=VMEM_LIMIT
        ),
        name="scan_backward",
    )(step, act, b_wide, c_wide, keep_wide, rates, incoming, grad)


def everyone_peer_greeting():
    devices, groups, me = flat_place()
    greet_everyone(devices, groups, me)
    return (devices, groups, me)


def one_hot_turned(ids, height):
    numbers = lax.broadcasted_iota(jnp.int32, (height, ids.shape[1]), 0)
    return (numbers == ids).astype(jnp.float32).astype(jnp.bfloat16)


def start_kernel(
    sizes,
    pairs,
    pack_pairs,
    own_vocab,
    number_ref,
    pack_ref,
    master_ref,
    numbers_ref,
    packs_ref,
    own_ref,
    table_ref,
    turned_ref,
    token_ref,
    target_ref,
    full_ref,
    tall_ref,
    pack_sem,
    send_sem,
    recv_sem,
    *scratch,
):
    place = my_place(sizes)
    meet(line_peers(place, sizes))
    _, groups, me = flat_place()
    seqs = sizes["x"] * sizes["core"]
    gather = Gather(sizes, pack_pairs, pack_ref, packs_ref, scratch[:8])
    scatter = Scatter(sizes, pairs, full_ref, own_ref, scratch[8:], False)
    own_pack = pltpu.make_async_copy(
        pack_ref, packs_ref.at[tuple(place[a] for a in NATURAL)], pack_sem
    )
    own_pack.start()

    number_order = ("z", "y", "x", "core")

    def number_copies(phase):
        axis = number_order[phase]
        block = tuple(
            slice(None) if a in number_order[:phase] else place[a] for a in NATURAL
        )
        return [
            pltpu.make_async_remote_copy(
                src_ref=number_ref if phase == 0 else numbers_ref.at[block],
                dst_ref=numbers_ref.at[block],
                send_sem=send_sem.at[phase, by],
                recv_sem=recv_sem.at[phase, by],
                device_id=device_of(moved(place, axis, by, sizes), sizes),
                device_id_type=MESH,
            )
            for by in range(1, sizes[axis])
        ]

    def numbers_next(phase):
        if phase > 0:
            for copy in number_copies(phase - 1):
                copy.wait_recv()
        if phase < 4:
            for copy in number_copies(phase):
                copy.start()

    def weights(turn):
        for phase in range(4, 0, -1):
            if 0 <= turn + 1 - phase < pack_pairs:
                gather.advance(turn + 1 - phase, phase)

    numbers_next(0)
    for pair in range(pack_pairs):
        gather.advance(pair, 0)
    numbers_ref[tuple(place[a] for a in NATURAL)] = number_ref[...]
    numbers_next(1)
    own_pack.wait()
    whole_tiles = own_vocab // 8 * 8
    tall_ref[whole_tiles:] = jnp.zeros_like(tall_ref[whole_tiles:])
    tall_ref[0:own_vocab] = master_ref[...]
    table_ref[...] = tall_ref[0 : table_ref.shape[0]].astype(jnp.bfloat16)
    for first in range(0, tall_ref.shape[0], LANES):
        turned_ref[:, first : first + LANES] = tall_ref[first : first + LANES].T.astype(
            jnp.bfloat16
        )
    numbers_next(2)

    def look_up(pair, seq):
        x, core = seq_place(seq, sizes)
        found = one_hot_turned(token_ref[pl.ds(pair * seqs + seq, 1)], turned_ref.shape[1])
        rows = matmul(turned_ref[...], found).T.astype(jnp.bfloat16)
        full_ref[x, core, :, :, pl.ds(pair * SPAN, SPAN), :] = rows.reshape(
            sizes["z"], sizes["y"], SPAN, D
        )

    per_tile = LANES // SPAN
    lane = lax.broadcasted_iota(jnp.int32, (2 * seqs, LANES), 1)
    for pair in range(pairs):
        for tile in range(groups // per_tile):
            local = jnp.zeros((2 * seqs, LANES), jnp.int32)
            for part in range(per_tile):
                z, y = divmod(tile * per_tile + part, sizes["y"])
                ids = numbers_ref[place["x"], place["core"], z, y, 0 : 2 * seqs]
                ids = pltpu.roll(ids, (part - pair) * SPAN % LANES, 1)
                local = jnp.where(lane // SPAN == part, ids, local)
            local = local - me * own_vocab
            local = jnp.where(local < own_vocab, local, -1)
            lanes = pl.ds(tile * LANES, LANES)
            token_ref[pair * seqs : (pair + 1) * seqs, lanes] = local[0:seqs]
            target_ref[pair * seqs : (pair + 1) * seqs, lanes] = local[seqs:]

    for turn in range(max(pairs + 4, pack_pairs + 3)):
        if turn < pairs:

            def one(seq, carry, turn=turn):
                look_up(turn, seq)
                return carry

            lax.fori_loop(0, seqs, one, 0)
            scatter.launch(turn, 0)
        for phase in range(3, -1, -1):
            if 0 <= turn - 1 - phase < pairs:
                scatter.advance(turn - 1 - phase, phase)
        weights(turn)
        if turn < 2:
            numbers_next(3 + turn)
    for phase in range(4):
        for copy in number_copies(phase):
            copy.wait_send()
    gather.finish()
    scatter.finish()


def start_all(numbers, pack, master, collective_id):
    sizes = axis_sizes()
    natural = tuple(sizes[a] for a in NATURAL)
    devices = lax.axis_size("seq") * lax.axis_size("group")
    tokens = numbers.shape[1]
    pairs, pack_pairs = (tokens // SPAN, pack.shape[0] // SPAN)
    own_vocab = master.shape[0]
    short, long = (-(-own_vocab // 16) * 16, -(-own_vocab // LANES) * LANES)
    spread = (devices * tokens // (SPAN * lax.axis_size("group")), SPAN * lax.axis_size("group"))
    vmem = pl.BlockSpec(memory_space=pltpu.VMEM)
    return pl.pallas_call(
        functools.partial(start_kernel, sizes, pairs, pack_pairs, own_vocab),
        out_shape=(
            jax.ShapeDtypeStruct(natural + numbers.shape, numbers.dtype),
            jax.ShapeDtypeStruct(natural + pack.shape, pack.dtype),
            jax.ShapeDtypeStruct((tokens, D), jnp.float32),
            jax.ShapeDtypeStruct((short, D), jnp.bfloat16),
            jax.ShapeDtypeStruct((D, long), jnp.bfloat16),
            jax.ShapeDtypeStruct(spread, jnp.int32),
            jax.ShapeDtypeStruct(spread, jnp.int32),
        ),
        in_specs=[vmem] * 3,
        out_specs=(vmem, pl.BlockSpec(memory_space=pl.ANY)) + (vmem,) * 5,
        scratch_shapes=[
            pltpu.VMEM(natural + (tokens, D), jnp.bfloat16),
            pltpu.VMEM((long, D), jnp.float32),
            pltpu.SemaphoreType.DMA,
            pltpu.SemaphoreType.DMA((4, max(sizes.values()))),
            pltpu.SemaphoreType.DMA((4, max(sizes.values()))),
        ]
        + gather_semaphores(sizes, pack_pairs)
        + scatter_scratch(sizes, pairs, D, False),
        compiler_params=pltpu.CompilerParams(
            collective_id=collective_id, has_side_effects=True, vmem_limit_bytes=VMEM_LIMIT
        ),
        name="start_all",
    )(numbers, pack, master)


def finish_kernel(
    sizes,
    pairs,
    pack_pairs,
    own_ref,
    pack_ref,
    token_ref,
    head_ref,
    scalar_ref,
    tgrad_ref,
    quarters_ref,
    sums_ref,
    all_ref,
    found_ref,
    mine_ref,
    ring_ref,
    own_sem,
    quarter_send,
    quarter_recv,
    ring_send,
    ring_recv,
    *scratch,
):
    place = my_place(sizes)
    meet(line_peers(place, sizes))
    seqs = sizes["x"] * sizes["core"]
    groups = sizes["z"] * sizes["y"]
    block = groups * SPAN
    height = head_ref.shape[0]
    gather = Gather(sizes, pairs, own_ref, all_ref, scratch[:8])
    scatter = Scatter(sizes, pack_pairs, pack_ref, mine_ref, scratch[8:], True)
    keep_own = pltpu.make_async_copy(
        own_ref, all_ref.at[tuple(place[a] for a in NATURAL)], own_sem
    )
    keep_own.start()

    def spread_table(pair):
        for seq in range(seqs):
            ids = token_ref[pair * seqs + seq : pair * seqs + seq + 1]
            found_ref[:, seq * block : (seq + 1) * block] = one_hot_turned(ids, height)
        rows = all_ref[:, :, :, :, pl.ds(pair * SPAN, SPAN), :].reshape(seqs * block, D)
        update = matmul(found_ref[...], rows)
        tgrad_ref[...] = (head_ref[...] if pair == 0 else tgrad_ref[...]) + update

    seq = place["x"] * sizes["core"] + place["core"]
    started = []
    x_sent, core_sent = ({}, [])

    def send_quarter(pair, axis, held):
        rows = pl.ds(pair * SPAN, SPAN)
        sent = []
        for by in range(1, sizes[axis]):
            number = len(started)
            copy = pltpu.make_async_remote_copy(
                src_ref=quarters_ref.at[held, rows],
                dst_ref=quarters_ref.at[held, rows],
                send_sem=quarter_send.at[number],
                recv_sem=quarter_recv.at[number],
                device_id=device_of(moved(place, axis, by, sizes), sizes),
                device_id_type=MESH,
            )
            copy.start()
            sent.append(copy)
            started.append(copy)
        return sent

    def own_quarter(pair):
        rows = pl.ds(pair * SPAN, SPAN)
        quarters_ref[seq, rows] = mine_ref[rows].astype(jnp.bfloat16)
        x_sent[pair] = send_quarter(pair, "x", seq)

    def pass_quarter(pair):
        for copy in x_sent[pair]:
            copy.wait_recv()
        for x in range(sizes["x"]):
            core_sent.extend(send_quarter(pair, "core", x * sizes["core"] + place["core"]))

    for pair in range(pack_pairs):
        scatter.launch(pair, 0)
        for kind in range(2):
            scatter.kept(kind, pair).start()
    for turn in range(max(pairs + 4, pack_pairs + 3)):
        if 0 <= turn - 4 < pairs:
            gather.advance(turn - 4, 4)
        for phase in range(3, -1, -1):
            if 0 <= turn - phase < pairs:
                gather.advance(turn - phase, phase)
            if 0 <= turn - phase < pack_pairs:
                scatter.advance(turn - phase, phase)
        if 0 <= turn - 3 < pack_pairs:
            own_quarter(turn - 3)
        if 0 <= turn - 4 < pack_pairs:
            pass_quarter(turn - 4)
        if turn == 0:
            keep_own.wait()
        if 0 <= turn - 4 < pairs:
            spread_table(turn - 4)

    square = jnp.sum(tgrad_ref[...] * tgrad_ref[...]) + jnp.sum(mine_ref[...] * mine_ref[...])
    row = lax.broadcasted_iota(jnp.int32, (8, LANES), 0)
    value = scalar_ref[...] + jnp.where(row < 4, square, 0.0)
    first = 0
    ring_started = []
    last_pair = pack_pairs - 1
    for axis in ("core", "x", "y", "z"):
        ring_ref[first + place[axis]] = value
        sent = []
        for by in range(1, sizes[axis]):
            copy = pltpu.make_async_remote_copy(
                src_ref=ring_ref.at[first + place[axis]],
                dst_ref=ring_ref.at[first + place[axis]],
                send_sem=ring_send.at[first + by],
                recv_sem=ring_recv.at[first + by],
                device_id=device_of(moved(place, axis, by, sizes), sizes),
                device_id_type=MESH,
            )
            copy.start()
            sent.append(copy)
        ring_started.extend(sent)
        if axis == "x" and max(pairs + 4, pack_pairs + 3) <= last_pair + 4:
            pass_quarter(last_pair)
        for copy in sent:
            copy.wait_recv()
        value = ring_ref[first]
        for other in range(1, sizes[axis]):
            value = value + ring_ref[first + other]
        first += sizes[axis]
    sums_ref[...] = value
    for copy in core_sent:
        copy.wait_recv()
    for copy in started + ring_started:
        copy.wait_send()
    gather.finish()
    scatter.finish()


def finish_all(rows, packs, token_rows, head_grad, scalars, collective_id):
    sizes = axis_sizes()
    natural = tuple(sizes[a] for a in NATURAL)
    tokens = rows.shape[0]
    seqs = sizes["x"] * sizes["core"]
    pack_rows, pack_width = packs.shape[-2:]
    pairs, pack_pairs = (tokens // SPAN, pack_rows // SPAN)
    slots = sum(sizes.values())
    quarter_copies = (sizes["x"] - 1) + (sizes["core"] - 1) * sizes["x"]
    quarter_copies = max(1, pack_pairs * quarter_copies)
    vmem = pl.BlockSpec(memory_space=pltpu.VMEM)
    return pl.pallas_call(
        functools.partial(finish_kernel, sizes, pairs, pack_pairs),
        out_shape=(
            jax.ShapeDtypeStruct(head_grad.shape, jnp.float32),
            jax.ShapeDtypeStruct((seqs, pack_rows, pack_width), jnp.bfloat16),
            jax.ShapeDtypeStruct((8, LANES), jnp.float32),
        ),
        in_specs=[vmem, pl.BlockSpec(memory_space=pl.ANY), vmem, vmem, vmem],
        out_specs=(vmem,) * 3,
        scratch_shapes=[
            pltpu.VMEM(natural + rows.shape, jnp.bfloat16),
            pltpu.VMEM((head_grad.shape[0], seqs * token_rows.shape[1]), jnp.bfloat16),
            pltpu.VMEM((pack_rows, pack_width), jnp.float32),
            pltpu.VMEM((slots, 8, LANES), jnp.float32),
            pltpu.SemaphoreType.DMA,
            pltpu.SemaphoreType.DMA((quarter_copies,)),
            pltpu.SemaphoreType.DMA((quarter_copies,)),
            pltpu.SemaphoreType.DMA((slots,)),
            pltpu.SemaphoreType.DMA((slots,)),
        ]
        + gather_semaphores(sizes, pairs)
        + scatter_scratch(sizes, pack_pairs, pack_width, True),
        compiler_params=pltpu.CompilerParams(
            collective_id=collective_id, has_side_effects=True, vmem_limit_bytes=VMEM_LIMIT
        ),
        name="finish_all",
    )(rows, packs.reshape(natural + (pack_rows, pack_width)), token_rows, head_grad, scalars)


def side_lanes(router, gain_columns):
    first = gain_columns[:, :1]
    rest = gain_columns[:, 1:]
    gap = LANES - SIDE_LANE - router.shape[1] - gain_columns.shape[1]
    return jnp.concatenate([jnp.pad(router, ((0, 0), (SIDE_LANE, gap))), rest, first], axis=1)


def row_tiles(values):
    return values.reshape(-1, 16, LANES).transpose(1, 0, 2).reshape(16, -1)


def own_pack_of(parts, seq_index, seq_count):
    mixer_in, mixer_x, mixer_out, channel, gains, router = [
        part.astype(jnp.bfloat16) for part in parts
    ]
    rows = mixer_x.shape[0] // seq_count
    some = mixer_in.shape[0] // seq_count
    top = lax.dynamic_slice_in_dim(mixer_in, seq_index * D, D, 1)
    middle = lax.dynamic_slice_in_dim(mixer_out, seq_index * rows, rows, 0)
    x_rows = lax.dynamic_slice_in_dim(mixer_x, seq_index * rows, rows, 0)
    extra = lax.dynamic_slice_in_dim(channel, seq_index * rows, rows, 1).T
    extra = jnp.pad(extra, ((0, 0), (0, LANES - extra.shape[1])))
    sides = lax.dynamic_slice_in_dim(
        side_lanes(router, gains.T), seq_index * some, some, 0
    )
    extra = extra + jnp.pad(sides, ((0, rows - some), (0, 0)))
    bottom = jnp.concatenate([row_tiles(x_rows), row_tiles(extra)], axis=1)
    return jnp.concatenate([top, middle, bottom])


def small_weights(packs, experts_total):
    tall, rows = pack_heights()
    seqs, groups = packs.shape[:2]
    extra = packs[:, :, tall + rows :, D // 2 :].reshape(seqs, groups, 16, rows // 16, LANES)
    extra = extra.transpose(1, 0, 3, 2, 4).reshape(groups, seqs, rows, LANES)
    channel = extra.reshape(-1, LANES)[:, : CONV + 3 + STATE].T
    sides = extra[:, :, : tall // seqs].reshape(D, LANES)
    gains = jnp.concatenate([sides[:, -1:], sides[:, -3:-1]], axis=1).T
    router = sides[:, SIDE_LANE : SIDE_LANE + experts_total]
    return (channel.astype(jnp.float32), gains.astype(jnp.float32), router)


def log_sum(value):
    return jnp.maximum(value, 0.0) + jnp.log1p(jnp.exp(-jnp.abs(value)))


def pack_heights():
    seqs, groups = (lax.axis_size("seq"), lax.axis_size("group"))
    return (D // groups, DI // (seqs * groups))


def collect_middle(packs_ref, outx_ref):
    seqs, groups = packs_ref.shape[:2]
    tall, rows = pack_heights()

    def one(step, carry):
        group, seq = (lax.div(step, seqs), lax.rem(step, seqs))
        start = step * rows
        outx_ref[pl.ds(pl.multiple_of(start, 16), rows), 0:D] = packs_ref[
            seq, group, tall : tall + rows
        ]
        for part in range(rows // 16):
            outx_ref[pl.ds(pl.multiple_of(start + part * 16, 16), 16), D:] = packs_ref[
                seq, group, tall + rows :, part * LANES : (part + 1) * LANES
            ]
        return carry

    lax.fori_loop(0, seqs * groups, one, 0)


def turned_step_weights(outx_ref):
    both = outx_ref[:, D:].astype(jnp.float32)
    lane = lax.broadcasted_iota(jnp.int32, both.shape, 1)
    shifted = pltpu.roll(both, RANK, 1)
    return jnp.where(lane < RANK, shifted, 0.0).astype(jnp.bfloat16)


def mixer_forward_kernel(
    experts_total,
    x_ref,
    packs_ref,
    vec_ref,
    gain_ref,
    mask_ref,
    router_ref,
    mixed_ref,
    moe_ref,
    prob_ref,
    z_ref,
    pad_ref,
    conv_ref,
    act_ref,
    dtin_ref,
    dtpre_ref,
    step_ref,
    b_ref,
    c_ref,
    in_ref,
    y_ref,
    outx_ref,
    keep_ref,
    rate_ref,
    halo_out,
    halo_in,
    out_buf,
    in_buf,
    ss,
    rs,
    halo_send,
    halo_recv,
):
    meet(chain_peers())
    seqs, groups = packs_ref.shape[:2]
    tall, _ = pack_heights()
    me = lax.axis_index("group")
    x = x_ref[...]
    tokens = x.shape[0]
    normed = (x * inverse_rms(x) * gain_ref[0:1]).astype(jnp.bfloat16)
    for seq in range(seqs):
        block = matmul(normed, packs_ref[seq, :, 0:tall, 0:D].reshape(D, D))
        first = seq * D
        if first < DI:
            pad_ref[8:, first : first + D] = block.astype(jnp.bfloat16).astype(jnp.float32)
        else:
            z_ref[:, first - DI : first - DI + D] = block
    halo_out[...] = pad_ref[tokens:]
    halo = pltpu.make_async_remote_copy(
        src_ref=halo_out,
        dst_ref=halo_in,
        send_sem=halo_send,
        recv_sem=halo_recv,
        device_id=(lax.axis_index("seq"), lax.rem(me + 1, groups)),
        device_id_type=MESH,
    )
    halo.start()
    collect_middle(packs_ref, outx_ref)
    rate_ref[...] = -jnp.exp(vec_ref[CONV + 3 : CONV + 3 + STATE])
    keep_ref[...] = jnp.broadcast_to(mask_ref[:, CONV : CONV + 1], keep_ref.shape)
    halo.wait_recv()
    pad_ref[0:8] = halo_in[...] * jnp.where(me > 0, 1.0, 0.0)
    conv = vec_ref[CONV : CONV + 1] + jnp.zeros_like(z_ref)
    for tap in range(CONV):
        first = 9 - CONV + tap
        conv = (
            conv
            + vec_ref[tap : tap + 1]
            * pad_ref[first : first + tokens]
            * mask_ref[:, tap : tap + 1]
        )
    activated = conv * jax.nn.sigmoid(conv)
    conv_ref[...] = conv
    act_ref[...] = activated
    projected = matmul(activated.astype(jnp.bfloat16), outx_ref[:, D:])
    lane = lax.broadcasted_iota(jnp.int32, projected.shape, 1)
    dt_input = jnp.where(lane < RANK, projected, 0.0).astype(jnp.bfloat16)
    dtin_ref[...] = dt_input
    dt_pre = matmul_nt(dt_input, turned_step_weights(outx_ref))
    dtpre_ref[...] = dt_pre
    step_ref[...] = log_sum(dt_pre + vec_ref[CONV + 1 : CONV + 2])
    for n in range(STATE):
        at = RANK + n
        b_ref[:, n, :] = jnp.broadcast_to(projected[:, at : at + 1], (tokens, LANES))
        at = RANK + STATE + n
        c_ref[:, n, :] = jnp.broadcast_to(projected[:, at : at + 1], (tokens, LANES))
    scan_forward_body(
        step_ref,
        act_ref,
        b_ref,
        c_ref,
        keep_ref,
        rate_ref,
        y_ref,
        in_ref,
        out_buf,
        in_buf,
        ss,
        rs,
    )
    scanned = y_ref[...] + vec_ref[CONV + 2 : CONV + 3] * act_ref[...]
    y_ref[...] = scanned
    gate_z = z_ref[...]
    gated = (scanned * (gate_z * jax.nn.sigmoid(gate_z))).astype(jnp.bfloat16)
    mixed = x + matmul(gated, outx_ref[:, :D])
    mixed_ref[...] = mixed
    moe_in = (mixed * inverse_rms(mixed) * gain_ref[1:2]).astype(jnp.bfloat16)
    moe_ref[...] = moe_in
    scores = matmul(moe_in, router_ref[...])
    scores = jnp.where(lane < experts_total, scores, -1e30)
    raised = jnp.exp(scores - jnp.max(scores, axis=1, keepdims=True))
    prob_ref[...] = raised / jnp.sum(raised, axis=1, keepdims=True)
    halo.wait_send()


def mixer_forward_all(x, packs, vectors, gains, masks, router, collective_id):
    tokens = x.shape[0]
    wide_shape = jax.ShapeDtypeStruct((tokens, DI), jnp.float32)
    state_shape = jax.ShapeDtypeStruct((tokens, STATE, LANES), jnp.float32)
    vmem = pl.BlockSpec(memory_space=pltpu.VMEM)
    return pl.pallas_call(
        functools.partial(mixer_forward_kernel, router.shape[1]),
        out_shape=(
            jax.ShapeDtypeStruct((tokens, D), jnp.float32),
            jax.ShapeDtypeStruct((tokens, D), jnp.bfloat16),
            jax.ShapeDtypeStruct((tokens, LANES), jnp.float32),
            wide_shape,
            jax.ShapeDtypeStruct((tokens + 8, DI), jnp.float32),
            wide_shape,
            wide_shape,
            jax.ShapeDtypeStruct((tokens, LANES), jnp.bfloat16),
            wide_shape,
            wide_shape,
            state_shape,
            state_shape,
            jax.ShapeDtypeStruct((STATE, DI), jnp.float32),
            wide_shape,
        ),
        in_specs=[vmem] * 6,
        out_specs=(vmem,) * 14,
        scratch_shapes=[
            pltpu.VMEM((DI, D + LANES), jnp.bfloat16),
            pltpu.VMEM((tokens, LANES), jnp.float32),
            pltpu.VMEM((STATE, DI), jnp.float32),
            pltpu.VMEM((8, DI), jnp.float32),
            pltpu.VMEM((8, DI), jnp.float32),
        ]
        + scan_scratch(DI)
        + [pltpu.SemaphoreType.DMA, pltpu.SemaphoreType.DMA],
        compiler_params=pltpu.CompilerParams(
            collective_id=collective_id, has_side_effects=True, vmem_limit_bytes=VMEM_LIMIT
        ),
        name="mixer_forward",
    )(x, packs, vectors, gains, masks, jnp.pad(router, ((0, 0), (0, LANES - router.shape[1]))))


def mixer_backward_kernel(
    grad_ref,
    side_ref,
    x_ref,
    packs_ref,
    vec_ref,
    gain_ref,
    mask_ref,
    z_ref,
    pad_ref,
    conv_ref,
    act_ref,
    dtin_ref,
    dtpre_ref,
    step_ref,
    b_ref,
    c_ref,
    in_ref,
    y_ref,
    embed_ref,
    gpack_ref,
    outx_ref,
    keep_ref,
    rate_ref,
    scan_grad_ref,
    along_ref,
    decayed_ref,
    gb_ref,
    gc_ref,
    grate_ref,
    prev_ref,
    carry_ref,
    gout_ref,
    both_ref,
    gpad_ref,
    chan_ref,
    turned_ref,
    merged_ref,
    halo_out,
    halo_in,
    out_buf,
    in_buf,
    ss,
    rs,
    halo_send,
    halo_recv,
):
    meet(chain_peers())
    seqs, groups = packs_ref.shape[:2]
    tall, rows = pack_heights()
    me = lax.axis_index("group")
    tokens = x_ref.shape[0]
    collect_middle(packs_ref, outx_ref)
    rate_ref[...] = -jnp.exp(vec_ref[CONV + 3 : CONV + 3 + STATE])
    keep_ref[...] = jnp.broadcast_to(mask_ref[:, CONV : CONV + 1], keep_ref.shape)
    grad_low = grad_ref[...].astype(jnp.bfloat16)
    grad_gated = matmul_nt(grad_low, outx_ref[:, :D])
    gate_z, scanned = (z_ref[...], y_ref[...])
    logistic = jax.nn.sigmoid(gate_z)
    gate_act = gate_z * logistic
    gated = (scanned * gate_act).astype(jnp.bfloat16)
    gout_ref[:, :D] = matmul_tn(gated, grad_low).astype(jnp.bfloat16)
    grad_scan = grad_gated * gate_act
    scan_grad_ref[...] = grad_scan
    grad_z = grad_gated * scanned * (logistic * (1.0 + gate_z * (1.0 - logistic)))
    both_ref[:, DI:] = grad_z.astype(jnp.bfloat16)
    chan_ref[...] = jnp.zeros_like(chan_ref)
    chan_ref[CONV + 2 : CONV + 3] = jnp.sum(grad_scan * act_ref[...], axis=0, keepdims=True)
    scan_backward_body(
        step_ref,
        act_ref,
        b_ref,
        c_ref,
        keep_ref,
        rate_ref,
        in_ref,
        scan_grad_ref,
        along_ref,
        decayed_ref,
        gb_ref,
        gc_ref,
        grate_ref,
        prev_ref,
        carry_ref,
        out_buf,
        in_buf,
        ss,
        rs,
    )
    chan_ref[CONV + 3 : CONV + 3 + STATE] = grate_ref[...]
    along, activated = (along_ref[...], act_ref[...])
    grad_act = scan_grad_ref[...] * vec_ref[CONV + 2 : CONV + 3] + along * step_ref[...]
    grad_step = decayed_ref[...] + along * activated
    grad_dtpre = grad_step * jax.nn.sigmoid(dtpre_ref[...] + vec_ref[CONV + 1 : CONV + 2])
    chan_ref[CONV + 1 : CONV + 2] = jnp.sum(grad_dtpre, axis=0, keepdims=True)
    grad_dtlow = grad_dtpre.astype(jnp.bfloat16)
    grad_wdt = matmul_tn(grad_dtlow, dtin_ref[...])
    grad_proj = matmul(grad_dtlow, turned_step_weights(outx_ref))
    lane = lax.broadcasted_iota(jnp.int32, grad_proj.shape, 1)
    for n in range(STATE):
        for first, ref in ((RANK, gb_ref), (RANK + STATE, gc_ref)):
            column = jnp.sum(ref[:, n, :], axis=1, keepdims=True)
            grad_proj = jnp.where(lane == first + n, column, grad_proj)
    grad_proj = grad_proj.astype(jnp.bfloat16)
    grad_wx = matmul_tn(activated.astype(jnp.bfloat16), grad_proj)
    wide_lane = lax.broadcasted_iota(jnp.int32, grad_wx.shape, 1)
    grad_wx = jnp.where(
        wide_lane < RANK + 2 * STATE, grad_wx, pltpu.roll(grad_wdt, RANK + 2 * STATE, 1)
    )
    gout_ref[:, D:] = grad_wx.astype(jnp.bfloat16)
    grad_act = grad_act + matmul_nt(grad_proj, outx_ref[:, D:])
    conv = conv_ref[...]
    logistic = jax.nn.sigmoid(conv)
    grad_conv = grad_act * (logistic * (1.0 + conv * (1.0 - logistic)))
    chan_ref[CONV : CONV + 1] = jnp.sum(grad_conv, axis=0, keepdims=True)
    gpad_ref[...] = jnp.zeros_like(gpad_ref)
    for tap in range(CONV):
        same = grad_conv * mask_ref[:, tap : tap + 1]
        first = 9 - CONV + tap
        chan_ref[tap : tap + 1] = jnp.sum(
            same * pad_ref[first : first + tokens], axis=0, keepdims=True
        )
        gpad_ref[first : first + tokens] += vec_ref[tap : tap + 1] * same
    halo_out[...] = gpad_ref[0:8]
    halo = pltpu.make_async_remote_copy(
        src_ref=halo_out,
        dst_ref=halo_in,
        send_sem=halo_send,
        recv_sem=halo_recv,
        device_id=(lax.axis_index("seq"), lax.rem(me + groups - 1, groups)),
        device_id_type=MESH,
    )
    halo.start()
    for first in range(0, DI, LANES):
        turned_ref[first : first + LANES] = chan_ref[:, first : first + LANES].T

    def place_middle(step, carry):
        group, seq = (lax.div(step, seqs), lax.rem(step, seqs))
        start = step * rows
        gpack_ref[seq, group, tall : tall + rows] = gout_ref[
            pl.ds(pl.multiple_of(start, 16), rows), 0:D
        ]
        for part in range(rows // 16):
            gpack_ref[seq, group, tall + rows :, part * LANES : (part + 1) * LANES] = gout_ref[
                pl.ds(pl.multiple_of(start + part * 16, 16), 16), D:
            ]
        return carry

    lax.fori_loop(0, seqs * groups, place_middle, 0)
    halo.wait_recv()
    gpad_ref[tokens : tokens + 8] += halo_in[...] * jnp.where(me < groups - 1, 1.0, 0.0)
    both_ref[:, :DI] = gpad_ref[8 : 8 + tokens].astype(jnp.bfloat16)
    x = x_ref[...]
    scale = inverse_rms(x)
    normed = (x * scale * gain_ref[0:1]).astype(jnp.bfloat16)
    grad_normed = jnp.zeros((tokens, D), jnp.float32)
    for seq in range(seqs):
        part = both_ref[:, seq * D : (seq + 1) * D]
        grad_normed += matmul_nt(part, packs_ref[seq, :, 0:tall, 0:D].reshape(D, D))
        gpack_ref[seq, :, 0:tall, 0:D] = (
            matmul_tn(normed, part).astype(jnp.bfloat16).reshape(groups, tall, D)
        )
    scaled = grad_normed * gain_ref[0:1]
    grad_x = scale * scaled - x * scale**3 * jnp.mean(scaled * x, axis=-1, keepdims=True)
    embed_ref[...] = (grad_ref[...] + grad_x).astype(jnp.bfloat16)
    grad_gain = jnp.sum(grad_normed * x * scale, axis=0, keepdims=True)
    grad_gain = jnp.broadcast_to(grad_gain, (LANES, D)).T
    side_lane = lax.broadcasted_iota(jnp.int32, side_ref.shape, 1)
    merged_ref[...] = jnp.where(side_lane == LANES - 1, grad_gain, side_ref[...])
    some = tall // seqs

    def place_extra(step, carry):
        group, seq = (lax.div(step, seqs), lax.rem(step, seqs))
        start = pl.multiple_of(step * rows, 16)
        first = pl.multiple_of(group * tall + seq * some, 8)
        turned_ref[pl.ds(start, some)] += merged_ref[pl.ds(first, some)]
        for part in range(rows // 16):
            lanes = pl.ds(D // 2 + part * LANES, LANES)
            gpack_ref[seq, group, tall + rows :, lanes] = turned_ref[
                pl.ds(pl.multiple_of(start + part * 16, 16), 16)
            ].astype(jnp.bfloat16)
        return carry

    lax.fori_loop(0, seqs * groups, place_extra, 0)
    halo.wait_send()


def mixer_backward_all(grad, sides, x, packs, vectors, gains, masks, saved, collective_id):
    tokens = x.shape[0]
    vmem = pl.BlockSpec(memory_space=pltpu.VMEM)
    wide = (tokens, DI)
    return pl.pallas_call(
        mixer_backward_kernel,
        out_shape=(
            jax.ShapeDtypeStruct((tokens, D), jnp.bfloat16),
            jax.ShapeDtypeStruct(packs.shape, jnp.bfloat16),
        ),
        in_specs=[vmem] * (7 + len(saved)),
        out_specs=(vmem,) * 2,
        scratch_shapes=[
            pltpu.VMEM((DI, D + LANES), jnp.bfloat16),
            pltpu.VMEM((tokens, LANES), jnp.float32),
            pltpu.VMEM((STATE, DI), jnp.float32),
            pltpu.VMEM(wide, jnp.float32),
            pltpu.VMEM(wide, jnp.float32),
            pltpu.VMEM(wide, jnp.float32),
            pltpu.VMEM((tokens, STATE, LANES), jnp.float32),
            pltpu.VMEM((tokens, STATE, LANES), jnp.float32),
            pltpu.VMEM((STATE, DI), jnp.float32),
            pltpu.VMEM((tokens, STATE, DI), jnp.float32),
            pltpu.VMEM((STATE, DI), jnp.float32),
            pltpu.VMEM((DI, D + LANES), jnp.bfloat16),
            pltpu.VMEM((tokens, 2 * DI), jnp.bfloat16),
            pltpu.VMEM((tokens + 8, DI), jnp.float32),
            pltpu.VMEM((LANES, DI), jnp.float32),
            pltpu.VMEM((DI, LANES), jnp.float32),
            pltpu.VMEM((D, LANES), jnp.float32),
            pltpu.VMEM((8, DI), jnp.float32),
            pltpu.VMEM((8, DI), jnp.float32),
        ]
        + scan_scratch(DI)
        + [pltpu.SemaphoreType.DMA, pltpu.SemaphoreType.DMA],
        compiler_params=pltpu.CompilerParams(
            collective_id=collective_id, has_side_effects=True, vmem_limit_bytes=VMEM_LIMIT
        ),
        name="mixer_backward",
    )(grad, sides, x, packs, vectors, gains, masks, *saved)


def update_kernel(quarters_ref, sums_ref, *refs):
    inputs, outputs, turned_ref, side_ref = (refs[:18], refs[18:36], refs[36], refs[37])
    seqs = quarters_ref.shape[0]
    tall, rows = pack_heights()
    norm = jnp.sqrt(sums_ref[0:1, 0:1])
    clip_factor = jnp.minimum(1.0, CLIP / (norm + 1e-06))

    def renew(which, index, gradient, rate):
        master, moment, average = (inputs[3 * which + k] for k in range(3))
        fresh = renewed(
            master[index], moment[index], average[index], gradient, clip_factor, rate
        )
        for k in range(3):
            outputs[3 * which + k][index] = fresh[k]

    for seq in range(seqs):
        columns = slice(seq * D, (seq + 1) * D)
        renew(0, (slice(None), columns), quarters_ref[seq, 0:tall, :D].astype(jnp.float32), LRATE)
        own = slice(seq * rows, (seq + 1) * rows)
        middle = quarters_ref[seq, tall : tall + rows, :].astype(jnp.float32)
        renew(2, (own,), middle, LRATE)
        bottom = quarters_ref[seq, tall + rows :, :].astype(jnp.float32)
        for part in range(rows // 16):
            first = seq * rows + part * 16
            lanes = slice(part * LANES, (part + 1) * LANES)
            renew(1, (slice(first, first + 16),), bottom[:, lanes], LRATE)
            lanes = slice(D // 2 + part * LANES, D // 2 + (part + 1) * LANES)
            turned_ref[first : first + 16] = bottom[:, lanes]
        some = tall // seqs
        side_ref[seq * some : (seq + 1) * some] = turned_ref[seq * rows : seq * rows + some]
    width = inputs[9].shape[1]
    turned_ref[seqs * rows :] = jnp.zeros_like(turned_ref[seqs * rows :])
    side_ref[tall:] = jnp.zeros_like(side_ref[tall:])
    everything = (slice(None),)
    renew(3, everything, turned_ref[...].T[0 : CONV + 3 + STATE, 0:width], CHANNEL_LRATE)
    gains = side_ref[...].T[:, 0:tall]
    renew(4, everything, jnp.concatenate([gains[-1:], gains[-3:-1]], axis=0), LRATE)
    router_lanes = slice(SIDE_LANE, SIDE_LANE + inputs[15].shape[1])
    renew(5, everything, side_ref[0:tall, router_lanes], LRATE)


def update_all(quarters, sums, states):
    vmem = pl.BlockSpec(memory_space=pltpu.VMEM)
    flat = [part for state in states for part in state]
    tall, rows = pack_heights()
    height = -(-quarters.shape[0] * rows // LANES) * LANES
    return pl.pallas_call(
        update_kernel,
        out_shape=tuple(jax.ShapeDtypeStruct(part.shape, part.dtype) for part in flat),
        in_specs=[vmem] * (2 + len(flat)),
        out_specs=(vmem,) * len(flat),
        scratch_shapes=[
            pltpu.VMEM((height, LANES), jnp.float32),
            pltpu.VMEM((-(-tall // LANES) * LANES, LANES), jnp.float32),
        ],
        compiler_params=pltpu.CompilerParams(vmem_limit_bytes=VMEM_LIMIT),
        name="update_all",
    )(quarters, sums, *flat)


def from_behind(value, axis, by):
    devices = lax.axis_size(axis)
    pairs = [(i, i + by) for i in range(devices) if 0 <= i + by < devices]
    return lax.ppermute(value, axis, pairs)


def matmul(left, right):
    return jnp.dot(left, right, preferred_element_type=jnp.float32)


def matmul_nt(left, right):
    return lax.dot_general(
        left, right, (((1,), (1,)), ((), ())), preferred_element_type=jnp.float32
    )


def matmul_tn(left, right):
    return lax.dot_general(
        left, right, (((0,), (0,)), ((), ())), preferred_element_type=jnp.float32
    )


def silu_slope(preact):
    logistic = jax.nn.sigmoid(preact)
    return logistic * (1.0 + preact * (1.0 - logistic))


def inverse_rms(values):
    return lax.rsqrt(jnp.mean(values * values, axis=-1, keepdims=True) + EPS)


def norm_back(values, inv_scale, gain_row, grad_in):
    scaled = grad_in * gain_row
    grad_gain = jnp.sum(grad_in * values * inv_scale, axis=0)
    grad_values = inv_scale * scaled - values * inv_scale**3 * jnp.mean(
        scaled * values, axis=-1, keepdims=True
    )
    return (grad_values, grad_gain)


def neighbour_rows(edge_rows, offset):
    return from_behind(edge_rows, "group", offset)


def doc_layout(doc_lengths, first_pos, span_len):
    doc_ends = jnp.cumsum(doc_lengths, axis=1)
    doc_begins = doc_ends - doc_lengths
    where_at = first_pos + jnp.arange(span_len, dtype=jnp.int32)
    segment = jnp.sum((where_at[None, :, None] >= doc_ends[:, None, :]).astype(jnp.int32), axis=2)
    onehot_doc = (
        segment[:, :, None] == jnp.arange(doc_lengths.shape[1], dtype=jnp.int32)[None, None, :]
    ).astype(jnp.float32)
    weight = jnp.sum(onehot_doc / doc_lengths[:, None, :].astype(jnp.float32), axis=2)
    starting = jnp.sum(
        (where_at[None, :, None] == doc_begins[:, None, :]).astype(jnp.float32), axis=2
    )
    return (segment, weight, 1.0 - starting)


def spread_weights(doc_lengths, tokens, groups):
    ends = jnp.cumsum(doc_lengths, axis=1)
    begins = ends - doc_lengths
    shape = (tokens // SPAN, groups * SPAN)
    pair, lane = (lax.broadcasted_iota(jnp.int32, shape, axis) for axis in range(2))
    where_at = (lane // SPAN * tokens + pair * SPAN + lane % SPAN)[:, None, :]
    total = jnp.zeros((shape[0], doc_lengths.shape[0], shape[1]), jnp.float32)
    for doc in range(doc_lengths.shape[1]):
        inside = (where_at >= begins[None, :, doc, None]) & (where_at < ends[None, :, doc, None])
        share = 1.0 / doc_lengths[:, doc].astype(jnp.float32)
        total = total + jnp.where(inside, share[None, :, None], 0.0)
    return total.reshape(-1, shape[1])


def lane_copies(columns):
    return jnp.broadcast_to(columns[..., None], columns.shape + (LANES,))


def mixer_forward(embedded, segment, keeping, weight_in, weight_x, weight_out, channel, gain_row):
    tokens = embedded.shape[0]
    scale_in = inverse_rms(embedded)
    normed = (embedded * scale_in * gain_row).astype(jnp.bfloat16)
    projected_in = matmul(normed, weight_in)
    conv_input = projected_in[:, :DI].astype(jnp.bfloat16)
    gate_z = projected_in[:, DI:]
    rim_rows = neighbour_rows(conv_input[tokens - CONV + 1 :].astype(jnp.float32), 1)
    padded = jnp.concatenate([rim_rows, conv_input.astype(jnp.float32)])
    same_doc = [
        (segment[conv_tap : conv_tap + tokens] == segment[CONV - 1 :]).astype(jnp.float32)[:, None]
        for conv_tap in range(CONV)
    ]
    conv_out = channel[CONV] + jnp.zeros_like(padded[CONV - 1 :])
    for conv_tap in range(CONV):
        conv_out = (
            conv_out + channel[conv_tap] * padded[conv_tap : conv_tap + tokens] * same_doc[conv_tap]
        )
    activated = jax.nn.silu(conv_out)
    act_low = activated.astype(jnp.bfloat16)
    projected = matmul(act_low, weight_x[:, : RANK + 2 * STATE])
    dt_input = projected[:, :RANK].astype(jnp.bfloat16)
    dt_pre = matmul_nt(dt_input, weight_x[:, RANK + 2 * STATE :])
    step_size = jax.nn.softplus(dt_pre + channel[CONV + 1])
    decay_rates = -jnp.exp(channel[CONV + 3 :])
    b_wide = lane_copies(projected[:, RANK : RANK + STATE])
    c_wide = lane_copies(projected[:, RANK + STATE :])
    keep_wide = lane_copies(keeping)
    reached, incoming = scan_forward(
        step_size, activated, b_wide, c_wide, keep_wide, decay_rates, 4
    )
    scanned = reached + channel[CONV + 2] * activated
    gate_act = jax.nn.silu(gate_z)
    gated = (scanned * gate_act).astype(jnp.bfloat16)
    mixed_out = embedded + matmul(gated, weight_out)
    kept_values = (
        scale_in,
        normed,
        gate_z,
        padded,
        same_doc,
        conv_out,
        activated,
        act_low,
        b_wide,
        c_wide,
        keep_wide,
        dt_input,
        dt_pre,
        step_size,
        decay_rates,
        incoming,
        scanned,
        gate_act,
        gated,
    )
    return (mixed_out, kept_values)


def mixer_backward(
    grad_out, embedded, kept_values, weight_in, weight_x, weight_out, channel, gain_row
):
    (
        scale_in,
        normed,
        gate_z,
        padded,
        same_doc,
        conv_out,
        activated,
        act_low,
        b_wide,
        c_wide,
        keep_wide,
        dt_input,
        dt_pre,
        step_size,
        decay_rates,
        incoming,
        scanned,
        gate_act,
        gated,
    ) = kept_values
    tokens = embedded.shape[0]
    grad_low = grad_out.astype(jnp.bfloat16)
    grad_wout = matmul_tn(gated, grad_low)
    grad_gated = matmul_nt(grad_low, weight_out)
    grad_scan = grad_gated * gate_act
    grad_z = grad_gated * scanned * silu_slope(gate_z)
    grad_skip = jnp.sum(grad_scan * activated, axis=0)
    along_b, decayed, wide_gb, wide_gc, grad_rates_log = scan_backward(
        step_size, activated, b_wide, c_wide, keep_wide, decay_rates, incoming, grad_scan, 5
    )
    grad_b = jnp.sum(wide_gb, axis=2)
    grad_c = jnp.sum(wide_gc, axis=2)
    grad_act = grad_scan * channel[CONV + 2] + along_b * step_size
    grad_step = decayed + along_b * activated
    grad_dtpre = grad_step * jax.nn.sigmoid(dt_pre + channel[CONV + 1])
    grad_dtbias = jnp.sum(grad_dtpre, axis=0)
    grad_dtlow = grad_dtpre.astype(jnp.bfloat16)
    grad_wdt = matmul_tn(grad_dtlow, dt_input)
    grad_dtin = matmul(grad_dtlow, weight_x[:, RANK + 2 * STATE :])
    grad_proj = jnp.concatenate([grad_dtin, grad_b, grad_c], axis=1).astype(jnp.bfloat16)
    grad_wx = jnp.concatenate([matmul_tn(act_low, grad_proj), grad_wdt], axis=1)
    grad_act = grad_act + matmul_nt(grad_proj, weight_x[:, : RANK + 2 * STATE])
    grad_conv = grad_act * silu_slope(conv_out)
    grad_taps = [
        jnp.sum(grad_conv * padded[conv_tap : conv_tap + tokens] * same_doc[conv_tap], axis=0)
        for conv_tap in range(CONV)
    ]
    grad_padded = sum(
        (
            jnp.pad(
                channel[conv_tap] * grad_conv * same_doc[conv_tap],
                ((conv_tap, CONV - 1 - conv_tap), (0, 0)),
            )
            for conv_tap in range(CONV)
        )
    )
    from_next = neighbour_rows(grad_padded[: CONV - 1], -1)
    grad_input = grad_padded[CONV - 1 :] + jnp.pad(from_next, ((tokens - CONV + 1, 0), (0, 0)))
    grad_both = jnp.concatenate([grad_input, grad_z], axis=1).astype(jnp.bfloat16)
    grad_win = matmul_tn(normed, grad_both)
    grad_normed = matmul_nt(grad_both, weight_in)
    grad_embed, grad_gain = norm_back(embedded, scale_in, gain_row, grad_normed)
    grad_channel = jnp.concatenate(
        [
            jnp.stack(grad_taps),
            jnp.sum(grad_conv, axis=0)[None],
            grad_dtbias[None],
            grad_skip[None],
            grad_rates_log,
        ]
    )
    return (grad_out + grad_embed, grad_win, grad_wx, grad_wout, grad_channel, grad_gain)


def choice_of(route_flat, experts_total):
    return (route_flat[:, None] == jnp.arange(experts_total, dtype=jnp.int32)[None, :]).astype(
        jnp.float32
    )


def dispatch_table(routes, first_expert, experts_here, capacity):
    tokens = routes.shape[1]
    chosen = (
        routes[:, :, None] == first_expert + jnp.arange(experts_here, dtype=jnp.int32)
    ).astype(jnp.float32)
    earlier = jnp.cumsum(chosen, axis=1) - chosen
    rank = jnp.sum(earlier * chosen, axis=2).astype(jnp.int32)
    local = routes - first_expert
    slot = jnp.where((local >= 0) & (local < experts_here), local * capacity + rank, -1)
    return (
        slot[:, None, :] == jnp.arange(experts_here * capacity, dtype=jnp.int32)[None, :, None]
    ).astype(jnp.bfloat16)


def to_slots(select, rows, experts_here, capacity):
    slots = jnp.einsum("bst,btd->bsd", select, rows, preferred_element_type=jnp.float32)
    slots = slots.astype(jnp.bfloat16).reshape(-1, experts_here, capacity, D)
    return jnp.swapaxes(slots, 0, 1).reshape(experts_here, -1, D)


def to_rows(select, slots, capacity):
    experts_here = slots.shape[0]
    slots = slots.astype(jnp.bfloat16).reshape(experts_here, -1, capacity, D)
    slots = jnp.swapaxes(slots, 0, 1).reshape(-1, experts_here * capacity, D)
    return jnp.einsum("bst,bsd->btd", select, slots, preferred_element_type=jnp.float32).astype(
        jnp.bfloat16
    )


def packed_rows(arrays, devices_seq):
    flat = jnp.concatenate([part.reshape(-1) for part in arrays])
    unit = devices_seq * SPAN * D
    size = -(-flat.shape[0] // unit) * unit
    return jnp.pad(flat, (0, size - flat.shape[0])).reshape(-1, D)


def unpacked(flat, shapes):
    parts, first = ([], 0)
    for shape in shapes:
        size = 1
        for extent in shape:
            size *= extent
        parts.append(flat[..., first : first + size].reshape(flat.shape[:-1] + shape))
        first += size
    return parts


def whole_of(shards, axis):
    moved_axis = jnp.moveaxis(shards, 0, axis)
    shape = moved_axis.shape
    return moved_axis.reshape(shape[:axis] + (shape[axis] * shape[axis + 1],) + shape[axis + 2 :])


def shards_of(whole, axis, count):
    shape = whole.shape
    split = whole.reshape(shape[:axis] + (count, shape[axis] // count) + shape[axis + 1 :])
    return jnp.moveaxis(split, axis, 0)


def renewed(master, moment, average, gradient, clip_factor, rate):
    scaled = clip_factor * gradient
    moment_new = MOMENTUM * moment + scaled
    master_new = master - rate * (scaled + MOMENTUM * moment_new)
    return (master_new, moment_new, EMA_KEEP * average + (1.0 - EMA_KEEP) * master_new)


def per_device(
    token_ids,
    target_ids,
    doc_lengths,
    expert_ids,
    vocab_table,
    vocab_table_mom,
    vocab_table_ema,
    mixer_in,
    mixer_in_mom,
    mixer_in_ema,
    mixer_x,
    mixer_x_mom,
    mixer_x_ema,
    mixer_out,
    mixer_out_mom,
    mixer_out_ema,
    channel,
    channel_mom,
    channel_ema,
    norm_gains,
    norm_gains_mom,
    norm_gains_ema,
    router,
    router_mom,
    router_ema,
    experts,
    experts_mom,
    experts_ema,
):
    seq_count = lax.axis_size("seq")
    group_count = lax.axis_size("group")
    seq_index = lax.axis_index("seq")
    group_index = lax.axis_index("group")
    devices = seq_count * group_count
    tokens = token_ids.shape[1]
    sequences = token_ids.shape[0]
    experts_total = router.shape[1]
    local_experts = experts.shape[1]
    capacity = max(2, 2 * tokens // experts_total)
    own_vocab = vocab_table.shape[0]
    routes = expert_ids.reshape(1, tokens)
    numbers = jnp.concatenate([token_ids, target_ids, routes])
    numbers = jnp.pad(numbers, ((0, -numbers.shape[0] % 8), (0, 0)))
    mixer_parts = (mixer_in, mixer_x, mixer_out, channel, norm_gains, router)
    part_axes = (0, 0, 0, 1, 1, 0)
    part_shapes = [part.shape for part in mixer_parts]
    table_low = vocab_table.astype(jnp.bfloat16)
    experts_low = experts.astype(jnp.bfloat16)
    up_weight, down_weight = (experts_low[0], experts_low[1])
    vocab_start = (seq_index * group_count + group_index) * own_vocab
    column_ids = jnp.arange(own_vocab, dtype=jnp.int32)
    wide_rows = DI // (seq_count * group_count)
    compact = devices * tokens <= 4096 and 2 * DI == seq_count * D and 16 * wide_rows == D
    if compact:
        own_pack = own_pack_of(mixer_parts, seq_index, seq_count)
        numbers_all, packs, embedded, table_padded, table_turned, token_local, target_local = (
            start_all(numbers, own_pack, vocab_table, 1)
        )
        numbers_all = numbers_all.reshape((devices,) + numbers.shape)
        packs = packs.reshape((seq_count, group_count) + own_pack.shape)
        channel_vals, gain_vals, router_low = small_weights(packs, experts_total)
        router_vals = router_low.astype(jnp.float32)
    else:
        numbers_all = share_small(numbers, 1)
    from_groups = jnp.swapaxes(numbers_all[:group_count, : 2 * sequences], 0, 1)
    tokens_all = from_groups[:sequences].reshape(-1)
    targets_all = from_groups[sequences:].reshape(-1)
    routes_all = numbers_all[:, 2 * sequences]
    if not compact:
        pack = packed_rows([part.astype(jnp.bfloat16) for part in mixer_parts], seq_count)
        pack_rows = pack.shape[0] // seq_count
        own_pack = lax.dynamic_slice_in_dim(pack, seq_index * pack_rows, pack_rows, 0)
        packs = gather_all(own_pack, 2).reshape(seq_count, group_count, pack_rows * D)
        shards = unpacked(jnp.swapaxes(packs, 0, 1).reshape(group_count, -1), part_shapes)
        weight_in, weight_x, weight_out, channel_low, gains_low, router_low = [
            whole_of(shard, axis) for shard, axis in zip(shards, part_axes)
        ]
        held_token = (tokens_all - vocab_start)[:, None] == column_ids[None, :]
        held_token = held_token.astype(jnp.bfloat16)
        looked_up = matmul(held_token, table_low).astype(jnp.bfloat16)
        embedded = scatter_all(looked_up.reshape(devices, tokens, D), 3)
        channel_vals = channel_low.astype(jnp.float32)
        gain_vals = gains_low.astype(jnp.float32)
        router_vals = router_low.astype(jnp.float32)

    segment_all, weight_all, keep_all = doc_layout(
        doc_lengths, group_index * tokens - CONV + 1, tokens + CONV - 1
    )
    own_segment = lax.dynamic_index_in_dim(segment_all, seq_index, 0, keepdims=False)
    keeping = lax.dynamic_index_in_dim(keep_all, seq_index, 0, keepdims=False)[CONV - 1 :]
    own_weight = lax.dynamic_index_in_dim(weight_all, seq_index, 0, keepdims=False)[CONV - 1 :]
    chosen = choice_of(expert_ids.reshape(-1), experts_total)
    if compact:
        same = [
            (own_segment[tap : tap + tokens] == own_segment[CONV - 1 :]).astype(jnp.float32)
            for tap in range(CONV)
        ]
        masks = jnp.stack(same + [keeping], axis=1)
        vectors = jnp.pad(channel_vals, ((0, 1), (0, 0)))
        mixed_out, moe_in, probability, *saved = mixer_forward_all(
            embedded, packs, vectors, gain_vals, masks, router_low, 4
        )
        probability = probability[:, :experts_total]
        scale_mid = inverse_rms(mixed_out)
    else:
        mixed_out, kept_values = mixer_forward(
            embedded,
            own_segment,
            keeping,
            weight_in,
            weight_x,
            weight_out,
            channel_vals,
            gain_vals[0],
        )
        scale_mid = inverse_rms(mixed_out)
        moe_in = (mixed_out * scale_mid * gain_vals[1]).astype(jnp.bfloat16)
        probability = jax.nn.softmax(matmul(moe_in, router_low), axis=-1)
    select = dispatch_table(routes_all, seq_index * local_experts, local_experts, capacity)
    gate_value = jnp.sum(probability * chosen, axis=1)
    arrived = to_slots(select, gather_all(moe_in, 6), local_experts, capacity)
    before = jnp.einsum("erd,efd->erf", arrived, up_weight, preferred_element_type=jnp.float32)
    inner_act = jax.nn.gelu(before).astype(jnp.bfloat16)
    partial_out = jnp.einsum(
        "erf,efd->erd", inner_act, down_weight, preferred_element_type=jnp.float32
    )
    returned = scatter_all(to_rows(select, partial_out, capacity), 3)
    expert_value = returned.astype(jnp.bfloat16).astype(jnp.float32)
    branch = gate_value[:, None] * expert_value
    hidden = mixed_out + branch
    scale_out = inverse_rms(hidden)
    final_low = (hidden * scale_out * gain_vals[2]).astype(jnp.bfloat16)
    if compact:
        all_final, stats = head_forward(final_low, table_padded, own_vocab, target_local, 7)
        own_entropy = (stats[0] - stats[1]).reshape(-1, seq_count, group_count, SPAN)
        own_entropy = lax.dynamic_index_in_dim(own_entropy, seq_index, 1, keepdims=False)
        own_entropy = lax.dynamic_index_in_dim(own_entropy, group_index, 1, keepdims=False)
        loss_part = jnp.sum(own_weight * own_entropy.reshape(-1))
        grad_final, table_grad = head_backward(
            all_final,
            table_padded,
            table_turned,
            own_vocab,
            target_local,
            stats[0],
            spread_weights(doc_lengths, tokens, group_count),
            10,
        )
    else:
        all_final = gather_all(final_low, 6).reshape(devices * tokens, D)
        valid_cols = vocab_start + column_ids < VOCAB_REAL
        hit_target = (targets_all - vocab_start)[:, None] == column_ids[None, :]
        logits = jnp.where(valid_cols[None, :], matmul_nt(all_final, table_low), -1e30)
        largest = jnp.max(logits, axis=1)
        exp_total = jnp.sum(jnp.exp(logits - largest[:, None]), axis=1)
        picked = jnp.sum(jnp.where(hit_target, logits, 0.0), axis=1)
        parts = jnp.stack([largest, exp_total, picked]).reshape(3, devices, tokens)
        parts = jnp.pad(jnp.swapaxes(parts, 0, 1), ((0, 0), (0, 5), (0, 0)))
        levels, entropy = combine_stats(parts, 7)
        log_total = levels[:, 0].reshape(-1)
        loss_part = jnp.sum(own_weight * entropy[0])
        _, every_weight, _ = doc_layout(doc_lengths, 0, tokens * group_count)
        row_weight = every_weight.reshape(-1)
        grad_logits = (
            row_weight[:, None]
            * (jnp.exp(logits - log_total[:, None]) - hit_target.astype(jnp.float32))
        ).astype(jnp.bfloat16)
        table_grad = matmul_tn(grad_logits, all_final)
        grad_rows = matmul(grad_logits, table_low).astype(jnp.bfloat16)
        grad_final = scatter_all(grad_rows.reshape(devices, tokens, D), 3)
    grad_hidden, grad_gain_out = norm_back(hidden, scale_out, gain_vals[2], grad_final)
    grad_gate = jnp.sum(grad_hidden * expert_value, axis=1)
    grad_expert = (gate_value[:, None] * grad_hidden).astype(jnp.bfloat16)
    grad_arrived = to_slots(select, gather_all(grad_expert, 6), local_experts, capacity)
    grad_inner = jnp.einsum(
        "erd,efd->erf", grad_arrived, down_weight, preferred_element_type=jnp.float32
    )
    grad_before = jax.vjp(jax.nn.gelu, before)[1](grad_inner)[0].astype(jnp.bfloat16)
    grad_down = jnp.einsum(
        "erf,erd->efd", inner_act, grad_arrived, preferred_element_type=jnp.float32
    )
    grad_up = jnp.einsum("erf,erd->efd", grad_before, arrived, preferred_element_type=jnp.float32)
    grad_part = jnp.einsum(
        "erf,efd->erd", grad_before, up_weight, preferred_element_type=jnp.float32
    )
    grad_moe_in = scatter_all(to_rows(select, grad_part, capacity), 3)
    grad_moe_in = grad_moe_in.astype(jnp.bfloat16).astype(jnp.float32)
    grad_router_logits = (grad_gate * gate_value)[:, None] * (chosen - probability)
    grad_moe_in = grad_moe_in + jnp.dot(
        grad_router_logits, router_vals.T, precision=HIGHEST
    )
    grad_router = jnp.dot(moe_in.astype(jnp.float32).T, grad_router_logits, precision=HIGHEST)
    grad_mid, grad_gain_mid = norm_back(mixed_out, scale_mid, gain_vals[1], grad_moe_in)
    grad_mixed = grad_hidden + grad_mid
    if compact:
        gain_columns = jnp.stack([grad_gain_out * 0.0, grad_gain_mid, grad_gain_out], axis=1)
        grad_embedded, grad_pack = mixer_backward_all(
            grad_mixed,
            side_lanes(grad_router, gain_columns),
            embedded,
            packs,
            vectors,
            gain_vals,
            masks,
            saved,
            5,
        )
    else:
        grad_embedded, grad_win, grad_wx, grad_wout, grad_channel, grad_gain_in = mixer_backward(
            grad_mixed,
            embedded,
            kept_values,
            weight_in,
            weight_x,
            weight_out,
            channel_vals,
            gain_vals[0],
        )
        grad_gains = jnp.stack([grad_gain_in, grad_gain_mid, grad_gain_out])
        mixer_wholes = (grad_win, grad_wx, grad_wout, grad_channel, grad_gains, grad_router)
    grad_experts = jnp.stack([grad_up, grad_down])
    experts_square = jnp.sum(grad_experts * grad_experts)
    if compact:
        scalars = jnp.concatenate(
            [jnp.full((4, LANES), experts_square), jnp.full((4, LANES), loss_part)], axis=0
        )
        table_grad, quarters, sums = finish_all(
            grad_embedded,
            grad_pack,
            token_local,
            table_grad,
            scalars,
            9,
        )
        table_grad = table_grad[:own_vocab]
    else:
        all_grad_embed = gather_all(grad_embedded.astype(jnp.bfloat16), 6).reshape(-1, D)
        table_grad = table_grad + matmul_tn(held_token, all_grad_embed)
        wholes_low = [
            shards_of(whole.astype(jnp.bfloat16), axis, group_count).reshape(group_count, -1)
            for whole, axis in zip(mixer_wholes, part_axes)
        ]
        flat = jnp.concatenate(wholes_low, axis=1)
        flat = jnp.pad(flat, ((0, 0), (0, seq_count * pack_rows * D - flat.shape[1])))
        flat = jnp.swapaxes(flat.reshape(group_count, seq_count, pack_rows, D), 0, 1)
        own_quarter = scatter_all(flat.reshape(devices, pack_rows, D), 8)
        quarters = lax.all_gather(own_quarter, "seq", axis=0, tiled=True).reshape(-1)
        mixer_grads = unpacked(quarters, part_shapes)
        local_square = (
            jnp.sum(table_grad * table_grad) + experts_square + jnp.sum(own_quarter * own_quarter)
        )
        two = jnp.concatenate(
            [jnp.full((4, LANES), local_square), jnp.full((4, LANES), loss_part)], axis=0
        )
        sums = jnp.sum(share_small(two, 9), axis=0)
    total_square, loss_sum = (sums[0, 0], sums[4, 0])
    grad_norm = jnp.sqrt(total_square)
    clip_factor = jnp.minimum(1.0, CLIP / (grad_norm + 1e-06))
    table_new = renewed(
        vocab_table, vocab_table_mom, vocab_table_ema, table_grad, clip_factor, LRATE
    )
    mixer_states = (
        (mixer_in, mixer_in_mom, mixer_in_ema),
        (mixer_x, mixer_x_mom, mixer_x_ema),
        (mixer_out, mixer_out_mom, mixer_out_ema),
        (channel, channel_mom, channel_ema),
        (norm_gains, norm_gains_mom, norm_gains_ema),
        (router, router_mom, router_ema),
    )
    if compact:
        fresh = update_all(quarters, sums, mixer_states)
    else:
        rates = (LRATE, LRATE, LRATE, CHANNEL_LRATE, LRATE, LRATE)
        fresh = [
            part
            for state, gradient, rate in zip(mixer_states, mixer_grads, rates)
            for part in renewed(*state, gradient, clip_factor, rate)
        ]
    experts_new = renewed(experts, experts_mom, experts_ema, grad_experts, clip_factor, LRATE)
    return (
        loss_sum,
        grad_norm,
        branch.reshape(1, tokens, D),
        table_new[0],
        table_new[1],
        table_new[2],
        *fresh,
        experts_new[0],
        experts_new[1],
        experts_new[2],
    )


def solution(mesh):
    placed = (
        P(None, "group"),
        P(None, "group"),
        P(),
        P("seq", "group", None),
        P(("seq", "group"), None),
        P(("seq", "group"), None),
        P(("seq", "group"), None),
        P("group", None),
        P("group", None),
        P("group", None),
        P("group", None),
        P("group", None),
        P("group", None),
        P("group", None),
        P("group", None),
        P("group", None),
        P(None, "group"),
        P(None, "group"),
        P(None, "group"),
        P(None, "group"),
        P(None, "group"),
        P(None, "group"),
        P("group", None),
        P("group", None),
        P("group", None),
        P(None, "seq", "group", None),
        P(None, "seq", "group", None),
        P(None, "seq", "group", None),
    )
    return jax.shard_map(
        per_device,
        mesh=mesh,
        in_specs=placed,
        out_specs=(
            P(),
            P(),
            P("seq", "group", None),
            P(("seq", "group"), None),
            P(("seq", "group"), None),
            P(("seq", "group"), None),
            P("group", None),
            P("group", None),
            P("group", None),
            P("group", None),
            P("group", None),
            P("group", None),
            P("group", None),
            P("group", None),
            P("group", None),
            P(None, "group"),
            P(None, "group"),
            P(None, "group"),
            P(None, "group"),
            P(None, "group"),
            P(None, "group"),
            P("group", None),
            P("group", None),
            P("group", None),
            P(None, "seq", "group", None),
            P(None, "seq", "group", None),
            P(None, "seq", "group", None),
        ),
        check_vma=False,
    )
```

```python
import functools

import jax
import jax.numpy as jnp
from jax import lax
from jax.experimental import pallas as pl
from jax.experimental.pallas import tpu as pltpu
from jax.sharding import PartitionSpec as P

D = 768
DI = 1536
STATE = 16
RANK = 48
CONV = 4
VOCAB_REAL = 50257


EPS = 1e-05
CLIP = 0.1
MOMENTUM = 0.9
LRATE = 1000.0
CHANNEL_LRATE = 10000.0
EMA_KEEP = 0.8
HIGHEST = lax.Precision.HIGHEST
MESH = pl.DeviceIdType.MESH
VMEM_LIMIT = 58 << 20
LANES = 128
SIDE_LANE = 32


def axis_sizes():
    seq, group = (lax.axis_size("seq"), lax.axis_size("group"))
    core = 2 if seq % 2 == 0 else 1
    y = 1
    while 4 * y * y <= group and group % (2 * y) == 0:
        y *= 2
    return {"x": seq // core, "core": core, "z": group // y, "y": y}


def my_place(sizes):
    seq, group = (lax.axis_index("seq"), lax.axis_index("group"))
    return {
        "x": seq // sizes["core"],
        "core": seq % sizes["core"],
        "z": group // sizes["y"],
        "y": group % sizes["y"],
    }


def device_of(place, sizes):
    return (place["x"] * sizes["core"] + place["core"], place["z"] * sizes["y"] + place["y"])


def moved(place, axis, by, sizes):
    return {**place, axis: lax.rem(place[axis] + by + sizes[axis], sizes[axis])}


def block_of(place, sizes):
    seq, group = device_of(place, sizes)
    return seq * (sizes["z"] * sizes["y"]) + group


def meet(peers):
    barrier = pltpu.get_barrier_semaphore()
    for peer in peers:
        pl.semaphore_signal(barrier, inc=1, device_id=peer, device_id_type=MESH)
    pl.semaphore_wait(barrier, len(peers))


def line_peers(place, sizes):
    return [
        device_of(moved(place, axis, by, sizes), sizes)
        for axis in ("x", "core", "z", "y")
        for by in range(1, sizes[axis])
    ]


GATHER_ORDERS = (
    ("z", "y", "x", "core"),
    ("z", "x", "y", "core"),
    ("x", "z", "y", "core"),
    ("y", "z", "x", "core"),
)


def gather_kernel(sizes, pieces, own_ref, all_ref, local_sem, send_sem, recv_sem):
    place = my_place(sizes)
    meet(line_peers(place, sizes))
    keep_own = pltpu.make_async_copy(own_ref, all_ref.at[block_of(place, sizes)], local_sem)
    keep_own.start()
    held = [[(place, None)] for _ in pieces]
    sends = []
    for phase in range(4):
        fresh = [[] for _ in pieces]
        for turn in range(max(len(blocks) for blocks in held)):
            for which, (order, first, rows) in enumerate(pieces):
                if turn >= len(held[which]):
                    continue
                axis = order[phase]
                where, arrival = held[which][turn]
                if arrival is not None:
                    copy, seen = arrival
                    if not seen:
                        copy.wait_recv()
                        held[which][turn] = (where, (copy, True))
                span = pl.ds(first, rows)
                for by in range(1, sizes[axis]):
                    block = block_of(where, sizes)
                    source = own_ref.at[span] if arrival is None else all_ref.at[block, span]
                    number = len(sends)
                    copy = pltpu.make_async_remote_copy(
                        src_ref=source,
                        dst_ref=all_ref.at[block, span],
                        send_sem=send_sem.at[number],
                        recv_sem=recv_sem.at[number],
                        device_id=device_of(moved(place, axis, by, sizes), sizes),
                        device_id_type=MESH,
                    )
                    copy.start()
                    sends.append(copy)
                    fresh[which].append((moved(where, axis, -by, sizes), (copy, False)))
        held = [old + new for old, new in zip(held, fresh)]
    for blocks in held:
        for _, arrival in blocks:
            if arrival is not None and not arrival[1]:
                arrival[0].wait_recv()
    for copy in sends:
        copy.wait_send()
    keep_own.wait()


def split_rows(rows, orders):
    unit = 32 if rows % 32 == 0 else 16
    count = rows // unit
    pieces, first = ([], 0)
    for which in range(min(count, 4)):
        size = (count * (which + 1) // min(count, 4)) * unit - first
        pieces.append((orders[which % len(orders)], first, size))
        first += size
    return pieces


def gather_all(rows, collective_id):
    sizes = axis_sizes()
    devices = sizes["x"] * sizes["core"] * sizes["z"] * sizes["y"]
    pieces = split_rows(rows.shape[0], GATHER_ORDERS)
    copies = (devices - 1) * len(pieces)
    return pl.pallas_call(
        functools.partial(gather_kernel, sizes, pieces),
        out_shape=jax.ShapeDtypeStruct((devices,) + rows.shape, rows.dtype),
        in_specs=[pl.BlockSpec(memory_space=pltpu.VMEM)],
        out_specs=pl.BlockSpec(memory_space=pl.ANY),
        scratch_shapes=[
            pltpu.SemaphoreType.DMA,
            pltpu.SemaphoreType.DMA((copies,)),
            pltpu.SemaphoreType.DMA((copies,)),
        ],
        compiler_params=pltpu.CompilerParams(
            collective_id=collective_id, has_side_effects=True, vmem_limit_bytes=VMEM_LIMIT
        ),
        name="gather_all",
    )(rows)


SCATTER_ORDERS = (("core", "x", "y", "z"), ("core", "y", "x", "z"))
GATHER_PAIR = (("z", "y", "x", "core"), ("z", "x", "y", "core"))
NATURAL = ("x", "core", "z", "y")
PIECE = 16
SPAN = 2 * PIECE


def unravel(number, extents):
    places = []
    for extent in reversed(extents):
        places.append(lax.rem(number, extent))
        number = lax.div(number, extent)
    return tuple(reversed(places))


def piece_rows(pair, kind):
    first = pair * SPAN + kind * PIECE
    if not isinstance(first, int):
        first = pl.multiple_of(first, PIECE)
    return pl.ds(first, PIECE)


def scatter_scratch(sizes, pairs, width, keep):
    scratch = []
    for order in SCATTER_ORDERS:
        landings, sums, semaphores = ([], [], [])
        for phase in range(4):
            left = tuple(sizes[a] for a in NATURAL if a not in order[: phase + 1])
            others = max(1, sizes[order[phase]] - 1)
            landings.append(pltpu.VMEM((pairs, others) + left + (PIECE, width), jnp.bfloat16))
            if phase < 3:
                sums.append(pltpu.VMEM((pairs,) + left + (PIECE, width), jnp.bfloat16))
            semaphores.append(pltpu.SemaphoreType.DMA((pairs, others)))
            semaphores.append(pltpu.SemaphoreType.DMA((pairs, others)))
        scratch += landings + sums + semaphores
        scratch += [pltpu.SemaphoreType.DMA((pairs,))] if keep else []
    return scratch


class Scatter:
    def __init__(self, sizes, pairs, full_ref, own_ref, scratch, keep):
        self.sizes, self.pairs, self.keep = (sizes, pairs, keep)
        self.full_ref, self.own_ref = (full_ref, own_ref)
        self.place = my_place(sizes)
        size = len(scratch) // 2
        self.refs = (scratch[:size], scratch[size:])

    def kept(self, kind, pair):
        order = SCATTER_ORDERS[kind]
        index = tuple(self.place[a] if a == order[0] else slice(None) for a in NATURAL)
        return pltpu.make_async_copy(
            self.full_ref.at[index + (piece_rows(pair, kind),)],
            self.refs[kind][4].at[pair],
            self.refs[kind][15].at[pair],
        )

    def copies(self, kind, pair, phase):
        order, refs, sizes = (SCATTER_ORDERS[kind], self.refs[kind], self.sizes)
        axis = order[phase]
        left = [a for a in NATURAL if a not in order[:phase]]
        made = []
        for by in range(1, sizes[axis]):
            to = moved(self.place, axis, by, sizes)
            index = tuple(to[axis] if a == axis else slice(None) for a in left)
            if phase == 0:
                source = self.full_ref.at[index + (piece_rows(pair, kind),)]
            else:
                source = refs[3 + phase].at[(pair,) + index]
            made.append(
                pltpu.make_async_remote_copy(
                    src_ref=source,
                    dst_ref=refs[phase].at[pair, by - 1],
                    send_sem=refs[7 + 2 * phase].at[pair, by - 1],
                    recv_sem=refs[8 + 2 * phase].at[pair, by - 1],
                    device_id=device_of(to, sizes),
                    device_id_type=MESH,
                )
            )
        return made

    def launch(self, pair, phase):
        for kind in range(2):
            for copy in self.copies(kind, pair, phase):
                copy.start()

    def absorb(self, kind, pair, phase):
        order, refs, sizes, place = (
            SCATTER_ORDERS[kind],
            self.refs[kind],
            self.sizes,
            self.place,
        )
        axis = order[phase]
        before = [a for a in NATURAL if a not in order[:phase]]
        after = [a for a in before if a != axis]
        if phase == 0 and self.keep:
            self.kept(kind, pair).wait()
        for copy in self.copies(kind, pair, phase):
            copy.wait_recv()
        extents = tuple(sizes[a] for a in after)
        number = 1
        for extent in extents:
            number *= extent

        def add(step, carry):
            spot = dict(zip(after, unravel(step, extents)))
            mine = tuple(place[axis] if a == axis else spot[a] for a in before)
            there = tuple(spot[a] for a in after)
            if phase > 0:
                kept_part = refs[3 + phase][(pair,) + mine]
            elif self.keep:
                kept_part = refs[4][(pair,) + there]
            else:
                kept_part = self.full_ref[mine + (piece_rows(pair, kind),)]
            total = kept_part.astype(jnp.float32)
            for by in range(1, sizes[axis]):
                total = total + refs[phase][(pair, by - 1) + there].astype(jnp.float32)
            if phase == 3:
                self.own_ref[piece_rows(pair, kind)] = total
            else:
                refs[4 + phase][(pair,) + there] = total.astype(jnp.bfloat16)
            return carry

        if number == 1:
            add(0, 0)
        else:
            lax.fori_loop(0, number, add, 0)

    def advance(self, pair, phase):
        for kind in range(2):
            self.absorb(kind, pair, phase)
            if phase < 3:
                for copy in self.copies(kind, pair, phase + 1):
                    copy.start()

    def finish(self):
        def one(pair, carry):
            for kind in range(2):
                for phase in range(4):
                    for copy in self.copies(kind, pair, phase):
                        copy.wait_send()
            return carry

        lax.fori_loop(0, self.pairs, one, 0)


def wave(pairs, phases, act):
    def step(turn, carry):
        for phase in range(phases - 1, -1, -1):
            pair = turn - phase

            @pl.when((pair >= 0) & (pair < pairs))
            def _(pair=pair, phase=phase):
                act(pair, phase)

        return carry

    lax.fori_loop(0, pairs + phases - 1, step, 0)


def scatter_kernel(sizes, pairs, full_ref, own_ref, *scratch):
    meet(line_peers(my_place(sizes), sizes))
    scatter = Scatter(sizes, pairs, full_ref, own_ref, scratch, True)
    for pair in range(pairs):
        scatter.launch(pair, 0)
        for kind in range(2):
            scatter.kept(kind, pair).start()
    wave(pairs, 4, scatter.advance)
    scatter.finish()


def scatter_all(blocks, collective_id):
    sizes = axis_sizes()
    rows, width = blocks.shape[-2:]
    pairs = rows // SPAN
    shaped = blocks.reshape(tuple(sizes[a] for a in NATURAL) + (rows, width))
    return pl.pallas_call(
        functools.partial(scatter_kernel, sizes, pairs),
        out_shape=jax.ShapeDtypeStruct((rows, width), jnp.float32),
        in_specs=[pl.BlockSpec(memory_space=pl.ANY)],
        out_specs=pl.BlockSpec(memory_space=pltpu.VMEM),
        scratch_shapes=scatter_scratch(sizes, pairs, width, True),
        compiler_params=pltpu.CompilerParams(
            collective_id=collective_id, has_side_effects=True, vmem_limit_bytes=VMEM_LIMIT
        ),
        name="scatter_all",
    )(shaped)


class Gather:
    def __init__(self, sizes, pairs, own_ref, all_ref, semaphores):
        self.sizes, self.pairs = (sizes, pairs)
        self.own_ref, self.all_ref = (own_ref, all_ref)
        self.semaphores = semaphores
        self.place = my_place(sizes)

    def copies(self, kind, pair, phase):
        order = GATHER_PAIR[kind]
        axis, span = (order[phase], piece_rows(pair, kind))
        block = tuple(slice(None) if a in order[:phase] else self.place[a] for a in NATURAL)
        there = self.all_ref.at[block + (span,)]
        send_sem, recv_sem = (self.semaphores[2 * phase], self.semaphores[2 * phase + 1])
        return [
            pltpu.make_async_remote_copy(
                src_ref=self.own_ref.at[span] if phase == 0 else there,
                dst_ref=there,
                send_sem=send_sem.at[kind, pair, by - 1],
                recv_sem=recv_sem.at[kind, pair, by - 1],
                device_id=device_of(moved(self.place, axis, by, self.sizes), self.sizes),
                device_id_type=MESH,
            )
            for by in range(1, self.sizes[axis])
        ]

    def advance(self, pair, phase):
        for kind in range(2):
            if phase > 0:
                for copy in self.copies(kind, pair, phase - 1):
                    copy.wait_recv()
            if phase < 4:
                for copy in self.copies(kind, pair, phase):
                    copy.start()

    def finish(self):
        def one(pair, carry):
            for kind in range(2):
                for phase in range(4):
                    for copy in self.copies(kind, pair, phase):
                        copy.wait_send()
            return carry

        lax.fori_loop(0, self.pairs, one, 0)


def gather_semaphores(sizes, pairs):
    longest = max(sizes.values())
    return [pltpu.SemaphoreType.DMA((2, pairs, longest)) for _ in range(8)]


def seq_place(seq, sizes):
    return (lax.div(seq, sizes["core"]), lax.rem(seq, sizes["core"]))


def merge_stats(first, second):
    high = jnp.maximum(first[0], second[0])
    mass = first[1] * jnp.exp(first[0] - high) + second[1] * jnp.exp(second[0] - high)
    return (high, mass, first[2] + second[2])


def span_rows(pair):
    return pl.ds(pl.multiple_of(pair * SPAN, SPAN), SPAN)


def masked_logits(table_ref, rows_in, first_masked, limit):
    logits = matmul_nt(table_ref[...], rows_in)
    tail = logits[first_masked:]
    numbers = first_masked + lax.broadcasted_iota(jnp.int32, tail.shape, 0)
    return jnp.concatenate([logits[:first_masked], jnp.where(numbers < limit, tail, -1e30)], axis=0)


def vocab_limit(own_vocab):
    devices, _, me = flat_place()
    least = max(0, VOCAB_REAL - (devices - 1) * own_vocab)
    limit = jnp.minimum(own_vocab, VOCAB_REAL - me * own_vocab)
    return (min(least, own_vocab) // 16 * 16, limit)


def head_forward_kernel(
    sizes,
    pairs,
    own_vocab,
    own_ref,
    table_ref,
    target_ref,
    all_ref,
    stats_ref,
    mine_ref,
    landing_ref,
    local_sem,
    stat_send,
    stat_recv,
    *semaphores,
):
    place = my_place(sizes)
    meet(line_peers(place, sizes))
    gather = Gather(sizes, pairs, own_ref, all_ref, semaphores)
    keep_own = pltpu.make_async_copy(
        own_ref, all_ref.at[tuple(place[a] for a in NATURAL)], local_sem
    )
    keep_own.start()
    groups = sizes["z"] * sizes["y"]
    seqs = sizes["x"] * sizes["core"]
    first_masked, limit = vocab_limit(own_vocab)

    def seq_stats(pair, seq):
        x, core = seq_place(seq, sizes)
        rows_in = all_ref[x, core, :, :, span_rows(pair), :].reshape(groups * SPAN, D)
        logits = masked_logits(table_ref, rows_in, first_masked, limit)
        spot = pl.ds(pair * seqs + seq, 1)
        numbers = lax.broadcasted_iota(jnp.int32, logits.shape, 0)
        top = jnp.max(logits, axis=0, keepdims=True)
        mine_ref[0, 0, spot] = top
        mine_ref[0, 1, spot] = jnp.sum(jnp.exp(logits - top), axis=0, keepdims=True)
        mine_ref[0, 2, spot] = jnp.sum(
            jnp.where(numbers == target_ref[spot], logits, 0.0), axis=0, keepdims=True
        )

    def turn_step(turn, carry):
        for phase in range(4, -1, -1):
            pair = turn - phase

            @pl.when((pair >= 0) & (pair < pairs))
            def _(pair=pair, phase=phase):
                gather.advance(pair, phase)

        @pl.when(turn == 0)
        def _():
            keep_own.wait()

        @pl.when(turn >= 4)
        def _():
            def one(seq, carry):
                seq_stats(turn - 4, seq)
                return carry

            lax.fori_loop(0, seqs, one, 0)

        return carry

    lax.fori_loop(0, pairs + 4, turn_step, 0)
    started = []
    stats = tuple(mine_ref[0, k] for k in range(3))
    for phase, axis in enumerate(("core", "x", "y", "z")):
        arrivals = []
        for by in range(1, sizes[axis]):
            slot = len(started)
            copy = pltpu.make_async_remote_copy(
                src_ref=mine_ref.at[phase],
                dst_ref=landing_ref.at[slot],
                send_sem=stat_send.at[slot],
                recv_sem=stat_recv.at[slot],
                device_id=device_of(moved(place, axis, by, sizes), sizes),
                device_id_type=MESH,
            )
            copy.start()
            arrivals.append((copy, slot))
            started.append(copy)
        for copy, slot in arrivals:
            copy.wait_recv()
            stats = merge_stats(stats, tuple(landing_ref[slot, k] for k in range(3)))
        if phase < 3:
            for k in range(3):
                mine_ref[phase + 1, k] = stats[k]
    stats_ref[0] = stats[0] + jnp.log(stats[1])
    stats_ref[1] = stats[2]
    gather.finish()
    for copy in started:
        copy.wait_send()


def head_forward(rows, table, own_vocab, targets, collective_id):
    sizes = axis_sizes()
    pairs = rows.shape[0] // SPAN
    hops = sum(extent - 1 for extent in sizes.values())
    natural = tuple(sizes[a] for a in NATURAL)
    packed = (3,) + targets.shape
    vmem = pl.BlockSpec(memory_space=pltpu.VMEM)
    return pl.pallas_call(
        functools.partial(head_forward_kernel, sizes, pairs, own_vocab),
        out_shape=(
            jax.ShapeDtypeStruct(natural + rows.shape, rows.dtype),
            jax.ShapeDtypeStruct((2,) + targets.shape, jnp.float32),
        ),
        in_specs=[vmem] * 3,
        out_specs=(vmem,) * 2,
        scratch_shapes=[
            pltpu.VMEM((4,) + packed, jnp.float32),
            pltpu.VMEM((hops,) + packed, jnp.float32),
            pltpu.SemaphoreType.DMA,
            pltpu.SemaphoreType.DMA((hops,)),
            pltpu.SemaphoreType.DMA((hops,)),
        ]
        + gather_semaphores(sizes, pairs),
        compiler_params=pltpu.CompilerParams(
            collective_id=collective_id, has_side_effects=True, vmem_limit_bytes=VMEM_LIMIT
        ),
        name="head_forward",
    )(rows, table, targets)


def head_backward_kernel(
    sizes,
    pairs,
    own_vocab,
    all_ref,
    table_ref,
    turned_ref,
    target_ref,
    level_ref,
    weight_ref,
    own_ref,
    tgrad_ref,
    full_ref,
    grad_ref,
    *scratch,
):
    meet(line_peers(my_place(sizes), sizes))
    scatter = Scatter(sizes, pairs, full_ref, own_ref, scratch, False)
    groups = sizes["z"] * sizes["y"]
    seqs = sizes["x"] * sizes["core"]
    first_masked, limit = vocab_limit(own_vocab)
    height = table_ref.shape[0]
    block = groups * SPAN

    def seq_grads(pair, seq):
        x, core = divmod(seq, sizes["core"])
        rows_in = all_ref[x, core, :, :, span_rows(pair), :].reshape(block, D)
        logits = masked_logits(table_ref, rows_in, first_masked, limit)
        spot = pl.ds(pair * seqs + seq, 1)
        numbers = lax.broadcasted_iota(jnp.int32, logits.shape, 0)
        share = jnp.exp(logits - level_ref[spot])
        share = jnp.where(numbers == target_ref[spot], share - 1.0, share)
        grad_ref[pair, 0:height, seq * block : (seq + 1) * block] = (
            weight_ref[spot] * share
        ).astype(jnp.bfloat16)

    def row_product(pair):
        turned = matmul(turned_ref[...], grad_ref[pair])
        full_ref[:, :, :, :, span_rows(pair), :] = turned.T.astype(jnp.bfloat16).reshape(
            tuple(sizes[a] for a in NATURAL) + (SPAN, D)
        )

    def table_product(pair):
        rows_in = all_ref[:, :, :, :, span_rows(pair), :].reshape(seqs * block, D)
        return matmul(grad_ref[pair, 0:height], rows_in)

    if grad_ref.shape[1] > height:
        grad_ref[:, height:] = jnp.zeros_like(grad_ref[:, height:])

    def turn_step(turn, carry):
        def older(by, phase):
            pair = turn - by

            @pl.when((pair >= 0) & (pair < pairs))
            def _():
                scatter.advance(pair, phase)

        def compute(act):
            @pl.when(turn < pairs)
            def _():
                act()

        for part in range(4):
            for seq in range(part * seqs // 4, (part + 1) * seqs // 4):
                compute(lambda seq=seq: seq_grads(turn, seq))
            if part == 0:
                older(1, 0)
            elif part == 1:
                older(2, 3)
            elif part == 2:
                older(1, 1)
        compute(lambda: row_product(turn))
        older(1, 2)
        compute(lambda: scatter.launch(turn, 0))
        return carry

    lax.fori_loop(0, pairs, turn_step, 0)
    tgrad_ref[...] = table_product(0)
    scatter.advance(pairs - 1, 0)
    if pairs > 1:
        scatter.advance(pairs - 2, 3)

    def late(pair, carry):
        tgrad_ref[...] += table_product(pair)

        @pl.when(pair < 3)
        def _():
            for phase in (1, 2):

                @pl.when(pair == phase)
                def _(phase=phase):
                    scatter.advance(pairs - 1, phase)

        return carry

    lax.fori_loop(1, pairs, late, 0)
    for phase in range(max(1, pairs), 4):
        if phase < 3:
            scatter.advance(pairs - 1, phase)
    scatter.advance(pairs - 1, 3)
    scatter.finish()


def head_backward(all_rows, table, turned, own_vocab, targets, levels, weights, collective_id):
    sizes = axis_sizes()
    tokens = all_rows.shape[-2]
    pairs = tokens // SPAN
    vmem = pl.BlockSpec(memory_space=pltpu.VMEM)
    block = targets.shape[1]
    seqs = sizes["x"] * sizes["core"]
    return pl.pallas_call(
        functools.partial(head_backward_kernel, sizes, pairs, own_vocab),
        out_shape=(
            jax.ShapeDtypeStruct((tokens, D), jnp.float32),
            jax.ShapeDtypeStruct(table.shape, jnp.float32),
        ),
        in_specs=[vmem] * 6,
        out_specs=(vmem,) * 2,
        scratch_shapes=[
            pltpu.VMEM(all_rows.shape, jnp.bfloat16),
            pltpu.VMEM((pairs, turned.shape[1], seqs * block), jnp.bfloat16),
        ]
        + scatter_scratch(sizes, pairs, D, False),
        compiler_params=pltpu.CompilerParams(
            collective_id=collective_id, has_side_effects=True, vmem_limit_bytes=VMEM_LIMIT
        ),
        name="head_backward",
    )(all_rows, table, turned, targets, levels, weights)


def everyone(devices, groups, me, act):
    def step(by, carry):
        peer = lax.rem(me + by, devices)
        act(by, peer, (lax.div(peer, groups), lax.rem(peer, groups)))
        return carry

    lax.fori_loop(1, devices, step, 0)


def greet_everyone(devices, groups, me):
    barrier = pltpu.get_barrier_semaphore()

    def greet(by, peer, address):
        pl.semaphore_signal(barrier, inc=1, device_id=address, device_id_type=MESH)

    everyone(devices, groups, me, greet)
    pl.semaphore_wait(barrier, devices - 1)


def flat_place():
    groups = lax.axis_size("group")
    return (
        lax.axis_size("seq") * groups,
        groups,
        lax.axis_index("seq") * groups + lax.axis_index("group"),
    )


def share_kernel(own_ref, all_ref, send_sem, recv_sem):
    devices, groups, me = flat_place()
    greet_everyone(devices, groups, me)

    def copy_to(by, address):
        return pltpu.make_async_remote_copy(
            src_ref=own_ref,
            dst_ref=all_ref.at[me],
            send_sem=send_sem.at[by],
            recv_sem=recv_sem.at[by],
            device_id=address,
            device_id_type=MESH,
        )

    everyone(devices, groups, me, lambda by, peer, address: copy_to(by, address).start())
    all_ref[me] = own_ref[...]
    everyone(devices, groups, me, lambda by, peer, address: copy_to(by, address).wait())


def share_small(values, collective_id):
    devices = lax.axis_size("seq") * lax.axis_size("group")
    return pl.pallas_call(
        share_kernel,
        out_shape=jax.ShapeDtypeStruct((devices,) + values.shape, values.dtype),
        in_specs=[pl.BlockSpec(memory_space=pltpu.VMEM)],
        out_specs=pl.BlockSpec(memory_space=pltpu.VMEM),
        scratch_shapes=[
            pltpu.SemaphoreType.DMA((devices,)),
            pltpu.SemaphoreType.DMA((devices,)),
        ],
        compiler_params=pltpu.CompilerParams(collective_id=collective_id, has_side_effects=True),
        name="share_small",
    )(values)


def stats_kernel(parts_ref, all_ref, own_ref, got_ref, mine_ref, send_sem, recv_sem):
    devices, groups, me = flat_place()
    greet_everyone(devices, groups, me)

    def part_to(by, peer, address):
        return pltpu.make_async_remote_copy(
            src_ref=parts_ref.at[peer],
            dst_ref=got_ref.at[me],
            send_sem=send_sem.at[0, by],
            recv_sem=recv_sem.at[0, by],
            device_id=address,
            device_id_type=MESH,
        )

    def total_to(by, address):
        return pltpu.make_async_remote_copy(
            src_ref=mine_ref,
            dst_ref=all_ref.at[me],
            send_sem=send_sem.at[1, by],
            recv_sem=recv_sem.at[1, by],
            device_id=address,
            device_id_type=MESH,
        )

    everyone(devices, groups, me, lambda by, peer, address: part_to(by, peer, address).start())
    got_ref[me] = parts_ref[me]
    everyone(devices, groups, me, lambda by, peer, address: part_to(by, peer, address).wait())
    tops = got_ref[:, 0, :]
    top = jnp.max(tops, axis=0, keepdims=True)
    mass = jnp.sum(got_ref[:, 1, :] * jnp.exp(tops - top), axis=0, keepdims=True)
    hit = jnp.sum(got_ref[:, 2, :], axis=0, keepdims=True)
    level = top + jnp.log(mass)
    mine_ref[...] = jnp.broadcast_to(level, mine_ref.shape)
    everyone(devices, groups, me, lambda by, peer, address: total_to(by, address).start())
    all_ref[me] = mine_ref[...]
    own_ref[...] = jnp.broadcast_to(level - hit, own_ref.shape)
    everyone(devices, groups, me, lambda by, peer, address: total_to(by, address).wait())


def combine_stats(parts, collective_id):
    devices = parts.shape[0]
    shape = parts.shape[1:]
    return pl.pallas_call(
        stats_kernel,
        out_shape=(
            jax.ShapeDtypeStruct(parts.shape, jnp.float32),
            jax.ShapeDtypeStruct(shape, jnp.float32),
        ),
        in_specs=[pl.BlockSpec(memory_space=pltpu.VMEM)],
        out_specs=(pl.BlockSpec(memory_space=pltpu.VMEM),) * 2,
        scratch_shapes=[
            pltpu.VMEM(parts.shape, jnp.float32),
            pltpu.VMEM(shape, jnp.float32),
            pltpu.SemaphoreType.DMA((2, devices)),
            pltpu.SemaphoreType.DMA((2, devices)),
        ],
        compiler_params=pltpu.CompilerParams(collective_id=collective_id, has_side_effects=True),
        name="combine_stats",
    )(parts)


def chain_exchange(rates, total_step, flag, end_state, backwards, out_buf, in_buf, sems):
    devices, me = (lax.axis_size("group"), lax.axis_index("group"))
    seq = lax.axis_index("seq")
    send_sem, recv_sem = sems
    width = rates.shape[1]

    def join(first, second):
        return (
            jnp.exp(second[0] * rates) * second[1] * first[2] + second[2],
            first[0] + second[0],
            first[1] * second[1],
        )

    window = (total_step, flag, end_state)
    before = None
    distance, lap = (1, 0)
    copies = []
    while distance < devices:
        to = lax.rem(me + (devices - distance if backwards else distance), devices)
        out_buf[lap, 0:STATE] = window[2]
        out_buf[lap, STATE : STATE + 8] = jnp.concatenate(
            [
                jnp.broadcast_to(window[0], (4, width)),
                jnp.broadcast_to(window[1], (4, width)),
            ],
            axis=0,
        )
        copy = pltpu.make_async_remote_copy(
            src_ref=out_buf.at[lap],
            dst_ref=in_buf.at[lap],
            send_sem=send_sem.at[lap],
            recv_sem=recv_sem.at[lap],
            device_id=(seq, to),
            device_id_type=MESH,
        )
        copy.start()
        copies.append(copy)
        copy.wait_recv()
        reached = (me + distance < devices) if backwards else (me >= distance)
        real = jnp.where(reached, 1.0, 0.0)
        tail = in_buf[lap, STATE : STATE + 8]
        got = (
            tail[0:1] * real,
            tail[4:5] * real + (1.0 - real),
            in_buf[lap, 0:STATE] * real,
        )
        if before is None:
            before = got
        else:
            merged = join(got, before)
            before = (merged[1], merged[2], merged[0])
        merged = join(got, window)
        window = (merged[1], merged[2], merged[0])
        distance *= 2
        lap += 1
    for copy in copies:
        copy.wait_send()
    if before is None:
        return jnp.zeros_like(end_state)
    return before[2]


def chain_peers():
    devices, me = (lax.axis_size("group"), lax.axis_index("group"))
    seq = lax.axis_index("seq")
    distances = []
    distance = 1
    while distance < devices:
        distances += [distance, devices - distance]
        distance *= 2
    return [(seq, lax.rem(me + by, devices)) for by in sorted(set(distances))]


def chain_laps():
    laps, distance = (0, 1)
    while distance < lax.axis_size("group"):
        laps, distance = (laps + 1, distance * 2)
    return max(1, laps)


def spans(width):
    size = 512 if width % 512 == 0 else width
    return [slice(first, first + size) for first in range(0, width, size)]


def wide(value, copies):
    return jnp.concatenate([value] * copies, axis=1)


def folded(value):
    total = value[:, :LANES]
    for first in range(LANES, value.shape[1], LANES):
        total = total + value[:, first : first + LANES]
    return total


def scan_forward_kernel(*refs):
    meet(chain_peers())
    scan_forward_body(*refs)


def scan_forward_body(
    step_ref, act_ref, b_ref, c_ref, keep_ref, rate_ref, y_ref, in_ref, out_buf, in_buf, ss, rs
):
    tokens, width = step_ref.shape
    ends = []
    for span in spans(width):
        copies = (span.stop - span.start) // LANES
        rates = rate_ref[:, span]

        def advance(block, state, span=span, copies=copies, rates=rates):
            rows = pl.ds(pl.multiple_of(block * 8, 8), 8)
            steps = step_ref[rows, span]
            drives = steps * act_ref[rows, span]
            keeps = wide(keep_ref[rows, :], copies)
            for r in range(8):
                decay = jnp.exp(steps[r : r + 1] * rates) * keeps[r : r + 1]
                state = decay * state + drives[r : r + 1] * wide(b_ref[block * 8 + r], copies)
            return state

        ends.append(
            lax.fori_loop(
                0, tokens // 8, advance, jnp.zeros((STATE, span.stop - span.start), jnp.float32)
            )
        )
    total_step = jnp.sum(step_ref[...], axis=0, keepdims=True)
    flag = wide(jnp.min(keep_ref[...], axis=0, keepdims=True), width // LANES)
    incoming = chain_exchange(
        rate_ref[...],
        total_step,
        flag,
        jnp.concatenate(ends, axis=1),
        False,
        out_buf,
        in_buf,
        (ss, rs),
    )
    in_ref[...] = incoming
    for span in spans(width):
        copies = (span.stop - span.start) // LANES
        rates = rate_ref[:, span]

        def produce(block, state, span=span, copies=copies, rates=rates):
            rows = pl.ds(pl.multiple_of(block * 8, 8), 8)
            steps = step_ref[rows, span]
            drives = steps * act_ref[rows, span]
            keeps = wide(keep_ref[rows, :], copies)
            results = []
            for r in range(8):
                decay = jnp.exp(steps[r : r + 1] * rates) * keeps[r : r + 1]
                state = decay * state + drives[r : r + 1] * wide(b_ref[block * 8 + r], copies)
                results.append(
                    jnp.sum(state * wide(c_ref[block * 8 + r], copies), axis=0, keepdims=True)
                )
            y_ref[rows, span] = jnp.concatenate(results, axis=0)
            return state

        lax.fori_loop(0, tokens // 8, produce, in_ref[:, span])


def scan_scratch(width):
    laps = chain_laps()
    return [
        pltpu.VMEM((laps, STATE + 8, width), jnp.float32),
        pltpu.VMEM((laps, STATE + 8, width), jnp.float32),
        pltpu.SemaphoreType.DMA((laps,)),
        pltpu.SemaphoreType.DMA((laps,)),
    ]


def scan_forward(step, act, b_wide, c_wide, keep_wide, rates, collective_id):
    tokens, width = step.shape
    return pl.pallas_call(
        scan_forward_kernel,
        out_shape=(
            jax.ShapeDtypeStruct((tokens, width), jnp.float32),
            jax.ShapeDtypeStruct((STATE, width), jnp.float32),
        ),
        in_specs=[pl.BlockSpec(memory_space=pltpu.VMEM)] * 6,
        out_specs=(pl.BlockSpec(memory_space=pltpu.VMEM),) * 2,
        scratch_shapes=scan_scratch(width),
        compiler_params=pltpu.CompilerParams(
            collective_id=collective_id, has_side_effects=True, vmem_limit_bytes=VMEM_LIMIT
        ),
        name="scan_forward",
    )(step, act, b_wide, c_wide, keep_wide, rates)


def scan_backward_kernel(*refs):
    meet(chain_peers())
    scan_backward_body(*refs)


def scan_backward_body(
    step_ref,
    act_ref,
    b_ref,
    c_ref,
    keep_ref,
    rate_ref,
    in_ref,
    grad_ref,
    along_ref,
    decayed_ref,
    gb_ref,
    gc_ref,
    grate_ref,
    prev_ref,
    carry_ref,
    out_buf,
    in_buf,
    ss,
    rs,
):
    tokens, width = step_ref.shape
    blocks = tokens // 8
    ends = []
    for number, span in enumerate(spans(width)):
        size = span.stop - span.start
        copies = size // LANES
        rates = rate_ref[:, span]

        def replay(block, state, number=number, span=span, copies=copies, rates=rates):
            rows = pl.ds(pl.multiple_of(block * 8, 8), 8)
            steps = step_ref[rows, span]
            drives = steps * act_ref[rows, span]
            keeps = wide(keep_ref[rows, :], copies)
            grads = grad_ref[rows, span]
            for r in range(8):
                at = block * 8 + r
                prev_ref[at, :, span] = state
                decay = jnp.exp(steps[r : r + 1] * rates) * keeps[r : r + 1]
                state = decay * state + drives[r : r + 1] * wide(b_ref[at], copies)
                share = folded(grads[r : r + 1] * state)
                gc_ref[at] = share if number == 0 else gc_ref[at] + share
            return state

        lax.fori_loop(0, blocks, replay, in_ref[:, span])

        def pull(lap, carry, span=span, copies=copies, rates=rates):
            block = blocks - 1 - lap
            rows = pl.ds(pl.multiple_of(block * 8, 8), 8)
            steps = step_ref[rows, span]
            keeps = wide(keep_ref[rows, :], copies)
            grads = grad_ref[rows, span]
            for r in range(7, -1, -1):
                decay = jnp.exp(steps[r : r + 1] * rates) * keeps[r : r + 1]
                adjoint = grads[r : r + 1] * wide(c_ref[block * 8 + r], copies) + carry
                carry = decay * adjoint
            return carry

        ends.append(lax.fori_loop(0, blocks, pull, jnp.zeros((STATE, size), jnp.float32)))
    total_step = jnp.sum(step_ref[...], axis=0, keepdims=True)
    flag = wide(jnp.min(keep_ref[...], axis=0, keepdims=True), width // LANES)
    carry_ref[...] = chain_exchange(
        rate_ref[...],
        total_step,
        flag,
        jnp.concatenate(ends, axis=1),
        True,
        out_buf,
        in_buf,
        (ss, rs),
    )
    for number, span in enumerate(spans(width)):
        size = span.stop - span.start
        copies = size // LANES
        rates = rate_ref[:, span]

        def settle(lap, carries, number=number, span=span, copies=copies, rates=rates):
            carry, rate_total = carries
            block = blocks - 1 - lap
            rows = pl.ds(pl.multiple_of(block * 8, 8), 8)
            steps = step_ref[rows, span]
            drives = steps * act_ref[rows, span]
            keeps = wide(keep_ref[rows, :], copies)
            grads = grad_ref[rows, span]
            alongs, decays = ([None] * 8, [None] * 8)
            for r in range(7, -1, -1):
                at = block * 8 + r
                decay = jnp.exp(steps[r : r + 1] * rates) * keeps[r : r + 1]
                adjoint = grads[r : r + 1] * wide(c_ref[at], copies) + carry
                carry = decay * adjoint
                grad_exp = carry * prev_ref[at, :, span]
                rate_total = rate_total + grad_exp * steps[r : r + 1]
                alongs[r] = jnp.sum(adjoint * wide(b_ref[at], copies), axis=0, keepdims=True)
                decays[r] = jnp.sum(grad_exp * rates, axis=0, keepdims=True)
                share = folded(adjoint * drives[r : r + 1])
                gb_ref[at] = share if number == 0 else gb_ref[at] + share
            along_ref[rows, span] = jnp.concatenate(alongs, axis=0)
            decayed_ref[rows, span] = jnp.concatenate(decays, axis=0)
            return (carry, rate_total)

        _, rate_total = lax.fori_loop(
            0, blocks, settle, (carry_ref[:, span], jnp.zeros((STATE, size), jnp.float32))
        )
        grate_ref[:, span] = rate_total * rates


def scan_backward(step, act, b_wide, c_wide, keep_wide, rates, incoming, grad, collective_id):
    tokens, width = step.shape
    full = jax.ShapeDtypeStruct((tokens, width), jnp.float32)
    return pl.pallas_call(
        scan_backward_kernel,
        out_shape=(
            full,
            full,
            jax.ShapeDtypeStruct(b_wide.shape, jnp.float32),
            jax.ShapeDtypeStruct(c_wide.shape, jnp.float32),
            jax.ShapeDtypeStruct((STATE, width), jnp.float32),
        ),
        in_specs=[pl.BlockSpec(memory_space=pltpu.VMEM)] * 8,
        out_specs=(pl.BlockSpec(memory_space=pltpu.VMEM),) * 5,
        scratch_shapes=[
            pltpu.VMEM((tokens, STATE, width), jnp.float32),
            pltpu.VMEM((STATE, width), jnp.float32),
        ]
        + scan_scratch(width),
        compiler_params=pltpu.CompilerParams(
            collective_id=collective_id, has_side_effects=True, vmem_limit_bytes=VMEM_LIMIT
        ),
        name="scan_backward",
    )(step, act, b_wide, c_wide, keep_wide, rates, incoming, grad)


def everyone_peer_greeting():
    devices, groups, me = flat_place()
    greet_everyone(devices, groups, me)
    return (devices, groups, me)


def one_hot_turned(ids, height):
    numbers = lax.broadcasted_iota(jnp.int32, (height, ids.shape[1]), 0)
    return (numbers == ids).astype(jnp.float32).astype(jnp.bfloat16)


def start_kernel(
    sizes,
    pairs,
    pack_pairs,
    own_vocab,
    number_ref,
    pack_ref,
    master_ref,
    numbers_ref,
    packs_ref,
    own_ref,
    table_ref,
    turned_ref,
    token_ref,
    target_ref,
    full_ref,
    tall_ref,
    pack_sem,
    send_sem,
    recv_sem,
    *scratch,
):
    place = my_place(sizes)
    meet(line_peers(place, sizes))
    _, groups, me = flat_place()
    seqs = sizes["x"] * sizes["core"]
    gather = Gather(sizes, pack_pairs, pack_ref, packs_ref, scratch[:8])
    scatter = Scatter(sizes, pairs, full_ref, own_ref, scratch[8:], False)
    own_pack = pltpu.make_async_copy(
        pack_ref, packs_ref.at[tuple(place[a] for a in NATURAL)], pack_sem
    )
    own_pack.start()

    number_order = ("z", "y", "x", "core")

    def number_copies(phase):
        axis = number_order[phase]
        block = tuple(
            slice(None) if a in number_order[:phase] else place[a] for a in NATURAL
        )
        return [
            pltpu.make_async_remote_copy(
                src_ref=number_ref if phase == 0 else numbers_ref.at[block],
                dst_ref=numbers_ref.at[block],
                send_sem=send_sem.at[phase, by],
                recv_sem=recv_sem.at[phase, by],
                device_id=device_of(moved(place, axis, by, sizes), sizes),
                device_id_type=MESH,
            )
            for by in range(1, sizes[axis])
        ]

    def numbers_next(phase):
        if phase > 0:
            for copy in number_copies(phase - 1):
                copy.wait_recv()
        if phase < 4:
            for copy in number_copies(phase):
                copy.start()

    def weights(turn):
        for phase in range(4, 0, -1):
            if 0 <= turn + 1 - phase < pack_pairs:
                gather.advance(turn + 1 - phase, phase)

    numbers_next(0)
    for pair in range(pack_pairs):
        gather.advance(pair, 0)
    numbers_ref[tuple(place[a] for a in NATURAL)] = number_ref[...]
    numbers_next(1)
    own_pack.wait()
    whole_tiles = own_vocab // 8 * 8
    tall_ref[whole_tiles:] = jnp.zeros_like(tall_ref[whole_tiles:])
    tall_ref[0:own_vocab] = master_ref[...]
    table_ref[...] = tall_ref[0 : table_ref.shape[0]].astype(jnp.bfloat16)
    for first in range(0, tall_ref.shape[0], LANES):
        turned_ref[:, first : first + LANES] = tall_ref[first : first + LANES].T.astype(
            jnp.bfloat16
        )
    numbers_next(2)

    def look_up(pair, seq):
        x, core = seq_place(seq, sizes)
        found = one_hot_turned(token_ref[pl.ds(pair * seqs + seq, 1)], turned_ref.shape[1])
        rows = matmul(turned_ref[...], found).T.astype(jnp.bfloat16)
        full_ref[x, core, :, :, pl.ds(pair * SPAN, SPAN), :] = rows.reshape(
            sizes["z"], sizes["y"], SPAN, D
        )

    per_tile = LANES // SPAN
    lane = lax.broadcasted_iota(jnp.int32, (2 * seqs, LANES), 1)
    for pair in range(pairs):
        for tile in range(groups // per_tile):
            local = jnp.zeros((2 * seqs, LANES), jnp.int32)
            for part in range(per_tile):
                z, y = divmod(tile * per_tile + part, sizes["y"])
                ids = numbers_ref[place["x"], place["core"], z, y, 0 : 2 * seqs]
                ids = pltpu.roll(ids, (part - pair) * SPAN % LANES, 1)
                local = jnp.where(lane // SPAN == part, ids, local)
            local = local - me * own_vocab
            local = jnp.where(local < own_vocab, local, -1)
            lanes = pl.ds(tile * LANES, LANES)
            token_ref[pair * seqs : (pair + 1) * seqs, lanes] = local[0:seqs]
            target_ref[pair * seqs : (pair + 1) * seqs, lanes] = local[seqs:]

    for turn in range(max(pairs + 4, pack_pairs + 3)):
        if turn < pairs:

            def one(seq, carry, turn=turn):
                look_up(turn, seq)
                return carry

            lax.fori_loop(0, seqs, one, 0)
            scatter.launch(turn, 0)
        for phase in range(3, -1, -1):
            if 0 <= turn - 1 - phase < pairs:
                scatter.advance(turn - 1 - phase, phase)
        weights(turn)
        if turn < 2:
            numbers_next(3 + turn)
    for phase in range(4):
        for copy in number_copies(phase):
            copy.wait_send()
    gather.finish()
    scatter.finish()


def start_all(numbers, pack, master, collective_id):
    sizes = axis_sizes()
    natural = tuple(sizes[a] for a in NATURAL)
    devices = lax.axis_size("seq") * lax.axis_size("group")
    tokens = numbers.shape[1]
    pairs, pack_pairs = (tokens // SPAN, pack.shape[0] // SPAN)
    own_vocab = master.shape[0]
    short, long = (-(-own_vocab // 16) * 16, -(-own_vocab // LANES) * LANES)
    spread = (devices * tokens // (SPAN * lax.axis_size("group")), SPAN * lax.axis_size("group"))
    vmem = pl.BlockSpec(memory_space=pltpu.VMEM)
    return pl.pallas_call(
        functools.partial(start_kernel, sizes, pairs, pack_pairs, own_vocab),
        out_shape=(
            jax.ShapeDtypeStruct(natural + numbers.shape, numbers.dtype),
            jax.ShapeDtypeStruct(natural + pack.shape, pack.dtype),
            jax.ShapeDtypeStruct((tokens, D), jnp.float32),
            jax.ShapeDtypeStruct((short, D), jnp.bfloat16),
            jax.ShapeDtypeStruct((D, long), jnp.bfloat16),
            jax.ShapeDtypeStruct(spread, jnp.int32),
            jax.ShapeDtypeStruct(spread, jnp.int32),
        ),
        in_specs=[vmem] * 3,
        out_specs=(vmem, pl.BlockSpec(memory_space=pl.ANY)) + (vmem,) * 5,
        scratch_shapes=[
            pltpu.VMEM(natural + (tokens, D), jnp.bfloat16),
            pltpu.VMEM((long, D), jnp.float32),
            pltpu.SemaphoreType.DMA,
            pltpu.SemaphoreType.DMA((4, max(sizes.values()))),
            pltpu.SemaphoreType.DMA((4, max(sizes.values()))),
        ]
        + gather_semaphores(sizes, pack_pairs)
        + scatter_scratch(sizes, pairs, D, False),
        compiler_params=pltpu.CompilerParams(
            collective_id=collective_id, has_side_effects=True, vmem_limit_bytes=VMEM_LIMIT
        ),
        name="start_all",
    )(numbers, pack, master)


def finish_kernel(
    sizes,
    pairs,
    pack_pairs,
    own_ref,
    pack_ref,
    token_ref,
    head_ref,
    scalar_ref,
    tgrad_ref,
    quarters_ref,
    sums_ref,
    all_ref,
    found_ref,
    mine_ref,
    ring_ref,
    own_sem,
    quarter_send,
    quarter_recv,
    ring_send,
    ring_recv,
    *scratch,
):
    place = my_place(sizes)
    meet(line_peers(place, sizes))
    seqs = sizes["x"] * sizes["core"]
    groups = sizes["z"] * sizes["y"]
    block = groups * SPAN
    height = head_ref.shape[0]
    gather = Gather(sizes, pairs, own_ref, all_ref, scratch[:8])
    scatter = Scatter(sizes, pack_pairs, pack_ref, mine_ref, scratch[8:], True)
    keep_own = pltpu.make_async_copy(
        own_ref, all_ref.at[tuple(place[a] for a in NATURAL)], own_sem
    )
    keep_own.start()

    def spread_table(pair):
        for seq in range(seqs):
            ids = token_ref[pair * seqs + seq : pair * seqs + seq + 1]
            found_ref[:, seq * block : (seq + 1) * block] = one_hot_turned(ids, height)
        rows = all_ref[:, :, :, :, pl.ds(pair * SPAN, SPAN), :].reshape(seqs * block, D)
        update = matmul(found_ref[...], rows)
        tgrad_ref[...] = (head_ref[...] if pair == 0 else tgrad_ref[...]) + update

    seq = place["x"] * sizes["core"] + place["core"]
    started = []
    x_sent, core_sent = ({}, [])

    def send_quarter(pair, axis, held):
        rows = pl.ds(pair * SPAN, SPAN)
        sent = []
        for by in range(1, sizes[axis]):
            number = len(started)
            copy = pltpu.make_async_remote_copy(
                src_ref=quarters_ref.at[held, rows],
                dst_ref=quarters_ref.at[held, rows],
                send_sem=quarter_send.at[number],
                recv_sem=quarter_recv.at[number],
                device_id=device_of(moved(place, axis, by, sizes), sizes),
                device_id_type=MESH,
            )
            copy.start()
            sent.append(copy)
            started.append(copy)
        return sent

    def own_quarter(pair):
        rows = pl.ds(pair * SPAN, SPAN)
        quarters_ref[seq, rows] = mine_ref[rows].astype(jnp.bfloat16)
        x_sent[pair] = send_quarter(pair, "x", seq)

    def pass_quarter(pair):
        for copy in x_sent[pair]:
            copy.wait_recv()
        for x in range(sizes["x"]):
            core_sent.extend(send_quarter(pair, "core", x * sizes["core"] + place["core"]))

    for pair in range(pack_pairs):
        scatter.launch(pair, 0)
        for kind in range(2):
            scatter.kept(kind, pair).start()
    for turn in range(max(pairs + 4, pack_pairs + 3)):
        if 0 <= turn - 4 < pairs:
            gather.advance(turn - 4, 4)
        for phase in range(3, -1, -1):
            if 0 <= turn - phase < pairs:
                gather.advance(turn - phase, phase)
            if 0 <= turn - phase < pack_pairs:
                scatter.advance(turn - phase, phase)
        if 0 <= turn - 3 < pack_pairs:
            own_quarter(turn - 3)
        if 0 <= turn - 4 < pack_pairs:
            pass_quarter(turn - 4)
        if turn == 0:
            keep_own.wait()
        if 0 <= turn - 4 < pairs:
            spread_table(turn - 4)

    square = jnp.sum(tgrad_ref[...] * tgrad_ref[...]) + jnp.sum(mine_ref[...] * mine_ref[...])
    row = lax.broadcasted_iota(jnp.int32, (8, LANES), 0)
    value = scalar_ref[...] + jnp.where(row < 4, square, 0.0)
    first = 0
    ring_started = []
    last_pair = pack_pairs - 1
    for axis in ("core", "x", "y", "z"):
        ring_ref[first + place[axis]] = value
        sent = []
        for by in range(1, sizes[axis]):
            copy = pltpu.make_async_remote_copy(
                src_ref=ring_ref.at[first + place[axis]],
                dst_ref=ring_ref.at[first + place[axis]],
                send_sem=ring_send.at[first + by],
                recv_sem=ring_recv.at[first + by],
                device_id=device_of(moved(place, axis, by, sizes), sizes),
                device_id_type=MESH,
            )
            copy.start()
            sent.append(copy)
        ring_started.extend(sent)
        if axis == "x" and max(pairs + 4, pack_pairs + 3) <= last_pair + 4:
            pass_quarter(last_pair)
        for copy in sent:
            copy.wait_recv()
        value = ring_ref[first]
        for other in range(1, sizes[axis]):
            value = value + ring_ref[first + other]
        first += sizes[axis]
    sums_ref[...] = value
    for copy in core_sent:
        copy.wait_recv()
    for copy in started + ring_started:
        copy.wait_send()
    gather.finish()
    scatter.finish()


def finish_all(rows, packs, token_rows, head_grad, scalars, collective_id):
    sizes = axis_sizes()
    natural = tuple(sizes[a] for a in NATURAL)
    tokens = rows.shape[0]
    seqs = sizes["x"] * sizes["core"]
    pack_rows, pack_width = packs.shape[-2:]
    pairs, pack_pairs = (tokens // SPAN, pack_rows // SPAN)
    slots = sum(sizes.values())
    quarter_copies = (sizes["x"] - 1) + (sizes["core"] - 1) * sizes["x"]
    quarter_copies = max(1, pack_pairs * quarter_copies)
    vmem = pl.BlockSpec(memory_space=pltpu.VMEM)
    return pl.pallas_call(
        functools.partial(finish_kernel, sizes, pairs, pack_pairs),
        out_shape=(
            jax.ShapeDtypeStruct(head_grad.shape, jnp.float32),
            jax.ShapeDtypeStruct((seqs, pack_rows, pack_width), jnp.bfloat16),
            jax.ShapeDtypeStruct((8, LANES), jnp.float32),
        ),
        in_specs=[vmem, pl.BlockSpec(memory_space=pl.ANY), vmem, vmem, vmem],
        out_specs=(vmem,) * 3,
        scratch_shapes=[
            pltpu.VMEM(natural + rows.shape, jnp.bfloat16),
            pltpu.VMEM((head_grad.shape[0], seqs * token_rows.shape[1]), jnp.bfloat16),
            pltpu.VMEM((pack_rows, pack_width), jnp.float32),
            pltpu.VMEM((slots, 8, LANES), jnp.float32),
            pltpu.SemaphoreType.DMA,
            pltpu.SemaphoreType.DMA((quarter_copies,)),
            pltpu.SemaphoreType.DMA((quarter_copies,)),
            pltpu.SemaphoreType.DMA((slots,)),
            pltpu.SemaphoreType.DMA((slots,)),
        ]
        + gather_semaphores(sizes, pairs)
        + scatter_scratch(sizes, pack_pairs, pack_width, True),
        compiler_params=pltpu.CompilerParams(
            collective_id=collective_id, has_side_effects=True, vmem_limit_bytes=VMEM_LIMIT
        ),
        name="finish_all",
    )(rows, packs.reshape(natural + (pack_rows, pack_width)), token_rows, head_grad, scalars)


def side_lanes(router, gain_columns):
    first = gain_columns[:, :1]
    rest = gain_columns[:, 1:]
    gap = LANES - SIDE_LANE - router.shape[1] - gain_columns.shape[1]
    return jnp.concatenate([jnp.pad(router, ((0, 0), (SIDE_LANE, gap))), rest, first], axis=1)


def row_tiles(values):
    return values.reshape(-1, 16, LANES).transpose(1, 0, 2).reshape(16, -1)


def own_pack_of(parts, seq_index, seq_count):
    mixer_in, mixer_x, mixer_out, channel, gains, router = [
        part.astype(jnp.bfloat16) for part in parts
    ]
    rows = mixer_x.shape[0] // seq_count
    some = mixer_in.shape[0] // seq_count
    top = lax.dynamic_slice_in_dim(mixer_in, seq_index * D, D, 1)
    middle = lax.dynamic_slice_in_dim(mixer_out, seq_index * rows, rows, 0)
    x_rows = lax.dynamic_slice_in_dim(mixer_x, seq_index * rows, rows, 0)
    extra = lax.dynamic_slice_in_dim(channel, seq_index * rows, rows, 1).T
    extra = jnp.pad(extra, ((0, 0), (0, LANES - extra.shape[1])))
    sides = lax.dynamic_slice_in_dim(
        side_lanes(router, gains.T), seq_index * some, some, 0
    )
    extra = extra + jnp.pad(sides, ((0, rows - some), (0, 0)))
    bottom = jnp.concatenate([row_tiles(x_rows), row_tiles(extra)], axis=1)
    return jnp.concatenate([top, middle, bottom])


def small_weights(packs, experts_total):
    tall, rows = pack_heights()
    seqs, groups = packs.shape[:2]
    extra = packs[:, :, tall + rows :, D // 2 :].reshape(seqs, groups, 16, rows // 16, LANES)
    extra = extra.transpose(1, 0, 3, 2, 4).reshape(groups, seqs, rows, LANES)
    channel = extra.reshape(-1, LANES)[:, : CONV + 3 + STATE].T
    sides = extra[:, :, : tall // seqs].reshape(D, LANES)
    gains = jnp.concatenate([sides[:, -1:], sides[:, -3:-1]], axis=1).T
    router = sides[:, SIDE_LANE : SIDE_LANE + experts_total]
    return (channel.astype(jnp.float32), gains.astype(jnp.float32), router)


def log_sum(value):
    return jnp.maximum(value, 0.0) + jnp.log1p(jnp.exp(-jnp.abs(value)))


def pack_heights():
    seqs, groups = (lax.axis_size("seq"), lax.axis_size("group"))
    return (D // groups, DI // (seqs * groups))


def collect_middle(packs_ref, outx_ref):
    seqs, groups = packs_ref.shape[:2]
    tall, rows = pack_heights()

    def one(step, carry):
        group, seq = (lax.div(step, seqs), lax.rem(step, seqs))
        start = step * rows
        outx_ref[pl.ds(pl.multiple_of(start, 16), rows), 0:D] = packs_ref[
            seq, group, tall : tall + rows
        ]
        for part in range(rows // 16):
            outx_ref[pl.ds(pl.multiple_of(start + part * 16, 16), 16), D:] = packs_ref[
                seq, group, tall + rows :, part * LANES : (part + 1) * LANES
            ]
        return carry

    lax.fori_loop(0, seqs * groups, one, 0)


def turned_step_weights(outx_ref):
    both = outx_ref[:, D:].astype(jnp.float32)
    lane = lax.broadcasted_iota(jnp.int32, both.shape, 1)
    shifted = pltpu.roll(both, RANK, 1)
    return jnp.where(lane < RANK, shifted, 0.0).astype(jnp.bfloat16)


def mixer_forward_kernel(
    experts_total,
    x_ref,
    packs_ref,
    vec_ref,
    gain_ref,
    mask_ref,
    router_ref,
    mixed_ref,
    moe_ref,
    prob_ref,
    z_ref,
    pad_ref,
    conv_ref,
    act_ref,
    dtin_ref,
    dtpre_ref,
    step_ref,
    b_ref,
    c_ref,
    in_ref,
    y_ref,
    outx_ref,
    keep_ref,
    rate_ref,
    halo_out,
    halo_in,
    out_buf,
    in_buf,
    ss,
    rs,
    halo_send,
    halo_recv,
):
    meet(chain_peers())
    seqs, groups = packs_ref.shape[:2]
    tall, _ = pack_heights()
    me = lax.axis_index("group")
    x = x_ref[...]
    tokens = x.shape[0]
    normed = (x * inverse_rms(x) * gain_ref[0:1]).astype(jnp.bfloat16)
    for seq in range(seqs):
        block = matmul(normed, packs_ref[seq, :, 0:tall, 0:D].reshape(D, D))
        first = seq * D
        if first < DI:
            pad_ref[8:, first : first + D] = block.astype(jnp.bfloat16).astype(jnp.float32)
        else:
            z_ref[:, first - DI : first - DI + D] = block
    halo_out[...] = pad_ref[tokens:]
    halo = pltpu.make_async_remote_copy(
        src_ref=halo_out,
        dst_ref=halo_in,
        send_sem=halo_send,
        recv_sem=halo_recv,
        device_id=(lax.axis_index("seq"), lax.rem(me + 1, groups)),
        device_id_type=MESH,
    )
    halo.start()
    collect_middle(packs_ref, outx_ref)
    rate_ref[...] = -jnp.exp(vec_ref[CONV + 3 : CONV + 3 + STATE])
    keep_ref[...] = jnp.broadcast_to(mask_ref[:, CONV : CONV + 1], keep_ref.shape)
    halo.wait_recv()
    pad_ref[0:8] = halo_in[...] * jnp.where(me > 0, 1.0, 0.0)
    conv = vec_ref[CONV : CONV + 1] + jnp.zeros_like(z_ref)
    for tap in range(CONV):
        first = 9 - CONV + tap
        conv = (
            conv
            + vec_ref[tap : tap + 1]
            * pad_ref[first : first + tokens]
            * mask_ref[:, tap : tap + 1]
        )
    activated = conv * jax.nn.sigmoid(conv)
    conv_ref[...] = conv
    act_ref[...] = activated
    projected = matmul(activated.astype(jnp.bfloat16), outx_ref[:, D:])
    lane = lax.broadcasted_iota(jnp.int32, projected.shape, 1)
    dt_input = jnp.where(lane < RANK, projected, 0.0).astype(jnp.bfloat16)
    dtin_ref[...] = dt_input
    dt_pre = matmul_nt(dt_input, turned_step_weights(outx_ref))
    dtpre_ref[...] = dt_pre
    step_ref[...] = log_sum(dt_pre + vec_ref[CONV + 1 : CONV + 2])
    for n in range(STATE):
        at = RANK + n
        b_ref[:, n, :] = jnp.broadcast_to(projected[:, at : at + 1], (tokens, LANES))
        at = RANK + STATE + n
        c_ref[:, n, :] = jnp.broadcast_to(projected[:, at : at + 1], (tokens, LANES))
    scan_forward_body(
        step_ref,
        act_ref,
        b_ref,
        c_ref,
        keep_ref,
        rate_ref,
        y_ref,
        in_ref,
        out_buf,
        in_buf,
        ss,
        rs,
    )
    scanned = y_ref[...] + vec_ref[CONV + 2 : CONV + 3] * act_ref[...]
    y_ref[...] = scanned
    gate_z = z_ref[...]
    gated = (scanned * (gate_z * jax.nn.sigmoid(gate_z))).astype(jnp.bfloat16)
    mixed = x + matmul(gated, outx_ref[:, :D])
    mixed_ref[...] = mixed
    moe_in = (mixed * inverse_rms(mixed) * gain_ref[1:2]).astype(jnp.bfloat16)
    moe_ref[...] = moe_in
    scores = matmul(moe_in, router_ref[...])
    scores = jnp.where(lane < experts_total, scores, -1e30)
    raised = jnp.exp(scores - jnp.max(scores, axis=1, keepdims=True))
    prob_ref[...] = raised / jnp.sum(raised, axis=1, keepdims=True)
    halo.wait_send()


def mixer_forward_all(x, packs, vectors, gains, masks, router, collective_id):
    tokens = x.shape[0]
    wide_shape = jax.ShapeDtypeStruct((tokens, DI), jnp.float32)
    state_shape = jax.ShapeDtypeStruct((tokens, STATE, LANES), jnp.float32)
    vmem = pl.BlockSpec(memory_space=pltpu.VMEM)
    return pl.pallas_call(
        functools.partial(mixer_forward_kernel, router.shape[1]),
        out_shape=(
            jax.ShapeDtypeStruct((tokens, D), jnp.float32),
            jax.ShapeDtypeStruct((tokens, D), jnp.bfloat16),
            jax.ShapeDtypeStruct((tokens, LANES), jnp.float32),
            wide_shape,
            jax.ShapeDtypeStruct((tokens + 8, DI), jnp.float32),
            wide_shape,
            wide_shape,
            jax.ShapeDtypeStruct((tokens, LANES), jnp.bfloat16),
            wide_shape,
            wide_shape,
            state_shape,
            state_shape,
            jax.ShapeDtypeStruct((STATE, DI), jnp.float32),
            wide_shape,
        ),
        in_specs=[vmem] * 6,
        out_specs=(vmem,) * 14,
        scratch_shapes=[
            pltpu.VMEM((DI, D + LANES), jnp.bfloat16),
            pltpu.VMEM((tokens, LANES), jnp.float32),
            pltpu.VMEM((STATE, DI), jnp.float32),
            pltpu.VMEM((8, DI), jnp.float32),
            pltpu.VMEM((8, DI), jnp.float32),
        ]
        + scan_scratch(DI)
        + [pltpu.SemaphoreType.DMA, pltpu.SemaphoreType.DMA],
        compiler_params=pltpu.CompilerParams(
            collective_id=collective_id, has_side_effects=True, vmem_limit_bytes=VMEM_LIMIT
        ),
        name="mixer_forward",
    )(x, packs, vectors, gains, masks, jnp.pad(router, ((0, 0), (0, LANES - router.shape[1]))))


def mixer_backward_kernel(
    grad_ref,
    side_ref,
    x_ref,
    packs_ref,
    vec_ref,
    gain_ref,
    mask_ref,
    z_ref,
    pad_ref,
    conv_ref,
    act_ref,
    dtin_ref,
    dtpre_ref,
    step_ref,
    b_ref,
    c_ref,
    in_ref,
    y_ref,
    embed_ref,
    gpack_ref,
    outx_ref,
    keep_ref,
    rate_ref,
    scan_grad_ref,
    along_ref,
    decayed_ref,
    gb_ref,
    gc_ref,
    grate_ref,
    prev_ref,
    carry_ref,
    gout_ref,
    both_ref,
    gpad_ref,
    chan_ref,
    turned_ref,
    merged_ref,
    halo_out,
    halo_in,
    out_buf,
    in_buf,
    ss,
    rs,
    halo_send,
    halo_recv,
):
    meet(chain_peers())
    seqs, groups = packs_ref.shape[:2]
    tall, rows = pack_heights()
    me = lax.axis_index("group")
    tokens = x_ref.shape[0]
    collect_middle(packs_ref, outx_ref)
    rate_ref[...] = -jnp.exp(vec_ref[CONV + 3 : CONV + 3 + STATE])
    keep_ref[...] = jnp.broadcast_to(mask_ref[:, CONV : CONV + 1], keep_ref.shape)
    grad_low = grad_ref[...].astype(jnp.bfloat16)
    grad_gated = matmul_nt(grad_low, outx_ref[:, :D])
    gate_z, scanned = (z_ref[...], y_ref[...])
    logistic = jax.nn.sigmoid(gate_z)
    gate_act = gate_z * logistic
    gated = (scanned * gate_act).astype(jnp.bfloat16)
    gout_ref[:, :D] = matmul_tn(gated, grad_low).astype(jnp.bfloat16)
    grad_scan = grad_gated * gate_act
    scan_grad_ref[...] = grad_scan
    grad_z = grad_gated * scanned * (logistic * (1.0 + gate_z * (1.0 - logistic)))
    both_ref[:, DI:] = grad_z.astype(jnp.bfloat16)
    chan_ref[...] = jnp.zeros_like(chan_ref)
    chan_ref[CONV + 2 : CONV + 3] = jnp.sum(grad_scan * act_ref[...], axis=0, keepdims=True)
    scan_backward_body(
        step_ref,
        act_ref,
        b_ref,
        c_ref,
        keep_ref,
        rate_ref,
        in_ref,
        scan_grad_ref,
        along_ref,
        decayed_ref,
        gb_ref,
        gc_ref,
        grate_ref,
        prev_ref,
        carry_ref,
        out_buf,
        in_buf,
        ss,
        rs,
    )
    chan_ref[CONV + 3 : CONV + 3 + STATE] = grate_ref[...]
    along, activated = (along_ref[...], act_ref[...])
    grad_act = scan_grad_ref[...] * vec_ref[CONV + 2 : CONV + 3] + along * step_ref[...]
    grad_step = decayed_ref[...] + along * activated
    grad_dtpre = grad_step * jax.nn.sigmoid(dtpre_ref[...] + vec_ref[CONV + 1 : CONV + 2])
    chan_ref[CONV + 1 : CONV + 2] = jnp.sum(grad_dtpre, axis=0, keepdims=True)
    grad_dtlow = grad_dtpre.astype(jnp.bfloat16)
    grad_wdt = matmul_tn(grad_dtlow, dtin_ref[...])
    grad_proj = matmul(grad_dtlow, turned_step_weights(outx_ref))
    lane = lax.broadcasted_iota(jnp.int32, grad_proj.shape, 1)
    for n in range(STATE):
        for first, ref in ((RANK, gb_ref), (RANK + STATE, gc_ref)):
            column = jnp.sum(ref[:, n, :], axis=1, keepdims=True)
            grad_proj = jnp.where(lane == first + n, column, grad_proj)
    grad_proj = grad_proj.astype(jnp.bfloat16)
    grad_wx = matmul_tn(activated.astype(jnp.bfloat16), grad_proj)
    wide_lane = lax.broadcasted_iota(jnp.int32, grad_wx.shape, 1)
    grad_wx = jnp.where(
        wide_lane < RANK + 2 * STATE, grad_wx, pltpu.roll(grad_wdt, RANK + 2 * STATE, 1)
    )
    gout_ref[:, D:] = grad_wx.astype(jnp.bfloat16)
    grad_act = grad_act + matmul_nt(grad_proj, outx_ref[:, D:])
    conv = conv_ref[...]
    logistic = jax.nn.sigmoid(conv)
    grad_conv = grad_act * (logistic * (1.0 + conv * (1.0 - logistic)))
    chan_ref[CONV : CONV + 1] = jnp.sum(grad_conv, axis=0, keepdims=True)
    gpad_ref[...] = jnp.zeros_like(gpad_ref)
    for tap in range(CONV):
        same = grad_conv * mask_ref[:, tap : tap + 1]
        first = 9 - CONV + tap
        chan_ref[tap : tap + 1] = jnp.sum(
            same * pad_ref[first : first + tokens], axis=0, keepdims=True
        )
        gpad_ref[first : first + tokens] += vec_ref[tap : tap + 1] * same
    halo_out[...] = gpad_ref[0:8]
    halo = pltpu.make_async_remote_copy(
        src_ref=halo_out,
        dst_ref=halo_in,
        send_sem=halo_send,
        recv_sem=halo_recv,
        device_id=(lax.axis_index("seq"), lax.rem(me + groups - 1, groups)),
        device_id_type=MESH,
    )
    halo.start()
    for first in range(0, DI, LANES):
        turned_ref[first : first + LANES] = chan_ref[:, first : first + LANES].T

    def place_middle(step, carry):
        group, seq = (lax.div(step, seqs), lax.rem(step, seqs))
        start = step * rows
        gpack_ref[seq, group, tall : tall + rows] = gout_ref[
            pl.ds(pl.multiple_of(start, 16), rows), 0:D
        ]
        for part in range(rows // 16):
            gpack_ref[seq, group, tall + rows :, part * LANES : (part + 1) * LANES] = gout_ref[
                pl.ds(pl.multiple_of(start + part * 16, 16), 16), D:
            ]
        return carry

    lax.fori_loop(0, seqs * groups, place_middle, 0)
    halo.wait_recv()
    gpad_ref[tokens : tokens + 8] += halo_in[...] * jnp.where(me < groups - 1, 1.0, 0.0)
    both_ref[:, :DI] = gpad_ref[8 : 8 + tokens].astype(jnp.bfloat16)
    x = x_ref[...]
    scale = inverse_rms(x)
    normed = (x * scale * gain_ref[0:1]).astype(jnp.bfloat16)
    grad_normed = jnp.zeros((tokens, D), jnp.float32)
    for seq in range(seqs):
        part = both_ref[:, seq * D : (seq + 1) * D]
        grad_normed += matmul_nt(part, packs_ref[seq, :, 0:tall, 0:D].reshape(D, D))
        gpack_ref[seq, :, 0:tall, 0:D] = (
            matmul_tn(normed, part).astype(jnp.bfloat16).reshape(groups, tall, D)
        )
    scaled = grad_normed * gain_ref[0:1]
    grad_x = scale * scaled - x * scale**3 * jnp.mean(scaled * x, axis=-1, keepdims=True)
    embed_ref[...] = (grad_ref[...] + grad_x).astype(jnp.bfloat16)
    grad_gain = jnp.sum(grad_normed * x * scale, axis=0, keepdims=True)
    grad_gain = jnp.broadcast_to(grad_gain, (LANES, D)).T
    side_lane = lax.broadcasted_iota(jnp.int32, side_ref.shape, 1)
    merged_ref[...] = jnp.where(side_lane == LANES - 1, grad_gain, side_ref[...])
    some = tall // seqs

    def place_extra(step, carry):
        group, seq = (lax.div(step, seqs), lax.rem(step, seqs))
        start = pl.multiple_of(step * rows, 16)
        first = pl.multiple_of(group * tall + seq * some, 8)
        turned_ref[pl.ds(start, some)] += merged_ref[pl.ds(first, some)]
        for part in range(rows // 16):
            lanes = pl.ds(D // 2 + part * LANES, LANES)
            gpack_ref[seq, group, tall + rows :, lanes] = turned_ref[
                pl.ds(pl.multiple_of(start + part * 16, 16), 16)
            ].astype(jnp.bfloat16)
        return carry

    lax.fori_loop(0, seqs * groups, place_extra, 0)
    halo.wait_send()


def mixer_backward_all(grad, sides, x, packs, vectors, gains, masks, saved, collective_id):
    tokens = x.shape[0]
    vmem = pl.BlockSpec(memory_space=pltpu.VMEM)
    wide = (tokens, DI)
    return pl.pallas_call(
        mixer_backward_kernel,
        out_shape=(
            jax.ShapeDtypeStruct((tokens, D), jnp.bfloat16),
            jax.ShapeDtypeStruct(packs.shape, jnp.bfloat16),
        ),
        in_specs=[vmem] * (7 + len(saved)),
        out_specs=(vmem,) * 2,
        scratch_shapes=[
            pltpu.VMEM((DI, D + LANES), jnp.bfloat16),
            pltpu.VMEM((tokens, LANES), jnp.float32),
            pltpu.VMEM((STATE, DI), jnp.float32),
            pltpu.VMEM(wide, jnp.float32),
            pltpu.VMEM(wide, jnp.float32),
            pltpu.VMEM(wide, jnp.float32),
            pltpu.VMEM((tokens, STATE, LANES), jnp.float32),
            pltpu.VMEM((tokens, STATE, LANES), jnp.float32),
            pltpu.VMEM((STATE, DI), jnp.float32),
            pltpu.VMEM((tokens, STATE, DI), jnp.float32),
            pltpu.VMEM((STATE, DI), jnp.float32),
            pltpu.VMEM((DI, D + LANES), jnp.bfloat16),
            pltpu.VMEM((tokens, 2 * DI), jnp.bfloat16),
            pltpu.VMEM((tokens + 8, DI), jnp.float32),
            pltpu.VMEM((LANES, DI), jnp.float32),
            pltpu.VMEM((DI, LANES), jnp.float32),
            pltpu.VMEM((D, LANES), jnp.float32),
            pltpu.VMEM((8, DI), jnp.float32),
            pltpu.VMEM((8, DI), jnp.float32),
        ]
        + scan_scratch(DI)
        + [pltpu.SemaphoreType.DMA, pltpu.SemaphoreType.DMA],
        compiler_params=pltpu.CompilerParams(
            collective_id=collective_id, has_side_effects=True, vmem_limit_bytes=VMEM_LIMIT
        ),
        name="mixer_backward",
    )(grad, sides, x, packs, vectors, gains, masks, *saved)


def update_kernel(quarters_ref, sums_ref, *refs):
    inputs, outputs, turned_ref, side_ref = (refs[:18], refs[18:36], refs[36], refs[37])
    seqs = quarters_ref.shape[0]
    tall, rows = pack_heights()
    norm = jnp.sqrt(sums_ref[0:1, 0:1])
    clip_factor = jnp.minimum(1.0, CLIP / (norm + 1e-06))

    def renew(which, index, gradient, rate):
        master, moment, average = (inputs[3 * which + k] for k in range(3))
        fresh = renewed(
            master[index], moment[index], average[index], gradient, clip_factor, rate
        )
        for k in range(3):
            outputs[3 * which + k][index] = fresh[k]

    for seq in range(seqs):
        columns = slice(seq * D, (seq + 1) * D)
        renew(0, (slice(None), columns), quarters_ref[seq, 0:tall, :D].astype(jnp.float32), LRATE)
        own = slice(seq * rows, (seq + 1) * rows)
        middle = quarters_ref[seq, tall : tall + rows, :].astype(jnp.float32)
        renew(2, (own,), middle, LRATE)
        bottom = quarters_ref[seq, tall + rows :, :].astype(jnp.float32)
        for part in range(rows // 16):
            first = seq * rows + part * 16
            lanes = slice(part * LANES, (part + 1) * LANES)
            renew(1, (slice(first, first + 16),), bottom[:, lanes], LRATE)
            lanes = slice(D // 2 + part * LANES, D // 2 + (part + 1) * LANES)
            turned_ref[first : first + 16] = bottom[:, lanes]
        some = tall // seqs
        side_ref[seq * some : (seq + 1) * some] = turned_ref[seq * rows : seq * rows + some]
    width = inputs[9].shape[1]
    turned_ref[seqs * rows :] = jnp.zeros_like(turned_ref[seqs * rows :])
    side_ref[tall:] = jnp.zeros_like(side_ref[tall:])
    everything = (slice(None),)
    renew(3, everything, turned_ref[...].T[0 : CONV + 3 + STATE, 0:width], CHANNEL_LRATE)
    gains = side_ref[...].T[:, 0:tall]
    renew(4, everything, jnp.concatenate([gains[-1:], gains[-3:-1]], axis=0), LRATE)
    router_lanes = slice(SIDE_LANE, SIDE_LANE + inputs[15].shape[0])
    renew(5, everything, side_ref[...].T[router_lanes, 0:tall], LRATE)


def update_all(quarters, sums, states):
    vmem = pl.BlockSpec(memory_space=pltpu.VMEM)
    flat = [part for state in states for part in state]
    tall, rows = pack_heights()
    height = -(-quarters.shape[0] * rows // LANES) * LANES
    return pl.pallas_call(
        update_kernel,
        out_shape=tuple(jax.ShapeDtypeStruct(part.shape, part.dtype) for part in flat),
        in_specs=[vmem] * (2 + len(flat)),
        out_specs=(vmem,) * len(flat),
        scratch_shapes=[
            pltpu.VMEM((height, LANES), jnp.float32),
            pltpu.VMEM((-(-tall // LANES) * LANES, LANES), jnp.float32),
        ],
        compiler_params=pltpu.CompilerParams(vmem_limit_bytes=VMEM_LIMIT),
        name="update_all",
    )(quarters, sums, *flat)


def pick_slots(slot_ref, block, slots):
    numbers = lax.broadcasted_iota(jnp.int32, (slots, slot_ref.shape[1]), 0)
    return (numbers == slot_ref[pl.ds(block, 1)]).astype(jnp.float32).astype(jnp.bfloat16)


def natural_place(block, sizes):
    return unravel(block, tuple(sizes[a] for a in NATURAL))


def rows_to_slots(sizes, capacity, slot_ref, all_ref, slots_ref):
    experts_here = slots_ref.shape[0]

    def one(block, carry):
        select = pick_slots(slot_ref, block, experts_here * capacity)
        picked = matmul(select, all_ref[block]).astype(jnp.bfloat16)
        first = pl.multiple_of(block * capacity, capacity)
        for expert in range(experts_here):
            slots_ref[expert, pl.ds(first, capacity)] = picked[
                expert * capacity : (expert + 1) * capacity
            ]
        return carry

    lax.fori_loop(0, slot_ref.shape[0], one, 0, unroll=8)


def slots_to_rows(sizes, capacity, slot_ref, slots_ref, full_ref):
    experts_here = slots_ref.shape[0]

    def one(block, carry):
        select = pick_slots(slot_ref, block, experts_here * capacity)
        first = pl.multiple_of(block * capacity, capacity)
        held = jnp.concatenate(
            [slots_ref[expert, pl.ds(first, capacity)] for expert in range(experts_here)], axis=0
        )
        full_ref[natural_place(block, sizes)] = matmul_tn(select, held).astype(jnp.bfloat16)
        return carry

    lax.fori_loop(0, slot_ref.shape[0], one, 0, unroll=8)


def flat_gather_semaphores(devices, rows):
    copies = (devices - 1) * len(split_rows(rows, GATHER_ORDERS))
    return [pltpu.SemaphoreType.DMA((copies,)), pltpu.SemaphoreType.DMA((copies,))]


def moe_forward_kernel(
    sizes,
    pairs,
    capacity,
    own_ref,
    slot_ref,
    weights_ref,
    result_ref,
    arrived_ref,
    before_ref,
    all_ref,
    part_ref,
    full_ref,
    local_sem,
    *scratch,
):
    pieces = split_rows(own_ref.shape[0], GATHER_ORDERS)
    gather_kernel(sizes, pieces, own_ref, all_ref, local_sem, scratch[0], scratch[1])
    scatter = Scatter(sizes, pairs, full_ref, result_ref, scratch[2:], False)
    rows_to_slots(sizes, capacity, slot_ref, all_ref, arrived_ref)

    def expert(number, carry):
        before = matmul_nt(arrived_ref[number], weights_ref[0, number])
        before_ref[number] = before
        inner = jax.nn.gelu(before).astype(jnp.bfloat16)
        part_ref[number] = matmul(inner, weights_ref[1, number]).astype(jnp.bfloat16)
        return carry

    lax.fori_loop(0, weights_ref.shape[1], expert, 0)
    slots_to_rows(sizes, capacity, slot_ref, part_ref, full_ref)
    for pair in range(pairs):
        scatter.launch(pair, 0)
    wave(pairs, 4, scatter.advance)
    scatter.finish()


def moe_forward(rows, slots, weights, capacity, collective_id):
    sizes = axis_sizes()
    natural = tuple(sizes[a] for a in NATURAL)
    pairs = rows.shape[0] // SPAN
    _, experts_here, hidden, _ = weights.shape
    held = (experts_here, slots.shape[0] * capacity)
    vmem = pl.BlockSpec(memory_space=pltpu.VMEM)
    return pl.pallas_call(
        functools.partial(moe_forward_kernel, sizes, pairs, capacity),
        out_shape=(
            jax.ShapeDtypeStruct(rows.shape, jnp.float32),
            jax.ShapeDtypeStruct(held + (D,), jnp.bfloat16),
            jax.ShapeDtypeStruct(held + (hidden,), jnp.float32),
        ),
        in_specs=[vmem] * 3,
        out_specs=(vmem,) * 3,
        scratch_shapes=[
            pltpu.VMEM((slots.shape[0],) + rows.shape, jnp.bfloat16),
            pltpu.VMEM(held + (D,), jnp.bfloat16),
            pltpu.VMEM(natural + rows.shape, jnp.bfloat16),
            pltpu.SemaphoreType.DMA,
        ]
        + flat_gather_semaphores(slots.shape[0], rows.shape[0])
        + scatter_scratch(sizes, pairs, D, False),
        compiler_params=pltpu.CompilerParams(
            collective_id=collective_id, has_side_effects=True, vmem_limit_bytes=VMEM_LIMIT
        ),
        name="moe_forward",
    )(rows, slots, weights)


def moe_backward_kernel(
    sizes,
    pairs,
    capacity,
    own_ref,
    slot_ref,
    weights_ref,
    arrived_ref,
    before_ref,
    result_ref,
    grads_ref,
    square_ref,
    all_ref,
    part_ref,
    full_ref,
    slots_ref,
    local_sem,
    *scratch,
):
    pieces = split_rows(own_ref.shape[0], GATHER_ORDERS)
    gather_kernel(sizes, pieces, own_ref, all_ref, local_sem, scratch[0], scratch[1])
    scatter = Scatter(sizes, pairs, full_ref, result_ref, scratch[2:], False)
    rows_to_slots(sizes, capacity, slot_ref, all_ref, slots_ref)

    def slope(number):
        grad_inner = matmul_nt(slots_ref[number], weights_ref[1, number])
        return jax.vjp(jax.nn.gelu, before_ref[number])[1](grad_inner)[0].astype(jnp.bfloat16)

    def back(number, carry):
        part_ref[number] = matmul(slope(number), weights_ref[0, number]).astype(jnp.bfloat16)
        return carry

    experts_here = weights_ref.shape[1]
    lax.fori_loop(0, experts_here, back, 0)
    slots_to_rows(sizes, capacity, slot_ref, part_ref, full_ref)
    for pair in range(pairs):
        scatter.launch(pair, 0)

    def weight_grads(number, total):
        grad_up = matmul_tn(slope(number), arrived_ref[number])
        inner = jax.nn.gelu(before_ref[number]).astype(jnp.bfloat16)
        grad_down = matmul_tn(inner, slots_ref[number])
        grads_ref[0, number] = grad_up
        grads_ref[1, number] = grad_down
        return total + jnp.sum(grad_up * grad_up) + jnp.sum(grad_down * grad_down)

    total = jnp.float32(0.0)
    turns = pairs + 3
    for turn in range(turns):
        for phase in range(3, -1, -1):
            if 0 <= turn - phase < pairs:
                scatter.advance(turn - phase, phase)
        first, last = (experts_here * turn // (turns - 1), experts_here * (turn + 1) // (turns - 1))
        if last > first and first < experts_here:
            total = lax.fori_loop(first, min(last, experts_here), weight_grads, total)
    square_ref[...] = jnp.full(square_ref.shape, total, jnp.float32)
    scatter.finish()


def moe_backward(rows, slots, weights, arrived, before, capacity, collective_id):
    sizes = axis_sizes()
    natural = tuple(sizes[a] for a in NATURAL)
    pairs = rows.shape[0] // SPAN
    vmem = pl.BlockSpec(memory_space=pltpu.VMEM)
    return pl.pallas_call(
        functools.partial(moe_backward_kernel, sizes, pairs, capacity),
        out_shape=(
            jax.ShapeDtypeStruct(rows.shape, jnp.float32),
            jax.ShapeDtypeStruct(weights.shape, jnp.float32),
            jax.ShapeDtypeStruct((8, LANES), jnp.float32),
        ),
        in_specs=[vmem] * 5,
        out_specs=(vmem,) * 3,
        scratch_shapes=[
            pltpu.VMEM((slots.shape[0],) + rows.shape, jnp.bfloat16),
            pltpu.VMEM(arrived.shape, jnp.bfloat16),
            pltpu.VMEM(natural + rows.shape, jnp.bfloat16),
            pltpu.VMEM(arrived.shape, jnp.bfloat16),
            pltpu.SemaphoreType.DMA,
        ]
        + flat_gather_semaphores(slots.shape[0], rows.shape[0])
        + scatter_scratch(sizes, pairs, D, False),
        compiler_params=pltpu.CompilerParams(
            collective_id=collective_id, has_side_effects=True, vmem_limit_bytes=VMEM_LIMIT
        ),
        name="moe_backward",
    )(rows, slots, weights, arrived, before)


def from_behind(value, axis, by):
    devices = lax.axis_size(axis)
    pairs = [(i, i + by) for i in range(devices) if 0 <= i + by < devices]
    return lax.ppermute(value, axis, pairs)


def matmul(left, right):
    return jnp.dot(left, right, preferred_element_type=jnp.float32)


def matmul_nt(left, right):
    return lax.dot_general(
        left, right, (((1,), (1,)), ((), ())), preferred_element_type=jnp.float32
    )


def matmul_tn(left, right):
    return lax.dot_general(
        left, right, (((0,), (0,)), ((), ())), preferred_element_type=jnp.float32
    )


def silu_slope(preact):
    logistic = jax.nn.sigmoid(preact)
    return logistic * (1.0 + preact * (1.0 - logistic))


def inverse_rms(values):
    return lax.rsqrt(jnp.mean(values * values, axis=-1, keepdims=True) + EPS)


def norm_back(values, inv_scale, gain_row, grad_in):
    scaled = grad_in * gain_row
    grad_gain = jnp.sum(grad_in * values * inv_scale, axis=0)
    grad_values = inv_scale * scaled - values * inv_scale**3 * jnp.mean(
        scaled * values, axis=-1, keepdims=True
    )
    return (grad_values, grad_gain)


def neighbour_rows(edge_rows, offset):
    return from_behind(edge_rows, "group", offset)


def doc_layout(doc_lengths, first_pos, span_len):
    doc_ends = jnp.cumsum(doc_lengths, axis=1)
    doc_begins = doc_ends - doc_lengths
    where_at = first_pos + jnp.arange(span_len, dtype=jnp.int32)
    segment = jnp.sum((where_at[None, :, None] >= doc_ends[:, None, :]).astype(jnp.int32), axis=2)
    onehot_doc = (
        segment[:, :, None] == jnp.arange(doc_lengths.shape[1], dtype=jnp.int32)[None, None, :]
    ).astype(jnp.float32)
    weight = jnp.sum(onehot_doc / doc_lengths[:, None, :].astype(jnp.float32), axis=2)
    starting = jnp.sum(
        (where_at[None, :, None] == doc_begins[:, None, :]).astype(jnp.float32), axis=2
    )
    return (segment, weight, 1.0 - starting)


def spread_weights(doc_lengths, tokens, groups):
    ends = jnp.cumsum(doc_lengths, axis=1)
    begins = ends - doc_lengths
    shape = (tokens // SPAN, groups * SPAN)
    pair, lane = (lax.broadcasted_iota(jnp.int32, shape, axis) for axis in range(2))
    where_at = (lane // SPAN * tokens + pair * SPAN + lane % SPAN)[:, None, :]
    total = jnp.zeros((shape[0], doc_lengths.shape[0], shape[1]), jnp.float32)
    for doc in range(doc_lengths.shape[1]):
        inside = (where_at >= begins[None, :, doc, None]) & (where_at < ends[None, :, doc, None])
        share = 1.0 / doc_lengths[:, doc].astype(jnp.float32)
        total = total + jnp.where(inside, share[None, :, None], 0.0)
    return total.reshape(-1, shape[1])


def lane_copies(columns):
    return jnp.broadcast_to(columns[..., None], columns.shape + (LANES,))


def mixer_forward(embedded, segment, keeping, weight_in, weight_x, weight_out, channel, gain_row):
    tokens = embedded.shape[0]
    scale_in = inverse_rms(embedded)
    normed = (embedded * scale_in * gain_row).astype(jnp.bfloat16)
    projected_in = matmul(normed, weight_in)
    conv_input = projected_in[:, :DI].astype(jnp.bfloat16)
    gate_z = projected_in[:, DI:]
    rim_rows = neighbour_rows(conv_input[tokens - CONV + 1 :].astype(jnp.float32), 1)
    padded = jnp.concatenate([rim_rows, conv_input.astype(jnp.float32)])
    same_doc = [
        (segment[conv_tap : conv_tap + tokens] == segment[CONV - 1 :]).astype(jnp.float32)[:, None]
        for conv_tap in range(CONV)
    ]
    conv_out = channel[CONV] + jnp.zeros_like(padded[CONV - 1 :])
    for conv_tap in range(CONV):
        conv_out = (
            conv_out + channel[conv_tap] * padded[conv_tap : conv_tap + tokens] * same_doc[conv_tap]
        )
    activated = jax.nn.silu(conv_out)
    act_low = activated.astype(jnp.bfloat16)
    projected = matmul(act_low, weight_x[:, : RANK + 2 * STATE])
    dt_input = projected[:, :RANK].astype(jnp.bfloat16)
    dt_pre = matmul_nt(dt_input, weight_x[:, RANK + 2 * STATE :])
    step_size = jax.nn.softplus(dt_pre + channel[CONV + 1])
    decay_rates = -jnp.exp(channel[CONV + 3 :])
    b_wide = lane_copies(projected[:, RANK : RANK + STATE])
    c_wide = lane_copies(projected[:, RANK + STATE :])
    keep_wide = lane_copies(keeping)
    reached, incoming = scan_forward(
        step_size, activated, b_wide, c_wide, keep_wide, decay_rates, 4
    )
    scanned = reached + channel[CONV + 2] * activated
    gate_act = jax.nn.silu(gate_z)
    gated = (scanned * gate_act).astype(jnp.bfloat16)
    mixed_out = embedded + matmul(gated, weight_out)
    kept_values = (
        scale_in,
        normed,
        gate_z,
        padded,
        same_doc,
        conv_out,
        activated,
        act_low,
        b_wide,
        c_wide,
        keep_wide,
        dt_input,
        dt_pre,
        step_size,
        decay_rates,
        incoming,
        scanned,
        gate_act,
        gated,
    )
    return (mixed_out, kept_values)


def mixer_backward(
    grad_out, embedded, kept_values, weight_in, weight_x, weight_out, channel, gain_row
):
    (
        scale_in,
        normed,
        gate_z,
        padded,
        same_doc,
        conv_out,
        activated,
        act_low,
        b_wide,
        c_wide,
        keep_wide,
        dt_input,
        dt_pre,
        step_size,
        decay_rates,
        incoming,
        scanned,
        gate_act,
        gated,
    ) = kept_values
    tokens = embedded.shape[0]
    grad_low = grad_out.astype(jnp.bfloat16)
    grad_wout = matmul_tn(gated, grad_low)
    grad_gated = matmul_nt(grad_low, weight_out)
    grad_scan = grad_gated * gate_act
    grad_z = grad_gated * scanned * silu_slope(gate_z)
    grad_skip = jnp.sum(grad_scan * activated, axis=0)
    along_b, decayed, wide_gb, wide_gc, grad_rates_log = scan_backward(
        step_size, activated, b_wide, c_wide, keep_wide, decay_rates, incoming, grad_scan, 5
    )
    grad_b = jnp.sum(wide_gb, axis=2)
    grad_c = jnp.sum(wide_gc, axis=2)
    grad_act = grad_scan * channel[CONV + 2] + along_b * step_size
    grad_step = decayed + along_b * activated
    grad_dtpre = grad_step * jax.nn.sigmoid(dt_pre + channel[CONV + 1])
    grad_dtbias = jnp.sum(grad_dtpre, axis=0)
    grad_dtlow = grad_dtpre.astype(jnp.bfloat16)
    grad_wdt = matmul_tn(grad_dtlow, dt_input)
    grad_dtin = matmul(grad_dtlow, weight_x[:, RANK + 2 * STATE :])
    grad_proj = jnp.concatenate([grad_dtin, grad_b, grad_c], axis=1).astype(jnp.bfloat16)
    grad_wx = jnp.concatenate([matmul_tn(act_low, grad_proj), grad_wdt], axis=1)
    grad_act = grad_act + matmul_nt(grad_proj, weight_x[:, : RANK + 2 * STATE])
    grad_conv = grad_act * silu_slope(conv_out)
    grad_taps = [
        jnp.sum(grad_conv * padded[conv_tap : conv_tap + tokens] * same_doc[conv_tap], axis=0)
        for conv_tap in range(CONV)
    ]
    grad_padded = sum(
        (
            jnp.pad(
                channel[conv_tap] * grad_conv * same_doc[conv_tap],
                ((conv_tap, CONV - 1 - conv_tap), (0, 0)),
            )
            for conv_tap in range(CONV)
        )
    )
    from_next = neighbour_rows(grad_padded[: CONV - 1], -1)
    grad_input = grad_padded[CONV - 1 :] + jnp.pad(from_next, ((tokens - CONV + 1, 0), (0, 0)))
    grad_both = jnp.concatenate([grad_input, grad_z], axis=1).astype(jnp.bfloat16)
    grad_win = matmul_tn(normed, grad_both)
    grad_normed = matmul_nt(grad_both, weight_in)
    grad_embed, grad_gain = norm_back(embedded, scale_in, gain_row, grad_normed)
    grad_channel = jnp.concatenate(
        [
            jnp.stack(grad_taps),
            jnp.sum(grad_conv, axis=0)[None],
            grad_dtbias[None],
            grad_skip[None],
            grad_rates_log,
        ]
    )
    return (grad_out + grad_embed, grad_win, grad_wx, grad_wout, grad_channel, grad_gain)


def choice_of(route_flat, experts_total):
    return (route_flat[:, None] == jnp.arange(experts_total, dtype=jnp.int32)[None, :]).astype(
        jnp.float32
    )


def dispatch_slots(routes, first_expert, experts_here, capacity):
    tokens = routes.shape[1]
    chosen = (
        routes[:, :, None] == first_expert + jnp.arange(experts_here, dtype=jnp.int32)
    ).astype(jnp.float32)
    earlier = jnp.cumsum(chosen, axis=1) - chosen
    rank = jnp.sum(earlier * chosen, axis=2).astype(jnp.int32)
    local = routes - first_expert
    return jnp.where((local >= 0) & (local < experts_here), local * capacity + rank, -1)


def dispatch_table(slot, experts_here, capacity):
    return (
        slot[:, None, :] == jnp.arange(experts_here * capacity, dtype=jnp.int32)[None, :, None]
    ).astype(jnp.bfloat16)


def to_slots(select, rows, experts_here, capacity):
    slots = jnp.einsum("bst,btd->bsd", select, rows, preferred_element_type=jnp.float32)
    slots = slots.astype(jnp.bfloat16).reshape(-1, experts_here, capacity, D)
    return jnp.swapaxes(slots, 0, 1).reshape(experts_here, -1, D)


def to_rows(select, slots, capacity):
    experts_here = slots.shape[0]
    slots = slots.astype(jnp.bfloat16).reshape(experts_here, -1, capacity, D)
    slots = jnp.swapaxes(slots, 0, 1).reshape(-1, experts_here * capacity, D)
    return jnp.einsum("bst,bsd->btd", select, slots, preferred_element_type=jnp.float32).astype(
        jnp.bfloat16
    )


def packed_rows(arrays, devices_seq):
    flat = jnp.concatenate([part.reshape(-1) for part in arrays])
    unit = devices_seq * SPAN * D
    size = -(-flat.shape[0] // unit) * unit
    return jnp.pad(flat, (0, size - flat.shape[0])).reshape(-1, D)


def unpacked(flat, shapes):
    parts, first = ([], 0)
    for shape in shapes:
        size = 1
        for extent in shape:
            size *= extent
        parts.append(flat[..., first : first + size].reshape(flat.shape[:-1] + shape))
        first += size
    return parts


def whole_of(shards, axis):
    moved_axis = jnp.moveaxis(shards, 0, axis)
    shape = moved_axis.shape
    return moved_axis.reshape(shape[:axis] + (shape[axis] * shape[axis + 1],) + shape[axis + 2 :])


def shards_of(whole, axis, count):
    shape = whole.shape
    split = whole.reshape(shape[:axis] + (count, shape[axis] // count) + shape[axis + 1 :])
    return jnp.moveaxis(split, axis, 0)


def renewed(master, moment, average, gradient, clip_factor, rate):
    scaled = clip_factor * gradient
    moment_new = MOMENTUM * moment + scaled
    master_new = master - rate * (scaled + MOMENTUM * moment_new)
    return (master_new, moment_new, EMA_KEEP * average + (1.0 - EMA_KEEP) * master_new)


def per_device(
    token_ids,
    target_ids,
    doc_lengths,
    expert_ids,
    vocab_table,
    vocab_table_mom,
    vocab_table_ema,
    mixer_in,
    mixer_in_mom,
    mixer_in_ema,
    mixer_x,
    mixer_x_mom,
    mixer_x_ema,
    mixer_out,
    mixer_out_mom,
    mixer_out_ema,
    channel,
    channel_mom,
    channel_ema,
    norm_gains,
    norm_gains_mom,
    norm_gains_ema,
    router,
    router_mom,
    router_ema,
    experts,
    experts_mom,
    experts_ema,
):
    seq_count = lax.axis_size("seq")
    group_count = lax.axis_size("group")
    seq_index = lax.axis_index("seq")
    group_index = lax.axis_index("group")
    devices = seq_count * group_count
    tokens = token_ids.shape[1]
    sequences = token_ids.shape[0]
    experts_total = router.shape[1]
    local_experts = experts.shape[1]
    capacity = max(2, 2 * tokens // experts_total)
    own_vocab = vocab_table.shape[0]
    routes = expert_ids.reshape(1, tokens)
    numbers = jnp.concatenate([token_ids, target_ids, routes])
    numbers = jnp.pad(numbers, ((0, -numbers.shape[0] % 8), (0, 0)))
    mixer_parts = (mixer_in, mixer_x, mixer_out, channel, norm_gains, router)
    part_axes = (0, 0, 0, 1, 1, 0)
    part_shapes = [part.shape for part in mixer_parts]
    table_low = vocab_table.astype(jnp.bfloat16)
    experts_low = experts.astype(jnp.bfloat16)
    up_weight, down_weight = (experts_low[0], experts_low[1])
    vocab_start = (seq_index * group_count + group_index) * own_vocab
    column_ids = jnp.arange(own_vocab, dtype=jnp.int32)
    wide_rows = DI // (seq_count * group_count)
    compact = devices * tokens <= 4096 and 2 * DI == seq_count * D and 16 * wide_rows == D
    if compact:
        own_pack = own_pack_of(mixer_parts, seq_index, seq_count)
        numbers_all, packs, embedded, table_padded, table_turned, token_local, target_local = (
            start_all(numbers, own_pack, vocab_table, 1)
        )
        numbers_all = numbers_all.reshape((devices,) + numbers.shape)
        packs = packs.reshape((seq_count, group_count) + own_pack.shape)
        channel_vals, gain_vals, router_low = small_weights(packs, experts_total)
        router_vals = router_low.astype(jnp.float32)
    else:
        numbers_all = share_small(numbers, 1)
    from_groups = jnp.swapaxes(numbers_all[:group_count, : 2 * sequences], 0, 1)
    tokens_all = from_groups[:sequences].reshape(-1)
    targets_all = from_groups[sequences:].reshape(-1)
    routes_all = numbers_all[:, 2 * sequences]
    if not compact:
        pack = packed_rows([part.astype(jnp.bfloat16) for part in mixer_parts], seq_count)
        pack_rows = pack.shape[0] // seq_count
        own_pack = lax.dynamic_slice_in_dim(pack, seq_index * pack_rows, pack_rows, 0)
        packs = gather_all(own_pack, 2).reshape(seq_count, group_count, pack_rows * D)
        shards = unpacked(jnp.swapaxes(packs, 0, 1).reshape(group_count, -1), part_shapes)
        weight_in, weight_x, weight_out, channel_low, gains_low, router_low = [
            whole_of(shard, axis) for shard, axis in zip(shards, part_axes)
        ]
        held_token = (tokens_all - vocab_start)[:, None] == column_ids[None, :]
        held_token = held_token.astype(jnp.bfloat16)
        looked_up = matmul(held_token, table_low).astype(jnp.bfloat16)
        embedded = scatter_all(looked_up.reshape(devices, tokens, D), 3)
        channel_vals = channel_low.astype(jnp.float32)
        gain_vals = gains_low.astype(jnp.float32)
        router_vals = router_low.astype(jnp.float32)

    segment_all, weight_all, keep_all = doc_layout(
        doc_lengths, group_index * tokens - CONV + 1, tokens + CONV - 1
    )
    own_segment = lax.dynamic_index_in_dim(segment_all, seq_index, 0, keepdims=False)
    keeping = lax.dynamic_index_in_dim(keep_all, seq_index, 0, keepdims=False)[CONV - 1 :]
    own_weight = lax.dynamic_index_in_dim(weight_all, seq_index, 0, keepdims=False)[CONV - 1 :]
    chosen = choice_of(expert_ids.reshape(-1), experts_total)
    if compact:
        same = [
            (own_segment[tap : tap + tokens] == own_segment[CONV - 1 :]).astype(jnp.float32)
            for tap in range(CONV)
        ]
        masks = jnp.stack(same + [keeping], axis=1)
        vectors = jnp.pad(channel_vals, ((0, 1), (0, 0)))
        mixed_out, moe_in, probability, *saved = mixer_forward_all(
            embedded, packs, vectors, gain_vals, masks, router_low, 4
        )
        probability = probability[:, :experts_total]
        scale_mid = inverse_rms(mixed_out)
    else:
        mixed_out, kept_values = mixer_forward(
            embedded,
            own_segment,
            keeping,
            weight_in,
            weight_x,
            weight_out,
            channel_vals,
            gain_vals[0],
        )
        scale_mid = inverse_rms(mixed_out)
        moe_in = (mixed_out * scale_mid * gain_vals[1]).astype(jnp.bfloat16)
        probability = jax.nn.softmax(matmul(moe_in, router_low), axis=-1)
    slots = dispatch_slots(routes_all, seq_index * local_experts, local_experts, capacity)
    gate_value = jnp.sum(probability * chosen, axis=1)
    if compact:
        returned, arrived, before = moe_forward(
            moe_in, slots, experts_low, capacity, 11
        )
    else:
        select = dispatch_table(slots, local_experts, capacity)
        arrived = to_slots(select, gather_all(moe_in, 6), local_experts, capacity)
        before = jnp.einsum("erd,efd->erf", arrived, up_weight, preferred_element_type=jnp.float32)
        inner_act = jax.nn.gelu(before).astype(jnp.bfloat16)
        partial_out = jnp.einsum(
            "erf,efd->erd", inner_act, down_weight, preferred_element_type=jnp.float32
        )
        returned = scatter_all(to_rows(select, partial_out, capacity), 3)
    expert_value = returned.astype(jnp.bfloat16).astype(jnp.float32)
    branch = gate_value[:, None] * expert_value
    hidden = mixed_out + branch
    scale_out = inverse_rms(hidden)
    final_low = (hidden * scale_out * gain_vals[2]).astype(jnp.bfloat16)
    if compact:
        all_final, stats = head_forward(final_low, table_padded, own_vocab, target_local, 7)
        own_entropy = (stats[0] - stats[1]).reshape(-1, seq_count, group_count, SPAN)
        own_entropy = lax.dynamic_index_in_dim(own_entropy, seq_index, 1, keepdims=False)
        own_entropy = lax.dynamic_index_in_dim(own_entropy, group_index, 1, keepdims=False)
        loss_part = jnp.sum(own_weight * own_entropy.reshape(-1))
        grad_final, table_grad = head_backward(
            all_final,
            table_padded,
            table_turned,
            own_vocab,
            target_local,
            stats[0],
            spread_weights(doc_lengths, tokens, group_count),
            10,
        )
    else:
        all_final = gather_all(final_low, 6).reshape(devices * tokens, D)
        valid_cols = vocab_start + column_ids < VOCAB_REAL
        hit_target = (targets_all - vocab_start)[:, None] == column_ids[None, :]
        logits = jnp.where(valid_cols[None, :], matmul_nt(all_final, table_low), -1e30)
        largest = jnp.max(logits, axis=1)
        exp_total = jnp.sum(jnp.exp(logits - largest[:, None]), axis=1)
        picked = jnp.sum(jnp.where(hit_target, logits, 0.0), axis=1)
        parts = jnp.stack([largest, exp_total, picked]).reshape(3, devices, tokens)
        parts = jnp.pad(jnp.swapaxes(parts, 0, 1), ((0, 0), (0, 5), (0, 0)))
        levels, entropy = combine_stats(parts, 7)
        log_total = levels[:, 0].reshape(-1)
        loss_part = jnp.sum(own_weight * entropy[0])
        _, every_weight, _ = doc_layout(doc_lengths, 0, tokens * group_count)
        row_weight = every_weight.reshape(-1)
        grad_logits = (
            row_weight[:, None]
            * (jnp.exp(logits - log_total[:, None]) - hit_target.astype(jnp.float32))
        ).astype(jnp.bfloat16)
        table_grad = matmul_tn(grad_logits, all_final)
        grad_rows = matmul(grad_logits, table_low).astype(jnp.bfloat16)
        grad_final = scatter_all(grad_rows.reshape(devices, tokens, D), 3)
    grad_hidden, grad_gain_out = norm_back(hidden, scale_out, gain_vals[2], grad_final)
    grad_gate = jnp.sum(grad_hidden * expert_value, axis=1)
    grad_expert = (gate_value[:, None] * grad_hidden).astype(jnp.bfloat16)
    if compact:
        grad_moe_in, grad_experts, square_tile = moe_backward(
            grad_expert, slots, experts_low, arrived, before, capacity, 12
        )
        experts_square = square_tile[0, 0]
    else:
        grad_arrived = to_slots(select, gather_all(grad_expert, 6), local_experts, capacity)
        grad_inner = jnp.einsum(
            "erd,efd->erf", grad_arrived, down_weight, preferred_element_type=jnp.float32
        )
        grad_before = jax.vjp(jax.nn.gelu, before)[1](grad_inner)[0].astype(jnp.bfloat16)
        grad_down = jnp.einsum(
            "erf,erd->efd", inner_act, grad_arrived, preferred_element_type=jnp.float32
        )
        grad_up = jnp.einsum("erf,erd->efd", grad_before, arrived, preferred_element_type=jnp.float32)
        grad_part = jnp.einsum(
            "erf,efd->erd", grad_before, up_weight, preferred_element_type=jnp.float32
        )
        grad_moe_in = scatter_all(to_rows(select, grad_part, capacity), 3)
        grad_experts = jnp.stack([grad_up, grad_down])
        experts_square = jnp.sum(grad_experts * grad_experts)
    grad_moe_in = grad_moe_in.astype(jnp.bfloat16).astype(jnp.float32)
    grad_router_logits = (grad_gate * gate_value)[:, None] * (chosen - probability)
    grad_moe_in = grad_moe_in + jnp.dot(
        grad_router_logits, router_vals.T, precision=HIGHEST
    )
    grad_router = jnp.dot(moe_in.astype(jnp.float32).T, grad_router_logits, precision=HIGHEST)
    grad_mid, grad_gain_mid = norm_back(mixed_out, scale_mid, gain_vals[1], grad_moe_in)
    grad_mixed = grad_hidden + grad_mid
    if compact:
        gain_columns = jnp.stack([grad_gain_out * 0.0, grad_gain_mid, grad_gain_out], axis=1)
        grad_embedded, grad_pack = mixer_backward_all(
            grad_mixed,
            side_lanes(grad_router, gain_columns),
            embedded,
            packs,
            vectors,
            gain_vals,
            masks,
            saved,
            5,
        )
    else:
        grad_embedded, grad_win, grad_wx, grad_wout, grad_channel, grad_gain_in = mixer_backward(
            grad_mixed,
            embedded,
            kept_values,
            weight_in,
            weight_x,
            weight_out,
            channel_vals,
            gain_vals[0],
        )
        grad_gains = jnp.stack([grad_gain_in, grad_gain_mid, grad_gain_out])
        mixer_wholes = (grad_win, grad_wx, grad_wout, grad_channel, grad_gains, grad_router)
    if compact:
        scalars = jnp.concatenate(
            [jnp.full((4, LANES), experts_square), jnp.full((4, LANES), loss_part)], axis=0
        )
        table_grad, quarters, sums = finish_all(
            grad_embedded,
            grad_pack,
            token_local,
            table_grad,
            scalars,
            9,
        )
        table_grad = table_grad[:own_vocab]
    else:
        all_grad_embed = gather_all(grad_embedded.astype(jnp.bfloat16), 6).reshape(-1, D)
        table_grad = table_grad + matmul_tn(held_token, all_grad_embed)
        wholes_low = [
            shards_of(whole.astype(jnp.bfloat16), axis, group_count).reshape(group_count, -1)
            for whole, axis in zip(mixer_wholes, part_axes)
        ]
        flat = jnp.concatenate(wholes_low, axis=1)
        flat = jnp.pad(flat, ((0, 0), (0, seq_count * pack_rows * D - flat.shape[1])))
        flat = jnp.swapaxes(flat.reshape(group_count, seq_count, pack_rows, D), 0, 1)
        own_quarter = scatter_all(flat.reshape(devices, pack_rows, D), 8)
        quarters = lax.all_gather(own_quarter, "seq", axis=0, tiled=True).reshape(-1)
        mixer_grads = unpacked(quarters, part_shapes)
        local_square = (
            jnp.sum(table_grad * table_grad) + experts_square + jnp.sum(own_quarter * own_quarter)
        )
        two = jnp.concatenate(
            [jnp.full((4, LANES), local_square), jnp.full((4, LANES), loss_part)], axis=0
        )
        sums = jnp.sum(share_small(two, 9), axis=0)
    total_square, loss_sum = (sums[0, 0], sums[4, 0])
    grad_norm = jnp.sqrt(total_square)
    clip_factor = jnp.minimum(1.0, CLIP / (grad_norm + 1e-06))
    table_new = renewed(
        vocab_table, vocab_table_mom, vocab_table_ema, table_grad, clip_factor, LRATE
    )
    mixer_states = (
        (mixer_in, mixer_in_mom, mixer_in_ema),
        (mixer_x, mixer_x_mom, mixer_x_ema),
        (mixer_out, mixer_out_mom, mixer_out_ema),
        (channel, channel_mom, channel_ema),
        (norm_gains, norm_gains_mom, norm_gains_ema),
        (router, router_mom, router_ema),
    )
    if compact:
        turned_states = mixer_states[:5] + (tuple(part.T for part in mixer_states[5]),)
        fresh = update_all(quarters, sums, turned_states)
        fresh = list(fresh[:15]) + [part.T for part in fresh[15:]]
    else:
        rates = (LRATE, LRATE, LRATE, CHANNEL_LRATE, LRATE, LRATE)
        fresh = [
            part
            for state, gradient, rate in zip(mixer_states, mixer_grads, rates)
            for part in renewed(*state, gradient, clip_factor, rate)
        ]
    experts_new = renewed(experts, experts_mom, experts_ema, grad_experts, clip_factor, LRATE)
    return (
        loss_sum,
        grad_norm,
        branch.reshape(1, tokens, D),
        table_new[0],
        table_new[1],
        table_new[2],
        *fresh,
        experts_new[0],
        experts_new[1],
        experts_new[2],
    )


def solution(mesh):
    placed = (
        P(None, "group"),
        P(None, "group"),
        P(),
        P("seq", "group", None),
        P(("seq", "group"), None),
        P(("seq", "group"), None),
        P(("seq", "group"), None),
        P("group", None),
        P("group", None),
        P("group", None),
        P("group", None),
        P("group", None),
        P("group", None),
        P("group", None),
        P("group", None),
        P("group", None),
        P(None, "group"),
        P(None, "group"),
        P(None, "group"),
        P(None, "group"),
        P(None, "group"),
        P(None, "group"),
        P("group", None),
        P("group", None),
        P("group", None),
        P(None, "seq", "group", None),
        P(None, "seq", "group", None),
        P(None, "seq", "group", None),
    )
    return jax.shard_map(
        per_device,
        mesh=mesh,
        in_specs=placed,
        out_specs=(
            P(),
            P(),
            P("seq", "group", None),
            P(("seq", "group"), None),
            P(("seq", "group"), None),
            P(("seq", "group"), None),
            P("group", None),
            P("group", None),
            P("group", None),
            P("group", None),
            P("group", None),
            P("group", None),
            P("group", None),
            P("group", None),
            P("group", None),
            P(None, "group"),
            P(None, "group"),
            P(None, "group"),
            P(None, "group"),
            P(None, "group"),
            P(None, "group"),
            P("group", None),
            P("group", None),
            P("group", None),
            P(None, "seq", "group", None),
            P(None, "seq", "group", None),
            P(None, "seq", "group", None),
        ),
        check_vma=False,
    )
```

```python
import functools

import jax
import jax.numpy as jnp
from jax import lax
from jax.experimental import pallas as pl
from jax.experimental.pallas import tpu as pltpu
from jax.sharding import PartitionSpec as P

D = 768
DI = 1536
STATE = 16
RANK = 48
CONV = 4
VOCAB_REAL = 50257


EPS = 1e-05
CLIP = 0.1
MOMENTUM = 0.9
LRATE = 1000.0
CHANNEL_LRATE = 10000.0
EMA_KEEP = 0.8
HIGHEST = lax.Precision.HIGHEST
MESH = pl.DeviceIdType.MESH
VMEM_LIMIT = 58 << 20
LANES = 128
SIDE_LANE = 32


def axis_sizes():
    seq, group = (lax.axis_size("seq"), lax.axis_size("group"))
    core = 2 if seq % 2 == 0 else 1
    y = 1
    while 4 * y * y <= group and group % (2 * y) == 0:
        y *= 2
    return {"x": seq // core, "core": core, "z": group // y, "y": y}


def my_place(sizes):
    seq, group = (lax.axis_index("seq"), lax.axis_index("group"))
    return {
        "x": seq // sizes["core"],
        "core": seq % sizes["core"],
        "z": group // sizes["y"],
        "y": group % sizes["y"],
    }


def device_of(place, sizes):
    return (place["x"] * sizes["core"] + place["core"], place["z"] * sizes["y"] + place["y"])


def moved(place, axis, by, sizes):
    return {**place, axis: lax.rem(place[axis] + by + sizes[axis], sizes[axis])}


def block_of(place, sizes):
    seq, group = device_of(place, sizes)
    return seq * (sizes["z"] * sizes["y"]) + group


def meet(peers):
    barrier = pltpu.get_barrier_semaphore()
    for peer in peers:
        pl.semaphore_signal(barrier, inc=1, device_id=peer, device_id_type=MESH)
    pl.semaphore_wait(barrier, len(peers))


def line_peers(place, sizes):
    return [
        device_of(moved(place, axis, by, sizes), sizes)
        for axis in ("x", "core", "z", "y")
        for by in range(1, sizes[axis])
    ]


GATHER_ORDERS = (
    ("z", "y", "x", "core"),
    ("z", "x", "y", "core"),
    ("x", "z", "y", "core"),
    ("y", "z", "x", "core"),
)


def gather_kernel(sizes, pieces, own_ref, all_ref, local_sem, send_sem, recv_sem):
    place = my_place(sizes)
    meet(line_peers(place, sizes))
    keep_own = pltpu.make_async_copy(own_ref, all_ref.at[block_of(place, sizes)], local_sem)
    keep_own.start()
    held = [[(place, None)] for _ in pieces]
    sends = []
    for phase in range(4):
        fresh = [[] for _ in pieces]
        for turn in range(max(len(blocks) for blocks in held)):
            for which, (order, first, rows) in enumerate(pieces):
                if turn >= len(held[which]):
                    continue
                axis = order[phase]
                where, arrival = held[which][turn]
                if arrival is not None:
                    copy, seen = arrival
                    if not seen:
                        copy.wait_recv()
                        held[which][turn] = (where, (copy, True))
                span = pl.ds(first, rows)
                for by in range(1, sizes[axis]):
                    block = block_of(where, sizes)
                    source = own_ref.at[span] if arrival is None else all_ref.at[block, span]
                    number = len(sends)
                    copy = pltpu.make_async_remote_copy(
                        src_ref=source,
                        dst_ref=all_ref.at[block, span],
                        send_sem=send_sem.at[number],
                        recv_sem=recv_sem.at[number],
                        device_id=device_of(moved(place, axis, by, sizes), sizes),
                        device_id_type=MESH,
                    )
                    copy.start()
                    sends.append(copy)
                    fresh[which].append((moved(where, axis, -by, sizes), (copy, False)))
        held = [old + new for old, new in zip(held, fresh)]
    for blocks in held:
        for _, arrival in blocks:
            if arrival is not None and not arrival[1]:
                arrival[0].wait_recv()
    for copy in sends:
        copy.wait_send()
    keep_own.wait()


def split_rows(rows, orders):
    unit = 32 if rows % 32 == 0 else 16
    count = rows // unit
    pieces, first = ([], 0)
    for which in range(min(count, 4)):
        size = (count * (which + 1) // min(count, 4)) * unit - first
        pieces.append((orders[which % len(orders)], first, size))
        first += size
    return pieces


def gather_all(rows, collective_id):
    sizes = axis_sizes()
    devices = sizes["x"] * sizes["core"] * sizes["z"] * sizes["y"]
    pieces = split_rows(rows.shape[0], GATHER_ORDERS)
    copies = (devices - 1) * len(pieces)
    return pl.pallas_call(
        functools.partial(gather_kernel, sizes, pieces),
        out_shape=jax.ShapeDtypeStruct((devices,) + rows.shape, rows.dtype),
        in_specs=[pl.BlockSpec(memory_space=pltpu.VMEM)],
        out_specs=pl.BlockSpec(memory_space=pl.ANY),
        scratch_shapes=[
            pltpu.SemaphoreType.DMA,
            pltpu.SemaphoreType.DMA((copies,)),
            pltpu.SemaphoreType.DMA((copies,)),
        ],
        compiler_params=pltpu.CompilerParams(
            collective_id=collective_id, has_side_effects=True, vmem_limit_bytes=VMEM_LIMIT
        ),
        name="gather_all",
    )(rows)


SCATTER_ORDERS = (("core", "x", "y", "z"), ("core", "y", "x", "z"))
GATHER_PAIR = (("z", "y", "x", "core"), ("z", "x", "y", "core"))
NATURAL = ("x", "core", "z", "y")
PIECE = 16
SPAN = 2 * PIECE


def unravel(number, extents):
    places = []
    for extent in reversed(extents):
        places.append(lax.rem(number, extent))
        number = lax.div(number, extent)
    return tuple(reversed(places))


def piece_rows(pair, kind):
    first = pair * SPAN + kind * PIECE
    if not isinstance(first, int):
        first = pl.multiple_of(first, PIECE)
    return pl.ds(first, PIECE)


def scatter_scratch(sizes, pairs, width, keep):
    scratch = []
    for order in SCATTER_ORDERS:
        landings, sums, semaphores = ([], [], [])
        for phase in range(4):
            left = tuple(sizes[a] for a in NATURAL if a not in order[: phase + 1])
            others = max(1, sizes[order[phase]] - 1)
            landings.append(pltpu.VMEM((pairs, others) + left + (PIECE, width), jnp.bfloat16))
            if phase < 3:
                sums.append(pltpu.VMEM((pairs,) + left + (PIECE, width), jnp.bfloat16))
            semaphores.append(pltpu.SemaphoreType.DMA((pairs, others)))
            semaphores.append(pltpu.SemaphoreType.DMA((pairs, others)))
        scratch += landings + sums + semaphores
        scratch += [pltpu.SemaphoreType.DMA((pairs,))] if keep else []
    return scratch


class Scatter:
    def __init__(self, sizes, pairs, full_ref, own_ref, scratch, keep):
        self.sizes, self.pairs, self.keep = (sizes, pairs, keep)
        self.full_ref, self.own_ref = (full_ref, own_ref)
        self.place = my_place(sizes)
        size = len(scratch) // 2
        self.refs = (scratch[:size], scratch[size:])

    def kept(self, kind, pair):
        order = SCATTER_ORDERS[kind]
        index = tuple(self.place[a] if a == order[0] else slice(None) for a in NATURAL)
        return pltpu.make_async_copy(
            self.full_ref.at[index + (piece_rows(pair, kind),)],
            self.refs[kind][4].at[pair],
            self.refs[kind][15].at[pair],
        )

    def copies(self, kind, pair, phase):
        order, refs, sizes = (SCATTER_ORDERS[kind], self.refs[kind], self.sizes)
        axis = order[phase]
        left = [a for a in NATURAL if a not in order[:phase]]
        made = []
        for by in range(1, sizes[axis]):
            to = moved(self.place, axis, by, sizes)
            index = tuple(to[axis] if a == axis else slice(None) for a in left)
            if phase == 0:
                source = self.full_ref.at[index + (piece_rows(pair, kind),)]
            else:
                source = refs[3 + phase].at[(pair,) + index]
            made.append(
                pltpu.make_async_remote_copy(
                    src_ref=source,
                    dst_ref=refs[phase].at[pair, by - 1],
                    send_sem=refs[7 + 2 * phase].at[pair, by - 1],
                    recv_sem=refs[8 + 2 * phase].at[pair, by - 1],
                    device_id=device_of(to, sizes),
                    device_id_type=MESH,
                )
            )
        return made

    def launch(self, pair, phase):
        for kind in range(2):
            for copy in self.copies(kind, pair, phase):
                copy.start()

    def absorb(self, kind, pair, phase):
        order, refs, sizes, place = (
            SCATTER_ORDERS[kind],
            self.refs[kind],
            self.sizes,
            self.place,
        )
        axis = order[phase]
        before = [a for a in NATURAL if a not in order[:phase]]
        after = [a for a in before if a != axis]
        if phase == 0 and self.keep:
            self.kept(kind, pair).wait()
        for copy in self.copies(kind, pair, phase):
            copy.wait_recv()
        extents = tuple(sizes[a] for a in after)
        number = 1
        for extent in extents:
            number *= extent

        def add(step, carry):
            spot = dict(zip(after, unravel(step, extents)))
            mine = tuple(place[axis] if a == axis else spot[a] for a in before)
            there = tuple(spot[a] for a in after)
            if phase > 0:
                kept_part = refs[3 + phase][(pair,) + mine]
            elif self.keep:
                kept_part = refs[4][(pair,) + there]
            else:
                kept_part = self.full_ref[mine + (piece_rows(pair, kind),)]
            total = kept_part.astype(jnp.float32)
            for by in range(1, sizes[axis]):
                total = total + refs[phase][(pair, by - 1) + there].astype(jnp.float32)
            if phase == 3:
                self.own_ref[piece_rows(pair, kind)] = total
            else:
                refs[4 + phase][(pair,) + there] = total.astype(jnp.bfloat16)
            return carry

        if number == 1:
            add(0, 0)
        else:
            lax.fori_loop(0, number, add, 0)

    def advance(self, pair, phase):
        for kind in range(2):
            self.absorb(kind, pair, phase)
            if phase < 3:
                for copy in self.copies(kind, pair, phase + 1):
                    copy.start()

    def finish(self):
        def one(pair, carry):
            for kind in range(2):
                for phase in range(4):
                    for copy in self.copies(kind, pair, phase):
                        copy.wait_send()
            return carry

        lax.fori_loop(0, self.pairs, one, 0)


def wave(pairs, phases, act):
    def step(turn, carry):
        for phase in range(phases - 1, -1, -1):
            pair = turn - phase

            @pl.when((pair >= 0) & (pair < pairs))
            def _(pair=pair, phase=phase):
                act(pair, phase)

        return carry

    lax.fori_loop(0, pairs + phases - 1, step, 0)


def scatter_kernel(sizes, pairs, full_ref, own_ref, *scratch):
    meet(line_peers(my_place(sizes), sizes))
    scatter = Scatter(sizes, pairs, full_ref, own_ref, scratch, True)
    for pair in range(pairs):
        scatter.launch(pair, 0)
        for kind in range(2):
            scatter.kept(kind, pair).start()
    wave(pairs, 4, scatter.advance)
    scatter.finish()


def scatter_all(blocks, collective_id):
    sizes = axis_sizes()
    rows, width = blocks.shape[-2:]
    pairs = rows // SPAN
    shaped = blocks.reshape(tuple(sizes[a] for a in NATURAL) + (rows, width))
    return pl.pallas_call(
        functools.partial(scatter_kernel, sizes, pairs),
        out_shape=jax.ShapeDtypeStruct((rows, width), jnp.float32),
        in_specs=[pl.BlockSpec(memory_space=pl.ANY)],
        out_specs=pl.BlockSpec(memory_space=pltpu.VMEM),
        scratch_shapes=scatter_scratch(sizes, pairs, width, True),
        compiler_params=pltpu.CompilerParams(
            collective_id=collective_id, has_side_effects=True, vmem_limit_bytes=VMEM_LIMIT
        ),
        name="scatter_all",
    )(shaped)


class Gather:
    def __init__(self, sizes, pairs, own_ref, all_ref, semaphores):
        self.sizes, self.pairs = (sizes, pairs)
        self.own_ref, self.all_ref = (own_ref, all_ref)
        self.semaphores = semaphores
        self.place = my_place(sizes)

    def copies(self, kind, pair, phase):
        order = GATHER_PAIR[kind]
        axis, span = (order[phase], piece_rows(pair, kind))
        block = tuple(slice(None) if a in order[:phase] else self.place[a] for a in NATURAL)
        there = self.all_ref.at[block + (span,)]
        send_sem, recv_sem = (self.semaphores[2 * phase], self.semaphores[2 * phase + 1])
        return [
            pltpu.make_async_remote_copy(
                src_ref=self.own_ref.at[span] if phase == 0 else there,
                dst_ref=there,
                send_sem=send_sem.at[kind, pair, by - 1],
                recv_sem=recv_sem.at[kind, pair, by - 1],
                device_id=device_of(moved(self.place, axis, by, self.sizes), self.sizes),
                device_id_type=MESH,
            )
            for by in range(1, self.sizes[axis])
        ]

    def advance(self, pair, phase):
        for kind in range(2):
            if phase > 0:
                for copy in self.copies(kind, pair, phase - 1):
                    copy.wait_recv()
            if phase < 4:
                for copy in self.copies(kind, pair, phase):
                    copy.start()

    def finish(self):
        def one(pair, carry):
            for kind in range(2):
                for phase in range(4):
                    for copy in self.copies(kind, pair, phase):
                        copy.wait_send()
            return carry

        lax.fori_loop(0, self.pairs, one, 0)


def gather_semaphores(sizes, pairs):
    longest = max(sizes.values())
    return [pltpu.SemaphoreType.DMA((2, pairs, longest)) for _ in range(8)]


def seq_place(seq, sizes):
    return (lax.div(seq, sizes["core"]), lax.rem(seq, sizes["core"]))


def merge_stats(first, second):
    high = jnp.maximum(first[0], second[0])
    mass = first[1] * jnp.exp(first[0] - high) + second[1] * jnp.exp(second[0] - high)
    return (high, mass, first[2] + second[2])


def span_rows(pair):
    return pl.ds(pl.multiple_of(pair * SPAN, SPAN), SPAN)


def masked_logits(table_ref, rows_in, first_masked, limit):
    logits = matmul_nt(table_ref[...], rows_in)
    tail = logits[first_masked:]
    numbers = first_masked + lax.broadcasted_iota(jnp.int32, tail.shape, 0)
    return jnp.concatenate([logits[:first_masked], jnp.where(numbers < limit, tail, -1e30)], axis=0)


def vocab_limit(own_vocab):
    devices, _, me = flat_place()
    least = max(0, VOCAB_REAL - (devices - 1) * own_vocab)
    limit = jnp.minimum(own_vocab, VOCAB_REAL - me * own_vocab)
    return (min(least, own_vocab) // 16 * 16, limit)


def head_forward_kernel(
    sizes,
    pairs,
    own_vocab,
    own_ref,
    table_ref,
    target_ref,
    all_ref,
    stats_ref,
    mine_ref,
    landing_ref,
    local_sem,
    stat_send,
    stat_recv,
    *semaphores,
):
    place = my_place(sizes)
    meet(line_peers(place, sizes))
    gather = Gather(sizes, pairs, own_ref, all_ref, semaphores)
    keep_own = pltpu.make_async_copy(
        own_ref, all_ref.at[tuple(place[a] for a in NATURAL)], local_sem
    )
    keep_own.start()
    groups = sizes["z"] * sizes["y"]
    seqs = sizes["x"] * sizes["core"]
    first_masked, limit = vocab_limit(own_vocab)

    def seq_stats(pair, seq):
        x, core = seq_place(seq, sizes)
        rows_in = all_ref[x, core, :, :, span_rows(pair), :].reshape(groups * SPAN, D)
        logits = masked_logits(table_ref, rows_in, first_masked, limit)
        spot = pl.ds(pair * seqs + seq, 1)
        numbers = lax.broadcasted_iota(jnp.int32, logits.shape, 0)
        top = jnp.max(logits, axis=0, keepdims=True)
        mine_ref[0, 0, spot] = top
        mine_ref[0, 1, spot] = jnp.sum(jnp.exp(logits - top), axis=0, keepdims=True)
        mine_ref[0, 2, spot] = jnp.sum(
            jnp.where(numbers == target_ref[spot], logits, 0.0), axis=0, keepdims=True
        )

    def turn_step(turn, carry):
        for phase in range(4, -1, -1):
            pair = turn - phase

            @pl.when((pair >= 0) & (pair < pairs))
            def _(pair=pair, phase=phase):
                gather.advance(pair, phase)

        @pl.when(turn == 0)
        def _():
            keep_own.wait()

        @pl.when(turn >= 4)
        def _():
            def one(seq, carry):
                seq_stats(turn - 4, seq)
                return carry

            lax.fori_loop(0, seqs, one, 0)

        return carry

    lax.fori_loop(0, pairs + 4, turn_step, 0)
    started = []
    stats = tuple(mine_ref[0, k] for k in range(3))
    for phase, axis in enumerate(("core", "x", "y", "z")):
        arrivals = []
        for by in range(1, sizes[axis]):
            slot = len(started)
            copy = pltpu.make_async_remote_copy(
                src_ref=mine_ref.at[phase],
                dst_ref=landing_ref.at[slot],
                send_sem=stat_send.at[slot],
                recv_sem=stat_recv.at[slot],
                device_id=device_of(moved(place, axis, by, sizes), sizes),
                device_id_type=MESH,
            )
            copy.start()
            arrivals.append((copy, slot))
            started.append(copy)
        for copy, slot in arrivals:
            copy.wait_recv()
            stats = merge_stats(stats, tuple(landing_ref[slot, k] for k in range(3)))
        if phase < 3:
            for k in range(3):
                mine_ref[phase + 1, k] = stats[k]
    stats_ref[0] = stats[0] + jnp.log(stats[1])
    stats_ref[1] = stats[2]
    gather.finish()
    for copy in started:
        copy.wait_send()


def head_forward(rows, table, own_vocab, targets, collective_id):
    sizes = axis_sizes()
    pairs = rows.shape[0] // SPAN
    hops = sum(extent - 1 for extent in sizes.values())
    natural = tuple(sizes[a] for a in NATURAL)
    packed = (3,) + targets.shape
    vmem = pl.BlockSpec(memory_space=pltpu.VMEM)
    return pl.pallas_call(
        functools.partial(head_forward_kernel, sizes, pairs, own_vocab),
        out_shape=(
            jax.ShapeDtypeStruct(natural + rows.shape, rows.dtype),
            jax.ShapeDtypeStruct((2,) + targets.shape, jnp.float32),
        ),
        in_specs=[vmem] * 3,
        out_specs=(vmem,) * 2,
        scratch_shapes=[
            pltpu.VMEM((4,) + packed, jnp.float32),
            pltpu.VMEM((hops,) + packed, jnp.float32),
            pltpu.SemaphoreType.DMA,
            pltpu.SemaphoreType.DMA((hops,)),
            pltpu.SemaphoreType.DMA((hops,)),
        ]
        + gather_semaphores(sizes, pairs),
        compiler_params=pltpu.CompilerParams(
            collective_id=collective_id, has_side_effects=True, vmem_limit_bytes=VMEM_LIMIT
        ),
        name="head_forward",
    )(rows, table, targets)


def head_backward_kernel(
    sizes,
    pairs,
    own_vocab,
    all_ref,
    table_ref,
    turned_ref,
    target_ref,
    level_ref,
    weight_ref,
    own_ref,
    tgrad_ref,
    full_ref,
    grad_ref,
    *scratch,
):
    meet(line_peers(my_place(sizes), sizes))
    scatter = Scatter(sizes, pairs, full_ref, own_ref, scratch, False)
    groups = sizes["z"] * sizes["y"]
    seqs = sizes["x"] * sizes["core"]
    first_masked, limit = vocab_limit(own_vocab)
    height = table_ref.shape[0]
    block = groups * SPAN

    def seq_grads(pair, seq):
        x, core = divmod(seq, sizes["core"])
        rows_in = all_ref[x, core, :, :, span_rows(pair), :].reshape(block, D)
        logits = masked_logits(table_ref, rows_in, first_masked, limit)
        spot = pl.ds(pair * seqs + seq, 1)
        numbers = lax.broadcasted_iota(jnp.int32, logits.shape, 0)
        share = jnp.exp(logits - level_ref[spot])
        share = jnp.where(numbers == target_ref[spot], share - 1.0, share)
        grad_ref[pair, 0:height, seq * block : (seq + 1) * block] = (
            weight_ref[spot] * share
        ).astype(jnp.bfloat16)

    def row_product(pair):
        turned = matmul(turned_ref[...], grad_ref[pair])
        full_ref[:, :, :, :, span_rows(pair), :] = turned.T.astype(jnp.bfloat16).reshape(
            tuple(sizes[a] for a in NATURAL) + (SPAN, D)
        )

    def table_product(pair):
        rows_in = all_ref[:, :, :, :, span_rows(pair), :].reshape(seqs * block, D)
        return matmul(grad_ref[pair, 0:height], rows_in)

    if grad_ref.shape[1] > height:
        grad_ref[:, height:] = jnp.zeros_like(grad_ref[:, height:])

    def turn_step(turn, carry):
        def older(by, phase):
            pair = turn - by

            @pl.when((pair >= 0) & (pair < pairs))
            def _():
                scatter.advance(pair, phase)

        def compute(act):
            @pl.when(turn < pairs)
            def _():
                act()

        for part in range(4):
            for seq in range(part * seqs // 4, (part + 1) * seqs // 4):
                compute(lambda seq=seq: seq_grads(turn, seq))
            if part == 0:
                older(1, 0)
            elif part == 1:
                older(2, 3)
            elif part == 2:
                older(1, 1)
        compute(lambda: row_product(turn))
        older(1, 2)
        compute(lambda: scatter.launch(turn, 0))
        return carry

    lax.fori_loop(0, pairs, turn_step, 0)
    tgrad_ref[...] = table_product(0)
    scatter.advance(pairs - 1, 0)
    if pairs > 1:
        scatter.advance(pairs - 2, 3)

    def late(pair, carry):
        tgrad_ref[...] += table_product(pair)

        @pl.when(pair < 3)
        def _():
            for phase in (1, 2):

                @pl.when(pair == phase)
                def _(phase=phase):
                    scatter.advance(pairs - 1, phase)

        return carry

    lax.fori_loop(1, pairs, late, 0)
    for phase in range(max(1, pairs), 4):
        if phase < 3:
            scatter.advance(pairs - 1, phase)
    scatter.advance(pairs - 1, 3)
    scatter.finish()


def head_backward(all_rows, table, turned, own_vocab, targets, levels, weights, collective_id):
    sizes = axis_sizes()
    tokens = all_rows.shape[-2]
    pairs = tokens // SPAN
    vmem = pl.BlockSpec(memory_space=pltpu.VMEM)
    block = targets.shape[1]
    seqs = sizes["x"] * sizes["core"]
    return pl.pallas_call(
        functools.partial(head_backward_kernel, sizes, pairs, own_vocab),
        out_shape=(
            jax.ShapeDtypeStruct((tokens, D), jnp.float32),
            jax.ShapeDtypeStruct(table.shape, jnp.float32),
        ),
        in_specs=[vmem] * 6,
        out_specs=(vmem,) * 2,
        scratch_shapes=[
            pltpu.VMEM(all_rows.shape, jnp.bfloat16),
            pltpu.VMEM((pairs, turned.shape[1], seqs * block), jnp.bfloat16),
        ]
        + scatter_scratch(sizes, pairs, D, False),
        compiler_params=pltpu.CompilerParams(
            collective_id=collective_id, has_side_effects=True, vmem_limit_bytes=VMEM_LIMIT
        ),
        name="head_backward",
    )(all_rows, table, turned, targets, levels, weights)


def everyone(devices, groups, me, act):
    def step(by, carry):
        peer = lax.rem(me + by, devices)
        act(by, peer, (lax.div(peer, groups), lax.rem(peer, groups)))
        return carry

    lax.fori_loop(1, devices, step, 0)


def greet_everyone(devices, groups, me):
    barrier = pltpu.get_barrier_semaphore()

    def greet(by, peer, address):
        pl.semaphore_signal(barrier, inc=1, device_id=address, device_id_type=MESH)

    everyone(devices, groups, me, greet)
    pl.semaphore_wait(barrier, devices - 1)


def flat_place():
    groups = lax.axis_size("group")
    return (
        lax.axis_size("seq") * groups,
        groups,
        lax.axis_index("seq") * groups + lax.axis_index("group"),
    )


def share_kernel(own_ref, all_ref, send_sem, recv_sem):
    devices, groups, me = flat_place()
    greet_everyone(devices, groups, me)

    def copy_to(by, address):
        return pltpu.make_async_remote_copy(
            src_ref=own_ref,
            dst_ref=all_ref.at[me],
            send_sem=send_sem.at[by],
            recv_sem=recv_sem.at[by],
            device_id=address,
            device_id_type=MESH,
        )

    everyone(devices, groups, me, lambda by, peer, address: copy_to(by, address).start())
    all_ref[me] = own_ref[...]
    everyone(devices, groups, me, lambda by, peer, address: copy_to(by, address).wait())


def share_small(values, collective_id):
    devices = lax.axis_size("seq") * lax.axis_size("group")
    return pl.pallas_call(
        share_kernel,
        out_shape=jax.ShapeDtypeStruct((devices,) + values.shape, values.dtype),
        in_specs=[pl.BlockSpec(memory_space=pltpu.VMEM)],
        out_specs=pl.BlockSpec(memory_space=pltpu.VMEM),
        scratch_shapes=[
            pltpu.SemaphoreType.DMA((devices,)),
            pltpu.SemaphoreType.DMA((devices,)),
        ],
        compiler_params=pltpu.CompilerParams(collective_id=collective_id, has_side_effects=True),
        name="share_small",
    )(values)


def stats_kernel(parts_ref, all_ref, own_ref, got_ref, mine_ref, send_sem, recv_sem):
    devices, groups, me = flat_place()
    greet_everyone(devices, groups, me)

    def part_to(by, peer, address):
        return pltpu.make_async_remote_copy(
            src_ref=parts_ref.at[peer],
            dst_ref=got_ref.at[me],
            send_sem=send_sem.at[0, by],
            recv_sem=recv_sem.at[0, by],
            device_id=address,
            device_id_type=MESH,
        )

    def total_to(by, address):
        return pltpu.make_async_remote_copy(
            src_ref=mine_ref,
            dst_ref=all_ref.at[me],
            send_sem=send_sem.at[1, by],
            recv_sem=recv_sem.at[1, by],
            device_id=address,
            device_id_type=MESH,
        )

    everyone(devices, groups, me, lambda by, peer, address: part_to(by, peer, address).start())
    got_ref[me] = parts_ref[me]
    everyone(devices, groups, me, lambda by, peer, address: part_to(by, peer, address).wait())
    tops = got_ref[:, 0, :]
    top = jnp.max(tops, axis=0, keepdims=True)
    mass = jnp.sum(got_ref[:, 1, :] * jnp.exp(tops - top), axis=0, keepdims=True)
    hit = jnp.sum(got_ref[:, 2, :], axis=0, keepdims=True)
    level = top + jnp.log(mass)
    mine_ref[...] = jnp.broadcast_to(level, mine_ref.shape)
    everyone(devices, groups, me, lambda by, peer, address: total_to(by, address).start())
    all_ref[me] = mine_ref[...]
    own_ref[...] = jnp.broadcast_to(level - hit, own_ref.shape)
    everyone(devices, groups, me, lambda by, peer, address: total_to(by, address).wait())


def combine_stats(parts, collective_id):
    devices = parts.shape[0]
    shape = parts.shape[1:]
    return pl.pallas_call(
        stats_kernel,
        out_shape=(
            jax.ShapeDtypeStruct(parts.shape, jnp.float32),
            jax.ShapeDtypeStruct(shape, jnp.float32),
        ),
        in_specs=[pl.BlockSpec(memory_space=pltpu.VMEM)],
        out_specs=(pl.BlockSpec(memory_space=pltpu.VMEM),) * 2,
        scratch_shapes=[
            pltpu.VMEM(parts.shape, jnp.float32),
            pltpu.VMEM(shape, jnp.float32),
            pltpu.SemaphoreType.DMA((2, devices)),
            pltpu.SemaphoreType.DMA((2, devices)),
        ],
        compiler_params=pltpu.CompilerParams(collective_id=collective_id, has_side_effects=True),
        name="combine_stats",
    )(parts)


def chain_exchange(rates, total_step, flag, end_state, backwards, out_buf, in_buf, sems):
    devices, me = (lax.axis_size("group"), lax.axis_index("group"))
    seq = lax.axis_index("seq")
    send_sem, recv_sem = sems
    width = rates.shape[1]

    def join(first, second):
        return (
            jnp.exp(second[0] * rates) * second[1] * first[2] + second[2],
            first[0] + second[0],
            first[1] * second[1],
        )

    window = (total_step, flag, end_state)
    before = None
    distance, lap = (1, 0)
    copies = []
    while distance < devices:
        to = lax.rem(me + (devices - distance if backwards else distance), devices)
        out_buf[lap, 0:STATE] = window[2]
        out_buf[lap, STATE : STATE + 8] = jnp.concatenate(
            [
                jnp.broadcast_to(window[0], (4, width)),
                jnp.broadcast_to(window[1], (4, width)),
            ],
            axis=0,
        )
        copy = pltpu.make_async_remote_copy(
            src_ref=out_buf.at[lap],
            dst_ref=in_buf.at[lap],
            send_sem=send_sem.at[lap],
            recv_sem=recv_sem.at[lap],
            device_id=(seq, to),
            device_id_type=MESH,
        )
        copy.start()
        copies.append(copy)
        copy.wait_recv()
        reached = (me + distance < devices) if backwards else (me >= distance)
        real = jnp.where(reached, 1.0, 0.0)
        tail = in_buf[lap, STATE : STATE + 8]
        got = (
            tail[0:1] * real,
            tail[4:5] * real + (1.0 - real),
            in_buf[lap, 0:STATE] * real,
        )
        if before is None:
            before = got
        else:
            merged = join(got, before)
            before = (merged[1], merged[2], merged[0])
        merged = join(got, window)
        window = (merged[1], merged[2], merged[0])
        distance *= 2
        lap += 1
    for copy in copies:
        copy.wait_send()
    if before is None:
        return jnp.zeros_like(end_state)
    return before[2]


def chain_peers():
    devices, me = (lax.axis_size("group"), lax.axis_index("group"))
    seq = lax.axis_index("seq")
    distances = []
    distance = 1
    while distance < devices:
        distances += [distance, devices - distance]
        distance *= 2
    return [(seq, lax.rem(me + by, devices)) for by in sorted(set(distances))]


def chain_laps():
    laps, distance = (0, 1)
    while distance < lax.axis_size("group"):
        laps, distance = (laps + 1, distance * 2)
    return max(1, laps)


def spans(width):
    size = 768 if width % 768 == 0 else width
    return [slice(first, first + size) for first in range(0, width, size)]


def wide(value, copies):
    return jnp.concatenate([value] * copies, axis=1)


def folded(value):
    total = value[:, :LANES]
    for first in range(LANES, value.shape[1], LANES):
        total = total + value[:, first : first + LANES]
    return total


def scan_forward_kernel(*refs):
    meet(chain_peers())
    scan_forward_body(*refs)


def scan_forward_body(
    step_ref, act_ref, b_ref, c_ref, keep_ref, rate_ref, y_ref, in_ref, out_buf, in_buf, ss, rs
):
    tokens, width = step_ref.shape
    ends = []
    for span in spans(width):
        copies = (span.stop - span.start) // LANES
        rates = rate_ref[:, span]

        def advance(block, state, span=span, copies=copies, rates=rates):
            rows = pl.ds(pl.multiple_of(block * 8, 8), 8)
            steps = step_ref[rows, span]
            drives = steps * act_ref[rows, span]
            keeps = wide(keep_ref[rows, :], copies)
            for r in range(8):
                decay = jnp.exp(steps[r : r + 1] * rates) * keeps[r : r + 1]
                state = decay * state + drives[r : r + 1] * wide(b_ref[block * 8 + r], copies)
            return state

        ends.append(
            lax.fori_loop(
                0, tokens // 8, advance, jnp.zeros((STATE, span.stop - span.start), jnp.float32)
            )
        )
    total_step = jnp.sum(step_ref[...], axis=0, keepdims=True)
    flag = wide(jnp.min(keep_ref[...], axis=0, keepdims=True), width // LANES)
    incoming = chain_exchange(
        rate_ref[...],
        total_step,
        flag,
        jnp.concatenate(ends, axis=1),
        False,
        out_buf,
        in_buf,
        (ss, rs),
    )
    in_ref[...] = incoming
    for span in spans(width):
        copies = (span.stop - span.start) // LANES
        rates = rate_ref[:, span]

        def produce(block, state, span=span, copies=copies, rates=rates):
            rows = pl.ds(pl.multiple_of(block * 8, 8), 8)
            steps = step_ref[rows, span]
            drives = steps * act_ref[rows, span]
            keeps = wide(keep_ref[rows, :], copies)
            results = []
            for r in range(8):
                decay = jnp.exp(steps[r : r + 1] * rates) * keeps[r : r + 1]
                state = decay * state + drives[r : r + 1] * wide(b_ref[block * 8 + r], copies)
                results.append(
                    jnp.sum(state * wide(c_ref[block * 8 + r], copies), axis=0, keepdims=True)
                )
            y_ref[rows, span] = jnp.concatenate(results, axis=0)
            return state

        lax.fori_loop(0, tokens // 8, produce, in_ref[:, span])


def scan_scratch(width):
    laps = chain_laps()
    return [
        pltpu.VMEM((laps, STATE + 8, width), jnp.float32),
        pltpu.VMEM((laps, STATE + 8, width), jnp.float32),
        pltpu.SemaphoreType.DMA((laps,)),
        pltpu.SemaphoreType.DMA((laps,)),
    ]


def scan_forward(step, act, b_wide, c_wide, keep_wide, rates, collective_id):
    tokens, width = step.shape
    return pl.pallas_call(
        scan_forward_kernel,
        out_shape=(
            jax.ShapeDtypeStruct((tokens, width), jnp.float32),
            jax.ShapeDtypeStruct((STATE, width), jnp.float32),
        ),
        in_specs=[pl.BlockSpec(memory_space=pltpu.VMEM)] * 6,
        out_specs=(pl.BlockSpec(memory_space=pltpu.VMEM),) * 2,
        scratch_shapes=scan_scratch(width),
        compiler_params=pltpu.CompilerParams(
            collective_id=collective_id, has_side_effects=True, vmem_limit_bytes=VMEM_LIMIT
        ),
        name="scan_forward",
    )(step, act, b_wide, c_wide, keep_wide, rates)


def scan_backward_kernel(*refs):
    meet(chain_peers())
    scan_backward_body(*refs)


def scan_backward_body(
    step_ref,
    act_ref,
    b_ref,
    c_ref,
    keep_ref,
    rate_ref,
    in_ref,
    grad_ref,
    along_ref,
    decayed_ref,
    gb_ref,
    gc_ref,
    grate_ref,
    prev_ref,
    carry_ref,
    out_buf,
    in_buf,
    ss,
    rs,
):
    tokens, width = step_ref.shape
    blocks = tokens // 8
    ends = []
    for number, span in enumerate(spans(width)):
        size = span.stop - span.start
        copies = size // LANES
        rates = rate_ref[:, span]

        def replay(block, state, number=number, span=span, copies=copies, rates=rates):
            rows = pl.ds(pl.multiple_of(block * 8, 8), 8)
            steps = step_ref[rows, span]
            drives = steps * act_ref[rows, span]
            keeps = wide(keep_ref[rows, :], copies)
            grads = grad_ref[rows, span]
            for r in range(8):
                at = block * 8 + r
                prev_ref[at, :, span] = state
                decay = jnp.exp(steps[r : r + 1] * rates) * keeps[r : r + 1]
                state = decay * state + drives[r : r + 1] * wide(b_ref[at], copies)
                share = folded(grads[r : r + 1] * state)
                gc_ref[at] = share if number == 0 else gc_ref[at] + share
            return state

        lax.fori_loop(0, blocks, replay, in_ref[:, span])

        def pull(lap, carry, span=span, copies=copies, rates=rates):
            block = blocks - 1 - lap
            rows = pl.ds(pl.multiple_of(block * 8, 8), 8)
            steps = step_ref[rows, span]
            keeps = wide(keep_ref[rows, :], copies)
            grads = grad_ref[rows, span]
            for r in range(7, -1, -1):
                decay = jnp.exp(steps[r : r + 1] * rates) * keeps[r : r + 1]
                adjoint = grads[r : r + 1] * wide(c_ref[block * 8 + r], copies) + carry
                carry = decay * adjoint
            return carry

        ends.append(lax.fori_loop(0, blocks, pull, jnp.zeros((STATE, size), jnp.float32)))
    total_step = jnp.sum(step_ref[...], axis=0, keepdims=True)
    flag = wide(jnp.min(keep_ref[...], axis=0, keepdims=True), width // LANES)
    carry_ref[...] = chain_exchange(
        rate_ref[...],
        total_step,
        flag,
        jnp.concatenate(ends, axis=1),
        True,
        out_buf,
        in_buf,
        (ss, rs),
    )
    for number, span in enumerate(spans(width)):
        size = span.stop - span.start
        copies = size // LANES
        rates = rate_ref[:, span]

        def settle(lap, carries, number=number, span=span, copies=copies, rates=rates):
            carry, rate_total = carries
            block = blocks - 1 - lap
            rows = pl.ds(pl.multiple_of(block * 8, 8), 8)
            steps = step_ref[rows, span]
            drives = steps * act_ref[rows, span]
            keeps = wide(keep_ref[rows, :], copies)
            grads = grad_ref[rows, span]
            alongs, decays = ([None] * 8, [None] * 8)
            for r in range(7, -1, -1):
                at = block * 8 + r
                decay = jnp.exp(steps[r : r + 1] * rates) * keeps[r : r + 1]
                adjoint = grads[r : r + 1] * wide(c_ref[at], copies) + carry
                carry = decay * adjoint
                grad_exp = carry * prev_ref[at, :, span]
                rate_total = rate_total + grad_exp * steps[r : r + 1]
                alongs[r] = jnp.sum(adjoint * wide(b_ref[at], copies), axis=0, keepdims=True)
                decays[r] = jnp.sum(grad_exp * rates, axis=0, keepdims=True)
                share = folded(adjoint * drives[r : r + 1])
                gb_ref[at] = share if number == 0 else gb_ref[at] + share
            along_ref[rows, span] = jnp.concatenate(alongs, axis=0)
            decayed_ref[rows, span] = jnp.concatenate(decays, axis=0)
            return (carry, rate_total)

        _, rate_total = lax.fori_loop(
            0, blocks, settle, (carry_ref[:, span], jnp.zeros((STATE, size), jnp.float32))
        )
        grate_ref[:, span] = rate_total * rates


def scan_backward(step, act, b_wide, c_wide, keep_wide, rates, incoming, grad, collective_id):
    tokens, width = step.shape
    full = jax.ShapeDtypeStruct((tokens, width), jnp.float32)
    return pl.pallas_call(
        scan_backward_kernel,
        out_shape=(
            full,
            full,
            jax.ShapeDtypeStruct(b_wide.shape, jnp.float32),
            jax.ShapeDtypeStruct(c_wide.shape, jnp.float32),
            jax.ShapeDtypeStruct((STATE, width), jnp.float32),
        ),
        in_specs=[pl.BlockSpec(memory_space=pltpu.VMEM)] * 8,
        out_specs=(pl.BlockSpec(memory_space=pltpu.VMEM),) * 5,
        scratch_shapes=[
            pltpu.VMEM((tokens, STATE, width), jnp.float32),
            pltpu.VMEM((STATE, width), jnp.float32),
        ]
        + scan_scratch(width),
        compiler_params=pltpu.CompilerParams(
            collective_id=collective_id, has_side_effects=True, vmem_limit_bytes=VMEM_LIMIT
        ),
        name="scan_backward",
    )(step, act, b_wide, c_wide, keep_wide, rates, incoming, grad)


def everyone_peer_greeting():
    devices, groups, me = flat_place()
    greet_everyone(devices, groups, me)
    return (devices, groups, me)


def one_hot_turned(ids, height):
    numbers = lax.broadcasted_iota(jnp.int32, (height, ids.shape[1]), 0)
    return (numbers == ids).astype(jnp.float32).astype(jnp.bfloat16)


def start_kernel(
    sizes,
    pairs,
    pack_pairs,
    own_vocab,
    number_ref,
    pack_ref,
    master_ref,
    numbers_ref,
    packs_ref,
    own_ref,
    table_ref,
    turned_ref,
    token_ref,
    target_ref,
    full_ref,
    tall_ref,
    pack_sem,
    send_sem,
    recv_sem,
    *scratch,
):
    place = my_place(sizes)
    meet(line_peers(place, sizes))
    _, groups, me = flat_place()
    seqs = sizes["x"] * sizes["core"]
    gather = Gather(sizes, pack_pairs, pack_ref, packs_ref, scratch[:8])
    scatter = Scatter(sizes, pairs, full_ref, own_ref, scratch[8:], False)
    own_pack = pltpu.make_async_copy(
        pack_ref, packs_ref.at[tuple(place[a] for a in NATURAL)], pack_sem
    )
    own_pack.start()

    number_order = ("z", "y", "x", "core")

    def number_copies(phase):
        axis = number_order[phase]
        block = tuple(
            slice(None) if a in number_order[:phase] else place[a] for a in NATURAL
        )
        return [
            pltpu.make_async_remote_copy(
                src_ref=number_ref if phase == 0 else numbers_ref.at[block],
                dst_ref=numbers_ref.at[block],
                send_sem=send_sem.at[phase, by],
                recv_sem=recv_sem.at[phase, by],
                device_id=device_of(moved(place, axis, by, sizes), sizes),
                device_id_type=MESH,
            )
            for by in range(1, sizes[axis])
        ]

    def numbers_next(phase):
        if phase > 0:
            for copy in number_copies(phase - 1):
                copy.wait_recv()
        if phase < 4:
            for copy in number_copies(phase):
                copy.start()

    def weights(turn):
        for phase in range(4, 0, -1):
            if 0 <= turn + 1 - phase < pack_pairs:
                gather.advance(turn + 1 - phase, phase)

    numbers_next(0)
    for pair in range(pack_pairs):
        gather.advance(pair, 0)
    numbers_ref[tuple(place[a] for a in NATURAL)] = number_ref[...]
    numbers_next(1)
    own_pack.wait()
    whole_tiles = own_vocab // 8 * 8
    tall_ref[whole_tiles:] = jnp.zeros_like(tall_ref[whole_tiles:])
    tall_ref[0:own_vocab] = master_ref[...]
    table_ref[...] = tall_ref[0 : table_ref.shape[0]].astype(jnp.bfloat16)
    for first in range(0, tall_ref.shape[0], LANES):
        turned_ref[:, first : first + LANES] = tall_ref[first : first + LANES].T.astype(
            jnp.bfloat16
        )
    numbers_next(2)

    def look_up(pair, seq):
        x, core = seq_place(seq, sizes)
        found = one_hot_turned(token_ref[pl.ds(pair * seqs + seq, 1)], turned_ref.shape[1])
        rows = matmul(turned_ref[...], found).T.astype(jnp.bfloat16)
        full_ref[x, core, :, :, pl.ds(pair * SPAN, SPAN), :] = rows.reshape(
            sizes["z"], sizes["y"], SPAN, D
        )

    per_tile = LANES // SPAN
    lane = lax.broadcasted_iota(jnp.int32, (2 * seqs, LANES), 1)
    for pair in range(pairs):
        for tile in range(groups // per_tile):
            local = jnp.zeros((2 * seqs, LANES), jnp.int32)
            for part in range(per_tile):
                z, y = divmod(tile * per_tile + part, sizes["y"])
                ids = numbers_ref[place["x"], place["core"], z, y, 0 : 2 * seqs]
                ids = pltpu.roll(ids, (part - pair) * SPAN % LANES, 1)
                local = jnp.where(lane // SPAN == part, ids, local)
            local = local - me * own_vocab
            local = jnp.where(local < own_vocab, local, -1)
            lanes = pl.ds(tile * LANES, LANES)
            token_ref[pair * seqs : (pair + 1) * seqs, lanes] = local[0:seqs]
            target_ref[pair * seqs : (pair + 1) * seqs, lanes] = local[seqs:]

    for turn in range(max(pairs + 4, pack_pairs + 3)):
        if turn < pairs:

            def one(seq, carry, turn=turn):
                look_up(turn, seq)
                return carry

            lax.fori_loop(0, seqs, one, 0)
            scatter.launch(turn, 0)
        for phase in range(3, -1, -1):
            if 0 <= turn - 1 - phase < pairs:
                scatter.advance(turn - 1 - phase, phase)
        weights(turn)
        if turn < 2:
            numbers_next(3 + turn)
    for phase in range(4):
        for copy in number_copies(phase):
            copy.wait_send()
    gather.finish()
    scatter.finish()


def start_all(numbers, pack, master, collective_id):
    sizes = axis_sizes()
    natural = tuple(sizes[a] for a in NATURAL)
    devices = lax.axis_size("seq") * lax.axis_size("group")
    tokens = numbers.shape[1]
    pairs, pack_pairs = (tokens // SPAN, pack.shape[0] // SPAN)
    own_vocab = master.shape[0]
    short, long = (-(-own_vocab // 16) * 16, -(-own_vocab // LANES) * LANES)
    spread = (devices * tokens // (SPAN * lax.axis_size("group")), SPAN * lax.axis_size("group"))
    vmem = pl.BlockSpec(memory_space=pltpu.VMEM)
    return pl.pallas_call(
        functools.partial(start_kernel, sizes, pairs, pack_pairs, own_vocab),
        out_shape=(
            jax.ShapeDtypeStruct(natural + numbers.shape, numbers.dtype),
            jax.ShapeDtypeStruct(natural + pack.shape, pack.dtype),
            jax.ShapeDtypeStruct((tokens, D), jnp.float32),
            jax.ShapeDtypeStruct((short, D), jnp.bfloat16),
            jax.ShapeDtypeStruct((D, long), jnp.bfloat16),
            jax.ShapeDtypeStruct(spread, jnp.int32),
            jax.ShapeDtypeStruct(spread, jnp.int32),
        ),
        in_specs=[vmem] * 3,
        out_specs=(vmem, pl.BlockSpec(memory_space=pl.ANY)) + (vmem,) * 5,
        scratch_shapes=[
            pltpu.VMEM(natural + (tokens, D), jnp.bfloat16),
            pltpu.VMEM((long, D), jnp.float32),
            pltpu.SemaphoreType.DMA,
            pltpu.SemaphoreType.DMA((4, max(sizes.values()))),
            pltpu.SemaphoreType.DMA((4, max(sizes.values()))),
        ]
        + gather_semaphores(sizes, pack_pairs)
        + scatter_scratch(sizes, pairs, D, False),
        compiler_params=pltpu.CompilerParams(
            collective_id=collective_id, has_side_effects=True, vmem_limit_bytes=VMEM_LIMIT
        ),
        name="start_all",
    )(numbers, pack, master)


def finish_kernel(
    sizes,
    pairs,
    pack_pairs,
    own_ref,
    pack_ref,
    token_ref,
    head_ref,
    scalar_ref,
    tgrad_ref,
    quarters_ref,
    sums_ref,
    all_ref,
    found_ref,
    mine_ref,
    ring_ref,
    own_sem,
    quarter_send,
    quarter_recv,
    ring_send,
    ring_recv,
    *scratch,
):
    place = my_place(sizes)
    meet(line_peers(place, sizes))
    seqs = sizes["x"] * sizes["core"]
    groups = sizes["z"] * sizes["y"]
    block = groups * SPAN
    height = head_ref.shape[0]
    gather = Gather(sizes, pairs, own_ref, all_ref, scratch[:8])
    scatter = Scatter(sizes, pack_pairs, pack_ref, mine_ref, scratch[8:], True)
    keep_own = pltpu.make_async_copy(
        own_ref, all_ref.at[tuple(place[a] for a in NATURAL)], own_sem
    )
    keep_own.start()

    def spread_table(pair):
        for seq in range(seqs):
            ids = token_ref[pair * seqs + seq : pair * seqs + seq + 1]
            found_ref[:, seq * block : (seq + 1) * block] = one_hot_turned(ids, height)
        rows = all_ref[:, :, :, :, pl.ds(pair * SPAN, SPAN), :].reshape(seqs * block, D)
        update = matmul(found_ref[...], rows)
        tgrad_ref[...] = (head_ref[...] if pair == 0 else tgrad_ref[...]) + update

    seq = place["x"] * sizes["core"] + place["core"]
    started = []
    x_sent, core_sent = ({}, [])

    def send_quarter(pair, axis, held):
        rows = pl.ds(pair * SPAN, SPAN)
        sent = []
        for by in range(1, sizes[axis]):
            number = len(started)
            copy = pltpu.make_async_remote_copy(
                src_ref=quarters_ref.at[held, rows],
                dst_ref=quarters_ref.at[held, rows],
                send_sem=quarter_send.at[number],
                recv_sem=quarter_recv.at[number],
                device_id=device_of(moved(place, axis, by, sizes), sizes),
                device_id_type=MESH,
            )
            copy.start()
            sent.append(copy)
            started.append(copy)
        return sent

    def own_quarter(pair):
        rows = pl.ds(pair * SPAN, SPAN)
        quarters_ref[seq, rows] = mine_ref[rows].astype(jnp.bfloat16)
        x_sent[pair] = send_quarter(pair, "x", seq)

    def pass_quarter(pair):
        for copy in x_sent[pair]:
            copy.wait_recv()
        for x in range(sizes["x"]):
            core_sent.extend(send_quarter(pair, "core", x * sizes["core"] + place["core"]))

    for pair in range(pack_pairs):
        scatter.launch(pair, 0)
        for kind in range(2):
            scatter.kept(kind, pair).start()
    for turn in range(max(pairs + 4, pack_pairs + 3)):
        if 0 <= turn - 4 < pairs:
            gather.advance(turn - 4, 4)
        for phase in range(3, -1, -1):
            if 0 <= turn - phase < pairs:
                gather.advance(turn - phase, phase)
            if 0 <= turn - phase < pack_pairs:
                scatter.advance(turn - phase, phase)
        if 0 <= turn - 3 < pack_pairs:
            own_quarter(turn - 3)
        if 0 <= turn - 4 < pack_pairs:
            pass_quarter(turn - 4)
        if turn == 0:
            keep_own.wait()
        if 0 <= turn - 4 < pairs:
            spread_table(turn - 4)

    square = jnp.sum(tgrad_ref[...] * tgrad_ref[...]) + jnp.sum(mine_ref[...] * mine_ref[...])
    row = lax.broadcasted_iota(jnp.int32, (8, LANES), 0)
    value = scalar_ref[...] + jnp.where(row < 4, square, 0.0)
    first = 0
    ring_started = []
    last_pair = pack_pairs - 1
    for axis in ("core", "x", "y", "z"):
        ring_ref[first + place[axis]] = value
        sent = []
        for by in range(1, sizes[axis]):
            copy = pltpu.make_async_remote_copy(
                src_ref=ring_ref.at[first + place[axis]],
                dst_ref=ring_ref.at[first + place[axis]],
                send_sem=ring_send.at[first + by],
                recv_sem=ring_recv.at[first + by],
                device_id=device_of(moved(place, axis, by, sizes), sizes),
                device_id_type=MESH,
            )
            copy.start()
            sent.append(copy)
        ring_started.extend(sent)
        if axis == "x" and max(pairs + 4, pack_pairs + 3) <= last_pair + 4:
            pass_quarter(last_pair)
        for copy in sent:
            copy.wait_recv()
        value = ring_ref[first]
        for other in range(1, sizes[axis]):
            value = value + ring_ref[first + other]
        first += sizes[axis]
    sums_ref[...] = value
    for copy in core_sent:
        copy.wait_recv()
    for copy in started + ring_started:
        copy.wait_send()
    gather.finish()
    scatter.finish()


def finish_all(rows, packs, token_rows, head_grad, scalars, collective_id):
    sizes = axis_sizes()
    natural = tuple(sizes[a] for a in NATURAL)
    tokens = rows.shape[0]
    seqs = sizes["x"] * sizes["core"]
    pack_rows, pack_width = packs.shape[-2:]
    pairs, pack_pairs = (tokens // SPAN, pack_rows // SPAN)
    slots = sum(sizes.values())
    quarter_copies = (sizes["x"] - 1) + (sizes["core"] - 1) * sizes["x"]
    quarter_copies = max(1, pack_pairs * quarter_copies)
    vmem = pl.BlockSpec(memory_space=pltpu.VMEM)
    return pl.pallas_call(
        functools.partial(finish_kernel, sizes, pairs, pack_pairs),
        out_shape=(
            jax.ShapeDtypeStruct(head_grad.shape, jnp.float32),
            jax.ShapeDtypeStruct((seqs, pack_rows, pack_width), jnp.bfloat16),
            jax.ShapeDtypeStruct((8, LANES), jnp.float32),
        ),
        in_specs=[vmem, pl.BlockSpec(memory_space=pl.ANY), vmem, vmem, vmem],
        out_specs=(vmem,) * 3,
        scratch_shapes=[
            pltpu.VMEM(natural + rows.shape, jnp.bfloat16),
            pltpu.VMEM((head_grad.shape[0], seqs * token_rows.shape[1]), jnp.bfloat16),
            pltpu.VMEM((pack_rows, pack_width), jnp.float32),
            pltpu.VMEM((slots, 8, LANES), jnp.float32),
            pltpu.SemaphoreType.DMA,
            pltpu.SemaphoreType.DMA((quarter_copies,)),
            pltpu.SemaphoreType.DMA((quarter_copies,)),
            pltpu.SemaphoreType.DMA((slots,)),
            pltpu.SemaphoreType.DMA((slots,)),
        ]
        + gather_semaphores(sizes, pairs)
        + scatter_scratch(sizes, pack_pairs, pack_width, True),
        compiler_params=pltpu.CompilerParams(
            collective_id=collective_id, has_side_effects=True, vmem_limit_bytes=VMEM_LIMIT
        ),
        name="finish_all",
    )(rows, packs.reshape(natural + (pack_rows, pack_width)), token_rows, head_grad, scalars)


def side_lanes(router, gain_columns):
    first = gain_columns[:, :1]
    rest = gain_columns[:, 1:]
    gap = LANES - SIDE_LANE - router.shape[1] - gain_columns.shape[1]
    return jnp.concatenate([jnp.pad(router, ((0, 0), (SIDE_LANE, gap))), rest, first], axis=1)


def row_tiles(values):
    return values.reshape(-1, 16, LANES).transpose(1, 0, 2).reshape(16, -1)


def own_pack_of(parts, seq_index, seq_count):
    mixer_in, mixer_x, mixer_out, channel, gains, router = [
        part.astype(jnp.bfloat16) for part in parts
    ]
    rows = mixer_x.shape[0] // seq_count
    some = mixer_in.shape[0] // seq_count
    top = lax.dynamic_slice_in_dim(mixer_in, seq_index * D, D, 1)
    middle = lax.dynamic_slice_in_dim(mixer_out, seq_index * rows, rows, 0)
    x_rows = lax.dynamic_slice_in_dim(mixer_x, seq_index * rows, rows, 0)
    extra = lax.dynamic_slice_in_dim(channel, seq_index * rows, rows, 1).T
    extra = jnp.pad(extra, ((0, 0), (0, LANES - extra.shape[1])))
    sides = lax.dynamic_slice_in_dim(
        side_lanes(router, gains.T), seq_index * some, some, 0
    )
    extra = extra + jnp.pad(sides, ((0, rows - some), (0, 0)))
    bottom = jnp.concatenate([row_tiles(x_rows), row_tiles(extra)], axis=1)
    return jnp.concatenate([top, middle, bottom])


def small_weights(packs, experts_total):
    tall, rows = pack_heights()
    seqs, groups = packs.shape[:2]
    extra = packs[:, :, tall + rows :, D // 2 :].reshape(seqs, groups, 16, rows // 16, LANES)
    extra = extra.transpose(1, 0, 3, 2, 4).reshape(groups, seqs, rows, LANES)
    channel = extra.reshape(-1, LANES)[:, : CONV + 3 + STATE].T
    sides = extra[:, :, : tall // seqs].reshape(D, LANES)
    gains = jnp.concatenate([sides[:, -1:], sides[:, -3:-1]], axis=1).T
    router = sides[:, SIDE_LANE : SIDE_LANE + experts_total]
    return (channel.astype(jnp.float32), gains.astype(jnp.float32), router)


def log_sum(value):
    return jnp.maximum(value, 0.0) + jnp.log1p(jnp.exp(-jnp.abs(value)))


def pack_heights():
    seqs, groups = (lax.axis_size("seq"), lax.axis_size("group"))
    return (D // groups, DI // (seqs * groups))


def collect_middle(packs_ref, outx_ref):
    seqs, groups = packs_ref.shape[:2]
    tall, rows = pack_heights()

    def one(step, carry):
        group, seq = (lax.div(step, seqs), lax.rem(step, seqs))
        start = step * rows
        outx_ref[pl.ds(pl.multiple_of(start, 16), rows), 0:D] = packs_ref[
            seq, group, tall : tall + rows
        ]
        for part in range(rows // 16):
            outx_ref[pl.ds(pl.multiple_of(start + part * 16, 16), 16), D:] = packs_ref[
                seq, group, tall + rows :, part * LANES : (part + 1) * LANES
            ]
        return carry

    lax.fori_loop(0, seqs * groups, one, 0)


def turned_step_weights(outx_ref):
    both = outx_ref[:, D:].astype(jnp.float32)
    lane = lax.broadcasted_iota(jnp.int32, both.shape, 1)
    shifted = pltpu.roll(both, RANK, 1)
    return jnp.where(lane < RANK, shifted, 0.0).astype(jnp.bfloat16)


def mixer_forward_kernel(
    experts_total,
    x_ref,
    packs_ref,
    vec_ref,
    gain_ref,
    mask_ref,
    router_ref,
    mixed_ref,
    moe_ref,
    prob_ref,
    z_ref,
    pad_ref,
    conv_ref,
    act_ref,
    dtin_ref,
    dtpre_ref,
    step_ref,
    b_ref,
    c_ref,
    in_ref,
    y_ref,
    outx_ref,
    keep_ref,
    rate_ref,
    halo_out,
    halo_in,
    out_buf,
    in_buf,
    ss,
    rs,
    halo_send,
    halo_recv,
):
    meet(chain_peers())
    seqs, groups = packs_ref.shape[:2]
    tall, _ = pack_heights()
    me = lax.axis_index("group")
    x = x_ref[...]
    tokens = x.shape[0]
    normed = (x * inverse_rms(x) * gain_ref[0:1]).astype(jnp.bfloat16)
    for seq in range(seqs):
        block = matmul(normed, packs_ref[seq, :, 0:tall, 0:D].reshape(D, D))
        first = seq * D
        if first < DI:
            pad_ref[8:, first : first + D] = block.astype(jnp.bfloat16).astype(jnp.float32)
        else:
            z_ref[:, first - DI : first - DI + D] = block
    halo_out[...] = pad_ref[tokens:]
    halo = pltpu.make_async_remote_copy(
        src_ref=halo_out,
        dst_ref=halo_in,
        send_sem=halo_send,
        recv_sem=halo_recv,
        device_id=(lax.axis_index("seq"), lax.rem(me + 1, groups)),
        device_id_type=MESH,
    )
    halo.start()
    collect_middle(packs_ref, outx_ref)
    rate_ref[...] = -jnp.exp(vec_ref[CONV + 3 : CONV + 3 + STATE])
    keep_ref[...] = jnp.broadcast_to(mask_ref[:, CONV : CONV + 1], keep_ref.shape)
    halo.wait_recv()
    pad_ref[0:8] = halo_in[...] * jnp.where(me > 0, 1.0, 0.0)
    conv = vec_ref[CONV : CONV + 1] + jnp.zeros_like(z_ref)
    for tap in range(CONV):
        first = 9 - CONV + tap
        conv = (
            conv
            + vec_ref[tap : tap + 1]
            * pad_ref[first : first + tokens]
            * mask_ref[:, tap : tap + 1]
        )
    activated = conv * jax.nn.sigmoid(conv)
    conv_ref[...] = conv
    act_ref[...] = activated
    projected = matmul(activated.astype(jnp.bfloat16), outx_ref[:, D:])
    lane = lax.broadcasted_iota(jnp.int32, projected.shape, 1)
    dt_input = jnp.where(lane < RANK, projected, 0.0).astype(jnp.bfloat16)
    dtin_ref[...] = dt_input
    dt_pre = matmul_nt(dt_input, turned_step_weights(outx_ref))
    dtpre_ref[...] = dt_pre
    step_ref[...] = log_sum(dt_pre + vec_ref[CONV + 1 : CONV + 2])
    for n in range(STATE):
        at = RANK + n
        b_ref[:, n, :] = jnp.broadcast_to(projected[:, at : at + 1], (tokens, LANES))
        at = RANK + STATE + n
        c_ref[:, n, :] = jnp.broadcast_to(projected[:, at : at + 1], (tokens, LANES))
    scan_forward_body(
        step_ref,
        act_ref,
        b_ref,
        c_ref,
        keep_ref,
        rate_ref,
        y_ref,
        in_ref,
        out_buf,
        in_buf,
        ss,
        rs,
    )
    scanned = y_ref[...] + vec_ref[CONV + 2 : CONV + 3] * act_ref[...]
    y_ref[...] = scanned
    gate_z = z_ref[...]
    gated = (scanned * (gate_z * jax.nn.sigmoid(gate_z))).astype(jnp.bfloat16)
    mixed = x + matmul(gated, outx_ref[:, :D])
    mixed_ref[...] = mixed
    moe_in = (mixed * inverse_rms(mixed) * gain_ref[1:2]).astype(jnp.bfloat16)
    moe_ref[...] = moe_in
    scores = matmul(moe_in, router_ref[...])
    scores = jnp.where(lane < experts_total, scores, -1e30)
    raised = jnp.exp(scores - jnp.max(scores, axis=1, keepdims=True))
    prob_ref[...] = raised / jnp.sum(raised, axis=1, keepdims=True)
    halo.wait_send()


def mixer_forward_all(x, packs, vectors, gains, masks, router, collective_id):
    tokens = x.shape[0]
    wide_shape = jax.ShapeDtypeStruct((tokens, DI), jnp.float32)
    state_shape = jax.ShapeDtypeStruct((tokens, STATE, LANES), jnp.float32)
    vmem = pl.BlockSpec(memory_space=pltpu.VMEM)
    return pl.pallas_call(
        functools.partial(mixer_forward_kernel, router.shape[1]),
        out_shape=(
            jax.ShapeDtypeStruct((tokens, D), jnp.float32),
            jax.ShapeDtypeStruct((tokens, D), jnp.bfloat16),
            jax.ShapeDtypeStruct((tokens, LANES), jnp.float32),
            wide_shape,
            jax.ShapeDtypeStruct((tokens + 8, DI), jnp.float32),
            wide_shape,
            wide_shape,
            jax.ShapeDtypeStruct((tokens, LANES), jnp.bfloat16),
            wide_shape,
            wide_shape,
            state_shape,
            state_shape,
            jax.ShapeDtypeStruct((STATE, DI), jnp.float32),
            wide_shape,
        ),
        in_specs=[vmem] * 6,
        out_specs=(vmem,) * 14,
        scratch_shapes=[
            pltpu.VMEM((DI, D + LANES), jnp.bfloat16),
            pltpu.VMEM((tokens, LANES), jnp.float32),
            pltpu.VMEM((STATE, DI), jnp.float32),
            pltpu.VMEM((8, DI), jnp.float32),
            pltpu.VMEM((8, DI), jnp.float32),
        ]
        + scan_scratch(DI)
        + [pltpu.SemaphoreType.DMA, pltpu.SemaphoreType.DMA],
        compiler_params=pltpu.CompilerParams(
            collective_id=collective_id, has_side_effects=True, vmem_limit_bytes=VMEM_LIMIT
        ),
        name="mixer_forward",
    )(x, packs, vectors, gains, masks, jnp.pad(router, ((0, 0), (0, LANES - router.shape[1]))))


def mixer_backward_kernel(
    grad_ref,
    side_ref,
    x_ref,
    packs_ref,
    vec_ref,
    gain_ref,
    mask_ref,
    z_ref,
    pad_ref,
    conv_ref,
    act_ref,
    dtin_ref,
    dtpre_ref,
    step_ref,
    b_ref,
    c_ref,
    in_ref,
    y_ref,
    embed_ref,
    gpack_ref,
    outx_ref,
    keep_ref,
    rate_ref,
    scan_grad_ref,
    along_ref,
    decayed_ref,
    gb_ref,
    gc_ref,
    grate_ref,
    prev_ref,
    carry_ref,
    gout_ref,
    both_ref,
    gpad_ref,
    chan_ref,
    turned_ref,
    merged_ref,
    halo_out,
    halo_in,
    out_buf,
    in_buf,
    ss,
    rs,
    halo_send,
    halo_recv,
):
    meet(chain_peers())
    seqs, groups = packs_ref.shape[:2]
    tall, rows = pack_heights()
    me = lax.axis_index("group")
    tokens = x_ref.shape[0]
    collect_middle(packs_ref, outx_ref)
    rate_ref[...] = -jnp.exp(vec_ref[CONV + 3 : CONV + 3 + STATE])
    keep_ref[...] = jnp.broadcast_to(mask_ref[:, CONV : CONV + 1], keep_ref.shape)
    grad_low = grad_ref[...].astype(jnp.bfloat16)
    grad_gated = matmul_nt(grad_low, outx_ref[:, :D])
    gate_z, scanned = (z_ref[...], y_ref[...])
    logistic = jax.nn.sigmoid(gate_z)
    gate_act = gate_z * logistic
    gated = (scanned * gate_act).astype(jnp.bfloat16)
    gout_ref[:, :D] = matmul_tn(gated, grad_low).astype(jnp.bfloat16)
    grad_scan = grad_gated * gate_act
    scan_grad_ref[...] = grad_scan
    grad_z = grad_gated * scanned * (logistic * (1.0 + gate_z * (1.0 - logistic)))
    both_ref[:, DI:] = grad_z.astype(jnp.bfloat16)
    chan_ref[...] = jnp.zeros_like(chan_ref)
    chan_ref[CONV + 2 : CONV + 3] = jnp.sum(grad_scan * act_ref[...], axis=0, keepdims=True)
    scan_backward_body(
        step_ref,
        act_ref,
        b_ref,
        c_ref,
        keep_ref,
        rate_ref,
        in_ref,
        scan_grad_ref,
        along_ref,
        decayed_ref,
        gb_ref,
        gc_ref,
        grate_ref,
        prev_ref,
        carry_ref,
        out_buf,
        in_buf,
        ss,
        rs,
    )
    chan_ref[CONV + 3 : CONV + 3 + STATE] = grate_ref[...]
    along, activated = (along_ref[...], act_ref[...])
    grad_act = scan_grad_ref[...] * vec_ref[CONV + 2 : CONV + 3] + along * step_ref[...]
    grad_step = decayed_ref[...] + along * activated
    grad_dtpre = grad_step * jax.nn.sigmoid(dtpre_ref[...] + vec_ref[CONV + 1 : CONV + 2])
    chan_ref[CONV + 1 : CONV + 2] = jnp.sum(grad_dtpre, axis=0, keepdims=True)
    grad_dtlow = grad_dtpre.astype(jnp.bfloat16)
    grad_wdt = matmul_tn(grad_dtlow, dtin_ref[...])
    grad_proj = matmul(grad_dtlow, turned_step_weights(outx_ref))
    lane = lax.broadcasted_iota(jnp.int32, grad_proj.shape, 1)
    for n in range(STATE):
        for first, ref in ((RANK, gb_ref), (RANK + STATE, gc_ref)):
            column = jnp.sum(ref[:, n, :], axis=1, keepdims=True)
            grad_proj = jnp.where(lane == first + n, column, grad_proj)
    grad_proj = grad_proj.astype(jnp.bfloat16)
    grad_wx = matmul_tn(activated.astype(jnp.bfloat16), grad_proj)
    wide_lane = lax.broadcasted_iota(jnp.int32, grad_wx.shape, 1)
    grad_wx = jnp.where(
        wide_lane < RANK + 2 * STATE, grad_wx, pltpu.roll(grad_wdt, RANK + 2 * STATE, 1)
    )
    gout_ref[:, D:] = grad_wx.astype(jnp.bfloat16)
    grad_act = grad_act + matmul_nt(grad_proj, outx_ref[:, D:])
    conv = conv_ref[...]
    logistic = jax.nn.sigmoid(conv)
    grad_conv = grad_act * (logistic * (1.0 + conv * (1.0 - logistic)))
    chan_ref[CONV : CONV + 1] = jnp.sum(grad_conv, axis=0, keepdims=True)
    gpad_ref[...] = jnp.zeros_like(gpad_ref)
    for tap in range(CONV):
        same = grad_conv * mask_ref[:, tap : tap + 1]
        first = 9 - CONV + tap
        chan_ref[tap : tap + 1] = jnp.sum(
            same * pad_ref[first : first + tokens], axis=0, keepdims=True
        )
        gpad_ref[first : first + tokens] += vec_ref[tap : tap + 1] * same
    halo_out[...] = gpad_ref[0:8]
    halo = pltpu.make_async_remote_copy(
        src_ref=halo_out,
        dst_ref=halo_in,
        send_sem=halo_send,
        recv_sem=halo_recv,
        device_id=(lax.axis_index("seq"), lax.rem(me + groups - 1, groups)),
        device_id_type=MESH,
    )
    halo.start()
    for first in range(0, DI, LANES):
        turned_ref[first : first + LANES] = chan_ref[:, first : first + LANES].T

    def place_middle(step, carry):
        group, seq = (lax.div(step, seqs), lax.rem(step, seqs))
        start = step * rows
        gpack_ref[seq, group, tall : tall + rows] = gout_ref[
            pl.ds(pl.multiple_of(start, 16), rows), 0:D
        ]
        for part in range(rows // 16):
            gpack_ref[seq, group, tall + rows :, part * LANES : (part + 1) * LANES] = gout_ref[
                pl.ds(pl.multiple_of(start + part * 16, 16), 16), D:
            ]
        return carry

    lax.fori_loop(0, seqs * groups, place_middle, 0)
    halo.wait_recv()
    gpad_ref[tokens : tokens + 8] += halo_in[...] * jnp.where(me < groups - 1, 1.0, 0.0)
    both_ref[:, :DI] = gpad_ref[8 : 8 + tokens].astype(jnp.bfloat16)
    x = x_ref[...]
    scale = inverse_rms(x)
    normed = (x * scale * gain_ref[0:1]).astype(jnp.bfloat16)
    grad_normed = jnp.zeros((tokens, D), jnp.float32)
    for seq in range(seqs):
        part = both_ref[:, seq * D : (seq + 1) * D]
        grad_normed += matmul_nt(part, packs_ref[seq, :, 0:tall, 0:D].reshape(D, D))
        gpack_ref[seq, :, 0:tall, 0:D] = (
            matmul_tn(normed, part).astype(jnp.bfloat16).reshape(groups, tall, D)
        )
    scaled = grad_normed * gain_ref[0:1]
    grad_x = scale * scaled - x * scale**3 * jnp.mean(scaled * x, axis=-1, keepdims=True)
    embed_ref[...] = (grad_ref[...] + grad_x).astype(jnp.bfloat16)
    grad_gain = jnp.sum(grad_normed * x * scale, axis=0, keepdims=True)
    grad_gain = jnp.broadcast_to(grad_gain, (LANES, D)).T
    side_lane = lax.broadcasted_iota(jnp.int32, side_ref.shape, 1)
    merged_ref[...] = jnp.where(side_lane == LANES - 1, grad_gain, side_ref[...])
    some = tall // seqs

    def place_extra(step, carry):
        group, seq = (lax.div(step, seqs), lax.rem(step, seqs))
        start = pl.multiple_of(step * rows, 16)
        first = pl.multiple_of(group * tall + seq * some, 8)
        turned_ref[pl.ds(start, some)] += merged_ref[pl.ds(first, some)]
        for part in range(rows // 16):
            lanes = pl.ds(D // 2 + part * LANES, LANES)
            gpack_ref[seq, group, tall + rows :, lanes] = turned_ref[
                pl.ds(pl.multiple_of(start + part * 16, 16), 16)
            ].astype(jnp.bfloat16)
        return carry

    lax.fori_loop(0, seqs * groups, place_extra, 0)
    halo.wait_send()


def mixer_backward_all(grad, sides, x, packs, vectors, gains, masks, saved, collective_id):
    tokens = x.shape[0]
    vmem = pl.BlockSpec(memory_space=pltpu.VMEM)
    wide = (tokens, DI)
    return pl.pallas_call(
        mixer_backward_kernel,
        out_shape=(
            jax.ShapeDtypeStruct((tokens, D), jnp.bfloat16),
            jax.ShapeDtypeStruct(packs.shape, jnp.bfloat16),
        ),
        in_specs=[vmem] * (7 + len(saved)),
        out_specs=(vmem,) * 2,
        scratch_shapes=[
            pltpu.VMEM((DI, D + LANES), jnp.bfloat16),
            pltpu.VMEM((tokens, LANES), jnp.float32),
            pltpu.VMEM((STATE, DI), jnp.float32),
            pltpu.VMEM(wide, jnp.float32),
            pltpu.VMEM(wide, jnp.float32),
            pltpu.VMEM(wide, jnp.float32),
            pltpu.VMEM((tokens, STATE, LANES), jnp.float32),
            pltpu.VMEM((tokens, STATE, LANES), jnp.float32),
            pltpu.VMEM((STATE, DI), jnp.float32),
            pltpu.VMEM((tokens, STATE, DI), jnp.float32),
            pltpu.VMEM((STATE, DI), jnp.float32),
            pltpu.VMEM((DI, D + LANES), jnp.bfloat16),
            pltpu.VMEM((tokens, 2 * DI), jnp.bfloat16),
            pltpu.VMEM((tokens + 8, DI), jnp.float32),
            pltpu.VMEM((LANES, DI), jnp.float32),
            pltpu.VMEM((DI, LANES), jnp.float32),
            pltpu.VMEM((D, LANES), jnp.float32),
            pltpu.VMEM((8, DI), jnp.float32),
            pltpu.VMEM((8, DI), jnp.float32),
        ]
        + scan_scratch(DI)
        + [pltpu.SemaphoreType.DMA, pltpu.SemaphoreType.DMA],
        compiler_params=pltpu.CompilerParams(
            collective_id=collective_id, has_side_effects=True, vmem_limit_bytes=VMEM_LIMIT
        ),
        name="mixer_backward",
    )(grad, sides, x, packs, vectors, gains, masks, *saved)


def update_kernel(quarters_ref, sums_ref, *refs):
    inputs, outputs, turned_ref, side_ref = (refs[:18], refs[18:36], refs[36], refs[37])
    seqs = quarters_ref.shape[0]
    tall, rows = pack_heights()
    norm = jnp.sqrt(sums_ref[0:1, 0:1])
    clip_factor = jnp.minimum(1.0, CLIP / (norm + 1e-06))

    def renew(which, index, gradient, rate):
        master, moment, average = (inputs[3 * which + k] for k in range(3))
        fresh = renewed(
            master[index], moment[index], average[index], gradient, clip_factor, rate
        )
        for k in range(3):
            outputs[3 * which + k][index] = fresh[k]

    for seq in range(seqs):
        columns = slice(seq * D, (seq + 1) * D)
        renew(0, (slice(None), columns), quarters_ref[seq, 0:tall, :D].astype(jnp.float32), LRATE)
        own = slice(seq * rows, (seq + 1) * rows)
        middle = quarters_ref[seq, tall : tall + rows, :].astype(jnp.float32)
        renew(2, (own,), middle, LRATE)
        bottom = quarters_ref[seq, tall + rows :, :].astype(jnp.float32)
        for part in range(rows // 16):
            first = seq * rows + part * 16
            lanes = slice(part * LANES, (part + 1) * LANES)
            renew(1, (slice(first, first + 16),), bottom[:, lanes], LRATE)
            lanes = slice(D // 2 + part * LANES, D // 2 + (part + 1) * LANES)
            turned_ref[first : first + 16] = bottom[:, lanes]
        some = tall // seqs
        side_ref[seq * some : (seq + 1) * some] = turned_ref[seq * rows : seq * rows + some]
    width = inputs[9].shape[1]
    turned_ref[seqs * rows :] = jnp.zeros_like(turned_ref[seqs * rows :])
    side_ref[tall:] = jnp.zeros_like(side_ref[tall:])
    everything = (slice(None),)
    renew(3, everything, turned_ref[...].T[0 : CONV + 3 + STATE, 0:width], CHANNEL_LRATE)
    gains = side_ref[...].T[:, 0:tall]
    renew(4, everything, jnp.concatenate([gains[-1:], gains[-3:-1]], axis=0), LRATE)
    router_lanes = slice(SIDE_LANE, SIDE_LANE + inputs[15].shape[0])
    renew(5, everything, side_ref[...].T[router_lanes, 0:tall], LRATE)


def update_all(quarters, sums, states):
    vmem = pl.BlockSpec(memory_space=pltpu.VMEM)
    flat = [part for state in states for part in state]
    tall, rows = pack_heights()
    height = -(-quarters.shape[0] * rows // LANES) * LANES
    return pl.pallas_call(
        update_kernel,
        out_shape=tuple(jax.ShapeDtypeStruct(part.shape, part.dtype) for part in flat),
        in_specs=[vmem] * (2 + len(flat)),
        out_specs=(vmem,) * len(flat),
        scratch_shapes=[
            pltpu.VMEM((height, LANES), jnp.float32),
            pltpu.VMEM((-(-tall // LANES) * LANES, LANES), jnp.float32),
        ],
        compiler_params=pltpu.CompilerParams(vmem_limit_bytes=VMEM_LIMIT),
        name="update_all",
    )(quarters, sums, *flat)


def pick_slots(slot_ref, block, slots):
    numbers = lax.broadcasted_iota(jnp.int32, (slots, slot_ref.shape[1]), 0)
    return (numbers == slot_ref[pl.ds(block, 1)]).astype(jnp.float32).astype(jnp.bfloat16)


def natural_place(block, sizes):
    return unravel(block, tuple(sizes[a] for a in NATURAL))


def rows_to_slots(sizes, capacity, slot_ref, all_ref, slots_ref):
    experts_here = slots_ref.shape[0]

    def one(block, carry):
        select = pick_slots(slot_ref, block, experts_here * capacity)
        picked = matmul(select, all_ref[block]).astype(jnp.bfloat16)
        first = pl.multiple_of(block * capacity, capacity)
        for expert in range(experts_here):
            slots_ref[expert, pl.ds(first, capacity)] = picked[
                expert * capacity : (expert + 1) * capacity
            ]
        return carry

    lax.fori_loop(0, slot_ref.shape[0], one, 0, unroll=8)


def slots_to_rows(sizes, capacity, slot_ref, slots_ref, full_ref):
    experts_here = slots_ref.shape[0]

    def one(block, carry):
        select = pick_slots(slot_ref, block, experts_here * capacity)
        first = pl.multiple_of(block * capacity, capacity)
        held = jnp.concatenate(
            [slots_ref[expert, pl.ds(first, capacity)] for expert in range(experts_here)], axis=0
        )
        full_ref[natural_place(block, sizes)] = matmul_tn(select, held).astype(jnp.bfloat16)
        return carry

    lax.fori_loop(0, slot_ref.shape[0], one, 0, unroll=8)


def flat_gather_semaphores(devices, rows):
    copies = (devices - 1) * len(split_rows(rows, GATHER_ORDERS))
    return [pltpu.SemaphoreType.DMA((copies,)), pltpu.SemaphoreType.DMA((copies,))]


def moe_forward_kernel(
    sizes,
    pairs,
    capacity,
    own_ref,
    slot_ref,
    master_ref,
    result_ref,
    arrived_ref,
    before_ref,
    weights_ref,
    wide_ref,
    wide_sem,
    all_ref,
    part_ref,
    full_ref,
    local_sem,
    *scratch,
):
    fetch = pltpu.make_async_copy(master_ref, wide_ref, wide_sem)
    fetch.start()
    pieces = split_rows(own_ref.shape[0], GATHER_ORDERS)
    gather_kernel(sizes, pieces, own_ref, all_ref, local_sem, scratch[0], scratch[1])
    scatter = Scatter(sizes, pairs, full_ref, result_ref, scratch[2:], False)
    fetch.wait()
    rows_to_slots(sizes, capacity, slot_ref, all_ref, arrived_ref)

    def expert(number, carry):
        for side in range(2):
            weights_ref[side, number] = wide_ref[side, number].astype(jnp.bfloat16)
        before = matmul_nt(arrived_ref[number], weights_ref[0, number])
        before_ref[number] = before
        inner = jax.nn.gelu(before).astype(jnp.bfloat16)
        part_ref[number] = matmul(inner, weights_ref[1, number]).astype(jnp.bfloat16)
        return carry

    lax.fori_loop(0, weights_ref.shape[1], expert, 0)
    slots_to_rows(sizes, capacity, slot_ref, part_ref, full_ref)
    for pair in range(pairs):
        scatter.launch(pair, 0)
    wave(pairs, 4, scatter.advance)
    scatter.finish()


def moe_forward(rows, slots, weights, capacity, collective_id):
    sizes = axis_sizes()
    natural = tuple(sizes[a] for a in NATURAL)
    pairs = rows.shape[0] // SPAN
    _, experts_here, hidden, _ = weights.shape
    held = (experts_here, slots.shape[0] * capacity)
    vmem = pl.BlockSpec(memory_space=pltpu.VMEM)
    return pl.pallas_call(
        functools.partial(moe_forward_kernel, sizes, pairs, capacity),
        out_shape=(
            jax.ShapeDtypeStruct(rows.shape, jnp.float32),
            jax.ShapeDtypeStruct(held + (D,), jnp.bfloat16),
            jax.ShapeDtypeStruct(held + (hidden,), jnp.float32),
            jax.ShapeDtypeStruct(weights.shape, jnp.bfloat16),
        ),
        in_specs=[vmem, vmem, pl.BlockSpec(memory_space=pl.ANY)],
        out_specs=(vmem,) * 4,
        scratch_shapes=[
            pltpu.VMEM(weights.shape, jnp.float32),
            pltpu.SemaphoreType.DMA,
            pltpu.VMEM((slots.shape[0],) + rows.shape, jnp.bfloat16),
            pltpu.VMEM(held + (D,), jnp.bfloat16),
            pltpu.VMEM(natural + rows.shape, jnp.bfloat16),
            pltpu.SemaphoreType.DMA,
        ]
        + flat_gather_semaphores(slots.shape[0], rows.shape[0])
        + scatter_scratch(sizes, pairs, D, False),
        compiler_params=pltpu.CompilerParams(
            collective_id=collective_id, has_side_effects=True, vmem_limit_bytes=VMEM_LIMIT
        ),
        name="moe_forward",
    )(rows, slots, weights)


def moe_backward_kernel(
    sizes,
    pairs,
    capacity,
    own_ref,
    slot_ref,
    weights_ref,
    arrived_ref,
    before_ref,
    result_ref,
    grads_ref,
    square_ref,
    all_ref,
    part_ref,
    full_ref,
    slots_ref,
    local_sem,
    *scratch,
):
    pieces = split_rows(own_ref.shape[0], GATHER_ORDERS)
    gather_kernel(sizes, pieces, own_ref, all_ref, local_sem, scratch[0], scratch[1])
    scatter = Scatter(sizes, pairs, full_ref, result_ref, scratch[2:], False)
    rows_to_slots(sizes, capacity, slot_ref, all_ref, slots_ref)

    def slope(number):
        grad_inner = matmul_nt(slots_ref[number], weights_ref[1, number])
        return jax.vjp(jax.nn.gelu, before_ref[number])[1](grad_inner)[0].astype(jnp.bfloat16)

    def back(number, carry):
        part_ref[number] = matmul(slope(number), weights_ref[0, number]).astype(jnp.bfloat16)
        return carry

    experts_here = weights_ref.shape[1]
    lax.fori_loop(0, experts_here, back, 0)
    slots_to_rows(sizes, capacity, slot_ref, part_ref, full_ref)
    for pair in range(pairs):
        scatter.launch(pair, 0)

    def weight_grads(number, total):
        grad_up = matmul_tn(slope(number), arrived_ref[number])
        inner = jax.nn.gelu(before_ref[number]).astype(jnp.bfloat16)
        grad_down = matmul_tn(inner, slots_ref[number])
        grads_ref[0, number] = grad_up
        grads_ref[1, number] = grad_down
        return total + jnp.sum(grad_up * grad_up) + jnp.sum(grad_down * grad_down)

    total = jnp.float32(0.0)
    turns = pairs + 3
    for turn in range(turns):
        for phase in range(3, -1, -1):
            if 0 <= turn - phase < pairs:
                scatter.advance(turn - phase, phase)
        first, last = (experts_here * turn // (turns - 1), experts_here * (turn + 1) // (turns - 1))
        if last > first and first < experts_here:
            total = lax.fori_loop(first, min(last, experts_here), weight_grads, total)
    square_ref[...] = jnp.full(square_ref.shape, total, jnp.float32)
    scatter.finish()


def moe_backward(rows, slots, weights, arrived, before, capacity, collective_id):
    sizes = axis_sizes()
    natural = tuple(sizes[a] for a in NATURAL)
    pairs = rows.shape[0] // SPAN
    vmem = pl.BlockSpec(memory_space=pltpu.VMEM)
    return pl.pallas_call(
        functools.partial(moe_backward_kernel, sizes, pairs, capacity),
        out_shape=(
            jax.ShapeDtypeStruct(rows.shape, jnp.float32),
            jax.ShapeDtypeStruct(weights.shape, jnp.float32),
            jax.ShapeDtypeStruct((8, LANES), jnp.float32),
        ),
        in_specs=[vmem] * 5,
        out_specs=(vmem,) * 3,
        scratch_shapes=[
            pltpu.VMEM((slots.shape[0],) + rows.shape, jnp.bfloat16),
            pltpu.VMEM(arrived.shape, jnp.bfloat16),
            pltpu.VMEM(natural + rows.shape, jnp.bfloat16),
            pltpu.VMEM(arrived.shape, jnp.bfloat16),
            pltpu.SemaphoreType.DMA,
        ]
        + flat_gather_semaphores(slots.shape[0], rows.shape[0])
        + scatter_scratch(sizes, pairs, D, False),
        compiler_params=pltpu.CompilerParams(
            collective_id=collective_id, has_side_effects=True, vmem_limit_bytes=VMEM_LIMIT
        ),
        name="moe_backward",
    )(rows, slots, weights, arrived, before)


def from_behind(value, axis, by):
    devices = lax.axis_size(axis)
    pairs = [(i, i + by) for i in range(devices) if 0 <= i + by < devices]
    return lax.ppermute(value, axis, pairs)


def matmul(left, right):
    return jnp.dot(left, right, preferred_element_type=jnp.float32)


def matmul_nt(left, right):
    return lax.dot_general(
        left, right, (((1,), (1,)), ((), ())), preferred_element_type=jnp.float32
    )


def matmul_tn(left, right):
    return lax.dot_general(
        left, right, (((0,), (0,)), ((), ())), preferred_element_type=jnp.float32
    )


def silu_slope(preact):
    logistic = jax.nn.sigmoid(preact)
    return logistic * (1.0 + preact * (1.0 - logistic))


def inverse_rms(values):
    return lax.rsqrt(jnp.mean(values * values, axis=-1, keepdims=True) + EPS)


def norm_back(values, inv_scale, gain_row, grad_in):
    scaled = grad_in * gain_row
    grad_gain = jnp.sum(grad_in * values * inv_scale, axis=0)
    grad_values = inv_scale * scaled - values * inv_scale**3 * jnp.mean(
        scaled * values, axis=-1, keepdims=True
    )
    return (grad_values, grad_gain)


def neighbour_rows(edge_rows, offset):
    return from_behind(edge_rows, "group", offset)


def doc_layout(doc_lengths, first_pos, span_len):
    doc_ends = jnp.cumsum(doc_lengths, axis=1)
    doc_begins = doc_ends - doc_lengths
    where_at = first_pos + jnp.arange(span_len, dtype=jnp.int32)
    segment = jnp.sum((where_at[None, :, None] >= doc_ends[:, None, :]).astype(jnp.int32), axis=2)
    onehot_doc = (
        segment[:, :, None] == jnp.arange(doc_lengths.shape[1], dtype=jnp.int32)[None, None, :]
    ).astype(jnp.float32)
    weight = jnp.sum(onehot_doc / doc_lengths[:, None, :].astype(jnp.float32), axis=2)
    starting = jnp.sum(
        (where_at[None, :, None] == doc_begins[:, None, :]).astype(jnp.float32), axis=2
    )
    return (segment, weight, 1.0 - starting)


def spread_weights(doc_lengths, tokens, groups):
    ends = jnp.cumsum(doc_lengths, axis=1)
    begins = ends - doc_lengths
    shape = (tokens // SPAN, groups * SPAN)
    pair, lane = (lax.broadcasted_iota(jnp.int32, shape, axis) for axis in range(2))
    where_at = (lane // SPAN * tokens + pair * SPAN + lane % SPAN)[:, None, :]
    total = jnp.zeros((shape[0], doc_lengths.shape[0], shape[1]), jnp.float32)
    for doc in range(doc_lengths.shape[1]):
        inside = (where_at >= begins[None, :, doc, None]) & (where_at < ends[None, :, doc, None])
        share = 1.0 / doc_lengths[:, doc].astype(jnp.float32)
        total = total + jnp.where(inside, share[None, :, None], 0.0)
    return total.reshape(-1, shape[1])


def lane_copies(columns):
    return jnp.broadcast_to(columns[..., None], columns.shape + (LANES,))


def mixer_forward(embedded, segment, keeping, weight_in, weight_x, weight_out, channel, gain_row):
    tokens = embedded.shape[0]
    scale_in = inverse_rms(embedded)
    normed = (embedded * scale_in * gain_row).astype(jnp.bfloat16)
    projected_in = matmul(normed, weight_in)
    conv_input = projected_in[:, :DI].astype(jnp.bfloat16)
    gate_z = projected_in[:, DI:]
    rim_rows = neighbour_rows(conv_input[tokens - CONV + 1 :].astype(jnp.float32), 1)
    padded = jnp.concatenate([rim_rows, conv_input.astype(jnp.float32)])
    same_doc = [
        (segment[conv_tap : conv_tap + tokens] == segment[CONV - 1 :]).astype(jnp.float32)[:, None]
        for conv_tap in range(CONV)
    ]
    conv_out = channel[CONV] + jnp.zeros_like(padded[CONV - 1 :])
    for conv_tap in range(CONV):
        conv_out = (
            conv_out + channel[conv_tap] * padded[conv_tap : conv_tap + tokens] * same_doc[conv_tap]
        )
    activated = jax.nn.silu(conv_out)
    act_low = activated.astype(jnp.bfloat16)
    projected = matmul(act_low, weight_x[:, : RANK + 2 * STATE])
    dt_input = projected[:, :RANK].astype(jnp.bfloat16)
    dt_pre = matmul_nt(dt_input, weight_x[:, RANK + 2 * STATE :])
    step_size = jax.nn.softplus(dt_pre + channel[CONV + 1])
    decay_rates = -jnp.exp(channel[CONV + 3 :])
    b_wide = lane_copies(projected[:, RANK : RANK + STATE])
    c_wide = lane_copies(projected[:, RANK + STATE :])
    keep_wide = lane_copies(keeping)
    reached, incoming = scan_forward(
        step_size, activated, b_wide, c_wide, keep_wide, decay_rates, 4
    )
    scanned = reached + channel[CONV + 2] * activated
    gate_act = jax.nn.silu(gate_z)
    gated = (scanned * gate_act).astype(jnp.bfloat16)
    mixed_out = embedded + matmul(gated, weight_out)
    kept_values = (
        scale_in,
        normed,
        gate_z,
        padded,
        same_doc,
        conv_out,
        activated,
        act_low,
        b_wide,
        c_wide,
        keep_wide,
        dt_input,
        dt_pre,
        step_size,
        decay_rates,
        incoming,
        scanned,
        gate_act,
        gated,
    )
    return (mixed_out, kept_values)


def mixer_backward(
    grad_out, embedded, kept_values, weight_in, weight_x, weight_out, channel, gain_row
):
    (
        scale_in,
        normed,
        gate_z,
        padded,
        same_doc,
        conv_out,
        activated,
        act_low,
        b_wide,
        c_wide,
        keep_wide,
        dt_input,
        dt_pre,
        step_size,
        decay_rates,
        incoming,
        scanned,
        gate_act,
        gated,
    ) = kept_values
    tokens = embedded.shape[0]
    grad_low = grad_out.astype(jnp.bfloat16)
    grad_wout = matmul_tn(gated, grad_low)
    grad_gated = matmul_nt(grad_low, weight_out)
    grad_scan = grad_gated * gate_act
    grad_z = grad_gated * scanned * silu_slope(gate_z)
    grad_skip = jnp.sum(grad_scan * activated, axis=0)
    along_b, decayed, wide_gb, wide_gc, grad_rates_log = scan_backward(
        step_size, activated, b_wide, c_wide, keep_wide, decay_rates, incoming, grad_scan, 5
    )
    grad_b = jnp.sum(wide_gb, axis=2)
    grad_c = jnp.sum(wide_gc, axis=2)
    grad_act = grad_scan * channel[CONV + 2] + along_b * step_size
    grad_step = decayed + along_b * activated
    grad_dtpre = grad_step * jax.nn.sigmoid(dt_pre + channel[CONV + 1])
    grad_dtbias = jnp.sum(grad_dtpre, axis=0)
    grad_dtlow = grad_dtpre.astype(jnp.bfloat16)
    grad_wdt = matmul_tn(grad_dtlow, dt_input)
    grad_dtin = matmul(grad_dtlow, weight_x[:, RANK + 2 * STATE :])
    grad_proj = jnp.concatenate([grad_dtin, grad_b, grad_c], axis=1).astype(jnp.bfloat16)
    grad_wx = jnp.concatenate([matmul_tn(act_low, grad_proj), grad_wdt], axis=1)
    grad_act = grad_act + matmul_nt(grad_proj, weight_x[:, : RANK + 2 * STATE])
    grad_conv = grad_act * silu_slope(conv_out)
    grad_taps = [
        jnp.sum(grad_conv * padded[conv_tap : conv_tap + tokens] * same_doc[conv_tap], axis=0)
        for conv_tap in range(CONV)
    ]
    grad_padded = sum(
        (
            jnp.pad(
                channel[conv_tap] * grad_conv * same_doc[conv_tap],
                ((conv_tap, CONV - 1 - conv_tap), (0, 0)),
            )
            for conv_tap in range(CONV)
        )
    )
    from_next = neighbour_rows(grad_padded[: CONV - 1], -1)
    grad_input = grad_padded[CONV - 1 :] + jnp.pad(from_next, ((tokens - CONV + 1, 0), (0, 0)))
    grad_both = jnp.concatenate([grad_input, grad_z], axis=1).astype(jnp.bfloat16)
    grad_win = matmul_tn(normed, grad_both)
    grad_normed = matmul_nt(grad_both, weight_in)
    grad_embed, grad_gain = norm_back(embedded, scale_in, gain_row, grad_normed)
    grad_channel = jnp.concatenate(
        [
            jnp.stack(grad_taps),
            jnp.sum(grad_conv, axis=0)[None],
            grad_dtbias[None],
            grad_skip[None],
            grad_rates_log,
        ]
    )
    return (grad_out + grad_embed, grad_win, grad_wx, grad_wout, grad_channel, grad_gain)


def choice_of(route_flat, experts_total):
    return (route_flat[:, None] == jnp.arange(experts_total, dtype=jnp.int32)[None, :]).astype(
        jnp.float32
    )


def dispatch_slots(routes, first_expert, experts_here, capacity):
    tokens = routes.shape[1]
    chosen = (
        routes[:, :, None] == first_expert + jnp.arange(experts_here, dtype=jnp.int32)
    ).astype(jnp.float32)
    order = jnp.arange(tokens, dtype=jnp.int32)
    ahead = (order[None, :] < order[:, None]).astype(jnp.float32)
    earlier = jnp.einsum("ij,bje->bie", ahead, chosen, preferred_element_type=jnp.float32)
    rank = jnp.sum(earlier * chosen, axis=2).astype(jnp.int32)
    local = routes - first_expert
    return jnp.where((local >= 0) & (local < experts_here), local * capacity + rank, -1)


def dispatch_table(slot, experts_here, capacity):
    return (
        slot[:, None, :] == jnp.arange(experts_here * capacity, dtype=jnp.int32)[None, :, None]
    ).astype(jnp.bfloat16)


def to_slots(select, rows, experts_here, capacity):
    slots = jnp.einsum("bst,btd->bsd", select, rows, preferred_element_type=jnp.float32)
    slots = slots.astype(jnp.bfloat16).reshape(-1, experts_here, capacity, D)
    return jnp.swapaxes(slots, 0, 1).reshape(experts_here, -1, D)


def to_rows(select, slots, capacity):
    experts_here = slots.shape[0]
    slots = slots.astype(jnp.bfloat16).reshape(experts_here, -1, capacity, D)
    slots = jnp.swapaxes(slots, 0, 1).reshape(-1, experts_here * capacity, D)
    return jnp.einsum("bst,bsd->btd", select, slots, preferred_element_type=jnp.float32).astype(
        jnp.bfloat16
    )


def packed_rows(arrays, devices_seq):
    flat = jnp.concatenate([part.reshape(-1) for part in arrays])
    unit = devices_seq * SPAN * D
    size = -(-flat.shape[0] // unit) * unit
    return jnp.pad(flat, (0, size - flat.shape[0])).reshape(-1, D)


def unpacked(flat, shapes):
    parts, first = ([], 0)
    for shape in shapes:
        size = 1
        for extent in shape:
            size *= extent
        parts.append(flat[..., first : first + size].reshape(flat.shape[:-1] + shape))
        first += size
    return parts


def whole_of(shards, axis):
    moved_axis = jnp.moveaxis(shards, 0, axis)
    shape = moved_axis.shape
    return moved_axis.reshape(shape[:axis] + (shape[axis] * shape[axis + 1],) + shape[axis + 2 :])


def shards_of(whole, axis, count):
    shape = whole.shape
    split = whole.reshape(shape[:axis] + (count, shape[axis] // count) + shape[axis + 1 :])
    return jnp.moveaxis(split, axis, 0)


def renewed(master, moment, average, gradient, clip_factor, rate):
    scaled = clip_factor * gradient
    moment_new = MOMENTUM * moment + scaled
    master_new = master - rate * (scaled + MOMENTUM * moment_new)
    return (master_new, moment_new, EMA_KEEP * average + (1.0 - EMA_KEEP) * master_new)


def per_device(
    token_ids,
    target_ids,
    doc_lengths,
    expert_ids,
    vocab_table,
    vocab_table_mom,
    vocab_table_ema,
    mixer_in,
    mixer_in_mom,
    mixer_in_ema,
    mixer_x,
    mixer_x_mom,
    mixer_x_ema,
    mixer_out,
    mixer_out_mom,
    mixer_out_ema,
    channel,
    channel_mom,
    channel_ema,
    norm_gains,
    norm_gains_mom,
    norm_gains_ema,
    router,
    router_mom,
    router_ema,
    experts,
    experts_mom,
    experts_ema,
):
    seq_count = lax.axis_size("seq")
    group_count = lax.axis_size("group")
    seq_index = lax.axis_index("seq")
    group_index = lax.axis_index("group")
    devices = seq_count * group_count
    tokens = token_ids.shape[1]
    sequences = token_ids.shape[0]
    experts_total = router.shape[1]
    local_experts = experts.shape[1]
    capacity = max(2, 2 * tokens // experts_total)
    own_vocab = vocab_table.shape[0]
    routes = expert_ids.reshape(1, tokens)
    numbers = jnp.concatenate([token_ids, target_ids, routes])
    numbers = jnp.pad(numbers, ((0, -numbers.shape[0] % 8), (0, 0)))
    mixer_parts = (mixer_in, mixer_x, mixer_out, channel, norm_gains, router)
    part_axes = (0, 0, 0, 1, 1, 0)
    part_shapes = [part.shape for part in mixer_parts]
    table_low = vocab_table.astype(jnp.bfloat16)
    experts_low = experts.astype(jnp.bfloat16)
    up_weight, down_weight = (experts_low[0], experts_low[1])
    vocab_start = (seq_index * group_count + group_index) * own_vocab
    column_ids = jnp.arange(own_vocab, dtype=jnp.int32)
    wide_rows = DI // (seq_count * group_count)
    compact = devices * tokens <= 4096 and 2 * DI == seq_count * D and 16 * wide_rows == D
    if compact:
        own_pack = own_pack_of(mixer_parts, seq_index, seq_count)
        numbers_all, packs, embedded, table_padded, table_turned, token_local, target_local = (
            start_all(numbers, own_pack, vocab_table, 1)
        )
        numbers_all = numbers_all.reshape((devices,) + numbers.shape)
        packs = packs.reshape((seq_count, group_count) + own_pack.shape)
        channel_vals, gain_vals, router_low = small_weights(packs, experts_total)
        router_vals = router_low.astype(jnp.float32)
    else:
        numbers_all = share_small(numbers, 1)
    from_groups = jnp.swapaxes(numbers_all[:group_count, : 2 * sequences], 0, 1)
    tokens_all = from_groups[:sequences].reshape(-1)
    targets_all = from_groups[sequences:].reshape(-1)
    routes_all = numbers_all[:, 2 * sequences]
    if not compact:
        pack = packed_rows([part.astype(jnp.bfloat16) for part in mixer_parts], seq_count)
        pack_rows = pack.shape[0] // seq_count
        own_pack = lax.dynamic_slice_in_dim(pack, seq_index * pack_rows, pack_rows, 0)
        packs = gather_all(own_pack, 2).reshape(seq_count, group_count, pack_rows * D)
        shards = unpacked(jnp.swapaxes(packs, 0, 1).reshape(group_count, -1), part_shapes)
        weight_in, weight_x, weight_out, channel_low, gains_low, router_low = [
            whole_of(shard, axis) for shard, axis in zip(shards, part_axes)
        ]
        held_token = (tokens_all - vocab_start)[:, None] == column_ids[None, :]
        held_token = held_token.astype(jnp.bfloat16)
        looked_up = matmul(held_token, table_low).astype(jnp.bfloat16)
        embedded = scatter_all(looked_up.reshape(devices, tokens, D), 3)
        channel_vals = channel_low.astype(jnp.float32)
        gain_vals = gains_low.astype(jnp.float32)
        router_vals = router_low.astype(jnp.float32)

    segment_all, weight_all, keep_all = doc_layout(
        doc_lengths, group_index * tokens - CONV + 1, tokens + CONV - 1
    )
    own_segment = lax.dynamic_index_in_dim(segment_all, seq_index, 0, keepdims=False)
    keeping = lax.dynamic_index_in_dim(keep_all, seq_index, 0, keepdims=False)[CONV - 1 :]
    own_weight = lax.dynamic_index_in_dim(weight_all, seq_index, 0, keepdims=False)[CONV - 1 :]
    chosen = choice_of(expert_ids.reshape(-1), experts_total)
    if compact:
        same = [
            (own_segment[tap : tap + tokens] == own_segment[CONV - 1 :]).astype(jnp.float32)
            for tap in range(CONV)
        ]
        masks = jnp.stack(same + [keeping], axis=1)
        vectors = jnp.pad(channel_vals, ((0, 1), (0, 0)))
        mixed_out, moe_in, probability, *saved = mixer_forward_all(
            embedded, packs, vectors, gain_vals, masks, router_low, 4
        )
        probability = probability[:, :experts_total]
        scale_mid = inverse_rms(mixed_out)
    else:
        mixed_out, kept_values = mixer_forward(
            embedded,
            own_segment,
            keeping,
            weight_in,
            weight_x,
            weight_out,
            channel_vals,
            gain_vals[0],
        )
        scale_mid = inverse_rms(mixed_out)
        moe_in = (mixed_out * scale_mid * gain_vals[1]).astype(jnp.bfloat16)
        probability = jax.nn.softmax(matmul(moe_in, router_low), axis=-1)
    slots = dispatch_slots(routes_all, seq_index * local_experts, local_experts, capacity)
    gate_value = jnp.sum(probability * chosen, axis=1)
    if compact:
        returned, arrived, before, experts_low = moe_forward(
            moe_in, slots, experts, capacity, 11
        )
    else:
        select = dispatch_table(slots, local_experts, capacity)
        arrived = to_slots(select, gather_all(moe_in, 6), local_experts, capacity)
        before = jnp.einsum("erd,efd->erf", arrived, up_weight, preferred_element_type=jnp.float32)
        inner_act = jax.nn.gelu(before).astype(jnp.bfloat16)
        partial_out = jnp.einsum(
            "erf,efd->erd", inner_act, down_weight, preferred_element_type=jnp.float32
        )
        returned = scatter_all(to_rows(select, partial_out, capacity), 3)
    expert_value = returned.astype(jnp.bfloat16).astype(jnp.float32)
    branch = gate_value[:, None] * expert_value
    hidden = mixed_out + branch
    scale_out = inverse_rms(hidden)
    final_low = (hidden * scale_out * gain_vals[2]).astype(jnp.bfloat16)
    if compact:
        all_final, stats = head_forward(final_low, table_padded, own_vocab, target_local, 7)
        own_entropy = (stats[0] - stats[1]).reshape(-1, seq_count, group_count, SPAN)
        own_entropy = lax.dynamic_index_in_dim(own_entropy, seq_index, 1, keepdims=False)
        own_entropy = lax.dynamic_index_in_dim(own_entropy, group_index, 1, keepdims=False)
        loss_part = jnp.sum(own_weight * own_entropy.reshape(-1))
        grad_final, table_grad = head_backward(
            all_final,
            table_padded,
            table_turned,
            own_vocab,
            target_local,
            stats[0],
            spread_weights(doc_lengths, tokens, group_count),
            10,
        )
    else:
        all_final = gather_all(final_low, 6).reshape(devices * tokens, D)
        valid_cols = vocab_start + column_ids < VOCAB_REAL
        hit_target = (targets_all - vocab_start)[:, None] == column_ids[None, :]
        logits = jnp.where(valid_cols[None, :], matmul_nt(all_final, table_low), -1e30)
        largest = jnp.max(logits, axis=1)
        exp_total = jnp.sum(jnp.exp(logits - largest[:, None]), axis=1)
        picked = jnp.sum(jnp.where(hit_target, logits, 0.0), axis=1)
        parts = jnp.stack([largest, exp_total, picked]).reshape(3, devices, tokens)
        parts = jnp.pad(jnp.swapaxes(parts, 0, 1), ((0, 0), (0, 5), (0, 0)))
        levels, entropy = combine_stats(parts, 7)
        log_total = levels[:, 0].reshape(-1)
        loss_part = jnp.sum(own_weight * entropy[0])
        _, every_weight, _ = doc_layout(doc_lengths, 0, tokens * group_count)
        row_weight = every_weight.reshape(-1)
        grad_logits = (
            row_weight[:, None]
            * (jnp.exp(logits - log_total[:, None]) - hit_target.astype(jnp.float32))
        ).astype(jnp.bfloat16)
        table_grad = matmul_tn(grad_logits, all_final)
        grad_rows = matmul(grad_logits, table_low).astype(jnp.bfloat16)
        grad_final = scatter_all(grad_rows.reshape(devices, tokens, D), 3)
    grad_hidden, grad_gain_out = norm_back(hidden, scale_out, gain_vals[2], grad_final)
    grad_gate = jnp.sum(grad_hidden * expert_value, axis=1)
    grad_expert = (gate_value[:, None] * grad_hidden).astype(jnp.bfloat16)
    if compact:
        grad_moe_in, grad_experts, square_tile = moe_backward(
            grad_expert, slots, experts_low, arrived, before, capacity, 12
        )
        experts_square = square_tile[0, 0]
    else:
        grad_arrived = to_slots(select, gather_all(grad_expert, 6), local_experts, capacity)
        grad_inner = jnp.einsum(
            "erd,efd->erf", grad_arrived, down_weight, preferred_element_type=jnp.float32
        )
        grad_before = jax.vjp(jax.nn.gelu, before)[1](grad_inner)[0].astype(jnp.bfloat16)
        grad_down = jnp.einsum(
            "erf,erd->efd", inner_act, grad_arrived, preferred_element_type=jnp.float32
        )
        grad_up = jnp.einsum("erf,erd->efd", grad_before, arrived, preferred_element_type=jnp.float32)
        grad_part = jnp.einsum(
            "erf,efd->erd", grad_before, up_weight, preferred_element_type=jnp.float32
        )
        grad_moe_in = scatter_all(to_rows(select, grad_part, capacity), 3)
        grad_experts = jnp.stack([grad_up, grad_down])
        experts_square = jnp.sum(grad_experts * grad_experts)
    grad_moe_in = grad_moe_in.astype(jnp.bfloat16).astype(jnp.float32)
    grad_router_logits = (grad_gate * gate_value)[:, None] * (chosen - probability)
    grad_moe_in = grad_moe_in + jnp.dot(
        grad_router_logits, router_vals.T, precision=HIGHEST
    )
    grad_router = jnp.dot(moe_in.astype(jnp.float32).T, grad_router_logits, precision=HIGHEST)
    grad_mid, grad_gain_mid = norm_back(mixed_out, scale_mid, gain_vals[1], grad_moe_in)
    grad_mixed = grad_hidden + grad_mid
    if compact:
        gain_columns = jnp.stack([grad_gain_out * 0.0, grad_gain_mid, grad_gain_out], axis=1)
        grad_embedded, grad_pack = mixer_backward_all(
            grad_mixed,
            side_lanes(grad_router, gain_columns),
            embedded,
            packs,
            vectors,
            gain_vals,
            masks,
            saved,
            5,
        )
    else:
        grad_embedded, grad_win, grad_wx, grad_wout, grad_channel, grad_gain_in = mixer_backward(
            grad_mixed,
            embedded,
            kept_values,
            weight_in,
            weight_x,
            weight_out,
            channel_vals,
            gain_vals[0],
        )
        grad_gains = jnp.stack([grad_gain_in, grad_gain_mid, grad_gain_out])
        mixer_wholes = (grad_win, grad_wx, grad_wout, grad_channel, grad_gains, grad_router)
    if compact:
        scalars = jnp.concatenate(
            [jnp.full((4, LANES), experts_square), jnp.full((4, LANES), loss_part)], axis=0
        )
        table_grad, quarters, sums = finish_all(
            grad_embedded,
            grad_pack,
            token_local,
            table_grad,
            scalars,
            9,
        )
        table_grad = table_grad[:own_vocab]
    else:
        all_grad_embed = gather_all(grad_embedded.astype(jnp.bfloat16), 6).reshape(-1, D)
        table_grad = table_grad + matmul_tn(held_token, all_grad_embed)
        wholes_low = [
            shards_of(whole.astype(jnp.bfloat16), axis, group_count).reshape(group_count, -1)
            for whole, axis in zip(mixer_wholes, part_axes)
        ]
        flat = jnp.concatenate(wholes_low, axis=1)
        flat = jnp.pad(flat, ((0, 0), (0, seq_count * pack_rows * D - flat.shape[1])))
        flat = jnp.swapaxes(flat.reshape(group_count, seq_count, pack_rows, D), 0, 1)
        own_quarter = scatter_all(flat.reshape(devices, pack_rows, D), 8)
        quarters = lax.all_gather(own_quarter, "seq", axis=0, tiled=True).reshape(-1)
        mixer_grads = unpacked(quarters, part_shapes)
        local_square = (
            jnp.sum(table_grad * table_grad) + experts_square + jnp.sum(own_quarter * own_quarter)
        )
        two = jnp.concatenate(
            [jnp.full((4, LANES), local_square), jnp.full((4, LANES), loss_part)], axis=0
        )
        sums = jnp.sum(share_small(two, 9), axis=0)
    total_square, loss_sum = (sums[0, 0], sums[4, 0])
    grad_norm = jnp.sqrt(total_square)
    clip_factor = jnp.minimum(1.0, CLIP / (grad_norm + 1e-06))
    table_new = renewed(
        vocab_table, vocab_table_mom, vocab_table_ema, table_grad, clip_factor, LRATE
    )
    mixer_states = (
        (mixer_in, mixer_in_mom, mixer_in_ema),
        (mixer_x, mixer_x_mom, mixer_x_ema),
        (mixer_out, mixer_out_mom, mixer_out_ema),
        (channel, channel_mom, channel_ema),
        (norm_gains, norm_gains_mom, norm_gains_ema),
        (router, router_mom, router_ema),
    )
    if compact:
        turned_states = mixer_states[:5] + (tuple(part.T for part in mixer_states[5]),)
        fresh = update_all(quarters, sums, turned_states)
        fresh = list(fresh[:15]) + [part.T for part in fresh[15:]]
    else:
        rates = (LRATE, LRATE, LRATE, CHANNEL_LRATE, LRATE, LRATE)
        fresh = [
            part
            for state, gradient, rate in zip(mixer_states, mixer_grads, rates)
            for part in renewed(*state, gradient, clip_factor, rate)
        ]
    experts_new = renewed(experts, experts_mom, experts_ema, grad_experts, clip_factor, LRATE)
    return (
        loss_sum,
        grad_norm,
        branch.reshape(1, tokens, D),
        table_new[0],
        table_new[1],
        table_new[2],
        *fresh,
        experts_new[0],
        experts_new[1],
        experts_new[2],
    )


def solution(mesh):
    placed = (
        P(None, "group"),
        P(None, "group"),
        P(),
        P("seq", "group", None),
        P(("seq", "group"), None),
        P(("seq", "group"), None),
        P(("seq", "group"), None),
        P("group", None),
        P("group", None),
        P("group", None),
        P("group", None),
        P("group", None),
        P("group", None),
        P("group", None),
        P("group", None),
        P("group", None),
        P(None, "group"),
        P(None, "group"),
        P(None, "group"),
        P(None, "group"),
        P(None, "group"),
        P(None, "group"),
        P("group", None),
        P("group", None),
        P("group", None),
        P(None, "seq", "group", None),
        P(None, "seq", "group", None),
        P(None, "seq", "group", None),
    )
    return jax.shard_map(
        per_device,
        mesh=mesh,
        in_specs=placed,
        out_specs=(
            P(),
            P(),
            P("seq", "group", None),
            P(("seq", "group"), None),
            P(("seq", "group"), None),
            P(("seq", "group"), None),
            P("group", None),
            P("group", None),
            P("group", None),
            P("group", None),
            P("group", None),
            P("group", None),
            P("group", None),
            P("group", None),
            P("group", None),
            P(None, "group"),
            P(None, "group"),
            P(None, "group"),
            P(None, "group"),
            P(None, "group"),
            P(None, "group"),
            P("group", None),
            P("group", None),
            P("group", None),
            P(None, "seq", "group", None),
            P(None, "seq", "group", None),
            P(None, "seq", "group", None),
        ),
        check_vma=False,
    )
```
